32 devices in a mesh: clip: 8 (over y, x, core), tok: 4 (over z).
Axes of the slice: x: 2, y: 2, z: 4, core: 2. Of those that a mesh axis runs over, the one named last changes fastest.
Arguments:
- frames: bfloat16 [8, 8, 196, 768], P('clip', 'tok'), may hold values from -6 to 6
- cotangent: bfloat16 [8, 8, 196, 768], P('clip', 'tok'), may hold values from -6 to 6
- entry_weights: float32 [27648, 128], P(('clip', 'tok')), may hold values from -0.21875 to 0.21875
- entry_momentum: float32 [27648, 128], P(('clip', 'tok')), may hold values from -640 to 640
- entry_variance: float32 [27648, 128], P(('clip', 'tok')), may hold values from 12544 to 50176
- temporal_weights: float32 [9216, 128], P(('clip', 'tok')), may hold values from -0.3125 to 0.3125
- temporal_momentum: float32 [9216, 128], P(('clip', 'tok')), may hold values from -640 to 640
- temporal_variance: float32 [9216, 128], P(('clip', 'tok')), may hold values from 12544 to 50176
- spatial_weights: float32 [4608, 128], P(('clip', 'tok')), may hold values from -1.75 to 1.75
- spatial_momentum: float32 [4608, 128], P(('clip', 'tok')), may hold values from -96 to 96
- spatial_variance: float32 [4608, 128], P(('clip', 'tok')), may hold values from 250.88 to 1003.52
- widen_weights: float32 [18432, 128], P(('clip', 'tok')), may hold values from -0.21875 to 0.21875
- widen_momentum: float32 [18432, 128], P(('clip', 'tok')), may hold values from -192 to 192
- widen_variance: float32 [18432, 128], P(('clip', 'tok')), may hold values from 1254.4 to 5017.6
- narrow_weights: float32 [18432, 128], P(('clip', 'tok')), may hold values from -0.109375 to 0.109375
- narrow_momentum: float32 [18432, 128], P(('clip', 'tok')), may hold values from -448 to 448
- narrow_variance: float32 [18432, 128], P(('clip', 'tok')), may hold values from 5017.6 to 20070.4
- norm_affine: float32 [2, 3, 768], P(None, None, ('clip', 'tok')), may hold values from -0.5 to 1.3, as said below
- affine_momentum: float32 [2, 3, 768], P(None, None, ('clip', 'tok')), may hold values from -640 to 640
- affine_variance: float32 [2, 3, 768], P(None, None, ('clip', 'tok')), may hold values from 12544 to 50176
Outputs:
- layer_output: bfloat16 [8, 8, 196, 768], P('clip', 'tok')
- input_gradient: float32 [8, 8, 196, 768], P('clip', 'tok')
- entry_updated: float32 [27648, 128], P(('clip', 'tok'))
- entry_averaged: float32 [27648, 128], P(('clip', 'tok'))
- entry_squared: float32 [27648, 128], P(('clip', 'tok'))
- temporal_updated: float32 [9216, 128], P(('clip', 'tok'))
- temporal_averaged: float32 [9216, 128], P(('clip', 'tok'))
- temporal_squared: float32 [9216, 128], P(('clip', 'tok'))
- spatial_updated: float32 [4608, 128], P(('clip', 'tok'))
- spatial_averaged: float32 [4608, 128], P(('clip', 'tok'))
- spatial_squared: float32 [4608, 128], P(('clip', 'tok'))
- widen_updated: float32 [18432, 128], P(('clip', 'tok'))
- widen_averaged: float32 [18432, 128], P(('clip', 'tok'))
- widen_squared: float32 [18432, 128], P(('clip', 'tok'))
- narrow_updated: float32 [18432, 128], P(('clip', 'tok'))
- narrow_averaged: float32 [18432, 128], P(('clip', 'tok'))
- narrow_squared: float32 [18432, 128], P(('clip', 'tok'))
- affine_updated: float32 [2, 3, 768], P(None, None, ('clip', 'tok'))
- affine_averaged: float32 [2, 3, 768], P(None, None, ('clip', 'tok'))
- affine_squared: float32 [2, 2, 768], P(None, None, ('clip', 'tok'))
- feed_squared: float32 [2, 768], P(None, ('clip', 'tok'))
The draws below stay inside these ranges and needn't reach their ends.
Inputs may be any that keep to these rules, and one draw needn't show every extreme that they name: `norm_affine`: index 0 of the first dimension holds gains, index 1 biases.
All inputs are finite; a program needn't handle non-finite values.
Results may differ from the reference program's by a relative error of at most 0.02.
The reference program's roundings to bfloat16 on the way count: a program that leaves them out, or rounds other values in their place, can miss the bound.
Values may be sent and summed in bfloat16 or wider, within the bound.
A program may use at most 192 MiB of HBM per device.

```python
import math
import jax
import jax.numpy as jnp
from jax import lax

D = 768
HEADS = 12
HEAD_DIM = 64
HID = 3072
FRAMES = 8
PATCHES = 196
STEP = 5
CLIPS = 8
TOKENS = 12544
ENTRY_ROWS = 27648
TEMPORAL_ROWS = 9216
SPATIAL_ROWS = 4608
WIDEN_ROWS = 18432


def draw_norm_affine(key, part):
    first, second = jax.random.split(key)
    gains = 1.0 + 0.1 * jnp.clip(jax.random.normal(first, (3, D), jnp.float32), -3.0, 3.0)
    shifts = 0.2 * jnp.clip(jax.random.normal(second, (3, D), jnp.float32), -2.5, 2.5)
    return jnp.stack([gains, shifts])


def steps_of(own_key, shape, shards, low, top_value):
    def one(axis_at, shards_of):
        steps = jax.random.uniform(jax.random.fold_in(jax.random.fold_in(own_key, 6), axis_at), (shards_of,), jnp.float32, low / len(shards), top_value / len(shards))
        return jnp.repeat(jnp.exp(steps), shape[axis_at] // shards_of).reshape((-1,) + (1,) * (len(shape) - axis_at - 1))

    loudness = one(*shards[0])
    for cut in shards[1:]:
        loudness = loudness * one(*cut)
    return loudness


def normal_values(rng, dims, spread, bound, pieces=(), dtype=jnp.bfloat16):
    array = jax.random.normal(rng, dims, jnp.float32) * spread
    if len(pieces) > 0:
        array = steps_of(rng, dims, pieces, -0.22, 0.18) * array
    return jnp.clip(array, min=-bound, max=bound).astype(dtype)


def setup_inputs(seed: int = 0) -> dict:
    seeds = jax.random.split(jax.random.key(seed), 21)
    return {
        "frames": normal_values(seeds[0], (CLIPS, FRAMES, PATCHES, D), 1.0, 6.0, ((0, 8), (1, 4))),
        "cotangent": normal_values(seeds[1], (CLIPS, FRAMES, PATCHES, D), 1.0, 6.0, ((0, 8), (1, 4))),
        "entry_weights": normal_values(seeds[2], (ENTRY_ROWS, 128), D ** -0.5, 0.21875, ((0, 32),), jnp.float32),
        "entry_momentum": normal_values(seeds[3], (ENTRY_ROWS, 128), (TOKENS ** 0.5), 640.0, ((0, 32),), jnp.float32),
        "entry_variance": jnp.clip(jnp.exp(math.log(50176.0) - 1.3862944 * jax.random.uniform(seeds[4], (ENTRY_ROWS, 128), jnp.float32) ** steps_of(seeds[4], (ENTRY_ROWS, 128), ((0, 32),), -0.2, 0.2)), 12544.0, 50176.0),
        "temporal_weights": normal_values(seeds[5], (TEMPORAL_ROWS, 128), (D // 2) ** -0.5, 0.3125, ((0, 32),), jnp.float32),
        "temporal_momentum": normal_values(seeds[6], (TEMPORAL_ROWS, 128), (TOKENS ** 0.5), 640.0, ((0, 32),), jnp.float32),
        "temporal_variance": jnp.clip(jnp.exp(math.log(50176.0) - 1.3862944 * jax.random.uniform(seeds[7], (TEMPORAL_ROWS, 128), jnp.float32) ** steps_of(seeds[7], (TEMPORAL_ROWS, 128), ((0, 32),), -0.2, 0.2)), 12544.0, 50176.0),
        "spatial_weights": normal_values(seeds[8], (SPATIAL_ROWS, 128), (3 * D // PATCHES) ** -0.5, 1.75, ((0, 32),), jnp.float32),
        "spatial_momentum": normal_values(seeds[9], (SPATIAL_ROWS, 128), (0.15 * TOKENS ** 0.5), 96.0, ((0, 32),), jnp.float32),
        "spatial_variance": jnp.clip(jnp.exp(math.log(1003.52) - 1.3862944 * jax.random.uniform(seeds[10], (SPATIAL_ROWS, 128), jnp.float32) ** steps_of(seeds[10], (SPATIAL_ROWS, 128), ((0, 32),), -0.2, 0.2)), 250.88, 1003.52),
        "widen_weights": normal_values(seeds[11], (WIDEN_ROWS, 128), D ** -0.5, 0.21875, ((0, 32),), jnp.float32),
        "widen_momentum": normal_values(seeds[12], (WIDEN_ROWS, 128), (0.3 * TOKENS ** 0.5), 192.0, ((0, 32),), jnp.float32),
        "widen_variance": jnp.clip(jnp.exp(math.log(5017.6) - 1.3862944 * jax.random.uniform(seeds[13], (WIDEN_ROWS, 128), jnp.float32) ** steps_of(seeds[13], (WIDEN_ROWS, 128), ((0, 32),), -0.2, 0.2)), 1254.4, 5017.6),
        "narrow_weights": normal_values(seeds[14], (WIDEN_ROWS, 128), HID ** -0.5, 0.109375, ((0, 32),), jnp.float32),
        "narrow_momentum": normal_values(seeds[15], (WIDEN_ROWS, 128), (0.65 * TOKENS ** 0.5), 448.0, ((0, 32),), jnp.float32),
        "narrow_variance": jnp.clip(jnp.exp(math.log(20070.4) - 1.3862944 * jax.random.uniform(seeds[16], (WIDEN_ROWS, 128), jnp.float32) ** steps_of(seeds[16], (WIDEN_ROWS, 128), ((0, 32),), -0.2, 0.2)), 5017.6, 20070.4),
        "norm_affine": draw_norm_affine(jax.random.fold_in(seeds[20], 71), 0),
        "affine_momentum": normal_values(seeds[18], (2, 3, D), (TOKENS ** 0.5), 640.0, ((2, 32),), jnp.float32),
        "affine_variance": jnp.clip(jnp.exp(math.log(50176.0) - 1.3862944 * jax.random.uniform(seeds[19], (2, 3, D), jnp.float32) ** steps_of(seeds[19], (2, 3, D), ((2, 32),), -0.2, 0.2)), 12544.0, 50176.0),
    }


@jax.custom_vjp
def low(v):
    return lax.optimization_barrier(v.astype(jnp.bfloat16)).astype(jnp.float32)

@jax.custom_vjp
def low_back(v):
    return v

def low_keep(v):
    return (low(v), None)

def low_pass(kept, grad):
    return (grad,)

def back_keep(v):
    return (v, None)

def back_low(kept, grad):
    return (low(grad),)
low.defvjp(low_keep, low_pass)
low_back.defvjp(back_keep, back_low)
highest = lax.Precision.HIGHEST

def matmul_high(left, right):
    return jnp.einsum('...a,ab->...b', left, right, precision=highest)

def layer_norm(values, gain, shift):
    center = values - lax.optimization_barrier(jnp.mean(values, axis=-1, keepdims=True))
    inverse = lax.rsqrt(lax.optimization_barrier(jnp.mean(center * center, axis=-1, keepdims=True)) + 1e-06)
    return center * inverse * gain + shift

def attention(merged, score_form, out_form):
    parts = merged.reshape(merged.shape[:-1] + (3, HEADS, HEAD_DIM))
    query = parts[..., 0, :, :]
    keys = parts[..., 1, :, :]
    values = parts[..., 2, :, :]
    scores = low_back(jnp.einsum(score_form, query, keys, precision=highest) * HEAD_DIM ** (-0.5))
    top = lax.optimization_barrier(jnp.max(scores, axis=-1, keepdims=True))
    expo = jnp.exp(scores - top)
    probs = low(expo / lax.optimization_barrier(jnp.sum(expo, axis=-1, keepdims=True)))
    mixed = jnp.einsum(out_form, probs, values, precision=highest)
    return low_back(low(mixed.reshape(mixed.shape[:-2] + (HEADS * HEAD_DIM,))))

def clip_layer(clip_in, entry, temporal, spatial, widen, narrow, affine):
    entry_low = low(entry).reshape(2, D, 3 * D)
    temporal_low = low(temporal).reshape(2, D, D)
    spatial_low = low(spatial).reshape(D, D)
    widen_low = low(widen).reshape(D, HID)
    narrow_low = low(narrow).reshape(HID, D)
    affine_low = low(affine)
    sent = low_back(clip_in)
    normed_t = low(layer_norm(sent, affine_low[0, 0], affine_low[1, 0]))
    merged_t = low_back(low(matmul_high(normed_t, entry_low[0])))
    mixed_t = attention(merged_t, 'fphe,gphe->phfg', 'phfg,gphe->fphe')
    first_t = low_back(low(matmul_high(mixed_t, temporal_low[0])))
    branch_t = low_back(low(matmul_high(first_t, temporal_low[1])))
    after_t = clip_in + branch_t
    normed_s = low(layer_norm(after_t, affine_low[0, 1], affine_low[1, 1]))
    merged_s = low_back(low(matmul_high(normed_s, entry_low[1])))
    mixed_s = attention(merged_s, 'fphe,fqhe->fhpq', 'fhpq,fqhe->fphe')
    after_s = after_t + low_back(matmul_high(mixed_s, spatial_low))
    normed_m = low(layer_norm(after_s, affine_low[0, 2], affine_low[1, 2]))
    widened = low_back(matmul_high(normed_m, widen_low))
    activated = low(jax.nn.gelu(widened, approximate=False))
    return after_s + matmul_high(activated, narrow_low)

def adamw(master, moment, square, grad, rate):
    fix = 1.0 - 0.5 ** STEP
    averaged = 0.5 * moment + 0.5 * grad
    squared = 0.5 * square + 0.5 * grad * grad
    updated = master - rate * (averaged / fix / (jnp.sqrt(squared / fix) + 1e-08) + 0.1 * master)
    return (updated, averaged, squared)

def reference(frames, cotangent, entry_weights, entry_momentum, entry_variance, temporal_weights, temporal_momentum, temporal_variance, spatial_weights, spatial_momentum, spatial_variance, widen_weights, widen_momentum, widen_variance, narrow_weights, narrow_momentum, narrow_variance, norm_affine, affine_momentum, affine_variance):
    params = (entry_weights, temporal_weights, spatial_weights, widen_weights, narrow_weights, norm_affine)

    def one_clip(totals, pair):
        clip_in, clip_back = pair
        result, pull = jax.vjp(clip_layer, clip_in.astype(jnp.float32), params[0], params[1], params[2], params[3], params[4], params[5])
        grads = pull(clip_back.astype(jnp.float32))
        totals = tuple((total + grad for total, grad in zip(totals, grads[1:])))
        return (totals, (result.astype(jnp.bfloat16), grads[0]))
    start = tuple((jnp.zeros(param.shape, jnp.float32) for param in params))
    totals, (layer_output, input_gradient) = lax.scan(one_clip, start, (frames, cotangent))
    entry_new = adamw(entry_weights, entry_momentum, entry_variance, totals[0], D ** (-0.5))
    temporal_new = adamw(temporal_weights, temporal_momentum, temporal_variance, totals[1], (D // 2) ** (-0.5))
    spatial_new = adamw(spatial_weights, spatial_momentum, spatial_variance, totals[2], (3 * D // PATCHES) ** (-0.5))
    widen_new = adamw(widen_weights, widen_momentum, widen_variance, totals[3], D ** (-0.5))
    narrow_new = adamw(narrow_weights, narrow_momentum, narrow_variance, totals[4], HID ** (-0.5))
    affine_new = adamw(norm_affine, affine_momentum, affine_variance, totals[5], 0.5)
    return (layer_output, input_gradient, entry_new[0], entry_new[1], entry_new[2], temporal_new[0], temporal_new[1], temporal_new[2], spatial_new[0], spatial_new[1], spatial_new[2], widen_new[0], widen_new[1], widen_new[2], narrow_new[0], narrow_new[1], narrow_new[2], affine_new[0], affine_new[1], affine_new[2][:, 0:2], affine_new[2][:, 2])
```

```python
import functools
import jax
import jax.numpy as jnp
from jax import lax
from jax.experimental import pallas as pl
from jax.experimental.pallas import tpu as pltpu
from jax.sharding import PartitionSpec as P

D = 768
HEADS = 12
HEAD_DIM = 64
HID = 3072
PATCHES = 196
STEP = 5


time_scores = "cfphe,cgphe->cphfg"
time_mixed = "cphfg,cgphe->cfphe"
time_flip = "cphfg,cfphe->cgphe"
space_scores = "cfphe,cfqhe->cfhpq"
space_mixed = "cfhpq,cfqhe->cfphe"
space_flip = "cfhpq,cfphe->cfqhe"


def project(inputs, weight):
    return jnp.einsum("cfpa,ab->cfpb", inputs, weight, preferred_element_type=jnp.float32)


def project_back(upstream, weight):
    return jnp.einsum("cfpb,ab->cfpa", upstream, weight, preferred_element_type=jnp.float32)


def weight_sum(inputs, upstream):
    return jnp.einsum("cfpa,cfpb->ab", inputs, upstream, preferred_element_type=jnp.float32)


def layer_norm(values, gain, shift):
    center = values - jnp.mean(values, axis=-1, keepdims=True)
    inverse = lax.rsqrt(jnp.mean(center * center, axis=-1, keepdims=True) + 1e-06)
    unit = center * inverse
    return (unit * gain + shift, unit, inverse)


def norm_back(upstream, unit, inverse, gain):
    scaled = upstream * gain
    inner = (
        scaled
        - jnp.mean(scaled, axis=-1, keepdims=True)
        - unit * jnp.mean(scaled * unit, axis=-1, keepdims=True)
    )
    return (
        inner * inverse,
        jnp.sum(upstream * unit, axis=(0, 1, 2)),
        jnp.sum(upstream, axis=(0, 1, 2)),
    )


def split_heads(merged):
    lowered = merged.astype(jnp.bfloat16)
    parts = lowered.reshape(lowered.shape[:-1] + (3, HEADS, HEAD_DIM))
    return (parts[..., 0, :, :], parts[..., 1, :, :], parts[..., 2, :, :])


def attend_forward(heads, score_form, mixed_form):
    query, keys, values = heads
    scores = jnp.einsum(score_form, query, keys, preferred_element_type=jnp.float32) * HEAD_DIM ** (
        -0.5
    )
    top = jnp.max(scores, axis=-1, keepdims=True)
    expo = jnp.exp(scores - top)
    total = jnp.sum(expo, axis=-1, keepdims=True)
    probs = (expo / total).astype(jnp.bfloat16)
    mixed = jnp.einsum(mixed_form, probs, values, preferred_element_type=jnp.float32)
    joined = mixed.reshape(mixed.shape[:-2] + (HEADS * HEAD_DIM,)).astype(jnp.bfloat16)
    return (joined, top + jnp.log(total))


def attend_backward(heads, logsum, upstream_joined, score_form, mixed_form, flip_form):
    query, keys, values = heads
    upstream = upstream_joined.reshape(upstream_joined.shape[:-1] + (HEADS, HEAD_DIM))
    scale = HEAD_DIM ** (-0.5)
    scores = jnp.einsum(score_form, query, keys, preferred_element_type=jnp.float32) * scale
    probs = jnp.exp(scores - logsum)
    dprobs = jnp.einsum(score_form, upstream, values, preferred_element_type=jnp.float32)
    dscores = (probs * (dprobs - jnp.sum(dprobs * probs, axis=-1, keepdims=True))).astype(
        jnp.bfloat16
    )
    dquery = jnp.einsum(mixed_form, dscores, keys, preferred_element_type=jnp.float32) * scale
    dkeys = jnp.einsum(flip_form, dscores, query, preferred_element_type=jnp.float32) * scale
    dvalues = jnp.einsum(
        flip_form, probs.astype(jnp.bfloat16), upstream, preferred_element_type=jnp.float32
    )
    stacked = jnp.stack([dquery, dkeys, dvalues], axis=-3)
    return stacked.reshape(stacked.shape[:-3] + (3 * HEADS * HEAD_DIM,)).astype(jnp.bfloat16)


MESH = pl.DeviceIdType.MESH
TOK = 4


def spot():
    clip = lax.axis_index("clip")
    return clip // 4, (clip // 2) % 2, clip % 2, lax.axis_index("tok")


def clip_of(y, x, core):
    return (y * 2 + x) * 2 + core


def greet(ny):
    y, x, core, t = spot()
    barrier = pltpu.get_barrier_semaphore()

    def tell(clip, tok):
        pl.semaphore_signal(barrier, inc=1, device_id=(clip, tok), device_id_type=MESH)

    tell(clip_of(y, x, 1 - core), t)
    tell(clip_of(y, 1 - x, core), t)
    for far in range(1, ny):
        tell(clip_of((y + far) % ny, x, core), t)
    for far in range(1, TOK):
        tell(clip_of(y, x, core), (t + far) % TOK)
    pl.semaphore_wait(barrier, 2 + (ny - 1) + (TOK - 1))


def gather_kernel(ny, count, *refs):
    owned, full = refs[:count], refs[count : 2 * count]
    local, got, got_late, sent_z, sent_x, sent_y, relay_x, relay_y, sent_c = refs[2 * count :]
    y, x, core, t = spot()
    greet(ny)
    me = clip_of(y, x, core) * TOK + t

    def slot(y_at, x_at, t_at):
        return clip_of(y_at, x_at, core) * TOK + t_at

    def send(k, at, sem, to, tok, half=None, source=None):
        width = full[k].shape[2]
        place = full[k].at[at]
        if half is not None:
            place = full[k].at[at, :, pl.ds(half * (width // 2), width // 2)]
        copy = pltpu.make_async_remote_copy(
            src_ref=place if source is None else source,
            dst_ref=place,
            send_sem=sem,
            recv_sem=(got_late if half == 1 else got).at[k, at],
            device_id=(to, tok),
            device_id_type=MESH,
        )
        return copy

    started = []

    def go(copy):
        copy.start()
        started.append(copy)

    def arrive(k, at, half=None):
        width = full[k].shape[2]
        place = full[k].at[at]
        if half is not None:
            place = full[k].at[at, :, pl.ds(half * (width // 2), width // 2)]
        pltpu.make_async_copy(place, place, (got_late if half == 1 else got).at[k, at]).wait()

    def to_core(k, at, number, source=None):
        go(send(k, at, sent_c.at[k, number], clip_of(y, x, 1 - core), t, source=source))

    def spread(k, j, source=None):
        at = slot(y, x, (t + j) % TOK)
        go(send(k, at, sent_x.at[k, j], clip_of(y, 1 - x, core), t, source=source))
        for far in range(1, ny):
            go(send(k, at, sent_y.at[k, j * ny + far], clip_of((y + far) % ny, x, core), t, source=source))
        to_core(k, at, j, source=source)

    splits = [full[k].shape[2] % 256 == 0 for k in range(count)]

    def crossing(k, j):
        tok = (t + j) % TOK
        from_x = slot(y, 1 - x, tok)
        arrive(k, from_x)
        for far in range(1, ny):
            if splits[k]:
                go(send(k, from_x, relay_y.at[k, j * ny + far], clip_of((y + far) % ny, x, core), t, half=1))
        to_core(k, from_x, 4 + j)
        for far in range(1, ny):
            from_y = slot((y + far) % ny, x, tok)
            arrive(k, from_y)
            go(
                send(
                    k,
                    from_y,
                    relay_x.at[k, j * ny + far],
                    clip_of(y, 1 - x, core),
                    t,
                    half=0 if splits[k] else None,
                )
            )
            to_core(k, from_y, 8 + (far - 1) * 8 + j)

    def corner(k, j):
        tok = (t + j) % TOK
        for far in range(1, ny):
            at = slot((y + far) % ny, 1 - x, tok)
            if splits[k]:
                arrive(k, at, 0)
                arrive(k, at, 1)
            else:
                arrive(k, at)
            to_core(k, at, 8 + (far - 1) * 8 + 4 + j)

    kept = []
    for k in range(count):
        own = pltpu.make_async_copy(owned[k], full[k].at[me], local.at[k])
        own.start()
        kept.append(own)
        for far in range(1, TOK):
            go(send(k, me, sent_z.at[k, far], clip_of(y, x, core), (t + far) % TOK, source=owned[k]))
        spread(k, 0, source=owned[k])
    steps = [(k, j) for k in range(count) for j in range(TOK)]
    for n in range(len(steps) + 2):
        if n < len(steps) and steps[n][1] > 0:
            k, j = steps[n]
            arrive(k, slot(y, x, (t + j) % TOK))
            spread(k, j)
        if 1 <= n < len(steps) + 1:
            crossing(*steps[n - 1])
        if n >= 2:
            corner(*steps[n - 2])
    for k in range(count):
        for at in range(2 * ny):
            for tok in range(TOK):
                place = (at * 2 + 1 - core) * TOK + tok
                arrive(k, place)
    for own in kept:
        own.wait()
    for copy in started:
        copy.wait_send()


def gather_all(owned, clips):
    ny = clips // 4
    count = len(owned)
    devices = clips * TOK
    dma = pltpu.SemaphoreType.DMA
    return pl.pallas_call(
        functools.partial(gather_kernel, ny, count),
        out_shape=[jax.ShapeDtypeStruct((devices,) + a.shape, a.dtype) for a in owned],
        in_specs=[pl.BlockSpec(memory_space=pl.ANY)] * count,
        out_specs=[pl.BlockSpec(memory_space=pl.ANY)] * count,
        scratch_shapes=[
            dma((count,)),
            dma((count, devices)),
            dma((count, devices)),
            dma((count, TOK)),
            dma((count, TOK)),
            dma((count, TOK * ny)),
            dma((count, TOK * ny)),
            dma((count, TOK * ny)),
            dma((count, 8 * ny)),
        ],
        compiler_params=pltpu.CompilerParams(collective_id=0, has_side_effects=True),
    )(*owned)


def scatter_kernel(ny, count, *refs):
    parts, totals = refs[:count], refs[count : 2 * count]
    rest = refs[2 * count :]
    held, core_in, side_in, part_in, z_in = (rest[i * count : (i + 1) * count] for i in range(5))
    load_sem, c_send, c_recv, d_send, d_recv, s_send, s_recv, z_send, z_recv = rest[5 * count :]
    y, x, core, t = spot()
    greet(ny)
    started = []

    def go(copy):
        copy.start()
        started.append(copy)
        return copy

    groups = [(dy, dx) for dy in range(1, ny) for dx in (1,)] + [(0, 1)] + [(dy, 0) for dy in range(1, ny)] + [(0, 0)]
    number = {pair: i for i, pair in enumerate(groups)}

    def absolute(pair):
        return (y + pair[0]) % ny, (x + pair[1]) % 2

    loads, cores = {}, {}

    def begin(k):
        for pair in groups:
            i = number[pair]
            ya, xa = absolute(pair)
            load = pltpu.make_async_copy(
                parts[k].at[pl.ds(clip_of(ya, xa, core) * TOK, TOK)], held[k].at[i], load_sem.at[k, i]
            )
            load.start()
            loads[k, pair] = load
            cores[k, pair] = go(
                pltpu.make_async_remote_copy(
                    src_ref=parts[k].at[pl.ds(clip_of(ya, xa, 1 - core) * TOK, TOK)],
                    dst_ref=core_in[k].at[i],
                    send_sem=c_send.at[k, i],
                    recv_sem=c_recv.at[k, i],
                    device_id=(clip_of(y, x, 1 - core), t),
                    device_id_type=MESH,
                )
            )

    def ready(k, pair):
        loads[k, pair].wait()
        cores[k, pair].wait_recv()

    def add_into(k, i, pieces):
        width = held[k].shape[3]
        cuts = sorted({0, width} | {c for _, a, b in pieces for c in (a, b)})
        for a, b in zip(cuts[:-1], cuts[1:]):
            live = [(make, lo) for make, lo, hi in pieces if lo <= a and b <= hi]

            def one(j, carry, a=a, b=b, live=live):
                total = held[k][i, j, :, a:b].astype(jnp.float32)
                for make, lo in live:
                    total = total + make(j, a - lo, b - lo).astype(jnp.float32)
                held[k][i, j, :, a:b] = total.astype(held[k].dtype)
                return carry

            lax.fori_loop(0, TOK, one, 0)

    def cut(k):
        width = held[k].shape[3]
        return width // 2 if width % 256 == 0 else width

    firsts, seconds, lasts = {}, {}, {}

    def step1(k):
        width, mid = held[k].shape[3], cut(k)
        for dy in range(1, ny):
            i = number[dy, 1]
            ready(k, (dy, 1))
            add_into(k, i, [(lambda j, a, b, i=i: core_in[k][i, j, :, a:b], 0, width)])
            firsts[k, dy, 0] = go(
                pltpu.make_async_remote_copy(
                    src_ref=held[k].at[i, :, :, pl.ds(0, mid)],
                    dst_ref=side_in[k].at[dy - 1, :, :, pl.ds(0, mid)],
                    send_sem=d_send.at[k, dy, 0],
                    recv_sem=d_recv.at[k, dy, 0],
                    device_id=(clip_of(y, 1 - x, core), t),
                    device_id_type=MESH,
                )
            )
            if mid < width:
                firsts[k, dy, 1] = go(
                    pltpu.make_async_remote_copy(
                        src_ref=held[k].at[i, :, :, pl.ds(mid, width - mid)],
                        dst_ref=side_in[k].at[dy - 1, :, :, pl.ds(mid, width - mid)],
                        send_sem=d_send.at[k, dy, 1],
                        recv_sem=d_recv.at[k, dy, 1],
                        device_id=(clip_of((y + dy) % ny, x, core), t),
                        device_id_type=MESH,
                    )
                )

    def step2(k):
        width, mid = held[k].shape[3], cut(k)
        for dy in range(1, ny):
            i = number[dy, 0]
            ready(k, (dy, 0))
            firsts[k, dy, 0].wait_recv()
            add_into(
                k,
                i,
                [
                    (lambda j, a, b, i=i: core_in[k][i, j, :, a:b], 0, width),
                    (lambda j, a, b, dy=dy: side_in[k][dy - 1, j, :, a:b], 0, mid),
                ],
            )
            seconds[k, dy] = go(
                pltpu.make_async_remote_copy(
                    src_ref=held[k].at[i],
                    dst_ref=part_in[k].at[dy],
                    send_sem=s_send.at[k, dy],
                    recv_sem=s_recv.at[k, dy],
                    device_id=(clip_of((y + dy) % ny, x, core), t),
                    device_id_type=MESH,
                )
            )
        i = number[0, 1]
        ready(k, (0, 1))
        pieces = [(lambda j, a, b, i=i: core_in[k][i, j, :, a:b], 0, width)]
        if mid < width:
            for dy in range(1, ny):
                firsts[k, dy, 1].wait_recv()
                pieces.append(
                    (lambda j, a, b, dy=dy: side_in[k][dy - 1, j, :, a + mid : b + mid], mid, width)
                )
        add_into(k, i, pieces)
        seconds[k, 0] = go(
            pltpu.make_async_remote_copy(
                src_ref=held[k].at[i],
                dst_ref=part_in[k].at[0],
                send_sem=s_send.at[k, 0],
                recv_sem=s_recv.at[k, 0],
                device_id=(clip_of(y, 1 - x, core), t),
                device_id_type=MESH,
            )
        )

    def step3(k):
        width = held[k].shape[3]
        i = number[0, 0]
        ready(k, (0, 0))
        for dy in range(ny):
            seconds[k, dy].wait_recv()
        pieces = [(lambda j, a, b, i=i: core_in[k][i, j, :, a:b], 0, width)]
        for dy in range(ny):
            pieces.append((lambda j, a, b, dy=dy: part_in[k][dy, j, :, a:b], 0, width))
        add_into(k, i, pieces)
        for far in range(1, TOK):
            lasts[k, far] = go(
                pltpu.make_async_remote_copy(
                    src_ref=held[k].at[i, (t + far) % TOK],
                    dst_ref=z_in[k].at[far - 1],
                    send_sem=z_send.at[k, far],
                    recv_sem=z_recv.at[k, far],
                    device_id=(clip_of(y, x, core), (t + far) % TOK),
                    device_id_type=MESH,
                )
            )

    def step4(k):
        i = number[0, 0]
        total = held[k][i, t].astype(jnp.float32)
        for far in range(1, TOK):
            lasts[k, far].wait_recv()
            total = total + z_in[k][far - 1].astype(jnp.float32)
        totals[k][...] = total

    for k in range(count):
        begin(k)
    for n in range(count + 3):
        for shift, step in enumerate((step1, step2, step3, step4)):
            if 0 <= n - shift < count:
                step(n - shift)
    for copy in started:
        copy.wait_send()


def scatter_all(parts, clips):
    ny = clips // 4
    count = len(parts)
    dma = pltpu.SemaphoreType.DMA
    shapes = [p.shape[1:] for p in parts]
    held = [pltpu.VMEM((2 * ny, TOK) + s, jnp.bfloat16) for s in shapes]
    side = [pltpu.VMEM((max(ny - 1, 1), TOK) + s, jnp.bfloat16) for s in shapes]
    part = [pltpu.VMEM((ny, TOK) + s, jnp.bfloat16) for s in shapes]
    last = [pltpu.VMEM((TOK - 1,) + s, jnp.bfloat16) for s in shapes]
    return pl.pallas_call(
        functools.partial(scatter_kernel, ny, count),
        out_shape=[jax.ShapeDtypeStruct(s, jnp.float32) for s in shapes],
        in_specs=[pl.BlockSpec(memory_space=pl.ANY)] * count,
        out_specs=[pl.BlockSpec(memory_space=pltpu.VMEM)] * count,
        scratch_shapes=held + held + side + part + last
        + [
            dma((count, 2 * ny)),
            dma((count, 2 * ny)),
            dma((count, 2 * ny)),
            dma((count, ny, 2)),
            dma((count, ny, 2)),
            dma((count, ny)),
            dma((count, ny)),
            dma((count, TOK)),
            dma((count, TOK)),
        ],
        compiler_params=pltpu.CompilerParams(
            collective_id=1, has_side_effects=True, vmem_limit_bytes=58 * 1024 * 1024
        ),
    )(*parts)


def as_rows(masters, devices):
    entry, temporal, spatial, widen, narrow, affine = (m.astype(jnp.bfloat16) for m in masters)
    each = affine.shape[2]
    return (
        entry.reshape(2 * D // devices, 3 * D),
        temporal.reshape(2 * D // devices, D),
        spatial.reshape(D // devices, D),
        widen.reshape(D // devices, HID),
        narrow.reshape(HID // devices, D),
        jnp.pad(affine.reshape(6, each), ((0, 10), (0, 128 - each))),
    )


def collect(masters, clips):
    devices = clips * TOK
    rows = as_rows(masters, devices)
    if clips == 8:
        full = gather_all(rows, clips)
    else:
        full = [lax.all_gather(r, ("clip", "tok"), axis=0) for r in rows]
    each = D // devices
    affine = full[5][:, :6, :each].transpose(1, 0, 2).reshape(2, 3, D)
    return (
        full[0].reshape(2, D, 3 * D),
        full[1].reshape(2, D, D),
        full[2].reshape(D, D),
        full[3].reshape(D, HID),
        full[4].reshape(HID, D),
        affine,
    )


def spread_sums(grads, clips):
    devices = clips * TOK
    each = D // devices
    affine = grads[5].reshape(6, devices, each).transpose(1, 0, 2)
    parts = (
        grads[0].reshape(devices, 2 * D // devices, 3 * D),
        grads[1].reshape(devices, 2 * D // devices, D),
        grads[2].reshape(devices, D // devices, D),
        grads[3].reshape(devices, D // devices, HID),
        grads[4].reshape(devices, HID // devices, D),
        jnp.pad(affine, ((0, 0), (0, 10), (0, 128 - each))),
    )
    parts = tuple(p.astype(jnp.bfloat16) for p in parts)
    if clips == 8:
        sums = scatter_all(parts, clips)
    else:
        sums = [
            lax.psum_scatter(p, ("clip", "tok"), scatter_dimension=0).astype(jnp.float32)
            for p in parts
        ]
    flat = tuple(s.reshape(-1, 128) for s in sums[:5])
    return flat + (sums[5][:6, :each].reshape(2, 3, each),)


def forward(frames, masters, clips):
    weights = collect(masters, clips)
    entry, temporal, spatial, widen, narrow, affine = weights
    gains = affine.astype(jnp.float32)
    patchwise = lax.all_to_all(frames, "tok", split_axis=2, concat_axis=1, tiled=True)
    normed_t, unit_t, inverse_t = layer_norm(
        patchwise.astype(jnp.float32), gains[0, 0], gains[1, 0]
    )
    lowered_t = normed_t.astype(jnp.bfloat16)
    heads_t = split_heads(project(lowered_t, entry[0]))
    mixed_t, lse_t = attend_forward(heads_t, time_scores, time_mixed)
    first_t = project(mixed_t, temporal[0]).astype(jnp.bfloat16)
    branch = project(first_t, temporal[1]).astype(jnp.bfloat16)
    returned = lax.all_to_all(branch, "tok", split_axis=1, concat_axis=2, tiled=True)
    after_t = frames.astype(jnp.float32) + returned.astype(jnp.float32)
    normed_s, unit_s, inverse_s = layer_norm(after_t, gains[0, 1], gains[1, 1])
    lowered_s = normed_s.astype(jnp.bfloat16)
    heads_s = split_heads(project(lowered_s, entry[1]))
    mixed_s, lse_s = attend_forward(heads_s, space_scores, space_mixed)
    after_s = after_t + project(mixed_s, spatial)
    normed_m, unit_m, inverse_m = layer_norm(after_s, gains[0, 2], gains[1, 2])
    lowered_m = normed_m.astype(jnp.bfloat16)
    widened = project(lowered_m, widen)
    activated = jax.nn.gelu(widened, approximate=False).astype(jnp.bfloat16)
    result = (after_s + project(activated, narrow)).astype(jnp.bfloat16)
    saved = {
        "weights": weights,
        "unit_t": unit_t,
        "inverse_t": inverse_t,
        "lowered_t": lowered_t,
        "heads_t": heads_t,
        "lse_t": lse_t,
        "mixed_t": mixed_t,
        "first_t": first_t,
        "unit_s": unit_s,
        "inverse_s": inverse_s,
        "lowered_s": lowered_s,
        "heads_s": heads_s,
        "lse_s": lse_s,
        "mixed_s": mixed_s,
        "unit_m": unit_m,
        "inverse_m": inverse_m,
        "lowered_m": lowered_m,
        "widened": widened,
        "activated": activated,
    }
    return (result, saved)


def adamw(master, moment, square, grad, rate):
    fix = 1.0 - 0.5**STEP
    averaged = 0.5 * moment + 0.5 * grad
    squared = 0.5 * square + 0.5 * grad * grad
    updated = master - rate * (averaged / fix / (jnp.sqrt(squared / fix) + 1e-08) + 0.1 * master)
    return (updated, averaged, squared)


def on_device(
    frames,
    cotangent,
    entry_weights,
    entry_momentum,
    entry_variance,
    temporal_weights,
    temporal_momentum,
    temporal_variance,
    spatial_weights,
    spatial_momentum,
    spatial_variance,
    widen_weights,
    widen_momentum,
    widen_variance,
    narrow_weights,
    narrow_momentum,
    narrow_variance,
    norm_affine,
    affine_momentum,
    affine_variance,
):
    masters = (
        entry_weights,
        temporal_weights,
        spatial_weights,
        widen_weights,
        narrow_weights,
        norm_affine,
    )
    clips = lax.axis_size("clip")
    result, saved = forward(frames, masters, clips)
    entry, temporal, spatial, widen, narrow, affine = saved["weights"]
    gains = affine.astype(jnp.float32)
    narrow_grad = weight_sum(saved["activated"], cotangent)
    widened = saved["widened"]
    slope = (
        0.5 * (1.0 + lax.erf(widened * 0.7071067811865476))
        + widened * jnp.exp(-0.5 * widened * widened) * 0.3989422804014327
    )
    dwidened = (project_back(cotangent, narrow) * slope).astype(jnp.bfloat16)
    widen_grad = weight_sum(saved["lowered_m"], dwidened)
    dpart_m, gain_m, shift_m = norm_back(
        project_back(dwidened, widen), saved["unit_m"], saved["inverse_m"], gains[0, 2]
    )
    dafter_s = cotangent.astype(jnp.float32) + dpart_m
    dspatial = dafter_s.astype(jnp.bfloat16)
    spatial_grad = weight_sum(saved["mixed_s"], dspatial)
    dmixed_s = project_back(dspatial, spatial).astype(jnp.bfloat16)
    dfused_s = attend_backward(
        saved["heads_s"], saved["lse_s"], dmixed_s, space_scores, space_mixed, space_flip
    )
    entry_grad_s = weight_sum(saved["lowered_s"], dfused_s)
    dpart_s, gain_s, shift_s = norm_back(
        project_back(dfused_s, entry[1]), saved["unit_s"], saved["inverse_s"], gains[0, 1]
    )
    dafter_t = dafter_s + dpart_s
    dbranch = lax.all_to_all(
        dafter_t.astype(jnp.bfloat16), "tok", split_axis=2, concat_axis=1, tiled=True
    )
    temporal_grad_b = weight_sum(saved["first_t"], dbranch)
    dfirst = project_back(dbranch, temporal[1]).astype(jnp.bfloat16)
    temporal_grad_a = weight_sum(saved["mixed_t"], dfirst)
    dmixed_t = project_back(dfirst, temporal[0]).astype(jnp.bfloat16)
    dfused_t = attend_backward(
        saved["heads_t"], saved["lse_t"], dmixed_t, time_scores, time_mixed, time_flip
    )
    entry_grad_t = weight_sum(saved["lowered_t"], dfused_t)
    dsent, gain_t, shift_t = norm_back(
        project_back(dfused_t, entry[0]), saved["unit_t"], saved["inverse_t"], gains[0, 0]
    )
    dreturned = lax.all_to_all(
        dsent.astype(jnp.bfloat16), "tok", split_axis=1, concat_axis=2, tiled=True
    )
    input_gradient = dafter_t + dreturned.astype(jnp.float32)
    members = (
        jnp.stack([entry_grad_t, entry_grad_s]),
        jnp.stack([temporal_grad_a, temporal_grad_b]),
        spatial_grad,
        widen_grad,
        narrow_grad,
        jnp.stack([jnp.stack([gain_t, gain_s, gain_m]), jnp.stack([shift_t, shift_s, shift_m])]),
    )
    totals = spread_sums(members, clips)
    entry_sum, temporal_sum, spatial_sum, widen_sum, narrow_sum, affine_sum = totals
    entry_new = adamw(entry_weights, entry_momentum, entry_variance, entry_sum, D ** (-0.5))
    temporal_new = adamw(
        temporal_weights, temporal_momentum, temporal_variance, temporal_sum, (D // 2) ** (-0.5)
    )
    spatial_new = adamw(
        spatial_weights,
        spatial_momentum,
        spatial_variance,
        spatial_sum,
        (3 * D // PATCHES) ** (-0.5),
    )
    widen_new = adamw(widen_weights, widen_momentum, widen_variance, widen_sum, D ** (-0.5))
    narrow_new = adamw(narrow_weights, narrow_momentum, narrow_variance, narrow_sum, HID ** (-0.5))
    affine_new = adamw(norm_affine, affine_momentum, affine_variance, affine_sum, 0.5)
    return (
        result,
        input_gradient,
        entry_new[0],
        entry_new[1],
        entry_new[2],
        temporal_new[0],
        temporal_new[1],
        temporal_new[2],
        spatial_new[0],
        spatial_new[1],
        spatial_new[2],
        widen_new[0],
        widen_new[1],
        widen_new[2],
        narrow_new[0],
        narrow_new[1],
        narrow_new[2],
        affine_new[0],
        affine_new[1],
        affine_new[2][:, 0:2],
        affine_new[2][:, 2],
    )


def solution(mesh):
    return jax.shard_map(
        on_device,
        mesh=mesh,
        in_specs=(
            P("clip", "tok", None, None),
            P("clip", "tok", None, None),
            P(("clip", "tok"), None),
            P(("clip", "tok"), None),
            P(("clip", "tok"), None),
            P(("clip", "tok"), None),
            P(("clip", "tok"), None),
            P(("clip", "tok"), None),
            P(("clip", "tok"), None),
            P(("clip", "tok"), None),
            P(("clip", "tok"), None),
            P(("clip", "tok"), None),
            P(("clip", "tok"), None),
            P(("clip", "tok"), None),
            P(("clip", "tok"), None),
            P(("clip", "tok"), None),
            P(("clip", "tok"), None),
            P(None, None, ("clip", "tok")),
            P(None, None, ("clip", "tok")),
            P(None, None, ("clip", "tok")),
        ),
        out_specs=(
            P("clip", "tok", None, None),
            P("clip", "tok", None, None),
            P(("clip", "tok"), None),
            P(("clip", "tok"), None),
            P(("clip", "tok"), None),
            P(("clip", "tok"), None),
            P(("clip", "tok"), None),
            P(("clip", "tok"), None),
            P(("clip", "tok"), None),
            P(("clip", "tok"), None),
            P(("clip", "tok"), None),
            P(("clip", "tok"), None),
            P(("clip", "tok"), None),
            P(("clip", "tok"), None),
            P(("clip", "tok"), None),
            P(("clip", "tok"), None),
            P(("clip", "tok"), None),
            P(None, None, ("clip", "tok")),
            P(None, None, ("clip", "tok")),
            P(None, None, ("clip", "tok")),
            P(None, ("clip", "tok")),
        ),
        check_vma=False,
    )
```

```python
import functools

import jax
import jax.numpy as jnp
from jax import lax
from jax.experimental import pallas as pl
from jax.experimental.pallas import tpu as pltpu
from jax.sharding import PartitionSpec as P

D = 768
HEADS = 12
HEAD_DIM = 64
HID = 3072
PATCHES = 196
STEP = 5

time_scores = "cfphe,cgphe->cphfg"
time_mixed = "cphfg,cgphe->cfphe"
time_flip = "cphfg,cfphe->cgphe"
space_scores = "cfphe,cfqhe->cfhpq"
space_mixed = "cfhpq,cfqhe->cfphe"
space_flip = "cfhpq,cfphe->cfqhe"


def project(inputs, weight):
    return jnp.einsum("cfpa,ab->cfpb", inputs, weight, preferred_element_type=jnp.float32)


def project_back(upstream, weight):
    return jnp.einsum("cfpb,ab->cfpa", upstream, weight, preferred_element_type=jnp.float32)


def weight_sum(inputs, upstream):
    return jnp.einsum("cfpa,cfpb->ab", inputs, upstream, preferred_element_type=jnp.float32)


def layer_norm(values, gain, shift):
    center = values - jnp.mean(values, axis=-1, keepdims=True)
    inverse = lax.rsqrt(jnp.mean(center * center, axis=-1, keepdims=True) + 1e-06)
    unit = center * inverse
    return (unit * gain + shift, unit, inverse)


def norm_back(upstream, unit, inverse, gain):
    scaled = upstream * gain
    inner = (
        scaled
        - jnp.mean(scaled, axis=-1, keepdims=True)
        - unit * jnp.mean(scaled * unit, axis=-1, keepdims=True)
    )
    return (
        inner * inverse,
        jnp.sum(upstream * unit, axis=(0, 1, 2)),
        jnp.sum(upstream, axis=(0, 1, 2)),
    )


def split_heads(merged):
    lowered = merged.astype(jnp.bfloat16)
    parts = lowered.reshape(lowered.shape[:-1] + (3, HEADS, HEAD_DIM))
    return (parts[..., 0, :, :], parts[..., 1, :, :], parts[..., 2, :, :])


def attend_forward(heads, score_form, mixed_form):
    query, keys, values = heads
    scores = jnp.einsum(score_form, query, keys, preferred_element_type=jnp.float32) * HEAD_DIM ** (
        -0.5
    )
    top = jnp.max(scores, axis=-1, keepdims=True)
    expo = jnp.exp(scores - top)
    total = jnp.sum(expo, axis=-1, keepdims=True)
    probs = (expo / total).astype(jnp.bfloat16)
    mixed = jnp.einsum(mixed_form, probs, values, preferred_element_type=jnp.float32)
    joined = mixed.reshape(mixed.shape[:-2] + (HEADS * HEAD_DIM,)).astype(jnp.bfloat16)
    return (joined, top + jnp.log(total))


def attend_backward(heads, logsum, upstream_joined, score_form, mixed_form, flip_form):
    query, keys, values = heads
    upstream = upstream_joined.reshape(upstream_joined.shape[:-1] + (HEADS, HEAD_DIM))
    scale = HEAD_DIM ** (-0.5)
    scores = jnp.einsum(score_form, query, keys, preferred_element_type=jnp.float32) * scale
    probs = jnp.exp(scores - logsum)
    dprobs = jnp.einsum(score_form, upstream, values, preferred_element_type=jnp.float32)
    dscores = (probs * (dprobs - jnp.sum(dprobs * probs, axis=-1, keepdims=True))).astype(
        jnp.bfloat16
    )
    dquery = jnp.einsum(mixed_form, dscores, keys, preferred_element_type=jnp.float32) * scale
    dkeys = jnp.einsum(flip_form, dscores, query, preferred_element_type=jnp.float32) * scale
    dvalues = jnp.einsum(
        flip_form, probs.astype(jnp.bfloat16), upstream, preferred_element_type=jnp.float32
    )
    stacked = jnp.stack([dquery, dkeys, dvalues], axis=-3)
    return stacked.reshape(stacked.shape[:-3] + (3 * HEADS * HEAD_DIM,)).astype(jnp.bfloat16)


def collect(masters):
    gathered = (
        lax.all_gather(masters[0].astype(jnp.bfloat16), ("clip", "tok"), axis=0, tiled=True),
        lax.all_gather(masters[1].astype(jnp.bfloat16), ("clip", "tok"), axis=0, tiled=True),
        lax.all_gather(masters[2].astype(jnp.bfloat16), ("clip", "tok"), axis=0, tiled=True),
        lax.all_gather(masters[3].astype(jnp.bfloat16), ("clip", "tok"), axis=0, tiled=True),
        lax.all_gather(masters[4].astype(jnp.bfloat16), ("clip", "tok"), axis=0, tiled=True),
        lax.all_gather(masters[5].astype(jnp.bfloat16), ("clip", "tok"), axis=2, tiled=True),
    )
    return (
        gathered[0].reshape(2, D, 3 * D),
        gathered[1].reshape(2, D, D),
        gathered[2].reshape(D, D),
        gathered[3].reshape(D, HID),
        gathered[4].reshape(HID, D),
        gathered[5],
    )


def plain_forward(frames, masters):
    weights = collect(masters)
    entry, temporal, spatial, widen, narrow, affine = weights
    gains = affine.astype(jnp.float32)
    patchwise = lax.all_to_all(frames, "tok", split_axis=2, concat_axis=1, tiled=True)
    normed_t, unit_t, inverse_t = layer_norm(
        patchwise.astype(jnp.float32), gains[0, 0], gains[1, 0]
    )
    lowered_t = normed_t.astype(jnp.bfloat16)
    heads_t = split_heads(project(lowered_t, entry[0]))
    mixed_t, lse_t = attend_forward(heads_t, time_scores, time_mixed)
    first_t = project(mixed_t, temporal[0]).astype(jnp.bfloat16)
    branch = project(first_t, temporal[1]).astype(jnp.bfloat16)
    returned = lax.all_to_all(branch, "tok", split_axis=1, concat_axis=2, tiled=True)
    after_t = frames.astype(jnp.float32) + returned.astype(jnp.float32)
    normed_s, unit_s, inverse_s = layer_norm(after_t, gains[0, 1], gains[1, 1])
    lowered_s = normed_s.astype(jnp.bfloat16)
    heads_s = split_heads(project(lowered_s, entry[1]))
    mixed_s, lse_s = attend_forward(heads_s, space_scores, space_mixed)
    after_s = after_t + project(mixed_s, spatial)
    normed_m, unit_m, inverse_m = layer_norm(after_s, gains[0, 2], gains[1, 2])
    lowered_m = normed_m.astype(jnp.bfloat16)
    widened = project(lowered_m, widen)
    activated = jax.nn.gelu(widened, approximate=False).astype(jnp.bfloat16)
    result = (after_s + project(activated, narrow)).astype(jnp.bfloat16)
    saved = {
        "weights": weights,
        "unit_t": unit_t,
        "inverse_t": inverse_t,
        "lowered_t": lowered_t,
        "heads_t": heads_t,
        "lse_t": lse_t,
        "mixed_t": mixed_t,
        "first_t": first_t,
        "unit_s": unit_s,
        "inverse_s": inverse_s,
        "lowered_s": lowered_s,
        "heads_s": heads_s,
        "lse_s": lse_s,
        "mixed_s": mixed_s,
        "unit_m": unit_m,
        "inverse_m": inverse_m,
        "lowered_m": lowered_m,
        "widened": widened,
        "activated": activated,
    }
    return (result, saved)


def adamw(master, moment, square, grad, rate):
    fix = 1.0 - 0.5**STEP
    averaged = 0.5 * moment + 0.5 * grad
    squared = 0.5 * square + 0.5 * grad * grad
    updated = master - rate * (averaged / fix / (jnp.sqrt(squared / fix) + 1e-08) + 0.1 * master)
    return (updated, averaged, squared)

def on_any(
    frames,
    cotangent,
    entry_weights,
    entry_momentum,
    entry_variance,
    temporal_weights,
    temporal_momentum,
    temporal_variance,
    spatial_weights,
    spatial_momentum,
    spatial_variance,
    widen_weights,
    widen_momentum,
    widen_variance,
    narrow_weights,
    narrow_momentum,
    narrow_variance,
    norm_affine,
    affine_momentum,
    affine_variance,
):
    masters = (
        entry_weights,
        temporal_weights,
        spatial_weights,
        widen_weights,
        narrow_weights,
        norm_affine,
    )
    result, saved = plain_forward(frames, masters)
    entry, temporal, spatial, widen, narrow, affine = saved["weights"]
    gains = affine.astype(jnp.float32)
    narrow_grad = weight_sum(saved["activated"], cotangent)
    widened = saved["widened"]
    slope = (
        0.5 * (1.0 + lax.erf(widened * 0.7071067811865476))
        + widened * jnp.exp(-0.5 * widened * widened) * 0.3989422804014327
    )
    dwidened = (project_back(cotangent, narrow) * slope).astype(jnp.bfloat16)
    widen_grad = weight_sum(saved["lowered_m"], dwidened)
    dpart_m, gain_m, shift_m = norm_back(
        project_back(dwidened, widen), saved["unit_m"], saved["inverse_m"], gains[0, 2]
    )
    dafter_s = cotangent.astype(jnp.float32) + dpart_m
    dspatial = dafter_s.astype(jnp.bfloat16)
    spatial_grad = weight_sum(saved["mixed_s"], dspatial)
    dmixed_s = project_back(dspatial, spatial).astype(jnp.bfloat16)
    dfused_s = attend_backward(
        saved["heads_s"], saved["lse_s"], dmixed_s, space_scores, space_mixed, space_flip
    )
    entry_grad_s = weight_sum(saved["lowered_s"], dfused_s)
    dpart_s, gain_s, shift_s = norm_back(
        project_back(dfused_s, entry[1]), saved["unit_s"], saved["inverse_s"], gains[0, 1]
    )
    dafter_t = dafter_s + dpart_s
    dbranch = lax.all_to_all(
        dafter_t.astype(jnp.bfloat16), "tok", split_axis=2, concat_axis=1, tiled=True
    )
    temporal_grad_b = weight_sum(saved["first_t"], dbranch)
    dfirst = project_back(dbranch, temporal[1]).astype(jnp.bfloat16)
    temporal_grad_a = weight_sum(saved["mixed_t"], dfirst)
    dmixed_t = project_back(dfirst, temporal[0]).astype(jnp.bfloat16)
    dfused_t = attend_backward(
        saved["heads_t"], saved["lse_t"], dmixed_t, time_scores, time_mixed, time_flip
    )
    entry_grad_t = weight_sum(saved["lowered_t"], dfused_t)
    dsent, gain_t, shift_t = norm_back(
        project_back(dfused_t, entry[0]), saved["unit_t"], saved["inverse_t"], gains[0, 0]
    )
    dreturned = lax.all_to_all(
        dsent.astype(jnp.bfloat16), "tok", split_axis=1, concat_axis=2, tiled=True
    )
    input_gradient = dafter_t + dreturned.astype(jnp.float32)
    members = (
        jnp.stack([entry_grad_t, entry_grad_s]).reshape(-1, 128),
        jnp.stack([temporal_grad_a, temporal_grad_b]).reshape(-1, 128),
        spatial_grad.reshape(-1, 128),
        widen_grad.reshape(-1, 128),
        narrow_grad.reshape(-1, 128),
        jnp.stack([jnp.stack([gain_t, gain_s, gain_m]), jnp.stack([shift_t, shift_s, shift_m])]),
    )
    totals = (
        lax.psum_scatter(members[0], ("clip", "tok"), scatter_dimension=0, tiled=True),
        lax.psum_scatter(members[1], ("clip", "tok"), scatter_dimension=0, tiled=True),
        lax.psum_scatter(members[2], ("clip", "tok"), scatter_dimension=0, tiled=True),
        lax.psum_scatter(members[3], ("clip", "tok"), scatter_dimension=0, tiled=True),
        lax.psum_scatter(members[4], ("clip", "tok"), scatter_dimension=0, tiled=True),
        lax.psum_scatter(members[5], ("clip", "tok"), scatter_dimension=2, tiled=True),
    )
    entry_sum, temporal_sum, spatial_sum, widen_sum, narrow_sum, affine_sum = totals
    entry_new = adamw(entry_weights, entry_momentum, entry_variance, entry_sum, D ** (-0.5))
    temporal_new = adamw(
        temporal_weights, temporal_momentum, temporal_variance, temporal_sum, (D // 2) ** (-0.5)
    )
    spatial_new = adamw(
        spatial_weights,
        spatial_momentum,
        spatial_variance,
        spatial_sum,
        (3 * D // PATCHES) ** (-0.5),
    )
    widen_new = adamw(widen_weights, widen_momentum, widen_variance, widen_sum, D ** (-0.5))
    narrow_new = adamw(narrow_weights, narrow_momentum, narrow_variance, narrow_sum, HID ** (-0.5))
    affine_new = adamw(norm_affine, affine_momentum, affine_variance, affine_sum, 0.5)
    return (
        result,
        input_gradient,
        entry_new[0],
        entry_new[1],
        entry_new[2],
        temporal_new[0],
        temporal_new[1],
        temporal_new[2],
        spatial_new[0],
        spatial_new[1],
        spatial_new[2],
        widen_new[0],
        widen_new[1],
        widen_new[2],
        narrow_new[0],
        narrow_new[1],
        narrow_new[2],
        affine_new[0],
        affine_new[1],
        affine_new[2][:, 0:2],
        affine_new[2][:, 2],
    )

MESH = pl.DeviceIdType.MESH
TOK = 4
UNIT = 768
ROWS = (48, 48, 24, 24, 96)
WIDTHS = (2304, 768, 768, 3072, 768)
AFFINE = 5
EACH = 24
ORDER_IN = (5, 0, 1, 2, 3, 4)
ORDER_MLP = (4, 3)
ORDER_REST = (0, 1, 2, 5)
VMEM_LIMIT = 60 * 1024 * 1024


def units_of(order):
    units = []
    for k in order:
        if k == AFFINE:
            units.append((k, 0, 128))
        else:
            units += [(k, c, UNIT) for c in range(0, WIDTHS[k], UNIT)]
    return units


def spot():
    clip = lax.axis_index("clip")
    return clip // 4, (clip // 2) % 2, clip % 2, lax.axis_index("tok")


def clip_of(y, x, core):
    return (y * 2 + x) * 2 + core


def greet():
    y, x, core, t = spot()
    barrier = pltpu.get_barrier_semaphore()

    def tell(clip, tok):
        pl.semaphore_signal(barrier, inc=1, device_id=(clip, tok), device_id_type=MESH)

    tell(clip_of(y, x, 1 - core), t)
    tell(clip_of(y, 1 - x, core), t)
    tell(clip_of(1 - y, x, core), t)
    for far in range(1, TOK):
        tell(clip_of(y, x, core), (t + far) % TOK)
    pl.semaphore_wait(barrier, 3 + (TOK - 1))


class Flight:
    def __init__(self):
        self.started = []

    def go(self, copy, when=None):
        if when is None:
            copy.start()
        else:
            pl.when(when)(copy.start)
        self.started.append((copy, when))
        return copy

    def drain(self):
        for copy, when in self.started:
            if when is None:
                copy.wait_send()
            else:
                pl.when(when)(copy.wait_send)


def gather_steps(units, owned, full, sems, flight):
    local, got, late, z_sem, x_sem, y_sem, rx_sem, ry_sem, c_sem = sems
    y, x, core, t = spot()
    here, by_x, by_y = clip_of(y, x, core), clip_of(y, 1 - x, core), clip_of(1 - y, x, core)
    mate = clip_of(y, x, 1 - core)
    corner_clip = clip_of(1 - y, 1 - x, core)
    local_copies = []

    def place(u, at, half=None):
        k, c, width = units[u]
        if half is not None:
            width = width // 2
            c = c + half * width
        return full[k].at[at, :, pl.ds(c, width)]

    def send(u, at, sem, to, tok, half=None, own=False):
        k, c, width = units[u]
        there = place(u, at, half)
        return pltpu.make_async_remote_copy(
            src_ref=owned[k].at[:, pl.ds(c, width)] if own else there,
            dst_ref=there,
            send_sem=sem,
            recv_sem=(late if half == 1 else got).at[u, at],
            device_id=(to, tok),
            device_id_type=MESH,
        )

    def arrive(u, at, half=None):
        there = place(u, at, half)
        pltpu.make_async_copy(there, there, (late if half == 1 else got).at[u, at]).wait()

    def spread(u, at, slot, own=False, when=None):
        flight.go(send(u, at, x_sem.at[u, slot], by_x, t, own=own), when)
        flight.go(send(u, at, y_sem.at[u, slot], by_y, t, own=own), when)
        flight.go(send(u, at, c_sem.at[u, slot], mate, t, own=own), when)

    def begin(u):
        k, c, width = units[u]
        me = here * TOK + t
        copy = pltpu.make_async_copy(owned[k].at[:, pl.ds(c, width)], place(u, me), local.at[u])
        copy.start()
        local_copies.append(copy)
        flight.go(send(u, me, z_sem.at[u, 0, 0], here, t + 1, own=True), t < TOK - 1)
        flight.go(send(u, me, z_sem.at[u, 0, 1], here, t - 1, own=True), t > 0)
        spread(u, me, 0, own=True)

    hops = [(far, way) for far in range(1, TOK) for way in (1, -1)]

    def guard(far, way):
        return t + far <= TOK - 1 if way == 1 else t - far >= 0

    def along(u):
        for slot, (far, way) in enumerate(hops, 1):
            at = here * TOK + t + far * way
            there = guard(far, way)
            pl.when(there)(functools.partial(arrive, u, at))
            onward = jnp.logical_and(there, t > 0 if way == 1 else t < TOK - 1)
            flight.go(send(u, at, z_sem.at[u, slot, 0], here, t - way), onward)
            spread(u, at, slot, when=there)

    def crossing(u):
        halves = units[u][2] % 256 == 0
        for slot, tok in enumerate((0, 1, 2, 3)):
            tok = (t + tok) % TOK
            from_x, from_y = by_x * TOK + tok, by_y * TOK + tok
            arrive(u, from_x)
            if halves:
                flight.go(send(u, from_x, ry_sem.at[u, slot], by_y, t, half=1))
            flight.go(send(u, from_x, c_sem.at[u, 7 + slot], mate, t))
            arrive(u, from_y)
            flight.go(send(u, from_y, rx_sem.at[u, slot], by_x, t, half=0 if halves else None))
            flight.go(send(u, from_y, c_sem.at[u, 11 + slot], mate, t))

    def corner(u):
        halves = units[u][2] % 256 == 0
        for slot in range(TOK):
            at = corner_clip * TOK + (t + slot) % TOK
            if halves:
                arrive(u, at, 0)
                arrive(u, at, 1)
            else:
                arrive(u, at)
            flight.go(send(u, at, c_sem.at[u, 15 + slot], mate, t))

    def settle(u):
        local_copies[u].wait()
        for group in range(4):
            for tok in range(TOK):
                arrive(u, (group * 2 + 1 - core) * TOK + tok)

    return begin, along, crossing, corner, settle


def gather_sems(count):
    dma = pltpu.SemaphoreType.DMA
    return [
        dma((count,)),
        dma((count, 32)),
        dma((count, 32)),
        dma((count, 7, 2)),
        dma((count, 7)),
        dma((count, 7)),
        dma((count, TOK)),
        dma((count, TOK)),
        dma((count, 19)),
    ]


def rows_from(flat, out):
    rows, n = out.shape[0], out.shape[1] // 128
    for c in range(n):
        out[:, c * 128 : (c + 1) * 128] = flat[pl.ds(c, rows, stride=n), :].astype(out.dtype)


def join_affine(blocks, out):
    lane = lax.broadcasted_iota(jnp.int32, (16, 128), 1)
    tiles = [jnp.zeros((16, 128), jnp.float32) for _ in range(6)]
    for i in range(32):
        block = jnp.where(lane < EACH, blocks[i].astype(jnp.float32), 0.0)
        tile, shift = (i * EACH) // 128, (i * EACH) % 128
        turned = pltpu.roll(block, shift, 1) if shift else block
        tiles[tile] = tiles[tile] + jnp.where(lane >= shift, turned, 0.0)
        if shift + EACH > 128:
            tiles[tile + 1] = tiles[tile + 1] + jnp.where(lane < shift, turned, 0.0)
    for i in range(6):
        out[:, i * 128 : (i + 1) * 128] = tiles[i]


def scatter_steps(units, parts, held, core_in, side_in, part_in, z_in, sems, flight, finals):
    load_sem, c_send, c_recv, d_send, d_recv, s_send, s_recv, z_send, z_recv = sems
    y, x, core, t = spot()
    here, by_x, by_y = clip_of(y, x, core), clip_of(y, 1 - x, core), clip_of(1 - y, x, core)
    mate = clip_of(y, x, 1 - core)
    homes = [(1 - y, 1 - x), (y, 1 - x), (1 - y, x), (y, x)]

    def cols(u, half=None):
        k, c, width = units[u]
        if half is None:
            return pl.ds(c, width)
        return pl.ds(c + half * (width // 2), width // 2)

    def remote(src, dst, send_sem, recv_sem, to, tok=None):
        return pltpu.make_async_remote_copy(
            src_ref=src,
            dst_ref=dst,
            send_sem=send_sem,
            recv_sem=recv_sem,
            device_id=(to, t if tok is None else tok),
            device_id_type=MESH,
        )

    def load(u, g):
        k = units[u][0]
        ya, xa = homes[g]
        return pltpu.make_async_copy(
            parts[k].at[pl.ds(clip_of(ya, xa, core) * TOK, TOK), :, cols(u)],
            held[k].at[g, :, :, cols(u)],
            load_sem.at[u, g],
        )

    def to_mate(u, g):
        k = units[u][0]
        ya, xa = homes[g]
        return remote(
            parts[k].at[pl.ds(clip_of(ya, xa, 1 - core) * TOK, TOK), :, cols(u)],
            core_in[k].at[g, :, :, cols(u)],
            c_send.at[u, g],
            c_recv.at[u, g],
            mate,
        )

    def begin(u):
        for g in range(4):
            load(u, g).start()
            flight.go(to_mate(u, g))

    def ready(u, g):
        load(u, g).wait()
        to_mate(u, g).wait_recv()

    def add_into(k, g, start, width, pieces):
        def one(j, carry):
            at = slice(start, start + width)
            total = held[k][g, j, :, at].astype(jnp.float32)
            for piece in pieces:
                total = total + piece[j, :, at].astype(jnp.float32)
            held[k][g, j, :, at] = total.astype(jnp.bfloat16)
            return carry

        lax.fori_loop(0, TOK, one, 0)

    def halves(u):
        return units[u][2] % 256 == 0

    def first(u, half):
        k = units[u][0]
        at = cols(u, half) if halves(u) else cols(u)
        return remote(
            held[k].at[0, :, :, at],
            side_in[k].at[:, :, at],
            d_send.at[u, half],
            d_recv.at[u, half],
            by_y if half else by_x,
        )

    def second(u, across):
        k = units[u][0]
        return remote(
            held[k].at[1 if across == 0 else 2, :, :, cols(u)],
            part_in[k].at[across, :, :, cols(u)],
            s_send.at[u, across],
            s_recv.at[u, across],
            by_x if across == 0 else by_y,
        )

    def last(u, far):
        k = units[u][0]
        tok = (t + far) % TOK
        return remote(
            held[k].at[3, tok, :, cols(u)],
            z_in[k].at[far - 1, :, cols(u)],
            z_send.at[u, far - 1],
            z_recv.at[u, far - 1],
            here,
            tok,
        )

    def step1(u):
        k, c, width = units[u]
        ready(u, 0)
        add_into(k, 0, c, width, [core_in[k].at[0]])
        flight.go(first(u, 0))
        if halves(u):
            flight.go(first(u, 1))

    def step2(u):
        k, c, width = units[u]
        half = width // 2 if halves(u) else width
        ready(u, 2)
        first(u, 0).wait_recv()
        add_into(k, 2, c, half, [core_in[k].at[2], side_in[k]])
        if halves(u):
            add_into(k, 2, c + half, half, [core_in[k].at[2]])
        flight.go(second(u, 1))
        ready(u, 1)
        if halves(u):
            first(u, 1).wait_recv()
            add_into(k, 1, c, half, [core_in[k].at[1]])
            add_into(k, 1, c + half, half, [core_in[k].at[1], side_in[k]])
        else:
            add_into(k, 1, c, width, [core_in[k].at[1]])
        flight.go(second(u, 0))

    def step3(u):
        k, c, width = units[u]
        ready(u, 3)
        second(u, 0).wait_recv()
        second(u, 1).wait_recv()
        add_into(k, 3, c, width, [core_in[k].at[3], part_in[k].at[0], part_in[k].at[1]])
        for far in range(1, TOK):
            flight.go(last(u, far))

    def step4(u):
        k, c, width = units[u]
        at = slice(c, c + width)
        total = held[k][3, t, :, at].astype(jnp.float32)
        for far in range(1, TOK):
            last(u, far).wait_recv()
            total = total + z_in[k][far - 1, :, at].astype(jnp.float32)
        finals(u, total)

    return begin, step1, step2, step3, step4


def scatter_scratch(shapes):
    bf16 = jnp.bfloat16
    held = [pltpu.VMEM((4, TOK) + s, bf16) for s in shapes]
    side = [pltpu.VMEM((TOK,) + s, bf16) for s in shapes]
    part = [pltpu.VMEM((2, TOK) + s, bf16) for s in shapes]
    last = [pltpu.VMEM((TOK - 1,) + s, bf16) for s in shapes]
    return held + held + side + part + last


def scatter_sems(count):
    dma = pltpu.SemaphoreType.DMA
    return [
        dma((count, 4)),
        dma((count, 4)),
        dma((count, 4)),
        dma((count, 2)),
        dma((count, 2)),
        dma((count, 2)),
        dma((count, 2)),
        dma((count, TOK - 1)),
        dma((count, TOK - 1)),
    ]


STEP_FIX = 1.0 - 0.5**STEP


def adamw_rows(rate, weights, moment, square, grad, out):
    averaged = 0.5 * moment + 0.5 * grad
    squared = 0.5 * square + 0.5 * grad * grad
    out[0][...] = weights - rate * (
        averaged / STEP_FIX / (jnp.sqrt(squared / STEP_FIX) + 1e-08) + 0.1 * weights
    )
    out[1][...] = averaged
    out[2][...] = squared


RATES = (768 ** (-0.5), 384 ** (-0.5), 11 ** (-0.5), 768 ** (-0.5), 3072 ** (-0.5))


def part_affine(norms, out):
    rows = [jnp.sum(n[0:8, :], axis=0, keepdims=True) for n in norms]
    rows += [jnp.sum(n[8:16, :], axis=0, keepdims=True) for n in norms]
    table = jnp.concatenate(rows + [jnp.zeros((10, 768), jnp.float32)], axis=0)
    lane = lax.broadcasted_iota(jnp.int32, (16, 128), 1)
    for i in range(32):
        tile, shift = (i * EACH) // 128, (i * EACH) % 128
        block = table[:, tile * 128 : (tile + 1) * 128]
        block = pltpu.roll(block, (128 - shift) % 128, 1) if shift else block
        if shift + EACH > 128:
            after = pltpu.roll(table[:, (tile + 1) * 128 : (tile + 2) * 128], 128 - shift, 1)
            block = jnp.where(lane < 128 - shift, block, after)
        out[i] = jnp.where(lane < EACH, block, 0.0).astype(jnp.bfloat16)

GROUPS = 7
T_ROWS = 448
S_PAD = 208
S_ROWS = 416
CHUNK = 256
MLP_CHUNK = 512
SCALE = HEAD_DIM ** (-0.5)
BIG = -1e30
NT = (((1,), (1,)), ((), ()))
TN = (((0,), (0,)), ((), ()))


def dot(left, right, dims=(((1,), (0,)), ((), ()))):
    return lax.dot_general(left, right, dims, preferred_element_type=jnp.float32)


def low(values):
    return values.astype(jnp.bfloat16)


def up(values):
    return values.astype(jnp.float32)


def center_rows(values):
    center = values - jnp.mean(values, axis=-1, keepdims=True)
    inverse = lax.rsqrt(jnp.mean(center * center, axis=-1, keepdims=True) + 1e-06)
    return center * inverse, inverse


def back_rows(upstream, unit, inverse, gain):
    scaled = upstream * gain
    inner = (
        scaled
        - jnp.mean(scaled, axis=-1, keepdims=True)
        - unit * jnp.mean(scaled * unit, axis=-1, keepdims=True)
    )
    return inner * inverse


def fold(values):
    return jnp.sum(values.reshape(-1, 8, values.shape[-1]), axis=0)


def columns(j, width):
    return pl.ds(pl.multiple_of(j * width, 128), width)


def rows_of(i, height):
    return pl.ds(pl.multiple_of(i * height, 8), height)


def times(out, left, weight, width=CHUNK):
    def step(j, carry):
        at = columns(j, width)
        out[:, at] = dot(left[...], weight[:, at]).astype(out.dtype)
        return carry

    lax.fori_loop(0, out.shape[1] // width, step, 0)


def lane_half(shape):
    return lax.broadcasted_iota(jnp.int32, shape, 1) < HEAD_DIM


def soft(query, keys, mask):
    scores = jnp.where(mask, dot(query, keys, NT) * SCALE, BIG)
    expo = jnp.exp(scores - jnp.max(scores, axis=-1, keepdims=True))
    return expo / jnp.sum(expo, axis=-1, keepdims=True)


def attend(query, keys, values, mask):
    half = lane_half(query.shape)
    zero = jnp.zeros_like(query)
    first = dot(low(soft(jnp.where(half, query, zero), keys, mask)), values)
    second = dot(low(soft(jnp.where(half, zero, query), keys, mask)), values)
    return low(jnp.where(half, first, second))


def attend_back(query, keys, values, upstream, mask):
    half = lane_half(query.shape)
    zero = jnp.zeros_like(query)

    def one(pick):
        probs = soft(pick(query, zero), keys, mask)
        dprobs = dot(pick(upstream, zero), values, NT)
        dscores = low(probs * (dprobs - jnp.sum(dprobs * probs, axis=-1, keepdims=True)))
        return (
            dot(dscores, keys) * SCALE,
            dot(dscores, query, TN) * SCALE,
            dot(low(probs), upstream, TN),
        )

    first = one(lambda a, b: jnp.where(half, a, b))
    second = one(lambda a, b: jnp.where(half, b, a))
    return tuple(low(jnp.where(half, a, b)) for a, b in zip(first, second))


def frame_mask(size):
    patch = lambda axis: (lambda i: (i // 64) * 8 + i % 8)(
        lax.broadcasted_iota(jnp.int32, (size, size), axis)
    )
    return patch(0) == patch(1)


def patch_mask():
    return lax.broadcasted_iota(jnp.int32, (S_PAD, S_PAD), 1) < PATCHES


T_BLOCKS = ((0, 128), (128, 128), (256, 128), (384, 64))


def mlp_kernel(lowered, after_s, cotangent, widen, narrow, affine, result, d_narrow, d_widen, d_after, d_norm, cot, turned, total, back):
    j = pl.program_id(0)

    @pl.when(j == 0)
    def start():
        cot[...] = jnp.zeros_like(cot)
        for f in range(2):
            back[pl.ds(f * S_PAD, PATCHES), :] = up(cotangent[f])
            back[pl.ds(f * S_PAD + PATCHES, S_PAD - PATCHES), :] = jnp.zeros((S_PAD - PATCHES, D), jnp.float32)
        cot[...] = low(back[...])
        turned[...] = lowered[...].T
        total[...] = after_s[...]
        back[...] = jnp.zeros_like(back)

    wide = dot(lowered[...], widen[...])
    phi = 0.5 * (1.0 + lax.erf(wide * 0.7071067811865476))
    active = low(wide * phi)
    slope = phi + wide * jnp.exp(-0.5 * wide * wide) * 0.3989422804014327
    d_wide = low(dot(cot[...], narrow[...], NT) * slope)
    total[...] += dot(active, narrow[...])
    d_narrow[...] = low(dot(active, cot[...], TN))
    d_widen[...] = low(dot(turned[...], d_wide))
    back[...] += dot(d_wide, widen[...], NT)

    @pl.when(j == pl.num_programs(0) - 1)
    def finish():
        for f in range(2):
            result[f] = low(total[pl.ds(f * S_PAD, PATCHES), :])

        def norm(b, carry):
            rows = rows_of(b, 32)
            unit, inverse = center_rows(after_s[rows, :])
            upstream = back[rows, :]
            d_after[rows, :] = up(cot[rows, :]) + back_rows(upstream, unit, inverse, affine[2:3, :])
            return carry[0] + fold(upstream * unit), carry[1] + fold(upstream)

        zero = jnp.zeros((8, D), jnp.float32)
        gain, shift = lax.fori_loop(0, S_ROWS // 32, norm, (zero, zero))
        d_norm[0:8, :] = gain
        d_norm[8:16, :] = shift


def mlp(lowered, after_s, cotangent, widen, narrow, affine):
    whole = lambda shape: pl.BlockSpec(shape, lambda j: (0,) * len(shape))
    steps = HID // MLP_CHUNK
    return pl.pallas_call(
        mlp_kernel,
        grid=(steps,),
        in_specs=[
            whole((S_ROWS, D)),
            whole((S_ROWS, D)),
            whole((2, PATCHES, D)),
            pl.BlockSpec((D, MLP_CHUNK), lambda j: (0, j)),
            pl.BlockSpec((MLP_CHUNK, D), lambda j: (j, 0)),
            whole((16, D)),
        ],
        out_specs=[
            whole((2, PATCHES, D)),
            pl.BlockSpec((MLP_CHUNK, D), lambda j: (j, 0)),
            pl.BlockSpec((D, MLP_CHUNK), lambda j: (0, j)),
            whole((S_ROWS, D)),
            whole((16, D)),
        ],
        out_shape=[
            jax.ShapeDtypeStruct((2, PATCHES, D), jnp.bfloat16),
            jax.ShapeDtypeStruct((HID, D), jnp.bfloat16),
            jax.ShapeDtypeStruct((D, HID), jnp.bfloat16),
            jax.ShapeDtypeStruct((S_ROWS, D), jnp.float32),
            jax.ShapeDtypeStruct((16, D), jnp.float32),
        ],
        scratch_shapes=[
            pltpu.VMEM((S_ROWS, D), jnp.bfloat16),
            pltpu.VMEM((D, S_ROWS), jnp.bfloat16),
            pltpu.VMEM((S_ROWS, D), jnp.float32),
            pltpu.VMEM((S_ROWS, D), jnp.float32),
        ],
        compiler_params=pltpu.CompilerParams(vmem_limit_bytes=56 * 1024 * 1024),
        cost_estimate=pl.CostEstimate(flops=12000000000, bytes_accessed=30000000, transcendentals=0),
    )(lowered, after_s, cotangent, widen, narrow, affine)

def pack(box, rows):
    extra = [rows(f, 192, 4) for f in range(2)]
    line = lax.broadcasted_iota(jnp.int32, (16, D), 0)
    for s in range(TOK):
        wide = [rows(f, 48 * s, 48) for f in range(2)]
        for b in range(6):
            pair = [w[8 * b : 8 * b + 8, :] for w in wide]
            box[s, b] = low(jnp.concatenate(pair, axis=0))
        one = [jnp.broadcast_to(e[s : s + 1, :], (16, D)) for e in extra]
        box[s, 6] = low(jnp.where(line == 0, one[0], jnp.where(line == 8, one[1], 0.0)))


def unpack(box, f, put):
    for s in range(TOK):
        for b in range(6):
            slab = up(box[s, b])
            put(48 * s + 8 * b, 8, slab[8 * f : 8 * f + 8, :])
    last = [up(box[s, 6])[8 * f : 8 * f + 1, :] for s in range(TOK)]
    put(192, TOK, jnp.concatenate(last, axis=0))


class Exchange:
    def __init__(self, source, target, sems, flight):
        self.source, self.target, self.flight = source, target, flight
        self.local, self.sent, self.got = sems
        self.clip, self.t = lax.axis_index("clip"), lax.axis_index("tok")

    def copy(self, far):
        return pltpu.make_async_remote_copy(
            src_ref=self.source((self.t + far) % TOK),
            dst_ref=self.target(self.t),
            send_sem=self.sent.at[far - 1],
            recv_sem=self.got.at[far - 1],
            device_id=(self.clip, (self.t + far) % TOK),
            device_id_type=MESH,
        )

    def own(self):
        return pltpu.make_async_copy(self.source(self.t), self.target(self.t), self.local.at[0])

    def start(self):
        for far in range(1, TOK):
            self.flight.go(self.copy(far))
        self.own().start()

    def wait(self):
        for far in range(1, TOK):
            there = self.target((self.t - far + TOK) % TOK)
            pltpu.make_async_copy(there, there, self.got.at[far - 1]).wait()
        self.own().wait()


def exchange_sems():
    dma = pltpu.SemaphoreType.DMA
    return [dma((1,)), dma((TOK - 1,)), dma((TOK - 1,))]


def pieces(count, step, size):
    def run(lo, hi):
        def one(j, carry):
            step(j)
            return carry

        lax.fori_loop(lo, hi, one, 0)

    return [functools.partial(run, lo, min(lo + size, count)) for lo in range(0, count, size)]


def product(out, left, weight, width=CHUNK):
    def step(j):
        at = columns(j, width)
        out[:, at] = dot(left(), weight[:, at]).astype(out.dtype)

    return step


def product_back(out, left, weight, width=CHUNK):
    def step(j):
        at = columns(j, width)
        out[:, at] = dot(left(), weight[at, :], NT).astype(out.dtype)

    return step


def gradient(out, turned, upstream, width=CHUNK):
    def step(j):
        at = columns(j, width)
        out[:, at] = low(dot(turned[...], upstream(at)))

    return step


def in_turn(first, second):
    for i in range(max(len(first), len(second))):
        if i < len(first):
            first[i]()
        if i < len(second):
            second[i]()


def full_kernel_steps(units, steps, shifts, lo, hi):
    calls = []
    for n in range(lo, hi):
        for shift, step in zip(shifts, steps):
            if 0 <= n - shift < len(units):
                calls.append(functools.partial(step, n - shift))
    return calls


def forward_kernel(units, *refs):
    masters, block, frames = refs[:5], refs[5], refs[6]
    full = list(refs[7:12])
    affine, patch, normed_t, merged_t, mixed_t, first_t = refs[12:18]
    after_t, normed_s, merged_s, mixed_s, after_s, lowered = refs[18:24]
    owned, gathered = list(refs[24:29]), refs[29]
    entry_w, temporal_w, spatial_w, outbox, sent, inbox, load_sem = refs[30:37]
    there_sems, back_sems = refs[37:40], refs[40:43]
    sems = refs[43:]
    greet()
    full.append(gathered)
    owned.append(block)
    flight = Flight()
    begin, along, crossing, corner, settle = gather_steps(units, owned, full, sems, flight)
    count = len(units)
    place = {k: [n for n in range(count) if units[n][0] == k] for k in range(6)}
    there = Exchange(lambda s: outbox.at[s], lambda s: patch.at[:, s], there_sems, flight)
    back = Exchange(lambda s: sent.at[:, s], lambda s: inbox.at[s], back_sems, flight)
    comm = lambda lo, hi: full_kernel_steps(units, (begin, along, crossing, corner), (0, 1, 2, 3), lo, hi)

    def settle_all(k):
        for n in place[k]:
            settle(n)

    ready = set()
    original = begin

    def begin(n):
        k = units[n][0]
        if k not in ready and k != AFFINE:
            rows_from(masters[k], owned[k])
            ready.add(k)
        original(n)

    comm = lambda lo, hi: full_kernel_steps(units, (begin, along, crossing, corner), (0, 1, 2, 3), lo, hi)
    for call in comm(0, 2):
        call()
    pack(outbox, lambda f, start, size: up(frames[f, start : start + size, :]))
    there.start()
    split = place[1][-1] + 4
    for call in comm(2, split):
        call()

    def load(part, source, target):
        return pltpu.make_async_copy(source, target, load_sem.at[part])

    loads = {
        "entry": load(0, full[0].at[pl.ds(0, 16)], entry_w),
        "temporal": load(1, full[1], temporal_w),
        "later": load(2, full[0].at[pl.ds(16, 16)], entry_w),
        "spatial": load(3, full[2], spatial_w),
    }
    settle_all(AFFINE)
    join_affine(gathered, affine)
    there.wait()

    def norm_t(b):
        unit, unused = center_rows(up(patch[b].reshape(64, D)))
        normed_t[rows_of(b, 64), :] = low(unit * affine[0:1, :] + affine[3:4, :])

    def heads_t(p):
        for start, size in T_BLOCKS:
            rows = pl.ds(start, size)
            query, keys, values = (merged_t[rows, columns(p + 6 * i, 128)] for i in range(3))
            mixed_t[rows, columns(p, 128)] = attend(query, keys, values, frame_mask(size))

    entry_m = lambda at: entry_w[:, :, at].reshape(D, CHUNK)

    def merge(out, left):
        def step(j):
            at = columns(j, CHUNK)
            out[:, at] = low(dot(left[...], entry_m(at)))

        return step

    def first_step(j):
        at = columns(j, CHUNK)
        first_t[:, at] = low(dot(mixed_t[...], temporal_w[0:16, :, at].reshape(D, CHUNK)))

    def branch_step(j):
        at = columns(j, CHUNK)
        value = low(dot(first_t[...], temporal_w[16:32, :, at].reshape(D, CHUNK)))
        sent[:, :, :, at] = value.reshape(GROUPS, TOK, 16, CHUNK)

    def start_temporal():
        settle_all(0)
        settle_all(1)
        loads["entry"].start()
        loads["temporal"].start()
        for call in pieces(GROUPS, norm_t, GROUPS):
            call()
        loads["entry"].wait()
        loads["temporal"].wait()

    def start_spatial():
        settle_all(2)
        loads["later"].start()
        loads["spatial"].start()
        back.wait()
        for f in range(2):

            def put(start, size, rows, f=f):
                after_t[f * S_PAD + start : f * S_PAD + start + size, :] = (
                    up(frames[f, start : start + size, :]) + rows
                )

            unpack(inbox, f, put)
            tail = f * S_PAD + PATCHES
            after_t[tail : (f + 1) * S_PAD, :] = jnp.zeros((S_PAD - PATCHES, D), jnp.float32)

    def norm_s(b):
        unit, unused = center_rows(after_t[rows_of(b, 32), :])
        normed_s[rows_of(b, 32), :] = low(unit * affine[1:2, :] + affine[4:5, :])

    def wait_spatial():
        loads["later"].wait()
        loads["spatial"].wait()

    def heads_s(n):
        p, f = n % 6, n // 6
        rows = pl.ds(pl.multiple_of(f * S_PAD, 16), S_PAD)
        query, keys, values = (merged_s[rows, columns(p + 6 * i, 128)] for i in range(3))
        mixed_s[rows, columns(p, 128)] = attend(query, keys, values, patch_mask())

    def out_s(j):
        at = columns(j, CHUNK)
        weight = low(up(spatial_w[:, :, at]).reshape(D, CHUNK))
        after_s[:, at] = after_t[:, at] + dot(mixed_s[...], weight)

    def norm_m(b):
        unit, unused = center_rows(after_s[rows_of(b, 32), :])
        lowered[rows_of(b, 32), :] = low(unit * affine[2:3, :] + affine[5:6, :])

    compute = (
        [start_temporal]
        + pieces(9, merge(merged_t, normed_t), 3)
        + pieces(6, heads_t, 1)
        + pieces(3, first_step, 3)
        + pieces(3, branch_step, 3)
        + [back.start]
    )
    more = (
        [start_spatial]
        + pieces(13, norm_s, 13)
        + [wait_spatial]
        + pieces(9, merge(merged_s, normed_s), 3)
        + pieces(12, heads_s, 1)
        + pieces(3, out_s, 3)
        + pieces(13, norm_m, 13)
    )
    rest = comm(split, count + 3)
    in_turn(compute + more, rest)
    for k in (3, 4):
        settle_all(k)
    flight.drain()


def forward(masters, block, frames):
    units = units_of(ORDER_IN)
    vmem = pl.BlockSpec(memory_space=pltpu.VMEM)
    anywhere = pl.BlockSpec(memory_space=pl.ANY)
    bf16, f32 = jnp.bfloat16, jnp.float32
    slab = (TOK, GROUPS, 16, D)
    group = (GROUPS, TOK, 16, D)
    saved = [
        ((16, D), f32),
        (group, bf16),
        ((T_ROWS, D), bf16),
        ((T_ROWS, 3 * D), bf16),
        ((T_ROWS, D), bf16),
        ((T_ROWS, D), bf16),
        ((S_ROWS, D), f32),
        ((S_ROWS, D), bf16),
        ((S_ROWS, 3 * D), bf16),
        ((S_ROWS, D), bf16),
        ((S_ROWS, D), f32),
        ((S_ROWS, D), bf16),
    ]
    return pl.pallas_call(
        functools.partial(forward_kernel, units),
        out_shape=[jax.ShapeDtypeStruct((32, r, w), bf16) for r, w in zip(ROWS, WIDTHS)]
        + [jax.ShapeDtypeStruct(s, t) for s, t in saved],
        in_specs=[vmem] * 7,
        out_specs=[anywhere] * 5 + [vmem] * 12,
        scratch_shapes=[pltpu.VMEM((r, w), bf16) for r, w in zip(ROWS, WIDTHS)]
        + [
            pltpu.VMEM((32, 16, 128), bf16),
            pltpu.VMEM((16, 48, 3 * D), bf16),
            pltpu.VMEM((32, 48, D), bf16),
            pltpu.VMEM((32, 24, D), bf16),
            pltpu.VMEM(slab, bf16),
            pltpu.VMEM(group, bf16),
            pltpu.VMEM(slab, bf16),
            pltpu.SemaphoreType.DMA((4,)),
        ]
        + exchange_sems()
        + exchange_sems()
        + gather_sems(len(units)),
        compiler_params=pltpu.CompilerParams(
            collective_id=0, has_side_effects=True, vmem_limit_bytes=VMEM_LIMIT
        ),
    )(*masters, block, frames)


def finals_of(states, outs, grads, affine_out=None):
    def finals(u, unit, total):
        k, c, width = unit
        if k == AFFINE:
            affine_out[...] = total
            return
        n, rows = WIDTHS[k] // 128, ROWS[k]
        for i in range(width // 128):
            grads[k][pl.ds(c // 128 + i, rows, stride=n), :] = total[:, i * 128 : (i + 1) * 128]
        if c + width == WIDTHS[k]:
            state = states[k]
            adamw_rows(RATES[k], state[0][...], state[1][...], state[2][...], grads[k][...], outs[k])

    return finals


def back_kernel(units, *refs):
    arrays = (3, 4)
    parts = dict(zip(arrays, refs[:2]))
    states = {k: refs[2 + 3 * i : 5 + 3 * i] for i, k in enumerate(arrays)}
    d_after_s, after_t, affine, spatial = refs[8:12]
    normed_s_in, merged_s_in, mixed_s_in, entry_in = refs[12:16]
    patch_in, normed_t_in, merged_t_in, mixed_t_in, first_t_in, temporal_in = refs[16:22]
    outs = {k: refs[22 + 3 * i : 25 + 3 * i] for i, k in enumerate(arrays)}
    input_gradient, d_spatial, d_entry_out, d_temporal, norm_s_out, norm_t_out = refs[28:34]
    pos = 34
    pools = []
    for i in range(5):
        pools.append(dict(zip(arrays, refs[pos : pos + 2])))
        pos += 2
    grads = dict(zip(arrays, refs[pos : pos + 2]))
    pos += 2
    normed_s, merged_s, mixed_s, entry_w = refs[pos : pos + 4]
    patch, normed_t, merged_t, mixed_t, first_t, temporal_w = refs[pos + 4 : pos + 10]
    d_after_t, d_entry, lowered, d_mixed, d_first, d_merged, turned_s, turned_t, back, outbox, grouped, sent, inbox, load_sem = refs[
        pos + 10 : pos + 24
    ]
    pos += 24
    there_sems, back_sems = refs[pos : pos + 3], refs[pos + 3 : pos + 6]
    sems = refs[pos + 6 :]
    sources = (normed_s_in, merged_s_in, mixed_s_in, entry_in.at[1])
    targets = (normed_s, merged_s, mixed_s, entry_w)
    sources += (patch_in, normed_t_in, merged_t_in, mixed_t_in, first_t_in, temporal_in)
    targets += (patch, normed_t, merged_t, mixed_t, first_t, temporal_w)
    loads = [pltpu.make_async_copy(a, b, load_sem.at[i]) for i, (a, b) in enumerate(zip(sources, targets))]
    for copy in loads:
        copy.start()
    entry_load = pltpu.make_async_copy(entry_in.at[0], entry_w, load_sem.at[10])
    entry_stores = [pltpu.make_async_copy(d_entry, d_entry_out.at[i], load_sem.at[12 - i]) for i in range(2)]
    greet()
    flight = Flight()
    finals = finals_of(states, outs, grads)
    steps = scatter_steps(
        units, parts, *pools, sems, flight, lambda u, total: finals(u, units[u], total)
    )
    there = Exchange(lambda s: outbox.at[s], lambda s: grouped.at[:, s], there_sems, flight)
    home = Exchange(lambda s: sent.at[:, s], lambda s: inbox.at[s], back_sems, flight)
    zero = jnp.zeros((8, D), jnp.float32)

    def begin_s():
        lowered[...] = low(d_after_s[...])
        for copy in loads[:3]:
            copy.wait()
        turned_s[...] = mixed_s[...].T

    def turn_s():
        turned_s[...] = normed_s[...].T

    def heads_s(n):
        p, f = n % 6, n // 6
        rows = pl.ds(pl.multiple_of(f * S_PAD, 16), S_PAD)
        query, keys, values = (merged_s[rows, columns(p + 6 * i, 128)] for i in range(3))
        found = attend_back(query, keys, values, d_mixed[rows, columns(p, 128)], patch_mask())
        for i in range(3):
            d_merged[rows, columns(p + 6 * i, 128)] = found[i]

    def s_back(j):
        at = columns(j, CHUNK)
        back[0:S_ROWS, at] = dot(d_merged[0:S_ROWS, :], entry_w[at, :], NT)

    def end_s():
        entry_load.start()

        def norm(b, carry):
            rows = rows_of(b, 32)
            unit, inverse = center_rows(after_t[rows, :])
            upstream = back[rows, :]
            d_after_t[rows, :] = d_after_s[rows, :] + back_rows(upstream, unit, inverse, affine[1:2, :])
            return carry[0] + fold(upstream * unit), carry[1] + fold(upstream)

        gain, shift = lax.fori_loop(0, S_ROWS // 32, norm, (zero, zero))
        norm_s_out[0:8, :] = gain
        norm_s_out[8:16, :] = shift
        pack(outbox, lambda f, start, size: d_after_t[f * S_PAD + start : f * S_PAD + start + size, :])
        there.start()

    def wait_entry():
        loads[3].wait()

    d_mixed_s = d_mixed.at[0:S_ROWS]
    compute = (
        [begin_s]
        + pieces(3, gradient(d_spatial, turned_s, lambda at: lowered[:, at]), 3)
        + pieces(3, product_back(d_mixed_s, lambda: lowered[...], spatial), 3)
        + [turn_s]
        + pieces(12, heads_s, 1)
        + [wait_entry]
        + pieces(3, s_back, 3)
        + [end_s]
        + pieces(9, gradient(d_entry, turned_s, lambda at: d_merged[0:S_ROWS, at]), 3)
        + [entry_stores[1].start]
    )

    def begin_t():
        for copy in loads[4:]:
            copy.wait()
        turned_t[...] = first_t[...].T
        there.wait()

    group_cols = lambda at: grouped[:, :, :, at].reshape(T_ROWS, CHUNK)

    def turn_mixed():
        turned_t[...] = mixed_t[...].T

    def turn_normed():
        turned_t[...] = normed_t[...].T

    def heads_t(p):
        for start, size in T_BLOCKS:
            rows = pl.ds(start, size)
            query, keys, values = (merged_t[rows, columns(p + 6 * i, 128)] for i in range(3))
            found = attend_back(query, keys, values, d_mixed[rows, columns(p, 128)], frame_mask(size))
            for i in range(3):
                d_merged[rows, columns(p + 6 * i, 128)] = found[i]

    def t_back(j):
        at = columns(j, CHUNK)
        back[:, at] = dot(d_merged[...], entry_w[at, :], NT)

    def end_t():
        def norm(b, carry):
            rows = rows_of(b, 64)
            unit, inverse = center_rows(up(patch[b].reshape(64, D)))
            upstream = back[rows, :]
            value = back_rows(upstream, unit, inverse, affine[0:1, :])
            sent[b] = low(value).reshape(TOK, 16, D)
            return carry[0] + fold(upstream * unit), carry[1] + fold(upstream)

        gain, shift = lax.fori_loop(0, GROUPS, norm, (zero, zero))
        norm_t_out[0:8, :] = gain
        norm_t_out[8:16, :] = shift
        home.start()

    def free_entry():
        entry_stores[1].wait()
        entry_load.wait()

    compute += (
        [begin_t]
        + pieces(3, gradient(d_temporal.at[1], turned_t, group_cols), 3)
        + pieces(3, product_back(d_first, lambda: grouped[...].reshape(T_ROWS, D), temporal_w.at[1]), 3)
        + [turn_mixed]
        + pieces(3, gradient(d_temporal.at[0], turned_t, lambda at: d_first[:, at]), 3)
        + pieces(3, product_back(d_mixed, lambda: d_first[...], temporal_w.at[0]), 3)
        + [turn_normed]
        + pieces(6, heads_t, 1)
        + [free_entry]
        + pieces(3, t_back, 3)
        + [end_t]
        + pieces(9, gradient(d_entry, turned_t, lambda at: d_merged[:, at]), 3)
        + [entry_stores[0].start]
    )
    rest = full_kernel_steps(units, steps, (0, 1, 2, 3, 4), 0, len(units) + 4)
    in_turn(rest, compute)
    home.wait()
    for f in range(2):

        def put(start, size, rows, f=f):
            at = f * S_PAD + start
            input_gradient[f, start : start + size, :] = d_after_t[at : at + size, :] + rows

        unpack(inbox, f, put)
    entry_stores[0].wait()
    flight.drain()


def backward(parts, states, d_after_s, after_t, affine, spatial, entry, temporal, saved_s, saved_t):
    units = units_of(ORDER_MLP)
    vmem = pl.BlockSpec(memory_space=pltpu.VMEM)
    anywhere = pl.BlockSpec(memory_space=pl.ANY)
    bf16, f32 = jnp.bfloat16, jnp.float32
    shapes = [(ROWS[k], WIDTHS[k]) for k in (3, 4)]
    flat = [(r * w // 128, 128) for r, w in shapes]
    slab = (TOK, GROUPS, 16, D)
    group = (GROUPS, TOK, 16, D)
    outs = [(s, f32) for s in flat for _ in range(3)] + [
        ((2, PATCHES, D), f32),
        ((D, D), bf16),
        ((2, D, 3 * D), bf16),
        ((2, D, D), bf16),
        ((16, D), f32),
        ((16, D), f32),
    ]
    return pl.pallas_call(
        functools.partial(back_kernel, units),
        out_shape=[jax.ShapeDtypeStruct(s, t) for s, t in outs],
        in_specs=[anywhere] * 2 + [vmem] * 10 + [anywhere] * 10,
        out_specs=[vmem] * 8 + [anywhere] + [vmem] * 3,
        scratch_shapes=scatter_scratch(shapes)
        + [pltpu.VMEM(s, f32) for s in flat]
        + [
            pltpu.VMEM((S_ROWS, D), bf16),
            pltpu.VMEM((S_ROWS, 3 * D), bf16),
            pltpu.VMEM((S_ROWS, D), bf16),
            pltpu.VMEM((D, 3 * D), bf16),
            pltpu.VMEM(group, bf16),
            pltpu.VMEM((T_ROWS, D), bf16),
            pltpu.VMEM((T_ROWS, 3 * D), bf16),
            pltpu.VMEM((T_ROWS, D), bf16),
            pltpu.VMEM((T_ROWS, D), bf16),
            pltpu.VMEM((2, D, D), bf16),
            pltpu.VMEM((S_ROWS, D), f32),
            pltpu.VMEM((D, 3 * D), bf16),
            pltpu.VMEM((S_ROWS, D), bf16),
            pltpu.VMEM((T_ROWS, D), bf16),
            pltpu.VMEM((T_ROWS, D), bf16),
            pltpu.VMEM((T_ROWS, 3 * D), bf16),
            pltpu.VMEM((D, S_ROWS), bf16),
            pltpu.VMEM((D, T_ROWS), bf16),
            pltpu.VMEM((T_ROWS, D), f32),
            pltpu.VMEM(slab, bf16),
            pltpu.VMEM(group, bf16),
            pltpu.VMEM(group, bf16),
            pltpu.VMEM(slab, bf16),
            pltpu.SemaphoreType.DMA((13,)),
        ]
        + exchange_sems()
        + exchange_sems()
        + scatter_sems(len(units)),
        compiler_params=pltpu.CompilerParams(
            collective_id=1, has_side_effects=True, vmem_limit_bytes=VMEM_LIMIT
        ),
    )(*parts, *states, d_after_s, after_t, affine, spatial, *saved_s, entry, *saved_t, temporal)


def rest_kernel(units, *refs):
    arrays = (0, 1, 2)
    parts = dict(zip(arrays, refs[:3]))
    norms = refs[3:6]
    states = {k: refs[6 + 3 * k : 9 + 3 * k] for k in arrays}
    outs = {k: refs[15 + 3 * k : 18 + 3 * k] for k in arrays}
    affine_out = refs[24]
    pos = 25
    pools = []
    for i in range(5):
        pools.append(dict(zip(arrays + (AFFINE,), refs[pos : pos + 4])))
        pos += 4
    parts[AFFINE] = refs[pos]
    grads = dict(zip(arrays, refs[pos + 1 : pos + 4]))
    sems = refs[pos + 4 :]
    greet()
    flight = Flight()
    finals = finals_of(states, outs, grads, affine_out)
    steps = scatter_steps(
        units, parts, *pools, sems, flight, lambda u, total: finals(u, units[u], total)
    )
    begin = steps[0]

    def begin_after(u):
        if units[u][0] == AFFINE:
            part_affine(norms, parts[AFFINE])
        begin(u)

    for call in full_kernel_steps(units, (begin_after,) + steps[1:], (0, 2, 3, 4, 5), 0, len(units) + 5):
        call()
    flight.drain()


def scatter_rest(parts, norms, states):
    units = units_of(ORDER_REST)
    vmem = pl.BlockSpec(memory_space=pltpu.VMEM)
    shapes = [(ROWS[k], WIDTHS[k]) for k in (0, 1, 2)]
    flat = [(r * w // 128, 128) for r, w in shapes]
    return pl.pallas_call(
        functools.partial(rest_kernel, units),
        out_shape=[jax.ShapeDtypeStruct(s, jnp.float32) for s in flat for _ in range(3)]
        + [jax.ShapeDtypeStruct((16, 128), jnp.float32)],
        in_specs=[pl.BlockSpec(memory_space=pl.ANY)] * 3 + [vmem] * 12,
        out_specs=[vmem] * 10,
        scratch_shapes=scatter_scratch(shapes + [(16, 128)])
        + [pltpu.VMEM((32, 16, 128), jnp.bfloat16)]
        + [pltpu.VMEM(s, jnp.float32) for s in flat]
        + scatter_sems(len(units)),
        compiler_params=pltpu.CompilerParams(
            collective_id=2, has_side_effects=True, vmem_limit_bytes=VMEM_LIMIT
        ),
    )(*parts, *norms, *states)


def on_device(
    frames,
    cotangent,
    entry_weights,
    entry_momentum,
    entry_variance,
    temporal_weights,
    temporal_momentum,
    temporal_variance,
    spatial_weights,
    spatial_momentum,
    spatial_variance,
    widen_weights,
    widen_momentum,
    widen_variance,
    narrow_weights,
    narrow_momentum,
    narrow_variance,
    norm_affine,
    affine_momentum,
    affine_variance,
):
    masters = (entry_weights, temporal_weights, spatial_weights, widen_weights, narrow_weights)
    block = jnp.pad(low(norm_affine).reshape(6, EACH), ((0, 10), (0, 128 - EACH)))
    found = forward(masters, block, frames[0])
    entry, temporal, spatial, widen, narrow = found[:5]
    entry = entry.reshape(2, D, 3 * D)
    temporal = temporal.reshape(2, D, D)
    spatial = spatial.reshape(D, D)
    widen = widen.reshape(D, HID)
    narrow = narrow.reshape(HID, D)
    affine, patch, normed_t, merged_t, mixed_t, first_t = found[5:11]
    after_t, normed_s, merged_s, mixed_s, after_s, lowered = found[11:17]
    result, narrow_grad, widen_grad, d_after_s, norm_m = mlp(
        lowered, after_s, cotangent[0], widen, narrow, affine
    )
    found = backward(
        (widen_grad.reshape(32, -1, HID), narrow_grad.reshape(32, -1, D)),
        (
            widen_weights,
            widen_momentum,
            widen_variance,
            narrow_weights,
            narrow_momentum,
            narrow_variance,
        ),
        d_after_s,
        after_t,
        affine,
        spatial,
        entry,
        temporal,
        (normed_s, merged_s, mixed_s),
        (patch, normed_t, merged_t, mixed_t, first_t),
    )
    widen_new, narrow_new = found[0:3], found[3:6]
    input_gradient, d_spatial, d_entry, d_temporal, norm_s, norm_t = found[6:12]
    found = scatter_rest(
        (d_entry.reshape(32, -1, 3 * D), d_temporal.reshape(32, -1, D), d_spatial.reshape(32, -1, D)),
        (norm_t, norm_s, norm_m),
        (
            entry_weights,
            entry_momentum,
            entry_variance,
            temporal_weights,
            temporal_momentum,
            temporal_variance,
            spatial_weights,
            spatial_momentum,
            spatial_variance,
        ),
    )
    affine_sum = found[9][:6, :EACH].reshape(2, 3, EACH)
    affine_new = adamw(norm_affine, affine_momentum, affine_variance, affine_sum, 0.5)
    return (
        result[None],
        input_gradient[None],
        *found[0:9],
        *widen_new,
        *narrow_new,
        affine_new[0],
        affine_new[1],
        affine_new[2][:, 0:2],
        affine_new[2][:, 2],
    )

def solution(mesh):
    return jax.shard_map(
        on_device if mesh.shape["clip"] == 8 and mesh.shape["tok"] == TOK else on_any,
        mesh=mesh,
        in_specs=(
            P("clip", "tok", None, None),
            P("clip", "tok", None, None),
            P(("clip", "tok"), None),
            P(("clip", "tok"), None),
            P(("clip", "tok"), None),
            P(("clip", "tok"), None),
            P(("clip", "tok"), None),
            P(("clip", "tok"), None),
            P(("clip", "tok"), None),
            P(("clip", "tok"), None),
            P(("clip", "tok"), None),
            P(("clip", "tok"), None),
            P(("clip", "tok"), None),
            P(("clip", "tok"), None),
            P(("clip", "tok"), None),
            P(("clip", "tok"), None),
            P(("clip", "tok"), None),
            P(None, None, ("clip", "tok")),
            P(None, None, ("clip", "tok")),
            P(None, None, ("clip", "tok")),
        ),
        out_specs=(
            P("clip", "tok", None, None),
            P("clip", "tok", None, None),
            P(("clip", "tok"), None),
            P(("clip", "tok"), None),
            P(("clip", "tok"), None),
            P(("clip", "tok"), None),
            P(("clip", "tok"), None),
            P(("clip", "tok"), None),
            P(("clip", "tok"), None),
            P(("clip", "tok"), None),
            P(("clip", "tok"), None),
            P(("clip", "tok"), None),
            P(("clip", "tok"), None),
            P(("clip", "tok"), None),
            P(("clip", "tok"), None),
            P(("clip", "tok"), None),
            P(("clip", "tok"), None),
            P(None, None, ("clip", "tok")),
            P(None, None, ("clip", "tok")),
            P(None, None, ("clip", "tok")),
            P(None, ("clip", "tok")),
        ),
        check_vma=False,
    )
```

```python
import functools

import jax
import jax.numpy as jnp
from jax import lax
from jax.experimental import pallas as pl
from jax.experimental.pallas import tpu as pltpu
from jax.sharding import PartitionSpec as P

D = 768
HEADS = 12
HEAD_DIM = 64
HID = 3072
PATCHES = 196
STEP = 5

time_scores = "cfphe,cgphe->cphfg"
time_mixed = "cphfg,cgphe->cfphe"
time_flip = "cphfg,cfphe->cgphe"
space_scores = "cfphe,cfqhe->cfhpq"
space_mixed = "cfhpq,cfqhe->cfphe"
space_flip = "cfhpq,cfphe->cfqhe"


def project(inputs, weight):
    return jnp.einsum("cfpa,ab->cfpb", inputs, weight, preferred_element_type=jnp.float32)


def project_back(upstream, weight):
    return jnp.einsum("cfpb,ab->cfpa", upstream, weight, preferred_element_type=jnp.float32)


def weight_sum(inputs, upstream):
    return jnp.einsum("cfpa,cfpb->ab", inputs, upstream, preferred_element_type=jnp.float32)


def layer_norm(values, gain, shift):
    center = values - jnp.mean(values, axis=-1, keepdims=True)
    inverse = lax.rsqrt(jnp.mean(center * center, axis=-1, keepdims=True) + 1e-06)
    unit = center * inverse
    return (unit * gain + shift, unit, inverse)


def norm_back(upstream, unit, inverse, gain):
    scaled = upstream * gain
    inner = (
        scaled
        - jnp.mean(scaled, axis=-1, keepdims=True)
        - unit * jnp.mean(scaled * unit, axis=-1, keepdims=True)
    )
    return (
        inner * inverse,
        jnp.sum(upstream * unit, axis=(0, 1, 2)),
        jnp.sum(upstream, axis=(0, 1, 2)),
    )


def split_heads(merged):
    lowered = merged.astype(jnp.bfloat16)
    parts = lowered.reshape(lowered.shape[:-1] + (3, HEADS, HEAD_DIM))
    return (parts[..., 0, :, :], parts[..., 1, :, :], parts[..., 2, :, :])


def attend_forward(heads, score_form, mixed_form):
    query, keys, values = heads
    scores = jnp.einsum(score_form, query, keys, preferred_element_type=jnp.float32) * HEAD_DIM ** (
        -0.5
    )
    top = jnp.max(scores, axis=-1, keepdims=True)
    expo = jnp.exp(scores - top)
    total = jnp.sum(expo, axis=-1, keepdims=True)
    probs = (expo / total).astype(jnp.bfloat16)
    mixed = jnp.einsum(mixed_form, probs, values, preferred_element_type=jnp.float32)
    joined = mixed.reshape(mixed.shape[:-2] + (HEADS * HEAD_DIM,)).astype(jnp.bfloat16)
    return (joined, top + jnp.log(total))


def attend_backward(heads, logsum, upstream_joined, score_form, mixed_form, flip_form):
    query, keys, values = heads
    upstream = upstream_joined.reshape(upstream_joined.shape[:-1] + (HEADS, HEAD_DIM))
    scale = HEAD_DIM ** (-0.5)
    scores = jnp.einsum(score_form, query, keys, preferred_element_type=jnp.float32) * scale
    probs = jnp.exp(scores - logsum)
    dprobs = jnp.einsum(score_form, upstream, values, preferred_element_type=jnp.float32)
    dscores = (probs * (dprobs - jnp.sum(dprobs * probs, axis=-1, keepdims=True))).astype(
        jnp.bfloat16
    )
    dquery = jnp.einsum(mixed_form, dscores, keys, preferred_element_type=jnp.float32) * scale
    dkeys = jnp.einsum(flip_form, dscores, query, preferred_element_type=jnp.float32) * scale
    dvalues = jnp.einsum(
        flip_form, probs.astype(jnp.bfloat16), upstream, preferred_element_type=jnp.float32
    )
    stacked = jnp.stack([dquery, dkeys, dvalues], axis=-3)
    return stacked.reshape(stacked.shape[:-3] + (3 * HEADS * HEAD_DIM,)).astype(jnp.bfloat16)


def collect(masters):
    gathered = (
        lax.all_gather(masters[0].astype(jnp.bfloat16), ("clip", "tok"), axis=0, tiled=True),
        lax.all_gather(masters[1].astype(jnp.bfloat16), ("clip", "tok"), axis=0, tiled=True),
        lax.all_gather(masters[2].astype(jnp.bfloat16), ("clip", "tok"), axis=0, tiled=True),
        lax.all_gather(masters[3].astype(jnp.bfloat16), ("clip", "tok"), axis=0, tiled=True),
        lax.all_gather(masters[4].astype(jnp.bfloat16), ("clip", "tok"), axis=0, tiled=True),
        lax.all_gather(masters[5].astype(jnp.bfloat16), ("clip", "tok"), axis=2, tiled=True),
    )
    return (
        gathered[0].reshape(2, D, 3 * D),
        gathered[1].reshape(2, D, D),
        gathered[2].reshape(D, D),
        gathered[3].reshape(D, HID),
        gathered[4].reshape(HID, D),
        gathered[5],
    )


def plain_forward(frames, masters):
    weights = collect(masters)
    entry, temporal, spatial, widen, narrow, affine = weights
    gains = affine.astype(jnp.float32)
    patchwise = lax.all_to_all(frames, "tok", split_axis=2, concat_axis=1, tiled=True)
    normed_t, unit_t, inverse_t = layer_norm(
        patchwise.astype(jnp.float32), gains[0, 0], gains[1, 0]
    )
    lowered_t = normed_t.astype(jnp.bfloat16)
    heads_t = split_heads(project(lowered_t, entry[0]))
    mixed_t, lse_t = attend_forward(heads_t, time_scores, time_mixed)
    first_t = project(mixed_t, temporal[0]).astype(jnp.bfloat16)
    branch = project(first_t, temporal[1]).astype(jnp.bfloat16)
    returned = lax.all_to_all(branch, "tok", split_axis=1, concat_axis=2, tiled=True)
    after_t = frames.astype(jnp.float32) + returned.astype(jnp.float32)
    normed_s, unit_s, inverse_s = layer_norm(after_t, gains[0, 1], gains[1, 1])
    lowered_s = normed_s.astype(jnp.bfloat16)
    heads_s = split_heads(project(lowered_s, entry[1]))
    mixed_s, lse_s = attend_forward(heads_s, space_scores, space_mixed)
    after_s = after_t + project(mixed_s, spatial)
    normed_m, unit_m, inverse_m = layer_norm(after_s, gains[0, 2], gains[1, 2])
    lowered_m = normed_m.astype(jnp.bfloat16)
    widened = project(lowered_m, widen)
    activated = jax.nn.gelu(widened, approximate=False).astype(jnp.bfloat16)
    result = (after_s + project(activated, narrow)).astype(jnp.bfloat16)
    saved = {
        "weights": weights,
        "unit_t": unit_t,
        "inverse_t": inverse_t,
        "lowered_t": lowered_t,
        "heads_t": heads_t,
        "lse_t": lse_t,
        "mixed_t": mixed_t,
        "first_t": first_t,
        "unit_s": unit_s,
        "inverse_s": inverse_s,
        "lowered_s": lowered_s,
        "heads_s": heads_s,
        "lse_s": lse_s,
        "mixed_s": mixed_s,
        "unit_m": unit_m,
        "inverse_m": inverse_m,
        "lowered_m": lowered_m,
        "widened": widened,
        "activated": activated,
    }
    return (result, saved)


def adamw(master, moment, square, grad, rate):
    fix = 1.0 - 0.5**STEP
    averaged = 0.5 * moment + 0.5 * grad
    squared = 0.5 * square + 0.5 * grad * grad
    updated = master - rate * (averaged / fix / (jnp.sqrt(squared / fix) + 1e-08) + 0.1 * master)
    return (updated, averaged, squared)

def on_any(
    frames,
    cotangent,
    entry_weights,
    entry_momentum,
    entry_variance,
    temporal_weights,
    temporal_momentum,
    temporal_variance,
    spatial_weights,
    spatial_momentum,
    spatial_variance,
    widen_weights,
    widen_momentum,
    widen_variance,
    narrow_weights,
    narrow_momentum,
    narrow_variance,
    norm_affine,
    affine_momentum,
    affine_variance,
):
    masters = (
        entry_weights,
        temporal_weights,
        spatial_weights,
        widen_weights,
        narrow_weights,
        norm_affine,
    )
    result, saved = plain_forward(frames, masters)
    entry, temporal, spatial, widen, narrow, affine = saved["weights"]
    gains = affine.astype(jnp.float32)
    narrow_grad = weight_sum(saved["activated"], cotangent)
    widened = saved["widened"]
    slope = (
        0.5 * (1.0 + lax.erf(widened * 0.7071067811865476))
        + widened * jnp.exp(-0.5 * widened * widened) * 0.3989422804014327
    )
    dwidened = (project_back(cotangent, narrow) * slope).astype(jnp.bfloat16)
    widen_grad = weight_sum(saved["lowered_m"], dwidened)
    dpart_m, gain_m, shift_m = norm_back(
        project_back(dwidened, widen), saved["unit_m"], saved["inverse_m"], gains[0, 2]
    )
    dafter_s = cotangent.astype(jnp.float32) + dpart_m
    dspatial = dafter_s.astype(jnp.bfloat16)
    spatial_grad = weight_sum(saved["mixed_s"], dspatial)
    dmixed_s = project_back(dspatial, spatial).astype(jnp.bfloat16)
    dfused_s = attend_backward(
        saved["heads_s"], saved["lse_s"], dmixed_s, space_scores, space_mixed, space_flip
    )
    entry_grad_s = weight_sum(saved["lowered_s"], dfused_s)
    dpart_s, gain_s, shift_s = norm_back(
        project_back(dfused_s, entry[1]), saved["unit_s"], saved["inverse_s"], gains[0, 1]
    )
    dafter_t = dafter_s + dpart_s
    dbranch = lax.all_to_all(
        dafter_t.astype(jnp.bfloat16), "tok", split_axis=2, concat_axis=1, tiled=True
    )
    temporal_grad_b = weight_sum(saved["first_t"], dbranch)
    dfirst = project_back(dbranch, temporal[1]).astype(jnp.bfloat16)
    temporal_grad_a = weight_sum(saved["mixed_t"], dfirst)
    dmixed_t = project_back(dfirst, temporal[0]).astype(jnp.bfloat16)
    dfused_t = attend_backward(
        saved["heads_t"], saved["lse_t"], dmixed_t, time_scores, time_mixed, time_flip
    )
    entry_grad_t = weight_sum(saved["lowered_t"], dfused_t)
    dsent, gain_t, shift_t = norm_back(
        project_back(dfused_t, entry[0]), saved["unit_t"], saved["inverse_t"], gains[0, 0]
    )
    dreturned = lax.all_to_all(
        dsent.astype(jnp.bfloat16), "tok", split_axis=1, concat_axis=2, tiled=True
    )
    input_gradient = dafter_t + dreturned.astype(jnp.float32)
    members = (
        jnp.stack([entry_grad_t, entry_grad_s]).reshape(-1, 128),
        jnp.stack([temporal_grad_a, temporal_grad_b]).reshape(-1, 128),
        spatial_grad.reshape(-1, 128),
        widen_grad.reshape(-1, 128),
        narrow_grad.reshape(-1, 128),
        jnp.stack([jnp.stack([gain_t, gain_s, gain_m]), jnp.stack([shift_t, shift_s, shift_m])]),
    )
    totals = (
        lax.psum_scatter(members[0], ("clip", "tok"), scatter_dimension=0, tiled=True),
        lax.psum_scatter(members[1], ("clip", "tok"), scatter_dimension=0, tiled=True),
        lax.psum_scatter(members[2], ("clip", "tok"), scatter_dimension=0, tiled=True),
        lax.psum_scatter(members[3], ("clip", "tok"), scatter_dimension=0, tiled=True),
        lax.psum_scatter(members[4], ("clip", "tok"), scatter_dimension=0, tiled=True),
        lax.psum_scatter(members[5], ("clip", "tok"), scatter_dimension=2, tiled=True),
    )
    entry_sum, temporal_sum, spatial_sum, widen_sum, narrow_sum, affine_sum = totals
    entry_new = adamw(entry_weights, entry_momentum, entry_variance, entry_sum, D ** (-0.5))
    temporal_new = adamw(
        temporal_weights, temporal_momentum, temporal_variance, temporal_sum, (D // 2) ** (-0.5)
    )
    spatial_new = adamw(
        spatial_weights,
        spatial_momentum,
        spatial_variance,
        spatial_sum,
        (3 * D // PATCHES) ** (-0.5),
    )
    widen_new = adamw(widen_weights, widen_momentum, widen_variance, widen_sum, D ** (-0.5))
    narrow_new = adamw(narrow_weights, narrow_momentum, narrow_variance, narrow_sum, HID ** (-0.5))
    affine_new = adamw(norm_affine, affine_momentum, affine_variance, affine_sum, 0.5)
    return (
        result,
        input_gradient,
        entry_new[0],
        entry_new[1],
        entry_new[2],
        temporal_new[0],
        temporal_new[1],
        temporal_new[2],
        spatial_new[0],
        spatial_new[1],
        spatial_new[2],
        widen_new[0],
        widen_new[1],
        widen_new[2],
        narrow_new[0],
        narrow_new[1],
        narrow_new[2],
        affine_new[0],
        affine_new[1],
        affine_new[2][:, 0:2],
        affine_new[2][:, 2],
    )

MESH = pl.DeviceIdType.MESH
TOK = 4
UNIT = 768
ROWS = (48, 48, 24, 24, 96)
WIDTHS = (2304, 768, 768, 3072, 768)
AFFINE = 5
EACH = 24
ORDER_IN = (5, 0, 1, 2, 3, 4)
ORDER_MLP = (4, 3)
ORDER_REST = (0, 1, 2, 5)
VMEM_LIMIT = 60 * 1024 * 1024


def units_of(order, unit=UNIT):
    units = []
    for k in order:
        if k == AFFINE:
            units.append((k, 0, 128))
        else:
            units += [(k, c, min(unit, WIDTHS[k] - c)) for c in range(0, WIDTHS[k], unit)]
    return units


def spot():
    clip = lax.axis_index("clip")
    return clip // 4, (clip // 2) % 2, clip % 2, lax.axis_index("tok")


def clip_of(y, x, core):
    return (y * 2 + x) * 2 + core


def greet():
    y, x, core, t = spot()
    barrier = pltpu.get_barrier_semaphore()

    def tell(clip, tok):
        pl.semaphore_signal(barrier, inc=1, device_id=(clip, tok), device_id_type=MESH)

    tell(clip_of(y, x, 1 - core), t)
    tell(clip_of(y, 1 - x, core), t)
    tell(clip_of(1 - y, x, core), t)
    for far in range(1, TOK):
        tell(clip_of(y, x, core), (t + far) % TOK)
    pl.semaphore_wait(barrier, 3 + (TOK - 1))


class Flight:
    def __init__(self):
        self.started = []

    def go(self, copy, when=None):
        if when is None:
            copy.start()
        else:
            pl.when(when)(copy.start)
        self.started.append((copy, when))
        return copy

    def drain(self):
        for copy, when in self.started:
            if when is None:
                copy.wait_send()
            else:
                pl.when(when)(copy.wait_send)


def gather_steps(units, owned, full, sems):
    local, got, late, core_got, out_sem, z_sem = sems
    y, x, core, t = spot()
    here, by_x, by_y = clip_of(y, x, core), clip_of(y, 1 - x, core), clip_of(1 - y, x, core)
    mate = clip_of(y, x, 1 - core)
    corner_clip = clip_of(1 - y, 1 - x, core)
    local_copies = []

    def place(u, at, half=None):
        k, c, width = units[u]
        if half is not None:
            width = width // 2
            c = c + half * width
        return full[k].at[at, :, pl.ds(c, width)]

    def send(u, at, to, tok=None, half=None, own=False, along_z=False, when=None):
        k, c, width = units[u]
        there = place(u, at, half)
        copy = pltpu.make_async_remote_copy(
            src_ref=owned[k].at[:, pl.ds(c, width)] if own else there,
            dst_ref=there,
            send_sem=(z_sem if along_z else out_sem).at[u],
            recv_sem=(late if half == 1 else got).at[u, at],
            device_id=(to, t if tok is None else tok),
            device_id_type=MESH,
        )
        if when is None:
            copy.start()
        else:
            pl.when(when)(copy.start)

    def many(u, count):
        k, c, width = units[u]
        return full[k].at[pl.ds(0, count), :, pl.ds(c, width)]

    def took(u, count, sem):
        there = many(u, count)
        pltpu.make_async_copy(there, there, sem.at[u]).wait()

    def arrive(u, at, half=None):
        there = place(u, at, half)
        pltpu.make_async_copy(there, there, (late if half == 1 else got).at[u, at]).wait()

    def spread(u, at, own=False, when=None):
        def both():
            send(u, at, by_x, own=own)
            send(u, at, by_y, own=own)

        if when is None:
            both()
        else:
            pl.when(when)(both)

    def begin(u):
        k, c, width = units[u]
        me = here * TOK + t
        copy = pltpu.make_async_copy(owned[k].at[:, pl.ds(c, width)], place(u, me), local.at[u])
        copy.start()
        local_copies.append(copy)
        send(u, me, here, t + 1, own=True, along_z=True, when=t < TOK - 1)
        send(u, me, here, t - 1, own=True, along_z=True, when=t > 0)
        spread(u, me, own=True)

    hops = [(far, way) for far in range(1, TOK) for way in (1, -1)]

    def guard(far, way):
        return t + far <= TOK - 1 if way == 1 else t - far >= 0

    def to_mate(u, clip):
        k, c, width = units[u]
        there = full[k].at[pl.ds(clip * TOK, TOK), :, pl.ds(c, width)]
        pltpu.make_async_remote_copy(
            src_ref=there,
            dst_ref=there,
            send_sem=out_sem.at[u],
            recv_sem=core_got.at[u],
            device_id=(mate, t),
            device_id_type=MESH,
        ).start()

    def along(u):
        for far, way in hops:
            at = here * TOK + t + far * way

            def passing(at=at, way=way):
                arrive(u, at)
                onward = t > 0 if way == 1 else t < TOK - 1
                send(u, at, here, t - way, along_z=True, when=onward)
                spread(u, at)

            pl.when(guard(far, way))(passing)
        local_copies[u].wait()
        to_mate(u, here)

    def crossing(u):
        halves = units[u][2] % 256 == 0
        for slot in range(TOK):
            tok = (t + slot) % TOK
            from_x, from_y = by_x * TOK + tok, by_y * TOK + tok
            arrive(u, from_x)
            if halves:
                send(u, from_x, by_y, half=1)
            arrive(u, from_y)
            send(u, from_y, by_x, half=0 if halves else None)
        to_mate(u, by_x)
        to_mate(u, by_y)

    def corner(u):
        halves = units[u][2] % 256 == 0
        for slot in range(TOK):
            at = corner_clip * TOK + (t + slot) % TOK
            if halves:
                arrive(u, at, 0)
                arrive(u, at, 1)
            else:
                arrive(u, at)
        to_mate(u, corner_clip)

    def settle(u):
        took(u, 16, core_got)

    def drain():
        edge = jnp.logical_or(t == 0, t == TOK - 1)
        for u in range(len(units)):
            took(u, 28, out_sem)

        def wait_z(count):
            for u in range(len(units)):
                took(u, count, z_sem)

        pl.when(edge)(functools.partial(wait_z, 1))
        pl.when(jnp.logical_not(edge))(functools.partial(wait_z, 5))

    return begin, along, crossing, corner, settle, drain


def gather_sems(count):
    dma = pltpu.SemaphoreType.DMA
    return [
        dma((count,)),
        dma((count, 32)),
        dma((count, 32)),
        dma((count,)),
        dma((count,)),
        dma((count,)),
    ]


def rows_from(flat, out):
    rows, n = out.shape[0], out.shape[1] // 128
    for c in range(n):
        out[:, c * 128 : (c + 1) * 128] = flat[pl.ds(c, rows, stride=n), :].astype(out.dtype)


def join_affine(blocks, out):
    lane = lax.broadcasted_iota(jnp.int32, (16, 128), 1)
    tiles = [jnp.zeros((16, 128), jnp.float32) for _ in range(6)]
    for i in range(32):
        block = jnp.where(lane < EACH, blocks[i].astype(jnp.float32), 0.0)
        tile, shift = (i * EACH) // 128, (i * EACH) % 128
        turned = pltpu.roll(block, shift, 1) if shift else block
        tiles[tile] = tiles[tile] + jnp.where(lane >= shift, turned, 0.0)
        if shift + EACH > 128:
            tiles[tile + 1] = tiles[tile + 1] + jnp.where(lane < shift, turned, 0.0)
    for i in range(6):
        out[:, i * 128 : (i + 1) * 128] = tiles[i]


def scatter_steps(units, parts, held, core_in, side_in, part_in, z_in, sems, flight, finals):
    load_sem, c_send, c_recv, d_send, d_recv, s_send, s_recv, z_send, z_recv = sems
    y, x, core, t = spot()
    here, by_x, by_y = clip_of(y, x, core), clip_of(y, 1 - x, core), clip_of(1 - y, x, core)
    mate = clip_of(y, x, 1 - core)
    homes = [(1 - y, 1 - x), (y, 1 - x), (1 - y, x), (y, x)]

    def cols(u, half=None):
        k, c, width = units[u]
        if half is None:
            return pl.ds(c, width)
        return pl.ds(c + half * (width // 2), width // 2)

    def remote(src, dst, send_sem, recv_sem, to, tok=None):
        return pltpu.make_async_remote_copy(
            src_ref=src,
            dst_ref=dst,
            send_sem=send_sem,
            recv_sem=recv_sem,
            device_id=(to, t if tok is None else tok),
            device_id_type=MESH,
        )

    def load(u, g):
        k = units[u][0]
        ya, xa = homes[g]
        return pltpu.make_async_copy(
            parts[k].at[pl.ds(clip_of(ya, xa, core) * TOK, TOK), :, cols(u)],
            held[k].at[g, :, :, cols(u)],
            load_sem.at[u, g],
        )

    def to_mate(u, g):
        k = units[u][0]
        ya, xa = homes[g]
        return remote(
            parts[k].at[pl.ds(clip_of(ya, xa, 1 - core) * TOK, TOK), :, cols(u)],
            core_in[k].at[g, :, :, cols(u)],
            c_send.at[u, g],
            c_recv.at[u, g],
            mate,
        )

    def begin(u):
        for g in range(4):
            load(u, g).start()
            flight.go(to_mate(u, g))

    def ready(u, g):
        load(u, g).wait()
        to_mate(u, g).wait_recv()

    def add_into(k, g, start, width, pieces):
        def one(j, carry):
            at = slice(start, start + width)
            total = held[k][g, j, :, at].astype(jnp.float32)
            for piece in pieces:
                total = total + piece[j, :, at].astype(jnp.float32)
            held[k][g, j, :, at] = total.astype(jnp.bfloat16)
            return carry

        lax.fori_loop(0, TOK, one, 0)

    def halves(u):
        return units[u][2] % 256 == 0

    def first(u, half):
        k = units[u][0]
        at = cols(u, half) if halves(u) else cols(u)
        return remote(
            held[k].at[0, :, :, at],
            side_in[k].at[:, :, at],
            d_send.at[u, half],
            d_recv.at[u, half],
            by_y if half else by_x,
        )

    def second(u, across):
        k = units[u][0]
        return remote(
            held[k].at[1 if across == 0 else 2, :, :, cols(u)],
            part_in[k].at[across, :, :, cols(u)],
            s_send.at[u, across],
            s_recv.at[u, across],
            by_x if across == 0 else by_y,
        )

    def last(u, far):
        k = units[u][0]
        tok = (t + far) % TOK
        return remote(
            held[k].at[3, tok, :, cols(u)],
            z_in[k].at[far - 1, :, cols(u)],
            z_send.at[u, far - 1],
            z_recv.at[u, far - 1],
            here,
            tok,
        )

    def step1(u):
        k, c, width = units[u]
        ready(u, 0)
        add_into(k, 0, c, width, [core_in[k].at[0]])
        flight.go(first(u, 0))
        if halves(u):
            flight.go(first(u, 1))

    def step2(u):
        k, c, width = units[u]
        half = width // 2 if halves(u) else width
        ready(u, 2)
        first(u, 0).wait_recv()
        add_into(k, 2, c, half, [core_in[k].at[2], side_in[k]])
        if halves(u):
            add_into(k, 2, c + half, half, [core_in[k].at[2]])
        flight.go(second(u, 1))
        ready(u, 1)
        if halves(u):
            first(u, 1).wait_recv()
            add_into(k, 1, c, half, [core_in[k].at[1]])
            add_into(k, 1, c + half, half, [core_in[k].at[1], side_in[k]])
        else:
            add_into(k, 1, c, width, [core_in[k].at[1]])
        flight.go(second(u, 0))

    def step3(u):
        k, c, width = units[u]
        ready(u, 3)
        second(u, 0).wait_recv()
        second(u, 1).wait_recv()
        add_into(k, 3, c, width, [core_in[k].at[3], part_in[k].at[0], part_in[k].at[1]])
        for far in range(1, TOK):
            flight.go(last(u, far))

    def step4(u):
        k, c, width = units[u]
        at = slice(c, c + width)
        total = held[k][3, t, :, at].astype(jnp.float32)
        for far in range(1, TOK):
            last(u, far).wait_recv()
            total = total + z_in[k][far - 1, :, at].astype(jnp.float32)
        finals(u, total)

    return begin, step1, step2, step3, step4


def scatter_scratch(shapes):
    bf16 = jnp.bfloat16
    held = [pltpu.VMEM((4, TOK) + s, bf16) for s in shapes]
    side = [pltpu.VMEM((TOK,) + s, bf16) for s in shapes]
    part = [pltpu.VMEM((2, TOK) + s, bf16) for s in shapes]
    last = [pltpu.VMEM((TOK - 1,) + s, bf16) for s in shapes]
    return held + held + side + part + last


def scatter_sems(count):
    dma = pltpu.SemaphoreType.DMA
    return [
        dma((count, 4)),
        dma((count, 4)),
        dma((count, 4)),
        dma((count, 2)),
        dma((count, 2)),
        dma((count, 2)),
        dma((count, 2)),
        dma((count, TOK - 1)),
        dma((count, TOK - 1)),
    ]


STEP_FIX = 1.0 - 0.5**STEP


def adamw_rows(rate, weights, moment, square, grad, out):
    averaged = 0.5 * moment + 0.5 * grad
    squared = 0.5 * square + 0.5 * grad * grad
    out[0][...] = weights - rate * (
        averaged / STEP_FIX / (jnp.sqrt(squared / STEP_FIX) + 1e-08) + 0.1 * weights
    )
    out[1][...] = averaged
    out[2][...] = squared


RATES = (768 ** (-0.5), 384 ** (-0.5), 11 ** (-0.5), 768 ** (-0.5), 3072 ** (-0.5))


def part_affine(norms, out):
    rows = [jnp.sum(n[0:8, :], axis=0, keepdims=True) for n in norms]
    rows += [jnp.sum(n[8:16, :], axis=0, keepdims=True) for n in norms]
    table = jnp.concatenate(rows + [jnp.zeros((10, 768), jnp.float32)], axis=0)
    lane = lax.broadcasted_iota(jnp.int32, (16, 128), 1)
    for i in range(32):
        tile, shift = (i * EACH) // 128, (i * EACH) % 128
        block = table[:, tile * 128 : (tile + 1) * 128]
        block = pltpu.roll(block, (128 - shift) % 128, 1) if shift else block
        if shift + EACH > 128:
            after = pltpu.roll(table[:, (tile + 1) * 128 : (tile + 2) * 128], 128 - shift, 1)
            block = jnp.where(lane < 128 - shift, block, after)
        out[i] = jnp.where(lane < EACH, block, 0.0).astype(jnp.bfloat16)

GROUPS = 7
T_ROWS = 448
S_PAD = 208
S_ROWS = 416
CHUNK = 768
MLP_CHUNK = 512
SCALE = HEAD_DIM ** (-0.5)
BIG = -1e30
NT = (((1,), (1,)), ((), ()))
TN = (((0,), (0,)), ((), ()))


def dot(left, right, dims=(((1,), (0,)), ((), ()))):
    return lax.dot_general(left, right, dims, preferred_element_type=jnp.float32)


def low(values):
    return values.astype(jnp.bfloat16)


def up(values):
    return values.astype(jnp.float32)


def center_rows(values):
    center = values - jnp.mean(values, axis=-1, keepdims=True)
    inverse = lax.rsqrt(jnp.mean(center * center, axis=-1, keepdims=True) + 1e-06)
    return center * inverse, inverse


def back_rows(upstream, unit, inverse, gain):
    scaled = upstream * gain
    inner = (
        scaled
        - jnp.mean(scaled, axis=-1, keepdims=True)
        - unit * jnp.mean(scaled * unit, axis=-1, keepdims=True)
    )
    return inner * inverse


def fold(values):
    return jnp.sum(values.reshape(-1, 8, values.shape[-1]), axis=0)


def columns(j, width):
    return pl.ds(pl.multiple_of(j * width, 128), width)


def rows_of(i, height):
    return pl.ds(pl.multiple_of(i * height, 8), height)


def times(out, left, weight, width=CHUNK):
    def step(j, carry):
        at = columns(j, width)
        out[:, at] = dot(left[...], weight[:, at]).astype(out.dtype)
        return carry

    lax.fori_loop(0, out.shape[1] // width, step, 0)


def lane_half(shape):
    return lax.broadcasted_iota(jnp.int32, shape, 1) < HEAD_DIM


def soft(query, keys, mask):
    scores = jnp.where(mask, dot(keys, query, NT), BIG)
    expo = jnp.exp(scores - jnp.max(scores, axis=0, keepdims=True))
    return expo * (1.0 / jnp.sum(expo, axis=0, keepdims=True))


def attend(query, keys, values, mask):
    half = lane_half(query.shape)
    zero = jnp.zeros_like(query)
    query = query * jnp.bfloat16(SCALE)
    first = dot(low(soft(jnp.where(half, query, zero), keys, mask)), values, TN)
    second = dot(low(soft(jnp.where(half, zero, query), keys, mask)), values, TN)
    return low(jnp.where(half, first, second))


def attend_back(query, keys, values, upstream, mask):
    half = lane_half(query.shape)
    zero = jnp.zeros_like(query)
    query = query * jnp.bfloat16(SCALE)
    scaled = keys * jnp.bfloat16(SCALE)

    def one(pick):
        probs = soft(pick(query, zero), keys, mask)
        dprobs = dot(values, pick(upstream, zero), NT)
        dscores = low(probs * (dprobs - jnp.sum(dprobs * probs, axis=0, keepdims=True)))
        return dot(dscores, scaled, TN), dot(dscores, query), dot(low(probs), upstream)

    first = one(lambda a, b: jnp.where(half, a, b))
    second = one(lambda a, b: jnp.where(half, b, a))
    return tuple(low(jnp.where(half, a, b)) for a, b in zip(first, second))


def frame_mask(size):
    patch = lambda axis: (lambda i: (i // 64) * 8 + i % 8)(
        lax.broadcasted_iota(jnp.int32, (size, size), axis)
    )
    return patch(0) == patch(1)


def patch_mask():
    return lax.broadcasted_iota(jnp.int32, (S_PAD, S_PAD), 0) < PATCHES


T_BLOCKS = ((0, 192), (192, 256))


def mlp_kernel(lowered, after_s, cotangent, widen, narrow, affine, result, d_narrow, d_widen, d_after, d_norm, cot, turned, total, back):
    j = pl.program_id(0)

    @pl.when(j == 0)
    def start():
        cot[...] = jnp.zeros_like(cot)
        for f in range(2):
            back[pl.ds(f * S_PAD, PATCHES), :] = up(cotangent[f])
            back[pl.ds(f * S_PAD + PATCHES, S_PAD - PATCHES), :] = jnp.zeros((S_PAD - PATCHES, D), jnp.float32)
        cot[...] = low(back[...])
        turned[...] = lowered[...].T
        total[...] = after_s[...]
        back[...] = jnp.zeros_like(back)

    wide = dot(lowered[...], widen[...])
    phi = 0.5 * (1.0 + lax.erf(wide * 0.7071067811865476))
    active = low(wide * phi)
    slope = phi + wide * jnp.exp(-0.5 * wide * wide) * 0.3989422804014327
    d_wide = low(dot(cot[...], narrow[...], NT) * slope)
    total[...] += dot(active, narrow[...])
    d_narrow[...] = low(dot(active, cot[...], TN))
    d_widen[...] = low(dot(turned[...], d_wide))
    back[...] += dot(d_wide, widen[...], NT)

    @pl.when(j == pl.num_programs(0) - 1)
    def finish():
        for f in range(2):
            result[f] = low(total[pl.ds(f * S_PAD, PATCHES), :])

        def norm(b, carry):
            rows = rows_of(b, 32)
            unit, inverse = center_rows(after_s[rows, :])
            upstream = back[rows, :]
            d_after[rows, :] = up(cot[rows, :]) + back_rows(upstream, unit, inverse, affine[2:3, :])
            return carry[0] + fold(upstream * unit), carry[1] + fold(upstream)

        zero = jnp.zeros((8, D), jnp.float32)
        gain, shift = lax.fori_loop(0, S_ROWS // 32, norm, (zero, zero))
        d_norm[0:8, :] = gain
        d_norm[8:16, :] = shift


def mlp(lowered, after_s, cotangent, widen, narrow, affine):
    whole = lambda shape: pl.BlockSpec(shape, lambda j: (0,) * len(shape))
    steps = HID // MLP_CHUNK
    return pl.pallas_call(
        mlp_kernel,
        grid=(steps,),
        in_specs=[
            whole((S_ROWS, D)),
            whole((S_ROWS, D)),
            whole((2, PATCHES, D)),
            pl.BlockSpec((D, MLP_CHUNK), lambda j: (0, j)),
            pl.BlockSpec((MLP_CHUNK, D), lambda j: (j, 0)),
            whole((16, D)),
        ],
        out_specs=[
            whole((2, PATCHES, D)),
            pl.BlockSpec((MLP_CHUNK, D), lambda j: (j, 0)),
            pl.BlockSpec((D, MLP_CHUNK), lambda j: (0, j)),
            whole((S_ROWS, D)),
            whole((16, D)),
        ],
        out_shape=[
            jax.ShapeDtypeStruct((2, PATCHES, D), jnp.bfloat16),
            jax.ShapeDtypeStruct((HID, D), jnp.bfloat16),
            jax.ShapeDtypeStruct((D, HID), jnp.bfloat16),
            jax.ShapeDtypeStruct((S_ROWS, D), jnp.float32),
            jax.ShapeDtypeStruct((16, D), jnp.float32),
        ],
        scratch_shapes=[
            pltpu.VMEM((S_ROWS, D), jnp.bfloat16),
            pltpu.VMEM((D, S_ROWS), jnp.bfloat16),
            pltpu.VMEM((S_ROWS, D), jnp.float32),
            pltpu.VMEM((S_ROWS, D), jnp.float32),
        ],
        compiler_params=pltpu.CompilerParams(vmem_limit_bytes=56 * 1024 * 1024),
        cost_estimate=pl.CostEstimate(flops=12000000000, bytes_accessed=30000000, transcendentals=0),
    )(lowered, after_s, cotangent, widen, narrow, affine)

def pack(box, rows):
    extra = [rows(f, 192, 4) for f in range(2)]
    line = lax.broadcasted_iota(jnp.int32, (16, D), 0)
    for s in range(TOK):
        wide = [rows(f, 48 * s, 48) for f in range(2)]
        for b in range(6):
            pair = [w[8 * b : 8 * b + 8, :] for w in wide]
            box[s, b] = low(jnp.concatenate(pair, axis=0))
        one = [jnp.broadcast_to(e[s : s + 1, :], (16, D)) for e in extra]
        box[s, 6] = low(jnp.where(line == 0, one[0], jnp.where(line == 8, one[1], 0.0)))


def unpack(box, f, put):
    for s in range(TOK):
        for b in range(6):
            slab = up(box[s, b])
            put(48 * s + 8 * b, 8, slab[8 * f : 8 * f + 8, :])
    last = [up(box[s, 6])[8 * f : 8 * f + 1, :] for s in range(TOK)]
    put(192, TOK, jnp.concatenate(last, axis=0))


class Exchange:
    def __init__(self, source, target, sems, flight):
        self.source, self.target, self.flight = source, target, flight
        self.local, self.sent, self.got = sems
        self.clip, self.t = lax.axis_index("clip"), lax.axis_index("tok")

    def copy(self, far):
        return pltpu.make_async_remote_copy(
            src_ref=self.source((self.t + far) % TOK),
            dst_ref=self.target(self.t),
            send_sem=self.sent.at[far - 1],
            recv_sem=self.got.at[far - 1],
            device_id=(self.clip, (self.t + far) % TOK),
            device_id_type=MESH,
        )

    def own(self):
        return pltpu.make_async_copy(self.source(self.t), self.target(self.t), self.local.at[0])

    def start(self):
        for far in range(1, TOK):
            self.flight.go(self.copy(far))
        self.own().start()

    def wait(self):
        for far in range(1, TOK):
            there = self.target((self.t - far + TOK) % TOK)
            pltpu.make_async_copy(there, there, self.got.at[far - 1]).wait()
        self.own().wait()


def exchange_sems():
    dma = pltpu.SemaphoreType.DMA
    return [dma((1,)), dma((TOK - 1,)), dma((TOK - 1,))]


def pieces(count, step, size):
    def run(lo, hi):
        def one(j, carry):
            step(j)
            return carry

        lax.fori_loop(lo, hi, one, 0)

    return [functools.partial(run, lo, min(lo + size, count)) for lo in range(0, count, size)]


def product(out, left, weight, width=CHUNK):
    def step(j):
        at = columns(j, width)
        out[:, at] = dot(left(), weight[:, at]).astype(out.dtype)

    return step


def product_back(out, left, weight, width=CHUNK):
    def step(j):
        at = columns(j, width)
        out[:, at] = dot(left(), weight[at, :], NT).astype(out.dtype)

    return step


def gradient(out, turned, upstream, width=CHUNK):
    def step(j):
        at = columns(j, width)
        out[:, at] = low(dot(turned[...], upstream(at)))

    return step


def in_turn(first, second):
    for i in range(max(len(first), len(second))):
        if i < len(first):
            first[i]()
        if i < len(second):
            second[i]()


def full_kernel_steps(units, steps, shifts, lo, hi):
    calls = []
    for n in range(lo, hi):
        for shift, step in zip(shifts, steps):
            if 0 <= n - shift < len(units):
                calls.append(functools.partial(step, n - shift))
    return calls


A2A_AT = 10
A2A_REST = 8


def gather_order(units):
    count = len(units)
    split = [n for n in range(count) if units[n][0] == 1][-1] + 4
    names = ("begin", "along", "crossing", "corner")
    both = []
    for lo, hi in ((0, split), (split, count + 3)):
        calls = []
        for n in range(lo, hi):
            calls += [(name, n - shift) for shift, name in enumerate(names) if 0 <= n - shift < count]
        both.append(calls)
    return both


def forward_kernel(units, *refs):
    masters, block, frames = refs[:5], refs[5], refs[6]
    full = list(refs[7:12])
    affine, patch, normed_t, merged_t, mixed_t, first_t = refs[12:18]
    after_t, normed_s, merged_s, mixed_s, after_s, lowered = refs[18:24]
    owned, gathered = list(refs[24:29]), refs[29]
    entry_w, temporal_w, spatial_w, outbox, sent, inbox, load_sem = refs[30:37]
    there_sems, back_sems = refs[37:40], refs[40:43]
    sems = refs[43:]
    greet()
    full.append(gathered)
    owned.append(block)
    flight = Flight()
    begin, along, crossing, corner, settle, drain = gather_steps(units, owned, full, sems)
    count = len(units)
    place = {k: [n for n in range(count) if units[n][0] == k] for k in range(6)}
    there = Exchange(lambda s: outbox.at[s], lambda s: patch.at[:, s], there_sems, flight)
    back = Exchange(lambda s: sent.at[:, s], lambda s: inbox.at[s], back_sems, flight)
    def settle_all(k):
        for n in place[k]:
            settle(n)

    ready = set()
    original = begin

    def begin(n):
        k = units[n][0]
        if k not in ready and k != AFFINE:
            rows_from(masters[k], owned[k])
            ready.add(k)
        original(n)

    steps = {"begin": begin, "along": along, "crossing": crossing, "corner": corner}
    head, rest = gather_order(units)
    head = [functools.partial(steps[name], n) for name, n in head]
    rest = [functools.partial(steps[name], n) for name, n in rest]
    for call in head[:A2A_AT]:
        call()
    pack(outbox, lambda f, start, size: up(frames[f, start : start + size, :]))
    there.start()
    for call in head[A2A_AT:]:
        call()

    def load(part, source, target):
        return pltpu.make_async_copy(source, target, load_sem.at[part])

    loads = {
        "entry": load(0, full[0].at[pl.ds(0, 16)], entry_w),
        "temporal": load(1, full[1], temporal_w),
        "later": load(2, full[0].at[pl.ds(16, 16)], entry_w),
        "spatial": load(3, full[2], spatial_w),
    }
    settle_all(AFFINE)
    join_affine(gathered, affine)
    there.wait()

    def norm_t(b):
        unit, unused = center_rows(up(patch[b].reshape(64, D)))
        normed_t[rows_of(b, 64), :] = low(unit * affine[0:1, :] + affine[3:4, :])

    def heads_t(p):
        found = []
        for start, size in T_BLOCKS:
            rows = pl.ds(start, size)
            query, keys, values = (merged_t[rows, columns(p + 6 * i, 128)] for i in range(3))
            found.append(attend(query, keys, values, frame_mask(size)))
        for (start, size), value in zip(T_BLOCKS, found):
            mixed_t[pl.ds(start, size), columns(p, 128)] = value

    entry_m = lambda at: entry_w[:, :, at].reshape(D, CHUNK)

    def merge(out, left):
        def step(j):
            at = columns(j, CHUNK)
            out[:, at] = low(dot(left[...], entry_m(at)))

        return step

    def first_step(j):
        at = columns(j, CHUNK)
        first_t[:, at] = low(dot(mixed_t[...], temporal_w[0:16, :, at].reshape(D, CHUNK)))

    def branch_step(j):
        at = columns(j, CHUNK)
        value = low(dot(first_t[...], temporal_w[16:32, :, at].reshape(D, CHUNK)))
        sent[:, :, :, at] = value.reshape(GROUPS, TOK, 16, CHUNK)

    def start_temporal():
        settle_all(0)
        settle_all(1)
        loads["entry"].start()
        loads["temporal"].start()
        for call in pieces(GROUPS, norm_t, GROUPS):
            call()
        loads["entry"].wait()
        loads["temporal"].wait()

    def start_spatial():
        settle_all(2)
        loads["later"].start()
        loads["spatial"].start()
        back.wait()
        for f in range(2):

            def put(start, size, rows, f=f):
                after_t[f * S_PAD + start : f * S_PAD + start + size, :] = (
                    up(frames[f, start : start + size, :]) + rows
                )

            unpack(inbox, f, put)
            tail = f * S_PAD + PATCHES
            after_t[tail : (f + 1) * S_PAD, :] = jnp.zeros((S_PAD - PATCHES, D), jnp.float32)

    def norm_s(b):
        unit, unused = center_rows(after_t[rows_of(b, 32), :])
        normed_s[rows_of(b, 32), :] = low(unit * affine[1:2, :] + affine[4:5, :])

    def wait_spatial():
        loads["later"].wait()
        loads["spatial"].wait()

    def heads_s(p):
        found = []
        for f in range(2):
            rows = pl.ds(f * S_PAD, S_PAD)
            query, keys, values = (merged_s[rows, columns(p + 6 * i, 128)] for i in range(3))
            found.append(attend(query, keys, values, patch_mask()))
        for f in range(2):
            mixed_s[pl.ds(f * S_PAD, S_PAD), columns(p, 128)] = found[f]

    def out_s(j):
        at = columns(j, CHUNK)
        weight = low(up(spatial_w[:, :, at]).reshape(D, CHUNK))
        after_s[:, at] = after_t[:, at] + dot(mixed_s[...], weight)

    def norm_m(b):
        unit, unused = center_rows(after_s[rows_of(b, 32), :])
        lowered[rows_of(b, 32), :] = low(unit * affine[2:3, :] + affine[5:6, :])

    compute = (
        [start_temporal]
        + pieces(3, merge(merged_t, normed_t), 1)
        + pieces(6, heads_t, 1)
        + pieces(1, first_step, 1)
        + pieces(1, branch_step, 1)
        + [back.start]
        + [lambda: None] * A2A_REST
    )
    more = (
        [start_spatial]
        + pieces(13, norm_s, 13)
        + [wait_spatial]
        + pieces(3, merge(merged_s, normed_s), 1)
        + pieces(6, heads_s, 1)
        + pieces(1, out_s, 1)
        + pieces(13, norm_m, 13)
    )
    in_turn(compute + more, rest)
    for k in (3, 4):
        settle_all(k)
    drain()
    flight.drain()


def forward(masters, block, frames):
    units = units_of(ORDER_IN, HID)
    vmem = pl.BlockSpec(memory_space=pltpu.VMEM)
    anywhere = pl.BlockSpec(memory_space=pl.ANY)
    bf16, f32 = jnp.bfloat16, jnp.float32
    slab = (TOK, GROUPS, 16, D)
    group = (GROUPS, TOK, 16, D)
    saved = [
        ((16, D), f32),
        (group, bf16),
        ((T_ROWS, D), bf16),
        ((T_ROWS, 3 * D), bf16),
        ((T_ROWS, D), bf16),
        ((T_ROWS, D), bf16),
        ((S_ROWS, D), f32),
        ((S_ROWS, D), bf16),
        ((S_ROWS, 3 * D), bf16),
        ((S_ROWS, D), bf16),
        ((S_ROWS, D), f32),
        ((S_ROWS, D), bf16),
    ]
    return pl.pallas_call(
        functools.partial(forward_kernel, units),
        out_shape=[jax.ShapeDtypeStruct((32, r, w), bf16) for r, w in zip(ROWS, WIDTHS)]
        + [jax.ShapeDtypeStruct(s, t) for s, t in saved],
        in_specs=[vmem] * 7,
        out_specs=[anywhere] * 5 + [vmem] * 12,
        scratch_shapes=[pltpu.VMEM((r, w), bf16) for r, w in zip(ROWS, WIDTHS)]
        + [
            pltpu.VMEM((32, 16, 128), bf16),
            pltpu.VMEM((16, 48, 3 * D), bf16),
            pltpu.VMEM((32, 48, D), bf16),
            pltpu.VMEM((32, 24, D), bf16),
            pltpu.VMEM(slab, bf16),
            pltpu.VMEM(group, bf16),
            pltpu.VMEM(slab, bf16),
            pltpu.SemaphoreType.DMA((4,)),
        ]
        + exchange_sems()
        + exchange_sems()
        + gather_sems(len(units)),
        compiler_params=pltpu.CompilerParams(
            collective_id=0, has_side_effects=True, vmem_limit_bytes=VMEM_LIMIT
        ),
    )(*masters, block, frames)


def finals_of(states, outs, grads, affine_out=None):
    def finals(u, unit, total):
        k, c, width = unit
        if k == AFFINE:
            affine_out[...] = total
            return
        n, rows = WIDTHS[k] // 128, ROWS[k]
        for i in range(width // 128):
            grads[k][pl.ds(c // 128 + i, rows, stride=n), :] = total[:, i * 128 : (i + 1) * 128]
        if c + width == WIDTHS[k]:
            state = states[k]
            adamw_rows(RATES[k], state[0][...], state[1][...], state[2][...], grads[k][...], outs[k])

    return finals


def back_kernel(units, *refs):
    arrays = (3, 4)
    parts = dict(zip(arrays, refs[:2]))
    states = {k: refs[2 + 3 * i : 5 + 3 * i] for i, k in enumerate(arrays)}
    d_after_s, after_t, affine, spatial = refs[8:12]
    normed_s_in, merged_s_in, mixed_s_in, entry_in = refs[12:16]
    patch_in, normed_t_in, merged_t_in, mixed_t_in, first_t_in, temporal_in = refs[16:22]
    outs = {k: refs[22 + 3 * i : 25 + 3 * i] for i, k in enumerate(arrays)}
    input_gradient, d_spatial, d_entry_out, d_temporal, norm_s_out, norm_t_out = refs[28:34]
    pos = 34
    pools = []
    for i in range(5):
        pools.append(dict(zip(arrays, refs[pos : pos + 2])))
        pos += 2
    grads = dict(zip(arrays, refs[pos : pos + 2]))
    pos += 2
    normed_s, merged_s, mixed_s, entry_w = refs[pos : pos + 4]
    patch, normed_t, merged_t, mixed_t, first_t, temporal_w = refs[pos + 4 : pos + 10]
    d_after_t, d_entry, lowered, d_mixed, d_first, d_merged, turned_s, turned_t, back, outbox, grouped, sent, inbox, load_sem = refs[
        pos + 10 : pos + 24
    ]
    pos += 24
    there_sems, back_sems = refs[pos : pos + 3], refs[pos + 3 : pos + 6]
    sems = refs[pos + 6 :]
    sources = (normed_s_in, merged_s_in, mixed_s_in, entry_in.at[1])
    targets = (normed_s, merged_s, mixed_s, entry_w)
    sources += (patch_in, normed_t_in, merged_t_in, mixed_t_in, first_t_in, temporal_in)
    targets += (patch, normed_t, merged_t, mixed_t, first_t, temporal_w)
    loads = [pltpu.make_async_copy(a, b, load_sem.at[i]) for i, (a, b) in enumerate(zip(sources, targets))]
    for copy in loads:
        copy.start()
    entry_load = pltpu.make_async_copy(entry_in.at[0], entry_w, load_sem.at[10])
    entry_stores = [pltpu.make_async_copy(d_entry, d_entry_out.at[i], load_sem.at[12 - i]) for i in range(2)]
    greet()
    flight = Flight()
    finals = finals_of(states, outs, grads)
    steps = scatter_steps(
        units, parts, *pools, sems, flight, lambda u, total: finals(u, units[u], total)
    )
    there = Exchange(lambda s: outbox.at[s], lambda s: grouped.at[:, s], there_sems, flight)
    home = Exchange(lambda s: sent.at[:, s], lambda s: inbox.at[s], back_sems, flight)
    zero = jnp.zeros((8, D), jnp.float32)

    def begin_s():
        lowered[...] = low(d_after_s[...])
        for copy in loads[:3]:
            copy.wait()
        turned_s[...] = mixed_s[...].T

    def turn_s():
        turned_s[...] = normed_s[...].T

    def heads_s(p):
        found = []
        for f in range(2):
            rows = pl.ds(f * S_PAD, S_PAD)
            query, keys, values = (merged_s[rows, columns(p + 6 * i, 128)] for i in range(3))
            found.append(
                attend_back(query, keys, values, d_mixed[rows, columns(p, 128)], patch_mask())
            )
        for f in range(2):
            for i in range(3):
                d_merged[pl.ds(f * S_PAD, S_PAD), columns(p + 6 * i, 128)] = found[f][i]

    def s_back(j):
        at = columns(j, CHUNK)
        back[0:S_ROWS, at] = dot(d_merged[0:S_ROWS, :], entry_w[at, :], NT)

    def end_s():
        entry_load.start()

        def norm(b, carry):
            rows = rows_of(b, 32)
            unit, inverse = center_rows(after_t[rows, :])
            upstream = back[rows, :]
            d_after_t[rows, :] = d_after_s[rows, :] + back_rows(upstream, unit, inverse, affine[1:2, :])
            return carry[0] + fold(upstream * unit), carry[1] + fold(upstream)

        gain, shift = lax.fori_loop(0, S_ROWS // 32, norm, (zero, zero))
        norm_s_out[0:8, :] = gain
        norm_s_out[8:16, :] = shift
        pack(outbox, lambda f, start, size: d_after_t[f * S_PAD + start : f * S_PAD + start + size, :])
        there.start()

    def wait_entry():
        loads[3].wait()

    d_mixed_s = d_mixed.at[0:S_ROWS]
    compute = (
        [begin_s]
        + pieces(1, gradient(d_spatial, turned_s, lambda at: lowered[:, at]), 1)
        + pieces(1, product_back(d_mixed_s, lambda: lowered[...], spatial), 1)
        + [turn_s]
        + pieces(6, heads_s, 1)
        + [wait_entry]
        + pieces(1, s_back, 1)
        + [end_s]
        + pieces(3, gradient(d_entry, turned_s, lambda at: d_merged[0:S_ROWS, at]), 1)
        + [entry_stores[1].start]
    )

    def begin_t():
        for copy in loads[4:]:
            copy.wait()
        turned_t[...] = first_t[...].T
        there.wait()

    group_cols = lambda at: grouped[:, :, :, at].reshape(T_ROWS, CHUNK)

    def turn_mixed():
        turned_t[...] = mixed_t[...].T

    def turn_normed():
        turned_t[...] = normed_t[...].T

    def heads_t(p):
        found = []
        for start, size in T_BLOCKS:
            rows = pl.ds(start, size)
            query, keys, values = (merged_t[rows, columns(p + 6 * i, 128)] for i in range(3))
            found.append(
                attend_back(query, keys, values, d_mixed[rows, columns(p, 128)], frame_mask(size))
            )
        for (start, size), values in zip(T_BLOCKS, found):
            for i in range(3):
                d_merged[pl.ds(start, size), columns(p + 6 * i, 128)] = values[i]

    def t_back(j):
        at = columns(j, CHUNK)
        back[:, at] = dot(d_merged[...], entry_w[at, :], NT)

    def end_t():
        def norm(b, carry):
            rows = rows_of(b, 64)
            unit, inverse = center_rows(up(patch[b].reshape(64, D)))
            upstream = back[rows, :]
            value = back_rows(upstream, unit, inverse, affine[0:1, :])
            sent[b] = low(value).reshape(TOK, 16, D)
            return carry[0] + fold(upstream * unit), carry[1] + fold(upstream)

        gain, shift = lax.fori_loop(0, GROUPS, norm, (zero, zero))
        norm_t_out[0:8, :] = gain
        norm_t_out[8:16, :] = shift
        home.start()

    def free_entry():
        entry_stores[1].wait()
        entry_load.wait()

    compute += (
        [begin_t]
        + pieces(1, gradient(d_temporal.at[1], turned_t, group_cols), 1)
        + pieces(1, product_back(d_first, lambda: grouped[...].reshape(T_ROWS, D), temporal_w.at[1]), 1)
        + [turn_mixed]
        + pieces(1, gradient(d_temporal.at[0], turned_t, lambda at: d_first[:, at]), 1)
        + pieces(1, product_back(d_mixed, lambda: d_first[...], temporal_w.at[0]), 1)
        + [turn_normed]
        + pieces(6, heads_t, 1)
        + [free_entry]
        + pieces(1, t_back, 1)
        + [end_t]
        + pieces(3, gradient(d_entry, turned_t, lambda at: d_merged[:, at]), 1)
        + [entry_stores[0].start]
    )
    rest = full_kernel_steps(units, steps, (0, 1, 2, 3, 4), 0, len(units) + 4)
    in_turn(rest, compute)
    home.wait()
    for f in range(2):

        def put(start, size, rows, f=f):
            at = f * S_PAD + start
            input_gradient[f, start : start + size, :] = d_after_t[at : at + size, :] + rows

        unpack(inbox, f, put)
    entry_stores[0].wait()
    flight.drain()


def backward(parts, states, d_after_s, after_t, affine, spatial, entry, temporal, saved_s, saved_t):
    units = units_of(ORDER_MLP)
    vmem = pl.BlockSpec(memory_space=pltpu.VMEM)
    anywhere = pl.BlockSpec(memory_space=pl.ANY)
    bf16, f32 = jnp.bfloat16, jnp.float32
    shapes = [(ROWS[k], WIDTHS[k]) for k in (3, 4)]
    flat = [(r * w // 128, 128) for r, w in shapes]
    slab = (TOK, GROUPS, 16, D)
    group = (GROUPS, TOK, 16, D)
    outs = [(s, f32) for s in flat for _ in range(3)] + [
        ((2, PATCHES, D), f32),
        ((D, D), bf16),
        ((2, D, 3 * D), bf16),
        ((2, D, D), bf16),
        ((16, D), f32),
        ((16, D), f32),
    ]
    return pl.pallas_call(
        functools.partial(back_kernel, units),
        out_shape=[jax.ShapeDtypeStruct(s, t) for s, t in outs],
        in_specs=[anywhere] * 2 + [vmem] * 10 + [anywhere] * 10,
        out_specs=[vmem] * 8 + [anywhere] + [vmem] * 3,
        scratch_shapes=scatter_scratch(shapes)
        + [pltpu.VMEM(s, f32) for s in flat]
        + [
            pltpu.VMEM((S_ROWS, D), bf16),
            pltpu.VMEM((S_ROWS, 3 * D), bf16),
            pltpu.VMEM((S_ROWS, D), bf16),
            pltpu.VMEM((D, 3 * D), bf16),
            pltpu.VMEM(group, bf16),
            pltpu.VMEM((T_ROWS, D), bf16),
            pltpu.VMEM((T_ROWS, 3 * D), bf16),
            pltpu.VMEM((T_ROWS, D), bf16),
            pltpu.VMEM((T_ROWS, D), bf16),
            pltpu.VMEM((2, D, D), bf16),
            pltpu.VMEM((S_ROWS, D), f32),
            pltpu.VMEM((D, 3 * D), bf16),
            pltpu.VMEM((S_ROWS, D), bf16),
            pltpu.VMEM((T_ROWS, D), bf16),
            pltpu.VMEM((T_ROWS, D), bf16),
            pltpu.VMEM((T_ROWS, 3 * D), bf16),
            pltpu.VMEM((D, S_ROWS), bf16),
            pltpu.VMEM((D, T_ROWS), bf16),
            pltpu.VMEM((T_ROWS, D), f32),
            pltpu.VMEM(slab, bf16),
            pltpu.VMEM(group, bf16),
            pltpu.VMEM(group, bf16),
            pltpu.VMEM(slab, bf16),
            pltpu.SemaphoreType.DMA((13,)),
        ]
        + exchange_sems()
        + exchange_sems()
        + scatter_sems(len(units)),
        compiler_params=pltpu.CompilerParams(
            collective_id=1, has_side_effects=True, vmem_limit_bytes=VMEM_LIMIT
        ),
    )(*parts, *states, d_after_s, after_t, affine, spatial, *saved_s, entry, *saved_t, temporal)


def rest_kernel(units, *refs):
    arrays = (0, 1, 2)
    parts = dict(zip(arrays, refs[:3]))
    norms = refs[3:6]
    states = {k: refs[6 + 3 * k : 9 + 3 * k] for k in arrays}
    outs = {k: refs[15 + 3 * k : 18 + 3 * k] for k in arrays}
    affine_out = refs[24]
    pos = 25
    pools = []
    for i in range(5):
        pools.append(dict(zip(arrays + (AFFINE,), refs[pos : pos + 4])))
        pos += 4
    parts[AFFINE] = refs[pos]
    grads = dict(zip(arrays, refs[pos + 1 : pos + 4]))
    sems = refs[pos + 4 :]
    greet()
    flight = Flight()
    finals = finals_of(states, outs, grads, affine_out)
    steps = scatter_steps(
        units, parts, *pools, sems, flight, lambda u, total: finals(u, units[u], total)
    )
    begin = steps[0]

    def begin_after(u):
        if units[u][0] == AFFINE:
            part_affine(norms, parts[AFFINE])
        begin(u)

    for call in full_kernel_steps(units, (begin_after,) + steps[1:], (0, 2, 3, 4, 5), 0, len(units) + 5):
        call()
    flight.drain()


def scatter_rest(parts, norms, states):
    units = units_of(ORDER_REST)
    vmem = pl.BlockSpec(memory_space=pltpu.VMEM)
    shapes = [(ROWS[k], WIDTHS[k]) for k in (0, 1, 2)]
    flat = [(r * w // 128, 128) for r, w in shapes]
    return pl.pallas_call(
        functools.partial(rest_kernel, units),
        out_shape=[jax.ShapeDtypeStruct(s, jnp.float32) for s in flat for _ in range(3)]
        + [jax.ShapeDtypeStruct((16, 128), jnp.float32)],
        in_specs=[pl.BlockSpec(memory_space=pl.ANY)] * 3 + [vmem] * 12,
        out_specs=[vmem] * 10,
        scratch_shapes=scatter_scratch(shapes + [(16, 128)])
        + [pltpu.VMEM((32, 16, 128), jnp.bfloat16)]
        + [pltpu.VMEM(s, jnp.float32) for s in flat]
        + scatter_sems(len(units)),
        compiler_params=pltpu.CompilerParams(
            collective_id=2, has_side_effects=True, vmem_limit_bytes=VMEM_LIMIT
        ),
    )(*parts, *norms, *states)


def on_device(
    frames,
    cotangent,
    entry_weights,
    entry_momentum,
    entry_variance,
    temporal_weights,
    temporal_momentum,
    temporal_variance,
    spatial_weights,
    spatial_momentum,
    spatial_variance,
    widen_weights,
    widen_momentum,
    widen_variance,
    narrow_weights,
    narrow_momentum,
    narrow_variance,
    norm_affine,
    affine_momentum,
    affine_variance,
):
    masters = (entry_weights, temporal_weights, spatial_weights, widen_weights, narrow_weights)
    block = jnp.pad(low(norm_affine).reshape(6, EACH), ((0, 10), (0, 128 - EACH)))
    found = forward(masters, block, frames[0])
    entry, temporal, spatial, widen, narrow = found[:5]
    entry = entry.reshape(2, D, 3 * D)
    temporal = temporal.reshape(2, D, D)
    spatial = spatial.reshape(D, D)
    widen = widen.reshape(D, HID)
    narrow = narrow.reshape(HID, D)
    affine, patch, normed_t, merged_t, mixed_t, first_t = found[5:11]
    after_t, normed_s, merged_s, mixed_s, after_s, lowered = found[11:17]
    result, narrow_grad, widen_grad, d_after_s, norm_m = mlp(
        lowered, after_s, cotangent[0], widen, narrow, affine
    )
    found = backward(
        (widen_grad.reshape(32, -1, HID), narrow_grad.reshape(32, -1, D)),
        (
            widen_weights,
            widen_momentum,
            widen_variance,
            narrow_weights,
            narrow_momentum,
            narrow_variance,
        ),
        d_after_s,
        after_t,
        affine,
        spatial,
        entry,
        temporal,
        (normed_s, merged_s, mixed_s),
        (patch, normed_t, merged_t, mixed_t, first_t),
    )
    widen_new, narrow_new = found[0:3], found[3:6]
    input_gradient, d_spatial, d_entry, d_temporal, norm_s, norm_t = found[6:12]
    found = scatter_rest(
        (d_entry.reshape(32, -1, 3 * D), d_temporal.reshape(32, -1, D), d_spatial.reshape(32, -1, D)),
        (norm_t, norm_s, norm_m),
        (
            entry_weights,
            entry_momentum,
            entry_variance,
            temporal_weights,
            temporal_momentum,
            temporal_variance,
            spatial_weights,
            spatial_momentum,
            spatial_variance,
        ),
    )
    affine_sum = found[9][:6, :EACH].reshape(2, 3, EACH)
    affine_new = adamw(norm_affine, affine_momentum, affine_variance, affine_sum, 0.5)
    return (
        result[None],
        input_gradient[None],
        *found[0:9],
        *widen_new,
        *narrow_new,
        affine_new[0],
        affine_new[1],
        affine_new[2][:, 0:2],
        affine_new[2][:, 2],
    )

def solution(mesh):
    return jax.shard_map(
        on_device if mesh.shape["clip"] == 8 and mesh.shape["tok"] == TOK else on_any,
        mesh=mesh,
        in_specs=(
            P("clip", "tok", None, None),
            P("clip", "tok", None, None),
            P(("clip", "tok"), None),
            P(("clip", "tok"), None),
            P(("clip", "tok"), None),
            P(("clip", "tok"), None),
            P(("clip", "tok"), None),
            P(("clip", "tok"), None),
            P(("clip", "tok"), None),
            P(("clip", "tok"), None),
            P(("clip", "tok"), None),
            P(("clip", "tok"), None),
            P(("clip", "tok"), None),
            P(("clip", "tok"), None),
            P(("clip", "tok"), None),
            P(("clip", "tok"), None),
            P(("clip", "tok"), None),
            P(None, None, ("clip", "tok")),
            P(None, None, ("clip", "tok")),
            P(None, None, ("clip", "tok")),
        ),
        out_specs=(
            P("clip", "tok", None, None),
            P("clip", "tok", None, None),
            P(("clip", "tok"), None),
            P(("clip", "tok"), None),
            P(("clip", "tok"), None),
            P(("clip", "tok"), None),
            P(("clip", "tok"), None),
            P(("clip", "tok"), None),
            P(("clip", "tok"), None),
            P(("clip", "tok"), None),
            P(("clip", "tok"), None),
            P(("clip", "tok"), None),
            P(("clip", "tok"), None),
            P(("clip", "tok"), None),
            P(("clip", "tok"), None),
            P(("clip", "tok"), None),
            P(("clip", "tok"), None),
            P(None, None, ("clip", "tok")),
            P(None, None, ("clip", "tok")),
            P(None, None, ("clip", "tok")),
            P(None, ("clip", "tok")),
        ),
        check_vma=False,
    )
```

```python
import functools

import jax
import jax.numpy as jnp
from jax import lax
from jax.experimental import pallas as pl
from jax.experimental.pallas import tpu as pltpu
from jax.sharding import PartitionSpec as P

D = 768
HEADS = 12
HEAD_DIM = 64
HID = 3072
PATCHES = 196
STEP = 5

time_scores = "cfphe,cgphe->cphfg"
time_mixed = "cphfg,cgphe->cfphe"
time_flip = "cphfg,cfphe->cgphe"
space_scores = "cfphe,cfqhe->cfhpq"
space_mixed = "cfhpq,cfqhe->cfphe"
space_flip = "cfhpq,cfphe->cfqhe"


def project(inputs, weight):
    return jnp.einsum("cfpa,ab->cfpb", inputs, weight, preferred_element_type=jnp.float32)


def project_back(upstream, weight):
    return jnp.einsum("cfpb,ab->cfpa", upstream, weight, preferred_element_type=jnp.float32)


def weight_sum(inputs, upstream):
    return jnp.einsum("cfpa,cfpb->ab", inputs, upstream, preferred_element_type=jnp.float32)


def layer_norm(values, gain, shift):
    center = values - jnp.mean(values, axis=-1, keepdims=True)
    inverse = lax.rsqrt(jnp.mean(center * center, axis=-1, keepdims=True) + 1e-06)
    unit = center * inverse
    return (unit * gain + shift, unit, inverse)


def norm_back(upstream, unit, inverse, gain):
    scaled = upstream * gain
    inner = (
        scaled
        - jnp.mean(scaled, axis=-1, keepdims=True)
        - unit * jnp.mean(scaled * unit, axis=-1, keepdims=True)
    )
    return (
        inner * inverse,
        jnp.sum(upstream * unit, axis=(0, 1, 2)),
        jnp.sum(upstream, axis=(0, 1, 2)),
    )


def split_heads(merged):
    lowered = merged.astype(jnp.bfloat16)
    parts = lowered.reshape(lowered.shape[:-1] + (3, HEADS, HEAD_DIM))
    return (parts[..., 0, :, :], parts[..., 1, :, :], parts[..., 2, :, :])


def attend_forward(heads, score_form, mixed_form):
    query, keys, values = heads
    scores = jnp.einsum(score_form, query, keys, preferred_element_type=jnp.float32) * HEAD_DIM ** (
        -0.5
    )
    top = jnp.max(scores, axis=-1, keepdims=True)
    expo = jnp.exp(scores - top)
    total = jnp.sum(expo, axis=-1, keepdims=True)
    probs = (expo / total).astype(jnp.bfloat16)
    mixed = jnp.einsum(mixed_form, probs, values, preferred_element_type=jnp.float32)
    joined = mixed.reshape(mixed.shape[:-2] + (HEADS * HEAD_DIM,)).astype(jnp.bfloat16)
    return (joined, top + jnp.log(total))


def attend_backward(heads, logsum, upstream_joined, score_form, mixed_form, flip_form):
    query, keys, values = heads
    upstream = upstream_joined.reshape(upstream_joined.shape[:-1] + (HEADS, HEAD_DIM))
    scale = HEAD_DIM ** (-0.5)
    scores = jnp.einsum(score_form, query, keys, preferred_element_type=jnp.float32) * scale
    probs = jnp.exp(scores - logsum)
    dprobs = jnp.einsum(score_form, upstream, values, preferred_element_type=jnp.float32)
    dscores = (probs * (dprobs - jnp.sum(dprobs * probs, axis=-1, keepdims=True))).astype(
        jnp.bfloat16
    )
    dquery = jnp.einsum(mixed_form, dscores, keys, preferred_element_type=jnp.float32) * scale
    dkeys = jnp.einsum(flip_form, dscores, query, preferred_element_type=jnp.float32) * scale
    dvalues = jnp.einsum(
        flip_form, probs.astype(jnp.bfloat16), upstream, preferred_element_type=jnp.float32
    )
    stacked = jnp.stack([dquery, dkeys, dvalues], axis=-3)
    return stacked.reshape(stacked.shape[:-3] + (3 * HEADS * HEAD_DIM,)).astype(jnp.bfloat16)


def collect(masters):
    gathered = (
        lax.all_gather(masters[0].astype(jnp.bfloat16), ("clip", "tok"), axis=0, tiled=True),
        lax.all_gather(masters[1].astype(jnp.bfloat16), ("clip", "tok"), axis=0, tiled=True),
        lax.all_gather(masters[2].astype(jnp.bfloat16), ("clip", "tok"), axis=0, tiled=True),
        lax.all_gather(masters[3].astype(jnp.bfloat16), ("clip", "tok"), axis=0, tiled=True),
        lax.all_gather(masters[4].astype(jnp.bfloat16), ("clip", "tok"), axis=0, tiled=True),
        lax.all_gather(masters[5].astype(jnp.bfloat16), ("clip", "tok"), axis=2, tiled=True),
    )
    return (
        gathered[0].reshape(2, D, 3 * D),
        gathered[1].reshape(2, D, D),
        gathered[2].reshape(D, D),
        gathered[3].reshape(D, HID),
        gathered[4].reshape(HID, D),
        gathered[5],
    )


def plain_forward(frames, masters):
    weights = collect(masters)
    entry, temporal, spatial, widen, narrow, affine = weights
    gains = affine.astype(jnp.float32)
    patchwise = lax.all_to_all(frames, "tok", split_axis=2, concat_axis=1, tiled=True)
    normed_t, unit_t, inverse_t = layer_norm(
        patchwise.astype(jnp.float32), gains[0, 0], gains[1, 0]
    )
    lowered_t = normed_t.astype(jnp.bfloat16)
    heads_t = split_heads(project(lowered_t, entry[0]))
    mixed_t, lse_t = attend_forward(heads_t, time_scores, time_mixed)
    first_t = project(mixed_t, temporal[0]).astype(jnp.bfloat16)
    branch = project(first_t, temporal[1]).astype(jnp.bfloat16)
    returned = lax.all_to_all(branch, "tok", split_axis=1, concat_axis=2, tiled=True)
    after_t = frames.astype(jnp.float32) + returned.astype(jnp.float32)
    normed_s, unit_s, inverse_s = layer_norm(after_t, gains[0, 1], gains[1, 1])
    lowered_s = normed_s.astype(jnp.bfloat16)
    heads_s = split_heads(project(lowered_s, entry[1]))
    mixed_s, lse_s = attend_forward(heads_s, space_scores, space_mixed)
    after_s = after_t + project(mixed_s, spatial)
    normed_m, unit_m, inverse_m = layer_norm(after_s, gains[0, 2], gains[1, 2])
    lowered_m = normed_m.astype(jnp.bfloat16)
    widened = project(lowered_m, widen)
    activated = jax.nn.gelu(widened, approximate=False).astype(jnp.bfloat16)
    result = (after_s + project(activated, narrow)).astype(jnp.bfloat16)
    saved = {
        "weights": weights,
        "unit_t": unit_t,
        "inverse_t": inverse_t,
        "lowered_t": lowered_t,
        "heads_t": heads_t,
        "lse_t": lse_t,
        "mixed_t": mixed_t,
        "first_t": first_t,
        "unit_s": unit_s,
        "inverse_s": inverse_s,
        "lowered_s": lowered_s,
        "heads_s": heads_s,
        "lse_s": lse_s,
        "mixed_s": mixed_s,
        "unit_m": unit_m,
        "inverse_m": inverse_m,
        "lowered_m": lowered_m,
        "widened": widened,
        "activated": activated,
    }
    return (result, saved)


def adamw(master, moment, square, grad, rate):
    fix = 1.0 - 0.5**STEP
    averaged = 0.5 * moment + 0.5 * grad
    squared = 0.5 * square + 0.5 * grad * grad
    updated = master - rate * (averaged / fix / (jnp.sqrt(squared / fix) + 1e-08) + 0.1 * master)
    return (updated, averaged, squared)

def on_any(
    frames,
    cotangent,
    entry_weights,
    entry_momentum,
    entry_variance,
    temporal_weights,
    temporal_momentum,
    temporal_variance,
    spatial_weights,
    spatial_momentum,
    spatial_variance,
    widen_weights,
    widen_momentum,
    widen_variance,
    narrow_weights,
    narrow_momentum,
    narrow_variance,
    norm_affine,
    affine_momentum,
    affine_variance,
):
    masters = (
        entry_weights,
        temporal_weights,
        spatial_weights,
        widen_weights,
        narrow_weights,
        norm_affine,
    )
    result, saved = plain_forward(frames, masters)
    entry, temporal, spatial, widen, narrow, affine = saved["weights"]
    gains = affine.astype(jnp.float32)
    narrow_grad = weight_sum(saved["activated"], cotangent)
    widened = saved["widened"]
    slope = (
        0.5 * (1.0 + lax.erf(widened * 0.7071067811865476))
        + widened * jnp.exp(-0.5 * widened * widened) * 0.3989422804014327
    )
    dwidened = (project_back(cotangent, narrow) * slope).astype(jnp.bfloat16)
    widen_grad = weight_sum(saved["lowered_m"], dwidened)
    dpart_m, gain_m, shift_m = norm_back(
        project_back(dwidened, widen), saved["unit_m"], saved["inverse_m"], gains[0, 2]
    )
    dafter_s = cotangent.astype(jnp.float32) + dpart_m
    dspatial = dafter_s.astype(jnp.bfloat16)
    spatial_grad = weight_sum(saved["mixed_s"], dspatial)
    dmixed_s = project_back(dspatial, spatial).astype(jnp.bfloat16)
    dfused_s = attend_backward(
        saved["heads_s"], saved["lse_s"], dmixed_s, space_scores, space_mixed, space_flip
    )
    entry_grad_s = weight_sum(saved["lowered_s"], dfused_s)
    dpart_s, gain_s, shift_s = norm_back(
        project_back(dfused_s, entry[1]), saved["unit_s"], saved["inverse_s"], gains[0, 1]
    )
    dafter_t = dafter_s + dpart_s
    dbranch = lax.all_to_all(
        dafter_t.astype(jnp.bfloat16), "tok", split_axis=2, concat_axis=1, tiled=True
    )
    temporal_grad_b = weight_sum(saved["first_t"], dbranch)
    dfirst = project_back(dbranch, temporal[1]).astype(jnp.bfloat16)
    temporal_grad_a = weight_sum(saved["mixed_t"], dfirst)
    dmixed_t = project_back(dfirst, temporal[0]).astype(jnp.bfloat16)
    dfused_t = attend_backward(
        saved["heads_t"], saved["lse_t"], dmixed_t, time_scores, time_mixed, time_flip
    )
    entry_grad_t = weight_sum(saved["lowered_t"], dfused_t)
    dsent, gain_t, shift_t = norm_back(
        project_back(dfused_t, entry[0]), saved["unit_t"], saved["inverse_t"], gains[0, 0]
    )
    dreturned = lax.all_to_all(
        dsent.astype(jnp.bfloat16), "tok", split_axis=1, concat_axis=2, tiled=True
    )
    input_gradient = dafter_t + dreturned.astype(jnp.float32)
    members = (
        jnp.stack([entry_grad_t, entry_grad_s]).reshape(-1, 128),
        jnp.stack([temporal_grad_a, temporal_grad_b]).reshape(-1, 128),
        spatial_grad.reshape(-1, 128),
        widen_grad.reshape(-1, 128),
        narrow_grad.reshape(-1, 128),
        jnp.stack([jnp.stack([gain_t, gain_s, gain_m]), jnp.stack([shift_t, shift_s, shift_m])]),
    )
    totals = (
        lax.psum_scatter(members[0], ("clip", "tok"), scatter_dimension=0, tiled=True),
        lax.psum_scatter(members[1], ("clip", "tok"), scatter_dimension=0, tiled=True),
        lax.psum_scatter(members[2], ("clip", "tok"), scatter_dimension=0, tiled=True),
        lax.psum_scatter(members[3], ("clip", "tok"), scatter_dimension=0, tiled=True),
        lax.psum_scatter(members[4], ("clip", "tok"), scatter_dimension=0, tiled=True),
        lax.psum_scatter(members[5], ("clip", "tok"), scatter_dimension=2, tiled=True),
    )
    entry_sum, temporal_sum, spatial_sum, widen_sum, narrow_sum, affine_sum = totals
    entry_new = adamw(entry_weights, entry_momentum, entry_variance, entry_sum, D ** (-0.5))
    temporal_new = adamw(
        temporal_weights, temporal_momentum, temporal_variance, temporal_sum, (D // 2) ** (-0.5)
    )
    spatial_new = adamw(
        spatial_weights,
        spatial_momentum,
        spatial_variance,
        spatial_sum,
        (3 * D // PATCHES) ** (-0.5),
    )
    widen_new = adamw(widen_weights, widen_momentum, widen_variance, widen_sum, D ** (-0.5))
    narrow_new = adamw(narrow_weights, narrow_momentum, narrow_variance, narrow_sum, HID ** (-0.5))
    affine_new = adamw(norm_affine, affine_momentum, affine_variance, affine_sum, 0.5)
    return (
        result,
        input_gradient,
        entry_new[0],
        entry_new[1],
        entry_new[2],
        temporal_new[0],
        temporal_new[1],
        temporal_new[2],
        spatial_new[0],
        spatial_new[1],
        spatial_new[2],
        widen_new[0],
        widen_new[1],
        widen_new[2],
        narrow_new[0],
        narrow_new[1],
        narrow_new[2],
        affine_new[0],
        affine_new[1],
        affine_new[2][:, 0:2],
        affine_new[2][:, 2],
    )

MESH = pl.DeviceIdType.MESH
TOK = 4
UNIT = 768
ROWS = (48, 48, 24, 24, 96)
WIDTHS = (2304, 768, 768, 3072, 768)
AFFINE = 5
EACH = 24
ORDER_IN = (5, 0, 1, 2, 3, 4)
ORDER_MLP = (4, 3)
ORDER_REST = (0, 1, 2, 5)
VMEM_LIMIT = 60 * 1024 * 1024


def units_of(order, unit=UNIT):
    units = []
    for k in order:
        if k == AFFINE:
            units.append((k, 0, 128))
        else:
            wide = unit if ROWS[k] < 96 or unit > UNIT else unit // 2
            units += [(k, c, min(wide, WIDTHS[k] - c)) for c in range(0, WIDTHS[k], wide)]
    return units


def spot():
    clip = lax.axis_index("clip")
    return clip // 4, (clip // 2) % 2, clip % 2, lax.axis_index("tok")


def clip_of(y, x, core):
    return (y * 2 + x) * 2 + core


def greet():
    y, x, core, t = spot()
    barrier = pltpu.get_barrier_semaphore()

    def tell(clip, tok):
        pl.semaphore_signal(barrier, inc=1, device_id=(clip, tok), device_id_type=MESH)

    tell(clip_of(y, x, 1 - core), t)
    tell(clip_of(y, 1 - x, core), t)
    tell(clip_of(1 - y, x, core), t)
    for far in range(1, TOK):
        tell(clip_of(y, x, core), (t + far) % TOK)
    pl.semaphore_wait(barrier, 3 + (TOK - 1))


class Flight:
    def __init__(self):
        self.started = []

    def go(self, copy, when=None):
        if when is None:
            copy.start()
        else:
            pl.when(when)(copy.start)
        self.started.append((copy, when))
        return copy

    def drain(self):
        for copy, when in self.started:
            if when is None:
                copy.wait_send()
            else:
                pl.when(when)(copy.wait_send)


def gather_steps(units, owned, full, sems):
    local, got, core_got, out_sem, z_sem = sems
    y, x, core, t = spot()
    here, by_x, by_y = clip_of(y, x, core), clip_of(y, 1 - x, core), clip_of(1 - y, x, core)
    mate = clip_of(y, x, 1 - core)
    corner_clip = clip_of(1 - y, 1 - x, core)
    local_copies = []

    def place(u, at):
        k, c, width = units[u]
        return full[k].at[at, :, pl.ds(c, width)]

    def send(u, at, to, tok=None, own=False, along_z=False, when=None):
        k, c, width = units[u]
        there = place(u, at)
        copy = pltpu.make_async_remote_copy(
            src_ref=owned[k].at[:, pl.ds(c, width)] if own else there,
            dst_ref=there,
            send_sem=(z_sem if along_z else out_sem).at[u],
            recv_sem=got.at[u, at],
            device_id=(to, t if tok is None else tok),
            device_id_type=MESH,
        )
        if when is None:
            copy.start()
        else:
            pl.when(when)(copy.start)

    def many(u, count):
        k, c, width = units[u]
        return full[k].at[pl.ds(0, count), :, pl.ds(c, width)]

    def took(u, count, sem):
        there = many(u, count)
        pltpu.make_async_copy(there, there, sem.at[u]).wait()

    def arrive(u, at):
        there = place(u, at)
        pltpu.make_async_copy(there, there, got.at[u, at]).wait()

    def spread(u, at, own=False, when=None):
        def both():
            send(u, at, by_x, own=own)
            send(u, at, by_y, own=own)

        if when is None:
            both()
        else:
            pl.when(when)(both)

    def begin(u):
        k, c, width = units[u]
        me = here * TOK + t
        copy = pltpu.make_async_copy(owned[k].at[:, pl.ds(c, width)], place(u, me), local.at[u])
        copy.start()
        local_copies.append(copy)
        send(u, me, here, t + 1, own=True, along_z=True, when=t < TOK - 1)
        send(u, me, here, t - 1, own=True, along_z=True, when=t > 0)
        spread(u, me, own=True)

    hops = [(far, way) for far in range(1, TOK) for way in (1, -1)]

    def guard(far, way):
        return t + far <= TOK - 1 if way == 1 else t - far >= 0

    def to_mate(u, clip):
        k, c, width = units[u]
        there = full[k].at[pl.ds(clip * TOK, TOK), :, pl.ds(c, width)]
        pltpu.make_async_remote_copy(
            src_ref=there,
            dst_ref=there,
            send_sem=out_sem.at[u],
            recv_sem=core_got.at[u],
            device_id=(mate, t),
            device_id_type=MESH,
        ).start()

    def along(u):
        for far, way in hops:
            at = here * TOK + t + far * way

            def passing(at=at, way=way):
                arrive(u, at)
                onward = t > 0 if way == 1 else t < TOK - 1
                send(u, at, here, t - way, along_z=True, when=onward)
                spread(u, at)

            pl.when(guard(far, way))(passing)
        local_copies[u].wait()
        to_mate(u, here)

    def crossing(u):
        for far in range(TOK):
            tok = (t + far) % TOK
            from_x, from_y = by_x * TOK + tok, by_y * TOK + tok
            arrive(u, from_x)
            if far % 2 == 1:
                send(u, from_x, by_y)
            arrive(u, from_y)
            if far % 2 == 0:
                send(u, from_y, by_x)
        to_mate(u, by_x)
        to_mate(u, by_y)

    def corner(u):
        for far in range(TOK):
            arrive(u, corner_clip * TOK + (t + far) % TOK)
        to_mate(u, corner_clip)

    def settle(u):
        took(u, 16, core_got)

    def drain():
        edge = jnp.logical_or(t == 0, t == TOK - 1)
        for u in range(len(units)):
            took(u, 28, out_sem)

        def wait_z(count):
            for u in range(len(units)):
                took(u, count, z_sem)

        pl.when(edge)(functools.partial(wait_z, 1))
        pl.when(jnp.logical_not(edge))(functools.partial(wait_z, 5))

    return begin, along, crossing, corner, settle, drain


def gather_sems(count):
    dma = pltpu.SemaphoreType.DMA
    return [
        dma((count,)),
        dma((count, 32)),
        dma((count,)),
        dma((count,)),
        dma((count,)),
    ]


def rows_from(flat, out):
    rows, n = out.shape[0], out.shape[1] // 128
    for c in range(n):
        out[:, c * 128 : (c + 1) * 128] = flat[pl.ds(c, rows, stride=n), :].astype(out.dtype)


def join_affine(blocks, out):
    lane = lax.broadcasted_iota(jnp.int32, (16, 128), 1)
    tiles = [jnp.zeros((16, 128), jnp.float32) for _ in range(6)]
    for i in range(32):
        block = jnp.where(lane < EACH, blocks[i].astype(jnp.float32), 0.0)
        tile, shift = (i * EACH) // 128, (i * EACH) % 128
        turned = pltpu.roll(block, shift, 1) if shift else block
        tiles[tile] = tiles[tile] + jnp.where(lane >= shift, turned, 0.0)
        if shift + EACH > 128:
            tiles[tile + 1] = tiles[tile + 1] + jnp.where(lane < shift, turned, 0.0)
    for i in range(6):
        out[:, i * 128 : (i + 1) * 128] = tiles[i]


def scatter_steps(units, parts, held, core_in, side_in, part_in, z_in, sems, flight, finals):
    load_sem, c_send, c_recv, d_send, d_recv, s_send, s_recv, z_send, z_recv = sems
    y, x, core, t = spot()
    here, by_x, by_y = clip_of(y, x, core), clip_of(y, 1 - x, core), clip_of(1 - y, x, core)
    mate = clip_of(y, x, 1 - core)
    homes = [(1 - y, 1 - x), (y, 1 - x), (1 - y, x), (y, x)]

    def cols(u):
        k, c, width = units[u]
        return pl.ds(c, width)

    def remote(src, dst, send_sem, recv_sem, to, tok=None):
        return pltpu.make_async_remote_copy(
            src_ref=src,
            dst_ref=dst,
            send_sem=send_sem,
            recv_sem=recv_sem,
            device_id=(to, t if tok is None else tok),
            device_id_type=MESH,
        )

    def load(u, g):
        k = units[u][0]
        ya, xa = homes[g]
        return pltpu.make_async_copy(
            parts[k].at[pl.ds(clip_of(ya, xa, core) * TOK, TOK), :, cols(u)],
            held[u].at[g],
            load_sem.at[u, g],
        )

    def to_mate(u, g):
        k = units[u][0]
        ya, xa = homes[g]
        return remote(
            parts[k].at[pl.ds(clip_of(ya, xa, 1 - core) * TOK, TOK), :, cols(u)],
            core_in[u].at[g],
            c_send.at[u, g],
            c_recv.at[u, g],
            mate,
        )

    def begin(u):
        for g in range(4):
            load(u, g).start()
            flight.go(to_mate(u, g))

    def ready(u, g):
        load(u, g).wait()
        to_mate(u, g).wait_recv()

    def add_into(u, g, lo, hi, pieces):
        def one(j, carry):
            total = up(held[u][g, j])
            for piece in pieces:
                total = total + up(piece[j])
            held[u][g, j] = low(total)
            return carry

        lax.fori_loop(lo, hi, one, 0)

    def first(u, half):
        return remote(
            held[u].at[0, pl.ds(2 * half, 2)],
            side_in[u].at[pl.ds(2 * half, 2)],
            d_send.at[u, half],
            d_recv.at[u, half],
            by_y if half else by_x,
        )

    def second(u, across):
        return remote(
            held[u].at[1 if across == 0 else 2],
            part_in[u].at[across],
            s_send.at[u, across],
            s_recv.at[u, across],
            by_x if across == 0 else by_y,
        )

    def last(u, far):
        tok = (t + far) % TOK
        return remote(
            held[u].at[3, tok],
            z_in[u].at[far - 1],
            z_send.at[u, far - 1],
            z_recv.at[u, far - 1],
            here,
            tok,
        )

    def step1(u):
        ready(u, 0)
        add_into(u, 0, 0, TOK, [core_in[u].at[0]])
        flight.go(first(u, 0))
        flight.go(first(u, 1))

    def step2(u):
        ready(u, 2)
        first(u, 0).wait_recv()
        add_into(u, 2, 0, 2, [core_in[u].at[2], side_in[u]])
        add_into(u, 2, 2, TOK, [core_in[u].at[2]])
        flight.go(second(u, 1))
        ready(u, 1)
        first(u, 1).wait_recv()
        add_into(u, 1, 0, 2, [core_in[u].at[1]])
        add_into(u, 1, 2, TOK, [core_in[u].at[1], side_in[u]])
        flight.go(second(u, 0))

    def step3(u):
        ready(u, 3)
        second(u, 0).wait_recv()
        second(u, 1).wait_recv()
        add_into(u, 3, 0, TOK, [core_in[u].at[3], part_in[u].at[0], part_in[u].at[1]])
        for far in range(1, TOK):
            flight.go(last(u, far))

    def step4(u):
        total = up(held[u][3, t])
        for far in range(1, TOK):
            last(u, far).wait_recv()
            total = total + up(z_in[u][far - 1])
        finals(u, total)

    return begin, step1, step2, step3, step4


def scatter_scratch(units):
    bf16 = jnp.bfloat16
    shapes = [(16 if k == AFFINE else ROWS[k], width) for k, c, width in units]
    held = [pltpu.VMEM((4, TOK) + s, bf16) for s in shapes]
    side = [pltpu.VMEM((TOK,) + s, bf16) for s in shapes]
    part = [pltpu.VMEM((2, TOK) + s, bf16) for s in shapes]
    last = [pltpu.VMEM((TOK - 1,) + s, bf16) for s in shapes]
    return held + held + side + part + last


def scatter_sems(count):
    dma = pltpu.SemaphoreType.DMA
    return [
        dma((count, 4)),
        dma((count, 4)),
        dma((count, 4)),
        dma((count, 2)),
        dma((count, 2)),
        dma((count, 2)),
        dma((count, 2)),
        dma((count, TOK - 1)),
        dma((count, TOK - 1)),
    ]


STEP_FIX = 1.0 - 0.5**STEP


def adamw_rows(rate, weights, moment, square, grad, out):
    averaged = 0.5 * moment + 0.5 * grad
    squared = 0.5 * square + 0.5 * grad * grad
    out[0][...] = weights - rate * (
        averaged / STEP_FIX / (jnp.sqrt(squared / STEP_FIX) + 1e-08) + 0.1 * weights
    )
    out[1][...] = averaged
    out[2][...] = squared


RATES = (768 ** (-0.5), 384 ** (-0.5), 11 ** (-0.5), 768 ** (-0.5), 3072 ** (-0.5))


def part_affine(norms, out):
    rows = [jnp.sum(n[0:8, :], axis=0, keepdims=True) for n in norms]
    rows += [jnp.sum(n[8:16, :], axis=0, keepdims=True) for n in norms]
    table = jnp.concatenate(rows + [jnp.zeros((10, 768), jnp.float32)], axis=0)
    lane = lax.broadcasted_iota(jnp.int32, (16, 128), 1)
    for i in range(32):
        tile, shift = (i * EACH) // 128, (i * EACH) % 128
        block = table[:, tile * 128 : (tile + 1) * 128]
        block = pltpu.roll(block, (128 - shift) % 128, 1) if shift else block
        if shift + EACH > 128:
            after = pltpu.roll(table[:, (tile + 1) * 128 : (tile + 2) * 128], 128 - shift, 1)
            block = jnp.where(lane < 128 - shift, block, after)
        out[i] = jnp.where(lane < EACH, block, 0.0).astype(jnp.bfloat16)

GROUPS = 7
T_ROWS = 448
S_PAD = 208
S_ROWS = 416
CHUNK = 768
MLP_CHUNK = 512
SCALE = HEAD_DIM ** (-0.5)
BIG = -1e30
NT = (((1,), (1,)), ((), ()))
TN = (((0,), (0,)), ((), ()))


def dot(left, right, dims=(((1,), (0,)), ((), ()))):
    return lax.dot_general(left, right, dims, preferred_element_type=jnp.float32)


def low(values):
    return values.astype(jnp.bfloat16)


def up(values):
    return values.astype(jnp.float32)


def center_rows(values):
    center = values - jnp.mean(values, axis=-1, keepdims=True)
    inverse = lax.rsqrt(jnp.mean(center * center, axis=-1, keepdims=True) + 1e-06)
    return center * inverse, inverse


def back_rows(upstream, unit, inverse, gain):
    scaled = upstream * gain
    inner = (
        scaled
        - jnp.mean(scaled, axis=-1, keepdims=True)
        - unit * jnp.mean(scaled * unit, axis=-1, keepdims=True)
    )
    return inner * inverse


def fold(values):
    return jnp.sum(values.reshape(-1, 8, values.shape[-1]), axis=0)


def columns(j, width):
    return pl.ds(pl.multiple_of(j * width, 128), width)


def rows_of(i, height):
    return pl.ds(pl.multiple_of(i * height, 8), height)


def times(out, left, weight, width=CHUNK):
    def step(j, carry):
        at = columns(j, width)
        out[:, at] = dot(left[...], weight[:, at]).astype(out.dtype)
        return carry

    lax.fori_loop(0, out.shape[1] // width, step, 0)


def lane_half(shape):
    return lax.broadcasted_iota(jnp.int32, shape, 1) < HEAD_DIM


def soft(query, keys, mask):
    scores = jnp.where(mask, dot(keys, query, NT), BIG)
    expo = jnp.exp(scores - jnp.max(scores, axis=0, keepdims=True))
    return expo * (1.0 / jnp.sum(expo, axis=0, keepdims=True))


def attend(query, keys, values, mask):
    half = lane_half(query.shape)
    zero = jnp.zeros_like(query)
    query = query * jnp.bfloat16(SCALE)
    first = dot(low(soft(jnp.where(half, query, zero), keys, mask)), values, TN)
    second = dot(low(soft(jnp.where(half, zero, query), keys, mask)), values, TN)
    return low(jnp.where(half, first, second))


def attend_back(query, keys, values, upstream, mask):
    half = lane_half(query.shape)
    zero = jnp.zeros_like(query)
    query = query * jnp.bfloat16(SCALE)
    scaled = keys * jnp.bfloat16(SCALE)

    def one(pick):
        probs = soft(pick(query, zero), keys, mask)
        dprobs = dot(values, pick(upstream, zero), NT)
        dscores = low(probs * (dprobs - jnp.sum(dprobs * probs, axis=0, keepdims=True)))
        return dot(dscores, scaled, TN), dot(dscores, query), dot(low(probs), upstream)

    first = one(lambda a, b: jnp.where(half, a, b))
    second = one(lambda a, b: jnp.where(half, b, a))
    return tuple(low(jnp.where(half, a, b)) for a, b in zip(first, second))


def frame_mask(size):
    patch = lambda axis: (lambda i: (i // 64) * 8 + i % 8)(
        lax.broadcasted_iota(jnp.int32, (size, size), axis)
    )
    return patch(0) == patch(1)


def patch_mask():
    return lax.broadcasted_iota(jnp.int32, (S_PAD, S_PAD), 0) < PATCHES


T_BLOCKS = ((0, 192), (192, 256))


def mlp_kernel(lowered, after_s, cotangent, widen, narrow, affine, result, d_narrow, d_widen, d_after, d_norm, cot, turned, total, back):
    j = pl.program_id(0)

    @pl.when(j == 0)
    def start():
        cot[...] = jnp.zeros_like(cot)
        for f in range(2):
            back[pl.ds(f * S_PAD, PATCHES), :] = up(cotangent[f])
            back[pl.ds(f * S_PAD + PATCHES, S_PAD - PATCHES), :] = jnp.zeros((S_PAD - PATCHES, D), jnp.float32)
        cot[...] = low(back[...])
        turned[...] = lowered[...].T
        total[...] = after_s[...]
        back[...] = jnp.zeros_like(back)

    wide = dot(lowered[...], widen[...])
    phi = 0.5 * (1.0 + lax.erf(wide * 0.7071067811865476))
    active = low(wide * phi)
    slope = phi + wide * jnp.exp(-0.5 * wide * wide) * 0.3989422804014327
    d_wide = low(dot(cot[...], narrow[...], NT) * slope)
    total[...] += dot(active, narrow[...])
    d_narrow[...] = low(dot(active, cot[...], TN))
    d_widen[...] = low(dot(turned[...], d_wide))
    back[...] += dot(d_wide, widen[...], NT)

    @pl.when(j == pl.num_programs(0) - 1)
    def finish():
        for f in range(2):
            result[f] = low(total[pl.ds(f * S_PAD, PATCHES), :])

        def norm(b, carry):
            rows = rows_of(b, 32)
            unit, inverse = center_rows(after_s[rows, :])
            upstream = back[rows, :]
            d_after[rows, :] = up(cot[rows, :]) + back_rows(upstream, unit, inverse, affine[2:3, :])
            return carry[0] + fold(upstream * unit), carry[1] + fold(upstream)

        zero = jnp.zeros((8, D), jnp.float32)
        gain, shift = lax.fori_loop(0, S_ROWS // 32, norm, (zero, zero))
        d_norm[0:8, :] = gain
        d_norm[8:16, :] = shift


def mlp(lowered, after_s, cotangent, widen, narrow, affine):
    whole = lambda shape: pl.BlockSpec(shape, lambda j: (0,) * len(shape))
    steps = HID // MLP_CHUNK
    return pl.pallas_call(
        mlp_kernel,
        grid=(steps,),
        in_specs=[
            whole((S_ROWS, D)),
            whole((S_ROWS, D)),
            whole((2, PATCHES, D)),
            pl.BlockSpec((D, MLP_CHUNK), lambda j: (0, j)),
            pl.BlockSpec((MLP_CHUNK, D), lambda j: (j, 0)),
            whole((16, D)),
        ],
        out_specs=[
            whole((2, PATCHES, D)),
            pl.BlockSpec((MLP_CHUNK, D), lambda j: (j, 0)),
            pl.BlockSpec((D, MLP_CHUNK), lambda j: (0, j)),
            whole((S_ROWS, D)),
            whole((16, D)),
        ],
        out_shape=[
            jax.ShapeDtypeStruct((2, PATCHES, D), jnp.bfloat16),
            jax.ShapeDtypeStruct((HID, D), jnp.bfloat16),
            jax.ShapeDtypeStruct((D, HID), jnp.bfloat16),
            jax.ShapeDtypeStruct((S_ROWS, D), jnp.float32),
            jax.ShapeDtypeStruct((16, D), jnp.float32),
        ],
        scratch_shapes=[
            pltpu.VMEM((S_ROWS, D), jnp.bfloat16),
            pltpu.VMEM((D, S_ROWS), jnp.bfloat16),
            pltpu.VMEM((S_ROWS, D), jnp.float32),
            pltpu.VMEM((S_ROWS, D), jnp.float32),
        ],
        compiler_params=pltpu.CompilerParams(vmem_limit_bytes=56 * 1024 * 1024),
        cost_estimate=pl.CostEstimate(flops=12000000000, bytes_accessed=30000000, transcendentals=0),
    )(lowered, after_s, cotangent, widen, narrow, affine)

def pack(box, rows):
    extra = [rows(f, 192, 4) for f in range(2)]
    line = lax.broadcasted_iota(jnp.int32, (16, D), 0)
    for s in range(TOK):
        wide = [rows(f, 48 * s, 48) for f in range(2)]
        for b in range(6):
            pair = [w[8 * b : 8 * b + 8, :] for w in wide]
            box[s, b] = low(jnp.concatenate(pair, axis=0))
        one = [jnp.broadcast_to(e[s : s + 1, :], (16, D)) for e in extra]
        box[s, 6] = low(jnp.where(line == 0, one[0], jnp.where(line == 8, one[1], 0.0)))


def unpack(box, f, put):
    for s in range(TOK):
        for b in range(6):
            slab = up(box[s, b])
            put(48 * s + 8 * b, 8, slab[8 * f : 8 * f + 8, :])
    last = [up(box[s, 6])[8 * f : 8 * f + 1, :] for s in range(TOK)]
    put(192, TOK, jnp.concatenate(last, axis=0))


class Exchange:
    def __init__(self, source, target, sems, flight):
        self.source, self.target, self.flight = source, target, flight
        self.local, self.sent, self.got = sems
        self.clip, self.t = lax.axis_index("clip"), lax.axis_index("tok")

    def copy(self, far):
        return pltpu.make_async_remote_copy(
            src_ref=self.source((self.t + far) % TOK),
            dst_ref=self.target(self.t),
            send_sem=self.sent.at[far - 1],
            recv_sem=self.got.at[far - 1],
            device_id=(self.clip, (self.t + far) % TOK),
            device_id_type=MESH,
        )

    def own(self):
        return pltpu.make_async_copy(self.source(self.t), self.target(self.t), self.local.at[0])

    def start(self):
        for far in range(1, TOK):
            self.flight.go(self.copy(far))
        self.own().start()

    def wait(self):
        for far in range(1, TOK):
            there = self.target((self.t - far + TOK) % TOK)
            pltpu.make_async_copy(there, there, self.got.at[far - 1]).wait()
        self.own().wait()


def exchange_sems():
    dma = pltpu.SemaphoreType.DMA
    return [dma((1,)), dma((TOK - 1,)), dma((TOK - 1,))]


def pieces(count, step, size):
    def run(lo, hi):
        def one(j, carry):
            step(j)
            return carry

        lax.fori_loop(lo, hi, one, 0)

    return [functools.partial(run, lo, min(lo + size, count)) for lo in range(0, count, size)]


def product(out, left, weight, width=CHUNK):
    def step(j):
        at = columns(j, width)
        out[:, at] = dot(left(), weight[:, at]).astype(out.dtype)

    return step


def product_back(out, left, weight, width=CHUNK):
    def step(j):
        at = columns(j, width)
        out[:, at] = dot(left(), weight[at, :], NT).astype(out.dtype)

    return step


def gradient(out, turned, upstream, width=CHUNK):
    def step(j):
        at = columns(j, width)
        out[:, at] = low(dot(turned[...], upstream(at)))

    return step


SUM_START = 6
SUM_RATE = 1.3
SUM_SHIFTS = (0, 1, 2, 3)


def spaced(compute, rest):
    done = 0
    for i, call in enumerate(compute):
        call()
        while done < len(rest) and SUM_START + done * SUM_RATE <= i + 1:
            rest[done]()
            done += 1
    for call in rest[done:]:
        call()


def full_kernel_steps(units, steps, shifts, lo, hi):
    calls = []
    for n in range(lo, hi):
        for shift, step in zip(shifts, steps):
            if 0 <= n - shift < len(units):
                calls.append(functools.partial(step, n - shift))
    return calls


A2A_AT = 10


def gather_head(units):
    count = len(units)
    last = [n for n in range(count) if units[n][0] == 1][-1]
    names = ("begin", "along", "crossing", "corner")
    calls = []
    for n in range(last + 3):
        calls += [(name, n - shift) for shift, name in enumerate(names) if 0 <= n - shift < count]
    return calls + [("begin", last + 3), ("along", last + 2), ("corner", last)]


def forward_kernel(units, *refs):
    masters, block, frames = refs[:5], refs[5], refs[6]
    full = list(refs[7:12])
    affine, patch, normed_t, merged_t, mixed_t, first_t = refs[12:18]
    after_t, normed_s, merged_s, mixed_s, after_s, lowered = refs[18:24]
    owned, gathered = list(refs[24:29]), refs[29]
    entry_w, temporal_w, spatial_w, outbox, sent, inbox, load_sem = refs[30:37]
    there_sems, back_sems = refs[37:40], refs[40:43]
    sems = refs[43:]
    greet()
    full.append(gathered)
    owned.append(block)
    flight = Flight()
    begin, along, crossing, corner, settle, drain = gather_steps(units, owned, full, sems)
    count = len(units)
    place = {k: [n for n in range(count) if units[n][0] == k] for k in range(6)}
    there = Exchange(lambda s: outbox.at[s], lambda s: patch.at[:, s], there_sems, flight)
    back = Exchange(lambda s: sent.at[:, s], lambda s: inbox.at[s], back_sems, flight)
    def settle_all(k):
        for n in place[k]:
            settle(n)

    ready = set()
    original = begin

    def begin(n):
        k = units[n][0]
        if k not in ready and k != AFFINE:
            rows_from(masters[k], owned[k])
            ready.add(k)
        original(n)

    steps = {"begin": begin, "along": along, "crossing": crossing, "corner": corner}
    head = [functools.partial(steps[name], n) for name, n in gather_head(units)]
    step = lambda name, n: [functools.partial(steps[name], n)]
    for call in head[:A2A_AT]:
        call()
    pack(outbox, lambda f, start, size: up(frames[f, start : start + size, :]))
    there.start()
    for call in head[A2A_AT:]:
        call()

    def load(part, source, target):
        return pltpu.make_async_copy(source, target, load_sem.at[part])

    loads = {
        "entry": load(0, full[0].at[pl.ds(0, 16)], entry_w),
        "temporal": load(1, full[1], temporal_w),
        "later": load(2, full[0].at[pl.ds(16, 16)], entry_w),
        "spatial": load(3, full[2], spatial_w),
    }
    settle_all(AFFINE)
    join_affine(gathered, affine)
    there.wait()

    def norm_t(b):
        unit, unused = center_rows(up(patch[b].reshape(64, D)))
        normed_t[rows_of(b, 64), :] = low(unit * affine[0:1, :] + affine[3:4, :])

    def heads_t(p):
        found = []
        for start, size in T_BLOCKS:
            rows = pl.ds(start, size)
            query, keys, values = (merged_t[rows, columns(p + 6 * i, 128)] for i in range(3))
            found.append(attend(query, keys, values, frame_mask(size)))
        for (start, size), value in zip(T_BLOCKS, found):
            mixed_t[pl.ds(start, size), columns(p, 128)] = value

    entry_m = lambda at: entry_w[:, :, at].reshape(D, CHUNK)

    def merge(out, left):
        def step(j):
            at = columns(j, CHUNK)
            out[:, at] = low(dot(left[...], entry_m(at)))

        return step

    def first_step(j):
        at = columns(j, CHUNK)
        first_t[:, at] = low(dot(mixed_t[...], temporal_w[0:16, :, at].reshape(D, CHUNK)))

    def branch_step(j):
        at = columns(j, CHUNK)
        value = low(dot(first_t[...], temporal_w[16:32, :, at].reshape(D, CHUNK)))
        sent[:, :, :, at] = value.reshape(GROUPS, TOK, 16, CHUNK)

    def start_temporal():
        settle_all(0)
        settle_all(1)
        loads["entry"].start()
        loads["temporal"].start()
        for call in pieces(GROUPS, norm_t, GROUPS):
            call()
        loads["entry"].wait()
        loads["temporal"].wait()

    def start_spatial():
        settle_all(2)
        loads["later"].start()
        loads["spatial"].start()
        back.wait()
        for f in range(2):

            def put(start, size, rows, f=f):
                after_t[f * S_PAD + start : f * S_PAD + start + size, :] = (
                    up(frames[f, start : start + size, :]) + rows
                )

            unpack(inbox, f, put)
            tail = f * S_PAD + PATCHES
            after_t[tail : (f + 1) * S_PAD, :] = jnp.zeros((S_PAD - PATCHES, D), jnp.float32)

    def norm_s(b):
        unit, unused = center_rows(after_t[rows_of(b, 32), :])
        normed_s[rows_of(b, 32), :] = low(unit * affine[1:2, :] + affine[4:5, :])

    def wait_spatial():
        loads["later"].wait()
        loads["spatial"].wait()

    def heads_s(p):
        found = []
        for f in range(2):
            rows = pl.ds(f * S_PAD, S_PAD)
            query, keys, values = (merged_s[rows, columns(p + 6 * i, 128)] for i in range(3))
            found.append(attend(query, keys, values, patch_mask()))
        for f in range(2):
            mixed_s[pl.ds(f * S_PAD, S_PAD), columns(p, 128)] = found[f]

    def out_s(j):
        at = columns(j, CHUNK)
        weight = low(up(spatial_w[:, :, at]).reshape(D, CHUNK))
        after_s[:, at] = after_t[:, at] + dot(mixed_s[...], weight)

    def norm_m(b):
        unit, unused = center_rows(after_s[rows_of(b, 32), :])
        lowered[rows_of(b, 32), :] = low(unit * affine[2:3, :] + affine[5:6, :])

    order = (
        [start_temporal]
        + step("crossing", 3)
        + pieces(3, merge(merged_t, normed_t), 1)
        + step("corner", 3)
        + step("along", 5)
        + pieces(6, heads_t, 2)
        + step("crossing", 4)
        + pieces(1, first_step, 1)
        + pieces(1, branch_step, 1)
        + [back.start]
        + step("corner", 4)
        + step("crossing", 5)
        + [start_spatial]
        + pieces(13, norm_s, 13)
        + [wait_spatial]
        + pieces(3, merge(merged_s, normed_s), 1)
        + pieces(6, heads_s, 3)
        + step("corner", 5)
        + pieces(1, out_s, 1)
        + pieces(13, norm_m, 13)
    )
    for call in order:
        call()
    for k in (3, 4):
        settle_all(k)
    drain()
    flight.drain()


def forward(masters, block, frames):
    units = units_of(ORDER_IN, HID)
    vmem = pl.BlockSpec(memory_space=pltpu.VMEM)
    anywhere = pl.BlockSpec(memory_space=pl.ANY)
    bf16, f32 = jnp.bfloat16, jnp.float32
    slab = (TOK, GROUPS, 16, D)
    group = (GROUPS, TOK, 16, D)
    saved = [
        ((16, D), f32),
        (group, bf16),
        ((T_ROWS, D), bf16),
        ((T_ROWS, 3 * D), bf16),
        ((T_ROWS, D), bf16),
        ((T_ROWS, D), bf16),
        ((S_ROWS, D), f32),
        ((S_ROWS, D), bf16),
        ((S_ROWS, 3 * D), bf16),
        ((S_ROWS, D), bf16),
        ((S_ROWS, D), f32),
        ((S_ROWS, D), bf16),
    ]
    return pl.pallas_call(
        functools.partial(forward_kernel, units),
        out_shape=[jax.ShapeDtypeStruct((32, r, w), bf16) for r, w in zip(ROWS, WIDTHS)]
        + [jax.ShapeDtypeStruct(s, t) for s, t in saved],
        in_specs=[vmem] * 7,
        out_specs=[anywhere] * 5 + [vmem] * 12,
        scratch_shapes=[pltpu.VMEM((r, w), bf16) for r, w in zip(ROWS, WIDTHS)]
        + [
            pltpu.VMEM((32, 16, 128), bf16),
            pltpu.VMEM((16, 48, 3 * D), bf16),
            pltpu.VMEM((32, 48, D), bf16),
            pltpu.VMEM((32, 24, D), bf16),
            pltpu.VMEM(slab, bf16),
            pltpu.VMEM(group, bf16),
            pltpu.VMEM(slab, bf16),
            pltpu.SemaphoreType.DMA((4,)),
        ]
        + exchange_sems()
        + exchange_sems()
        + gather_sems(len(units)),
        compiler_params=pltpu.CompilerParams(
            collective_id=0, has_side_effects=True, vmem_limit_bytes=VMEM_LIMIT
        ),
    )(*masters, block, frames)


def finals_of(states, outs, grads, affine_out=None):
    def finals(u, unit, total):
        k, c, width = unit
        if k == AFFINE:
            affine_out[...] = total
            return
        n, rows = WIDTHS[k] // 128, ROWS[k]
        for i in range(width // 128):
            grads[k][pl.ds(c // 128 + i, rows, stride=n), :] = total[:, i * 128 : (i + 1) * 128]
        if c + width == WIDTHS[k]:
            state = states[k]
            adamw_rows(RATES[k], state[0][...], state[1][...], state[2][...], grads[k][...], outs[k])

    return finals


def back_kernel(units, *refs):
    arrays = (3, 4)
    parts = dict(zip(arrays, refs[:2]))
    states = {k: refs[2 + 3 * i : 5 + 3 * i] for i, k in enumerate(arrays)}
    d_after_s, after_t, affine, spatial = refs[8:12]
    normed_s_in, merged_s_in, mixed_s_in, entry_in = refs[12:16]
    patch_in, normed_t_in, merged_t_in, mixed_t_in, first_t_in, temporal_in = refs[16:22]
    outs = {k: refs[22 + 3 * i : 25 + 3 * i] for i, k in enumerate(arrays)}
    sent, d_after_t, d_spatial, d_entry_out, d_temporal, norm_s_out, norm_t_out = refs[28:35]
    pos = 35
    pools = []
    for i in range(5):
        pools.append(refs[pos : pos + len(units)])
        pos += len(units)
    grads = dict(zip(arrays, refs[pos : pos + 2]))
    pos += 2
    normed_s, merged_s, mixed_s, entry_w = refs[pos : pos + 4]
    patch, normed_t, merged_t, mixed_t, first_t, temporal_w = refs[pos + 4 : pos + 10]
    d_entry, lowered, d_mixed, d_first, d_merged, turned_s, turned_t, back, outbox, grouped, load_sem = refs[
        pos + 10 : pos + 21
    ]
    pos += 21
    there_sems = refs[pos : pos + 3]
    sems = refs[pos + 3 :]
    sources = (normed_s_in, merged_s_in, mixed_s_in, entry_in.at[1])
    targets = (normed_s, merged_s, mixed_s, entry_w)
    sources += (patch_in, normed_t_in, merged_t_in, mixed_t_in, first_t_in, temporal_in)
    targets += (patch, normed_t, merged_t, mixed_t, first_t, temporal_w)
    loads = [pltpu.make_async_copy(a, b, load_sem.at[i]) for i, (a, b) in enumerate(zip(sources, targets))]
    for copy in loads:
        copy.start()
    entry_load = pltpu.make_async_copy(entry_in.at[0], entry_w, load_sem.at[10])
    entry_stores = [pltpu.make_async_copy(d_entry, d_entry_out.at[i], load_sem.at[12 - i]) for i in range(2)]
    greet()
    flight = Flight()
    finals = finals_of(states, outs, grads)
    steps = scatter_steps(
        units, parts, *pools, sems, flight, lambda u, total: finals(u, units[u], total)
    )
    there = Exchange(lambda s: outbox.at[s], lambda s: grouped.at[:, s], there_sems, flight)
    zero = jnp.zeros((8, D), jnp.float32)

    def begin_s():
        lowered[...] = low(d_after_s[...])
        for copy in loads[:3]:
            copy.wait()
        turned_s[...] = mixed_s[...].T

    def turn_s():
        turned_s[...] = normed_s[...].T

    def heads_s(p):
        found = []
        for f in range(2):
            rows = pl.ds(f * S_PAD, S_PAD)
            query, keys, values = (merged_s[rows, columns(p + 6 * i, 128)] for i in range(3))
            found.append(
                attend_back(query, keys, values, d_mixed[rows, columns(p, 128)], patch_mask())
            )
        for f in range(2):
            for i in range(3):
                d_merged[pl.ds(f * S_PAD, S_PAD), columns(p + 6 * i, 128)] = found[f][i]

    def s_back(j):
        at = columns(j, CHUNK)
        back[0:S_ROWS, at] = dot(d_merged[0:S_ROWS, :], entry_w[at, :], NT)

    def end_s():
        entry_load.start()

        def norm(b, carry):
            rows = rows_of(b, 32)
            unit, inverse = center_rows(after_t[rows, :])
            upstream = back[rows, :]
            d_after_t[rows, :] = d_after_s[rows, :] + back_rows(upstream, unit, inverse, affine[1:2, :])
            return carry[0] + fold(upstream * unit), carry[1] + fold(upstream)

        gain, shift = lax.fori_loop(0, S_ROWS // 32, norm, (zero, zero))
        norm_s_out[0:8, :] = gain
        norm_s_out[8:16, :] = shift
        pack(outbox, lambda f, start, size: d_after_t[f * S_PAD + start : f * S_PAD + start + size, :])
        there.start()

    def wait_entry():
        loads[3].wait()

    d_mixed_s = d_mixed.at[0:S_ROWS]
    compute = (
        [begin_s]
        + pieces(1, gradient(d_spatial, turned_s, lambda at: lowered[:, at]), 1)
        + pieces(1, product_back(d_mixed_s, lambda: lowered[...], spatial), 1)
        + [turn_s]
        + pieces(6, heads_s, 1)
        + [wait_entry]
        + pieces(1, s_back, 1)
        + [end_s]
        + pieces(3, gradient(d_entry, turned_s, lambda at: d_merged[0:S_ROWS, at]), 1)
        + [entry_stores[1].start]
    )

    def begin_t():
        for copy in loads[4:]:
            copy.wait()
        turned_t[...] = first_t[...].T
        there.wait()

    group_cols = lambda at: grouped[:, :, :, at].reshape(T_ROWS, CHUNK)

    def turn_mixed():
        turned_t[...] = mixed_t[...].T

    def turn_normed():
        turned_t[...] = normed_t[...].T

    def heads_t(p):
        found = []
        for start, size in T_BLOCKS:
            rows = pl.ds(start, size)
            query, keys, values = (merged_t[rows, columns(p + 6 * i, 128)] for i in range(3))
            found.append(
                attend_back(query, keys, values, d_mixed[rows, columns(p, 128)], frame_mask(size))
            )
        for (start, size), values in zip(T_BLOCKS, found):
            for i in range(3):
                d_merged[pl.ds(start, size), columns(p + 6 * i, 128)] = values[i]

    def t_back(j):
        at = columns(j, CHUNK)
        back[:, at] = dot(d_merged[...], entry_w[at, :], NT)

    def end_t():
        def norm(b, carry):
            rows = rows_of(b, 64)
            unit, inverse = center_rows(up(patch[b].reshape(64, D)))
            upstream = back[rows, :]
            value = back_rows(upstream, unit, inverse, affine[0:1, :])
            sent[b] = low(value).reshape(TOK, 16, D)
            return carry[0] + fold(upstream * unit), carry[1] + fold(upstream)

        gain, shift = lax.fori_loop(0, GROUPS, norm, (zero, zero))
        norm_t_out[0:8, :] = gain
        norm_t_out[8:16, :] = shift

    def free_entry():
        entry_stores[1].wait()
        entry_load.wait()

    compute += (
        [begin_t]
        + pieces(1, gradient(d_temporal.at[1], turned_t, group_cols), 1)
        + pieces(1, product_back(d_first, lambda: grouped[...].reshape(T_ROWS, D), temporal_w.at[1]), 1)
        + [turn_mixed]
        + pieces(1, gradient(d_temporal.at[0], turned_t, lambda at: d_first[:, at]), 1)
        + pieces(1, product_back(d_mixed, lambda: d_first[...], temporal_w.at[0]), 1)
        + [turn_normed]
        + pieces(6, heads_t, 1)
        + [free_entry]
        + pieces(1, t_back, 1)
        + [end_t]
        + pieces(3, gradient(d_entry, turned_t, lambda at: d_merged[:, at]), 1)
        + [entry_stores[0].start]
    )
    for u in range(len(units)):
        steps[0](u)
    rest = full_kernel_steps(units, steps[1:], SUM_SHIFTS, 0, len(units) + SUM_SHIFTS[-1])
    spaced(compute, rest)
    entry_stores[0].wait()
    flight.drain()


def backward(parts, states, d_after_s, after_t, affine, spatial, entry, temporal, saved_s, saved_t):
    units = units_of(ORDER_MLP)
    vmem = pl.BlockSpec(memory_space=pltpu.VMEM)
    anywhere = pl.BlockSpec(memory_space=pl.ANY)
    bf16, f32 = jnp.bfloat16, jnp.float32
    shapes = [(ROWS[k], WIDTHS[k]) for k in (3, 4)]
    flat = [(r * w // 128, 128) for r, w in shapes]
    slab = (TOK, GROUPS, 16, D)
    group = (GROUPS, TOK, 16, D)
    outs = [(s, f32) for s in flat for _ in range(3)] + [
        (group, bf16),
        ((S_ROWS, D), f32),
        ((D, D), bf16),
        ((2, D, 3 * D), bf16),
        ((2, D, D), bf16),
        ((16, D), f32),
        ((16, D), f32),
    ]
    return pl.pallas_call(
        functools.partial(back_kernel, units),
        out_shape=[jax.ShapeDtypeStruct(s, t) for s, t in outs],
        in_specs=[anywhere] * 2 + [vmem] * 10 + [anywhere] * 10,
        out_specs=[vmem] * 9 + [anywhere] + [vmem] * 3,
        scratch_shapes=scatter_scratch(units)
        + [pltpu.VMEM(s, f32) for s in flat]
        + [
            pltpu.VMEM((S_ROWS, D), bf16),
            pltpu.VMEM((S_ROWS, 3 * D), bf16),
            pltpu.VMEM((S_ROWS, D), bf16),
            pltpu.VMEM((D, 3 * D), bf16),
            pltpu.VMEM(group, bf16),
            pltpu.VMEM((T_ROWS, D), bf16),
            pltpu.VMEM((T_ROWS, 3 * D), bf16),
            pltpu.VMEM((T_ROWS, D), bf16),
            pltpu.VMEM((T_ROWS, D), bf16),
            pltpu.VMEM((2, D, D), bf16),
            pltpu.VMEM((D, 3 * D), bf16),
            pltpu.VMEM((S_ROWS, D), bf16),
            pltpu.VMEM((T_ROWS, D), bf16),
            pltpu.VMEM((T_ROWS, D), bf16),
            pltpu.VMEM((T_ROWS, 3 * D), bf16),
            pltpu.VMEM((D, S_ROWS), bf16),
            pltpu.VMEM((D, T_ROWS), bf16),
            pltpu.VMEM((T_ROWS, D), f32),
            pltpu.VMEM(slab, bf16),
            pltpu.VMEM(group, bf16),
            pltpu.SemaphoreType.DMA((13,)),
        ]
        + exchange_sems()
        + scatter_sems(len(units)),
        compiler_params=pltpu.CompilerParams(
            collective_id=1, has_side_effects=True, vmem_limit_bytes=VMEM_LIMIT
        ),
    )(*parts, *states, d_after_s, after_t, affine, spatial, *saved_s, entry, *saved_t, temporal)


HOME_AT = 4
HOME_END = 24


def rest_kernel(units, *refs):
    arrays = (0, 1, 2)
    parts = dict(zip(arrays, refs[:3]))
    norms = refs[3:6]
    states = {k: refs[6 + 3 * k : 9 + 3 * k] for k in arrays}
    sent, d_after_t = refs[15:17]
    outs = {k: refs[17 + 3 * k : 20 + 3 * k] for k in arrays}
    affine_out, input_gradient = refs[26:28]
    pos = 28
    pools = []
    for i in range(5):
        pools.append(refs[pos : pos + len(units)])
        pos += len(units)
    parts[AFFINE] = refs[pos]
    grads = dict(zip(arrays, refs[pos + 1 : pos + 4]))
    inbox, home_sems = refs[pos + 4], refs[pos + 5 : pos + 8]
    sems = refs[pos + 8 :]
    greet()
    flight = Flight()
    home = Exchange(lambda s: sent.at[:, s], lambda s: inbox.at[s], home_sems, flight)
    finals = finals_of(states, outs, grads, affine_out)
    steps = scatter_steps(
        units, parts, *pools, sems, flight, lambda u, total: finals(u, units[u], total)
    )
    begin = steps[0]

    def begin_after(u):
        if units[u][0] == AFFINE:
            part_affine(norms, parts[AFFINE])
        begin(u)

    def receive():
        home.wait()
        for f in range(2):

            def put(start, size, rows, f=f):
                at = f * S_PAD + start
                input_gradient[f, start : start + size, :] = d_after_t[at : at + size, :] + rows

            unpack(inbox, f, put)

    calls = full_kernel_steps(units, (begin_after,) + steps[1:], (0, 2, 3, 4, 5), 0, len(units) + 5)
    calls.insert(HOME_AT, home.start)
    calls.insert(HOME_END, receive)
    for call in calls:
        call()
    flight.drain()


def scatter_rest(parts, norms, states, sent, d_after_t):
    units = units_of(ORDER_REST)
    vmem = pl.BlockSpec(memory_space=pltpu.VMEM)
    shapes = [(ROWS[k], WIDTHS[k]) for k in (0, 1, 2)]
    flat = [(r * w // 128, 128) for r, w in shapes]
    return pl.pallas_call(
        functools.partial(rest_kernel, units),
        out_shape=[jax.ShapeDtypeStruct(s, jnp.float32) for s in flat for _ in range(3)]
        + [
            jax.ShapeDtypeStruct((16, 128), jnp.float32),
            jax.ShapeDtypeStruct((2, PATCHES, D), jnp.float32),
        ],
        in_specs=[pl.BlockSpec(memory_space=pl.ANY)] * 3 + [vmem] * 14,
        out_specs=[vmem] * 11,
        scratch_shapes=scatter_scratch(units)
        + [pltpu.VMEM((32, 16, 128), jnp.bfloat16)]
        + [pltpu.VMEM(s, jnp.float32) for s in flat]
        + [pltpu.VMEM((TOK, GROUPS, 16, D), jnp.bfloat16)]
        + exchange_sems()
        + scatter_sems(len(units)),
        compiler_params=pltpu.CompilerParams(
            collective_id=2, has_side_effects=True, vmem_limit_bytes=VMEM_LIMIT
        ),
    )(*parts, *norms, *states, sent, d_after_t)


def on_device(
    frames,
    cotangent,
    entry_weights,
    entry_momentum,
    entry_variance,
    temporal_weights,
    temporal_momentum,
    temporal_variance,
    spatial_weights,
    spatial_momentum,
    spatial_variance,
    widen_weights,
    widen_momentum,
    widen_variance,
    narrow_weights,
    narrow_momentum,
    narrow_variance,
    norm_affine,
    affine_momentum,
    affine_variance,
):
    masters = (entry_weights, temporal_weights, spatial_weights, widen_weights, narrow_weights)
    block = jnp.pad(low(norm_affine).reshape(6, EACH), ((0, 10), (0, 128 - EACH)))
    found = forward(masters, block, frames[0])
    entry, temporal, spatial, widen, narrow = found[:5]
    entry = entry.reshape(2, D, 3 * D)
    temporal = temporal.reshape(2, D, D)
    spatial = spatial.reshape(D, D)
    widen = widen.reshape(D, HID)
    narrow = narrow.reshape(HID, D)
    affine, patch, normed_t, merged_t, mixed_t, first_t = found[5:11]
    after_t, normed_s, merged_s, mixed_s, after_s, lowered = found[11:17]
    result, narrow_grad, widen_grad, d_after_s, norm_m = mlp(
        lowered, after_s, cotangent[0], widen, narrow, affine
    )
    found = backward(
        (widen_grad.reshape(32, -1, HID), narrow_grad.reshape(32, -1, D)),
        (
            widen_weights,
            widen_momentum,
            widen_variance,
            narrow_weights,
            narrow_momentum,
            narrow_variance,
        ),
        d_after_s,
        after_t,
        affine,
        spatial,
        entry,
        temporal,
        (normed_s, merged_s, mixed_s),
        (patch, normed_t, merged_t, mixed_t, first_t),
    )
    widen_new, narrow_new = found[0:3], found[3:6]
    sent, d_after_t, d_spatial, d_entry, d_temporal, norm_s, norm_t = found[6:13]
    found = scatter_rest(
        (d_entry.reshape(32, -1, 3 * D), d_temporal.reshape(32, -1, D), d_spatial.reshape(32, -1, D)),
        (norm_t, norm_s, norm_m),
        (
            entry_weights,
            entry_momentum,
            entry_variance,
            temporal_weights,
            temporal_momentum,
            temporal_variance,
            spatial_weights,
            spatial_momentum,
            spatial_variance,
        ),
        sent,
        d_after_t,
    )
    input_gradient = found[10]
    affine_sum = found[9][:6, :EACH].reshape(2, 3, EACH)
    affine_new = adamw(norm_affine, affine_momentum, affine_variance, affine_sum, 0.5)
    return (
        result[None],
        input_gradient[None],
        *found[0:9],
        *widen_new,
        *narrow_new,
        affine_new[0],
        affine_new[1],
        affine_new[2][:, 0:2],
        affine_new[2][:, 2],
    )

def solution(mesh):
    return jax.shard_map(
        on_device if mesh.shape["clip"] == 8 and mesh.shape["tok"] == TOK else on_any,
        mesh=mesh,
        in_specs=(
            P("clip", "tok", None, None),
            P("clip", "tok", None, None),
            P(("clip", "tok"), None),
            P(("clip", "tok"), None),
            P(("clip", "tok"), None),
            P(("clip", "tok"), None),
            P(("clip", "tok"), None),
            P(("clip", "tok"), None),
            P(("clip", "tok"), None),
            P(("clip", "tok"), None),
            P(("clip", "tok"), None),
            P(("clip", "tok"), None),
            P(("clip", "tok"), None),
            P(("clip", "tok"), None),
            P(("clip", "tok"), None),
            P(("clip", "tok"), None),
            P(("clip", "tok"), None),
            P(None, None, ("clip", "tok")),
            P(None, None, ("clip", "tok")),
            P(None, None, ("clip", "tok")),
        ),
        out_specs=(
            P("clip", "tok", None, None),
            P("clip", "tok", None, None),
            P(("clip", "tok"), None),
            P(("clip", "tok"), None),
            P(("clip", "tok"), None),
            P(("clip", "tok"), None),
            P(("clip", "tok"), None),
            P(("clip", "tok"), None),
            P(("clip", "tok"), None),
            P(("clip", "tok"), None),
            P(("clip", "tok"), None),
            P(("clip", "tok"), None),
            P(("clip", "tok"), None),
            P(("clip", "tok"), None),
            P(("clip", "tok"), None),
            P(("clip", "tok"), None),
            P(("clip", "tok"), None),
            P(None, None, ("clip", "tok")),
            P(None, None, ("clip", "tok")),
            P(None, None, ("clip", "tok")),
            P(None, ("clip", "tok")),
        ),
        check_vma=False,
    )
```

```python
import functools

import jax
import jax.numpy as jnp
from jax import lax
from jax.experimental import pallas as pl
from jax.experimental.pallas import tpu as pltpu
from jax.sharding import PartitionSpec as P

D = 768
HEADS = 12
HEAD_DIM = 64
HID = 3072
PATCHES = 196
STEP = 5

time_scores = "cfphe,cgphe->cphfg"
time_mixed = "cphfg,cgphe->cfphe"
time_flip = "cphfg,cfphe->cgphe"
space_scores = "cfphe,cfqhe->cfhpq"
space_mixed = "cfhpq,cfqhe->cfphe"
space_flip = "cfhpq,cfphe->cfqhe"


def project(inputs, weight):
    return jnp.einsum("cfpa,ab->cfpb", inputs, weight, preferred_element_type=jnp.float32)


def project_back(upstream, weight):
    return jnp.einsum("cfpb,ab->cfpa", upstream, weight, preferred_element_type=jnp.float32)


def weight_sum(inputs, upstream):
    return jnp.einsum("cfpa,cfpb->ab", inputs, upstream, preferred_element_type=jnp.float32)


def layer_norm(values, gain, shift):
    center = values - jnp.mean(values, axis=-1, keepdims=True)
    inverse = lax.rsqrt(jnp.mean(center * center, axis=-1, keepdims=True) + 1e-06)
    unit = center * inverse
    return (unit * gain + shift, unit, inverse)


def norm_back(upstream, unit, inverse, gain):
    scaled = upstream * gain
    inner = (
        scaled
        - jnp.mean(scaled, axis=-1, keepdims=True)
        - unit * jnp.mean(scaled * unit, axis=-1, keepdims=True)
    )
    return (
        inner * inverse,
        jnp.sum(upstream * unit, axis=(0, 1, 2)),
        jnp.sum(upstream, axis=(0, 1, 2)),
    )


def split_heads(merged):
    lowered = merged.astype(jnp.bfloat16)
    parts = lowered.reshape(lowered.shape[:-1] + (3, HEADS, HEAD_DIM))
    return (parts[..., 0, :, :], parts[..., 1, :, :], parts[..., 2, :, :])


def attend_forward(heads, score_form, mixed_form):
    query, keys, values = heads
    scores = jnp.einsum(score_form, query, keys, preferred_element_type=jnp.float32) * HEAD_DIM ** (
        -0.5
    )
    top = jnp.max(scores, axis=-1, keepdims=True)
    expo = jnp.exp(scores - top)
    total = jnp.sum(expo, axis=-1, keepdims=True)
    probs = (expo / total).astype(jnp.bfloat16)
    mixed = jnp.einsum(mixed_form, probs, values, preferred_element_type=jnp.float32)
    joined = mixed.reshape(mixed.shape[:-2] + (HEADS * HEAD_DIM,)).astype(jnp.bfloat16)
    return (joined, top + jnp.log(total))


def attend_backward(heads, logsum, upstream_joined, score_form, mixed_form, flip_form):
    query, keys, values = heads
    upstream = upstream_joined.reshape(upstream_joined.shape[:-1] + (HEADS, HEAD_DIM))
    scale = HEAD_DIM ** (-0.5)
    scores = jnp.einsum(score_form, query, keys, preferred_element_type=jnp.float32) * scale
    probs = jnp.exp(scores - logsum)
    dprobs = jnp.einsum(score_form, upstream, values, preferred_element_type=jnp.float32)
    dscores = (probs * (dprobs - jnp.sum(dprobs * probs, axis=-1, keepdims=True))).astype(
        jnp.bfloat16
    )
    dquery = jnp.einsum(mixed_form, dscores, keys, preferred_element_type=jnp.float32) * scale
    dkeys = jnp.einsum(flip_form, dscores, query, preferred_element_type=jnp.float32) * scale
    dvalues = jnp.einsum(
        flip_form, probs.astype(jnp.bfloat16), upstream, preferred_element_type=jnp.float32
    )
    stacked = jnp.stack([dquery, dkeys, dvalues], axis=-3)
    return stacked.reshape(stacked.shape[:-3] + (3 * HEADS * HEAD_DIM,)).astype(jnp.bfloat16)


def collect(masters):
    gathered = (
        lax.all_gather(masters[0].astype(jnp.bfloat16), ("clip", "tok"), axis=0, tiled=True),
        lax.all_gather(masters[1].astype(jnp.bfloat16), ("clip", "tok"), axis=0, tiled=True),
        lax.all_gather(masters[2].astype(jnp.bfloat16), ("clip", "tok"), axis=0, tiled=True),
        lax.all_gather(masters[3].astype(jnp.bfloat16), ("clip", "tok"), axis=0, tiled=True),
        lax.all_gather(masters[4].astype(jnp.bfloat16), ("clip", "tok"), axis=0, tiled=True),
        lax.all_gather(masters[5].astype(jnp.bfloat16), ("clip", "tok"), axis=2, tiled=True),
    )
    return (
        gathered[0].reshape(2, D, 3 * D),
        gathered[1].reshape(2, D, D),
        gathered[2].reshape(D, D),
        gathered[3].reshape(D, HID),
        gathered[4].reshape(HID, D),
        gathered[5],
    )


def plain_forward(frames, masters):
    weights = collect(masters)
    entry, temporal, spatial, widen, narrow, affine = weights
    gains = affine.astype(jnp.float32)
    patchwise = lax.all_to_all(frames, "tok", split_axis=2, concat_axis=1, tiled=True)
    normed_t, unit_t, inverse_t = layer_norm(
        patchwise.astype(jnp.float32), gains[0, 0], gains[1, 0]
    )
    lowered_t = normed_t.astype(jnp.bfloat16)
    heads_t = split_heads(project(lowered_t, entry[0]))
    mixed_t, lse_t = attend_forward(heads_t, time_scores, time_mixed)
    first_t = project(mixed_t, temporal[0]).astype(jnp.bfloat16)
    branch = project(first_t, temporal[1]).astype(jnp.bfloat16)
    returned = lax.all_to_all(branch, "tok", split_axis=1, concat_axis=2, tiled=True)
    after_t = frames.astype(jnp.float32) + returned.astype(jnp.float32)
    normed_s, unit_s, inverse_s = layer_norm(after_t, gains[0, 1], gains[1, 1])
    lowered_s = normed_s.astype(jnp.bfloat16)
    heads_s = split_heads(project(lowered_s, entry[1]))
    mixed_s, lse_s = attend_forward(heads_s, space_scores, space_mixed)
    after_s = after_t + project(mixed_s, spatial)
    normed_m, unit_m, inverse_m = layer_norm(after_s, gains[0, 2], gains[1, 2])
    lowered_m = normed_m.astype(jnp.bfloat16)
    widened = project(lowered_m, widen)
    activated = jax.nn.gelu(widened, approximate=False).astype(jnp.bfloat16)
    result = (after_s + project(activated, narrow)).astype(jnp.bfloat16)
    saved = {
        "weights": weights,
        "unit_t": unit_t,
        "inverse_t": inverse_t,
        "lowered_t": lowered_t,
        "heads_t": heads_t,
        "lse_t": lse_t,
        "mixed_t": mixed_t,
        "first_t": first_t,
        "unit_s": unit_s,
        "inverse_s": inverse_s,
        "lowered_s": lowered_s,
        "heads_s": heads_s,
        "lse_s": lse_s,
        "mixed_s": mixed_s,
        "unit_m": unit_m,
        "inverse_m": inverse_m,
        "lowered_m": lowered_m,
        "widened": widened,
        "activated": activated,
    }
    return (result, saved)


def adamw(master, moment, square, grad, rate):
    fix = 1.0 - 0.5**STEP
    averaged = 0.5 * moment + 0.5 * grad
    squared = 0.5 * square + 0.5 * grad * grad
    updated = master - rate * (averaged / fix / (jnp.sqrt(squared / fix) + 1e-08) + 0.1 * master)
    return (updated, averaged, squared)

def on_any(
    frames,
    cotangent,
    entry_weights,
    entry_momentum,
    entry_variance,
    temporal_weights,
    temporal_momentum,
    temporal_variance,
    spatial_weights,
    spatial_momentum,
    spatial_variance,
    widen_weights,
    widen_momentum,
    widen_variance,
    narrow_weights,
    narrow_momentum,
    narrow_variance,
    norm_affine,
    affine_momentum,
    affine_variance,
):
    masters = (
        entry_weights,
        temporal_weights,
        spatial_weights,
        widen_weights,
        narrow_weights,
        norm_affine,
    )
    result, saved = plain_forward(frames, masters)
    entry, temporal, spatial, widen, narrow, affine = saved["weights"]
    gains = affine.astype(jnp.float32)
    narrow_grad = weight_sum(saved["activated"], cotangent)
    widened = saved["widened"]
    slope = (
        0.5 * (1.0 + lax.erf(widened * 0.7071067811865476))
        + widened * jnp.exp(-0.5 * widened * widened) * 0.3989422804014327
    )
    dwidened = (project_back(cotangent, narrow) * slope).astype(jnp.bfloat16)
    widen_grad = weight_sum(saved["lowered_m"], dwidened)
    dpart_m, gain_m, shift_m = norm_back(
        project_back(dwidened, widen), saved["unit_m"], saved["inverse_m"], gains[0, 2]
    )
    dafter_s = cotangent.astype(jnp.float32) + dpart_m
    dspatial = dafter_s.astype(jnp.bfloat16)
    spatial_grad = weight_sum(saved["mixed_s"], dspatial)
    dmixed_s = project_back(dspatial, spatial).astype(jnp.bfloat16)
    dfused_s = attend_backward(
        saved["heads_s"], saved["lse_s"], dmixed_s, space_scores, space_mixed, space_flip
    )
    entry_grad_s = weight_sum(saved["lowered_s"], dfused_s)
    dpart_s, gain_s, shift_s = norm_back(
        project_back(dfused_s, entry[1]), saved["unit_s"], saved["inverse_s"], gains[0, 1]
    )
    dafter_t = dafter_s + dpart_s
    dbranch = lax.all_to_all(
        dafter_t.astype(jnp.bfloat16), "tok", split_axis=2, concat_axis=1, tiled=True
    )
    temporal_grad_b = weight_sum(saved["first_t"], dbranch)
    dfirst = project_back(dbranch, temporal[1]).astype(jnp.bfloat16)
    temporal_grad_a = weight_sum(saved["mixed_t"], dfirst)
    dmixed_t = project_back(dfirst, temporal[0]).astype(jnp.bfloat16)
    dfused_t = attend_backward(
        saved["heads_t"], saved["lse_t"], dmixed_t, time_scores, time_mixed, time_flip
    )
    entry_grad_t = weight_sum(saved["lowered_t"], dfused_t)
    dsent, gain_t, shift_t = norm_back(
        project_back(dfused_t, entry[0]), saved["unit_t"], saved["inverse_t"], gains[0, 0]
    )
    dreturned = lax.all_to_all(
        dsent.astype(jnp.bfloat16), "tok", split_axis=1, concat_axis=2, tiled=True
    )
    input_gradient = dafter_t + dreturned.astype(jnp.float32)
    members = (
        jnp.stack([entry_grad_t, entry_grad_s]).reshape(-1, 128),
        jnp.stack([temporal_grad_a, temporal_grad_b]).reshape(-1, 128),
        spatial_grad.reshape(-1, 128),
        widen_grad.reshape(-1, 128),
        narrow_grad.reshape(-1, 128),
        jnp.stack([jnp.stack([gain_t, gain_s, gain_m]), jnp.stack([shift_t, shift_s, shift_m])]),
    )
    totals = (
        lax.psum_scatter(members[0], ("clip", "tok"), scatter_dimension=0, tiled=True),
        lax.psum_scatter(members[1], ("clip", "tok"), scatter_dimension=0, tiled=True),
        lax.psum_scatter(members[2], ("clip", "tok"), scatter_dimension=0, tiled=True),
        lax.psum_scatter(members[3], ("clip", "tok"), scatter_dimension=0, tiled=True),
        lax.psum_scatter(members[4], ("clip", "tok"), scatter_dimension=0, tiled=True),
        lax.psum_scatter(members[5], ("clip", "tok"), scatter_dimension=2, tiled=True),
    )
    entry_sum, temporal_sum, spatial_sum, widen_sum, narrow_sum, affine_sum = totals
    entry_new = adamw(entry_weights, entry_momentum, entry_variance, entry_sum, D ** (-0.5))
    temporal_new = adamw(
        temporal_weights, temporal_momentum, temporal_variance, temporal_sum, (D // 2) ** (-0.5)
    )
    spatial_new = adamw(
        spatial_weights,
        spatial_momentum,
        spatial_variance,
        spatial_sum,
        (3 * D // PATCHES) ** (-0.5),
    )
    widen_new = adamw(widen_weights, widen_momentum, widen_variance, widen_sum, D ** (-0.5))
    narrow_new = adamw(narrow_weights, narrow_momentum, narrow_variance, narrow_sum, HID ** (-0.5))
    affine_new = adamw(norm_affine, affine_momentum, affine_variance, affine_sum, 0.5)
    return (
        result,
        input_gradient,
        entry_new[0],
        entry_new[1],
        entry_new[2],
        temporal_new[0],
        temporal_new[1],
        temporal_new[2],
        spatial_new[0],
        spatial_new[1],
        spatial_new[2],
        widen_new[0],
        widen_new[1],
        widen_new[2],
        narrow_new[0],
        narrow_new[1],
        narrow_new[2],
        affine_new[0],
        affine_new[1],
        affine_new[2][:, 0:2],
        affine_new[2][:, 2],
    )

MESH = pl.DeviceIdType.MESH
TOK = 4
UNIT = 768
ROWS = (48, 48, 24, 24, 96)
WIDTHS = (2304, 768, 768, 3072, 768)
AFFINE = 5
EACH = 24
ORDER_IN = (5, 0, 1, 2, 3, 4)
ORDER_MLP = (4, 3, 2)
ORDER_REST = (0, 1, 5)
VMEM_LIMIT = 60 * 1024 * 1024


def units_of(order, unit=UNIT):
    units = []
    for k in order:
        if k == AFFINE:
            units.append((k, 0, 128))
        else:
            wide = unit if ROWS[k] < 96 or unit > UNIT else unit // 2
            units += [(k, c, min(wide, WIDTHS[k] - c)) for c in range(0, WIDTHS[k], wide)]
    return units


def spot():
    clip = lax.axis_index("clip")
    return clip // 4, (clip // 2) % 2, clip % 2, lax.axis_index("tok")


def clip_of(y, x, core):
    return (y * 2 + x) * 2 + core


def greet():
    y, x, core, t = spot()
    barrier = pltpu.get_barrier_semaphore()

    def tell(clip, tok):
        pl.semaphore_signal(barrier, inc=1, device_id=(clip, tok), device_id_type=MESH)

    tell(clip_of(y, x, 1 - core), t)
    tell(clip_of(y, 1 - x, core), t)
    tell(clip_of(1 - y, x, core), t)
    for far in range(1, TOK):
        tell(clip_of(y, x, core), (t + far) % TOK)
    pl.semaphore_wait(barrier, 3 + (TOK - 1))


class Flight:
    def __init__(self):
        self.started = []

    def go(self, copy, when=None):
        if when is None:
            copy.start()
        else:
            pl.when(when)(copy.start)
        self.started.append((copy, when))
        return copy

    def drain(self):
        for copy, when in self.started:
            if when is None:
                copy.wait_send()
            else:
                pl.when(when)(copy.wait_send)


def gather_steps(units, owned, full, sems):
    local, got, core_got, out_sem, z_sem = sems
    y, x, core, t = spot()
    here, by_x, by_y = clip_of(y, x, core), clip_of(y, 1 - x, core), clip_of(1 - y, x, core)
    mate = clip_of(y, x, 1 - core)
    corner_clip = clip_of(1 - y, 1 - x, core)
    local_copies = []

    def place(u, at):
        k, c, width = units[u]
        return full[k].at[at, :, pl.ds(c, width)]

    def send(u, at, to, tok=None, own=False, along_z=False, when=None):
        k, c, width = units[u]
        there = place(u, at)
        copy = pltpu.make_async_remote_copy(
            src_ref=owned[k].at[:, pl.ds(c, width)] if own else there,
            dst_ref=there,
            send_sem=(z_sem if along_z else out_sem).at[u],
            recv_sem=got.at[u, at],
            device_id=(to, t if tok is None else tok),
            device_id_type=MESH,
        )
        if when is None:
            copy.start()
        else:
            pl.when(when)(copy.start)

    def many(u, count):
        k, c, width = units[u]
        return full[k].at[pl.ds(0, count), :, pl.ds(c, width)]

    def took(u, count, sem):
        there = many(u, count)
        pltpu.make_async_copy(there, there, sem.at[u]).wait()

    def arrive(u, at):
        there = place(u, at)
        pltpu.make_async_copy(there, there, got.at[u, at]).wait()

    def spread(u, at, own=False, when=None):
        def both():
            send(u, at, by_x, own=own)
            send(u, at, by_y, own=own)

        if when is None:
            both()
        else:
            pl.when(when)(both)

    def begin(u):
        k, c, width = units[u]
        me = here * TOK + t
        copy = pltpu.make_async_copy(owned[k].at[:, pl.ds(c, width)], place(u, me), local.at[u])
        copy.start()
        local_copies.append(copy)
        send(u, me, here, t + 1, own=True, along_z=True, when=t < TOK - 1)
        send(u, me, here, t - 1, own=True, along_z=True, when=t > 0)
        spread(u, me, own=True)

    hops = [(far, way) for far in range(1, TOK) for way in (1, -1)]

    def guard(far, way):
        return t + far <= TOK - 1 if way == 1 else t - far >= 0

    def to_mate(u, clip):
        k, c, width = units[u]
        there = full[k].at[pl.ds(clip * TOK, TOK), :, pl.ds(c, width)]
        pltpu.make_async_remote_copy(
            src_ref=there,
            dst_ref=there,
            send_sem=out_sem.at[u],
            recv_sem=core_got.at[u],
            device_id=(mate, t),
            device_id_type=MESH,
        ).start()

    def along(u):
        for far, way in hops:
            at = here * TOK + t + far * way

            def passing(at=at, way=way):
                arrive(u, at)
                onward = t > 0 if way == 1 else t < TOK - 1
                send(u, at, here, t - way, along_z=True, when=onward)
                spread(u, at)

            pl.when(guard(far, way))(passing)
        local_copies[u].wait()
        to_mate(u, here)

    def crossing(u):
        for far in range(TOK):
            tok = (t + far) % TOK
            from_x, from_y = by_x * TOK + tok, by_y * TOK + tok
            arrive(u, from_x)
            if far % 2 == 1:
                send(u, from_x, by_y)
            arrive(u, from_y)
            if far % 2 == 0:
                send(u, from_y, by_x)
        to_mate(u, by_x)
        to_mate(u, by_y)

    def corner(u):
        for far in range(TOK):
            arrive(u, corner_clip * TOK + (t + far) % TOK)
        to_mate(u, corner_clip)

    def settle(u):
        took(u, 16, core_got)

    def drain():
        edge = jnp.logical_or(t == 0, t == TOK - 1)
        for u in range(len(units)):
            took(u, 28, out_sem)

        def wait_z(count):
            for u in range(len(units)):
                took(u, count, z_sem)

        pl.when(edge)(functools.partial(wait_z, 1))
        pl.when(jnp.logical_not(edge))(functools.partial(wait_z, 5))

    return begin, along, crossing, corner, settle, drain


def gather_sems(count):
    dma = pltpu.SemaphoreType.DMA
    return [
        dma((count,)),
        dma((count, 32)),
        dma((count,)),
        dma((count,)),
        dma((count,)),
    ]


def rows_from(flat, out):
    rows, n = out.shape[0], out.shape[1] // 128
    for c in range(n):
        out[:, c * 128 : (c + 1) * 128] = flat[pl.ds(c, rows, stride=n), :].astype(out.dtype)


def join_affine(blocks, out):
    lane = lax.broadcasted_iota(jnp.int32, (16, 128), 1)
    tiles = [jnp.zeros((16, 128), jnp.float32) for _ in range(6)]
    for i in range(32):
        block = jnp.where(lane < EACH, blocks[i].astype(jnp.float32), 0.0)
        tile, shift = (i * EACH) // 128, (i * EACH) % 128
        turned = pltpu.roll(block, shift, 1) if shift else block
        tiles[tile] = tiles[tile] + jnp.where(lane >= shift, turned, 0.0)
        if shift + EACH > 128:
            tiles[tile + 1] = tiles[tile + 1] + jnp.where(lane < shift, turned, 0.0)
    for i in range(6):
        out[:, i * 128 : (i + 1) * 128] = tiles[i]


def scatter_steps(units, parts, held, core_in, side_in, part_in, z_in, sems, flight, finals):
    load_sem, c_send, c_recv, d_send, d_recv, s_send, s_recv, z_send, z_recv = sems
    y, x, core, t = spot()
    here, by_x, by_y = clip_of(y, x, core), clip_of(y, 1 - x, core), clip_of(1 - y, x, core)
    mate = clip_of(y, x, 1 - core)
    homes = [(1 - y, 1 - x), (y, 1 - x), (1 - y, x), (y, x)]

    def cols(u):
        k, c, width = units[u]
        return pl.ds(c, width)

    def remote(src, dst, send_sem, recv_sem, to, tok=None):
        return pltpu.make_async_remote_copy(
            src_ref=src,
            dst_ref=dst,
            send_sem=send_sem,
            recv_sem=recv_sem,
            device_id=(to, t if tok is None else tok),
            device_id_type=MESH,
        )

    def load(u, g):
        k = units[u][0]
        ya, xa = homes[g]
        return pltpu.make_async_copy(
            parts[k].at[pl.ds(clip_of(ya, xa, core) * TOK, TOK), :, cols(u)],
            held[u].at[g],
            load_sem.at[u, g],
        )

    def to_mate(u, g):
        k = units[u][0]
        ya, xa = homes[g]
        return remote(
            parts[k].at[pl.ds(clip_of(ya, xa, 1 - core) * TOK, TOK), :, cols(u)],
            core_in[u].at[g],
            c_send.at[u, g],
            c_recv.at[u, g],
            mate,
        )

    def begin(u):
        for g in range(4):
            load(u, g).start()
            flight.go(to_mate(u, g))

    def ready(u, g):
        load(u, g).wait()
        to_mate(u, g).wait_recv()

    def add_into(u, g, lo, hi, pieces):
        def one(j, carry):
            total = up(held[u][g, j])
            for piece in pieces:
                total = total + up(piece[j])
            held[u][g, j] = low(total)
            return carry

        lax.fori_loop(lo, hi, one, 0)

    def first(u, half):
        return remote(
            held[u].at[0, pl.ds(2 * half, 2)],
            side_in[u].at[pl.ds(2 * half, 2)],
            d_send.at[u, half],
            d_recv.at[u, half],
            by_y if half else by_x,
        )

    def second(u, across):
        return remote(
            held[u].at[1 if across == 0 else 2],
            part_in[u].at[across],
            s_send.at[u, across],
            s_recv.at[u, across],
            by_x if across == 0 else by_y,
        )

    def last(u, far):
        tok = (t + far) % TOK
        return remote(
            held[u].at[3, tok],
            z_in[u].at[far - 1],
            z_send.at[u, far - 1],
            z_recv.at[u, far - 1],
            here,
            tok,
        )

    def step1(u):
        ready(u, 0)
        add_into(u, 0, 0, TOK, [core_in[u].at[0]])
        flight.go(first(u, 0))
        flight.go(first(u, 1))

    def step2(u):
        ready(u, 2)
        first(u, 0).wait_recv()
        add_into(u, 2, 0, 2, [core_in[u].at[2], side_in[u]])
        add_into(u, 2, 2, TOK, [core_in[u].at[2]])
        flight.go(second(u, 1))
        ready(u, 1)
        first(u, 1).wait_recv()
        add_into(u, 1, 0, 2, [core_in[u].at[1]])
        add_into(u, 1, 2, TOK, [core_in[u].at[1], side_in[u]])
        flight.go(second(u, 0))

    def step3(u):
        ready(u, 3)
        second(u, 0).wait_recv()
        second(u, 1).wait_recv()
        add_into(u, 3, 0, TOK, [core_in[u].at[3], part_in[u].at[0], part_in[u].at[1]])
        for far in range(1, TOK):
            flight.go(last(u, far))

    def step4(u):
        total = up(held[u][3, t])
        for far in range(1, TOK):
            last(u, far).wait_recv()
            total = total + up(z_in[u][far - 1])
        finals(u, total)

    return begin, step1, step2, step3, step4


def scatter_scratch(units):
    bf16 = jnp.bfloat16
    shapes = [(16 if k == AFFINE else ROWS[k], width) for k, c, width in units]
    held = [pltpu.VMEM((4, TOK) + s, bf16) for s in shapes]
    side = [pltpu.VMEM((TOK,) + s, bf16) for s in shapes]
    part = [pltpu.VMEM((2, TOK) + s, bf16) for s in shapes]
    last = [pltpu.VMEM((TOK - 1,) + s, bf16) for s in shapes]
    return held + held + side + part + last


def scatter_sems(count):
    dma = pltpu.SemaphoreType.DMA
    return [
        dma((count, 4)),
        dma((count, 4)),
        dma((count, 4)),
        dma((count, 2)),
        dma((count, 2)),
        dma((count, 2)),
        dma((count, 2)),
        dma((count, TOK - 1)),
        dma((count, TOK - 1)),
    ]


STEP_FIX = 1.0 - 0.5**STEP


def adamw_rows(rate, weights, moment, square, grad, out):
    averaged = 0.5 * moment + 0.5 * grad
    squared = 0.5 * square + 0.5 * grad * grad
    out[0][...] = weights - rate * (
        averaged / STEP_FIX / (jnp.sqrt(squared / STEP_FIX) + 1e-08) + 0.1 * weights
    )
    out[1][...] = averaged
    out[2][...] = squared


RATES = (768 ** (-0.5), 384 ** (-0.5), 11 ** (-0.5), 768 ** (-0.5), 3072 ** (-0.5))


def part_affine(norms, out):
    rows = [jnp.sum(n[0:8, :], axis=0, keepdims=True) for n in norms]
    rows += [jnp.sum(n[8:16, :], axis=0, keepdims=True) for n in norms]
    table = jnp.concatenate(rows + [jnp.zeros((10, 768), jnp.float32)], axis=0)
    lane = lax.broadcasted_iota(jnp.int32, (16, 128), 1)
    for i in range(32):
        tile, shift = (i * EACH) // 128, (i * EACH) % 128
        block = table[:, tile * 128 : (tile + 1) * 128]
        block = pltpu.roll(block, (128 - shift) % 128, 1) if shift else block
        if shift + EACH > 128:
            after = pltpu.roll(table[:, (tile + 1) * 128 : (tile + 2) * 128], 128 - shift, 1)
            block = jnp.where(lane < 128 - shift, block, after)
        out[i] = jnp.where(lane < EACH, block, 0.0).astype(jnp.bfloat16)

GROUPS = 7
T_ROWS = 448
S_PAD = 208
S_ROWS = 416
CHUNK = 768
MLP_CHUNK = 512
SCALE = HEAD_DIM ** (-0.5)
BIG = -1e30
NT = (((1,), (1,)), ((), ()))
TN = (((0,), (0,)), ((), ()))


def dot(left, right, dims=(((1,), (0,)), ((), ()))):
    return lax.dot_general(left, right, dims, preferred_element_type=jnp.float32)


def low(values):
    return values.astype(jnp.bfloat16)


def up(values):
    return values.astype(jnp.float32)


def center_rows(values):
    center = values - jnp.mean(values, axis=-1, keepdims=True)
    inverse = lax.rsqrt(jnp.mean(center * center, axis=-1, keepdims=True) + 1e-06)
    return center * inverse, inverse


def back_rows(upstream, unit, inverse, gain):
    scaled = upstream * gain
    inner = (
        scaled
        - jnp.mean(scaled, axis=-1, keepdims=True)
        - unit * jnp.mean(scaled * unit, axis=-1, keepdims=True)
    )
    return inner * inverse


def fold(values):
    return jnp.sum(values.reshape(-1, 8, values.shape[-1]), axis=0)


def columns(j, width):
    return pl.ds(pl.multiple_of(j * width, 128), width)


def rows_of(i, height):
    return pl.ds(pl.multiple_of(i * height, 8), height)


def times(out, left, weight, width=CHUNK):
    def step(j, carry):
        at = columns(j, width)
        out[:, at] = dot(left[...], weight[:, at]).astype(out.dtype)
        return carry

    lax.fori_loop(0, out.shape[1] // width, step, 0)


def lane_half(shape):
    return lax.broadcasted_iota(jnp.int32, shape, 1) < HEAD_DIM


def soft(query, keys, mask):
    scores = jnp.where(mask, dot(keys, query, NT), BIG)
    expo = jnp.exp(scores - jnp.max(scores, axis=0, keepdims=True))
    return expo * (1.0 / jnp.sum(expo, axis=0, keepdims=True))


def attend(query, keys, values, mask):
    half = lane_half(query.shape)
    zero = jnp.zeros_like(query)
    query = query * jnp.bfloat16(SCALE)
    first = dot(low(soft(jnp.where(half, query, zero), keys, mask)), values, TN)
    second = dot(low(soft(jnp.where(half, zero, query), keys, mask)), values, TN)
    return low(jnp.where(half, first, second))


def attend_back(query, keys, values, upstream, mask):
    half = lane_half(query.shape)
    zero = jnp.zeros_like(query)
    query = query * jnp.bfloat16(SCALE)
    scaled = keys * jnp.bfloat16(SCALE)

    def one(pick):
        probs = soft(pick(query, zero), keys, mask)
        dprobs = dot(values, pick(upstream, zero), NT)
        dscores = low(probs * (dprobs - jnp.sum(dprobs * probs, axis=0, keepdims=True)))
        return dot(dscores, scaled, TN), dot(dscores, query), dot(low(probs), upstream)

    first = one(lambda a, b: jnp.where(half, a, b))
    second = one(lambda a, b: jnp.where(half, b, a))
    return tuple(low(jnp.where(half, a, b)) for a, b in zip(first, second))


def frame_mask(size):
    patch = lambda axis: (lambda i: (i // 64) * 8 + i % 8)(
        lax.broadcasted_iota(jnp.int32, (size, size), axis)
    )
    return patch(0) == patch(1)


def patch_mask():
    return lax.broadcasted_iota(jnp.int32, (S_PAD, S_PAD), 0) < PATCHES


T_BLOCKS = ((0, 192), (192, 256))


def mlp_kernel(lowered, after_s, cotangent, widen, narrow, affine, result, d_narrow, d_widen, d_after, d_norm, cot, turned, total, back):
    j = pl.program_id(0)

    @pl.when(j == 0)
    def start():
        cot[...] = jnp.zeros_like(cot)
        for f in range(2):
            back[pl.ds(f * S_PAD, PATCHES), :] = up(cotangent[f])
            back[pl.ds(f * S_PAD + PATCHES, S_PAD - PATCHES), :] = jnp.zeros((S_PAD - PATCHES, D), jnp.float32)
        cot[...] = low(back[...])
        turned[...] = lowered[...].T
        total[...] = after_s[...]
        back[...] = jnp.zeros_like(back)

    wide = dot(lowered[...], widen[...])
    phi = 0.5 * (1.0 + lax.erf(wide * 0.7071067811865476))
    active = low(wide * phi)
    slope = phi + wide * jnp.exp(-0.5 * wide * wide) * 0.3989422804014327
    d_wide = low(dot(cot[...], narrow[...], NT) * slope)
    total[...] += dot(active, narrow[...])
    d_narrow[...] = low(dot(active, cot[...], TN))
    d_widen[...] = low(dot(turned[...], d_wide))
    back[...] += dot(d_wide, widen[...], NT)

    @pl.when(j == pl.num_programs(0) - 1)
    def finish():
        for f in range(2):
            result[f] = low(total[pl.ds(f * S_PAD, PATCHES), :])

        def norm(b, carry):
            rows = rows_of(b, 32)
            unit, inverse = center_rows(after_s[rows, :])
            upstream = back[rows, :]
            d_after[rows, :] = up(cot[rows, :]) + back_rows(upstream, unit, inverse, affine[2:3, :])
            return carry[0] + fold(upstream * unit), carry[1] + fold(upstream)

        zero = jnp.zeros((8, D), jnp.float32)
        gain, shift = lax.fori_loop(0, S_ROWS // 32, norm, (zero, zero))
        d_norm[0:8, :] = gain
        d_norm[8:16, :] = shift


def mlp(lowered, after_s, cotangent, widen, narrow, affine):
    whole = lambda shape: pl.BlockSpec(shape, lambda j: (0,) * len(shape))
    steps = HID // MLP_CHUNK
    return pl.pallas_call(
        mlp_kernel,
        grid=(steps,),
        in_specs=[
            whole((S_ROWS, D)),
            whole((S_ROWS, D)),
            whole((2, PATCHES, D)),
            pl.BlockSpec((D, MLP_CHUNK), lambda j: (0, j)),
            pl.BlockSpec((MLP_CHUNK, D), lambda j: (j, 0)),
            whole((16, D)),
        ],
        out_specs=[
            whole((2, PATCHES, D)),
            pl.BlockSpec((MLP_CHUNK, D), lambda j: (j, 0)),
            pl.BlockSpec((D, MLP_CHUNK), lambda j: (0, j)),
            whole((S_ROWS, D)),
            whole((16, D)),
        ],
        out_shape=[
            jax.ShapeDtypeStruct((2, PATCHES, D), jnp.bfloat16),
            jax.ShapeDtypeStruct((HID, D), jnp.bfloat16),
            jax.ShapeDtypeStruct((D, HID), jnp.bfloat16),
            jax.ShapeDtypeStruct((S_ROWS, D), jnp.float32),
            jax.ShapeDtypeStruct((16, D), jnp.float32),
        ],
        scratch_shapes=[
            pltpu.VMEM((S_ROWS, D), jnp.bfloat16),
            pltpu.VMEM((D, S_ROWS), jnp.bfloat16),
            pltpu.VMEM((S_ROWS, D), jnp.float32),
            pltpu.VMEM((S_ROWS, D), jnp.float32),
        ],
        compiler_params=pltpu.CompilerParams(vmem_limit_bytes=56 * 1024 * 1024),
        cost_estimate=pl.CostEstimate(flops=12000000000, bytes_accessed=30000000, transcendentals=0),
    )(lowered, after_s, cotangent, widen, narrow, affine)

def pack(box, rows):
    extra = [rows(f, 192, 4) for f in range(2)]
    line = lax.broadcasted_iota(jnp.int32, (16, D), 0)
    for s in range(TOK):
        wide = [rows(f, 48 * s, 48) for f in range(2)]
        for b in range(6):
            pair = [w[8 * b : 8 * b + 8, :] for w in wide]
            box[s, b] = low(jnp.concatenate(pair, axis=0))
        one = [jnp.broadcast_to(e[s : s + 1, :], (16, D)) for e in extra]
        box[s, 6] = low(jnp.where(line == 0, one[0], jnp.where(line == 8, one[1], 0.0)))


def unpack(box, f, put):
    for s in range(TOK):
        for b in range(6):
            slab = up(box[s, b])
            put(48 * s + 8 * b, 8, slab[8 * f : 8 * f + 8, :])
    last = [up(box[s, 6])[8 * f : 8 * f + 1, :] for s in range(TOK)]
    put(192, TOK, jnp.concatenate(last, axis=0))


class Exchange:
    def __init__(self, source, target, sems, flight):
        self.source, self.target, self.flight = source, target, flight
        self.local, self.sent, self.got = sems
        self.clip, self.t = lax.axis_index("clip"), lax.axis_index("tok")

    def copy(self, far):
        return pltpu.make_async_remote_copy(
            src_ref=self.source((self.t + far) % TOK),
            dst_ref=self.target(self.t),
            send_sem=self.sent.at[far - 1],
            recv_sem=self.got.at[far - 1],
            device_id=(self.clip, (self.t + far) % TOK),
            device_id_type=MESH,
        )

    def own(self):
        return pltpu.make_async_copy(self.source(self.t), self.target(self.t), self.local.at[0])

    def start(self):
        for far in range(1, TOK):
            self.flight.go(self.copy(far))
        self.own().start()

    def wait(self):
        for far in range(1, TOK):
            there = self.target((self.t - far + TOK) % TOK)
            pltpu.make_async_copy(there, there, self.got.at[far - 1]).wait()
        self.own().wait()


def exchange_sems():
    dma = pltpu.SemaphoreType.DMA
    return [dma((1,)), dma((TOK - 1,)), dma((TOK - 1,))]


def pieces(count, step, size):
    def run(lo, hi):
        def one(j, carry):
            step(j)
            return carry

        lax.fori_loop(lo, hi, one, 0)

    return [functools.partial(run, lo, min(lo + size, count)) for lo in range(0, count, size)]


def product(out, left, weight, width=CHUNK):
    def step(j):
        at = columns(j, width)
        out[:, at] = dot(left(), weight[:, at]).astype(out.dtype)

    return step


def product_back(out, left, weight, width=CHUNK):
    def step(j):
        at = columns(j, width)
        out[:, at] = dot(left(), weight[at, :], NT).astype(out.dtype)

    return step


def gradient(out, turned, upstream, width=CHUNK):
    def step(j):
        at = columns(j, width)
        out[:, at] = low(dot(turned[...], upstream(at)))

    return step


SUM_START = 6
SUM_RATE = 1.0
SUM_SHIFTS = (0, 1, 2, 3)


def spaced(compute, rest):
    done = 0
    for i, call in enumerate(compute):
        call()
        while done < len(rest) and SUM_START + done * SUM_RATE <= i + 1:
            rest[done]()
            done += 1
    for call in rest[done:]:
        call()


def full_kernel_steps(units, steps, shifts, lo, hi):
    calls = []
    for n in range(lo, hi):
        for shift, step in zip(shifts, steps):
            if 0 <= n - shift < len(units):
                calls.append(functools.partial(step, n - shift))
    return calls


A2A_AT = 10


def gather_head(units):
    count = len(units)
    last = [n for n in range(count) if units[n][0] == 1][-1]
    names = ("begin", "along", "crossing", "corner")
    calls = []
    for n in range(last + 3):
        calls += [(name, n - shift) for shift, name in enumerate(names) if 0 <= n - shift < count]
    return calls + [("begin", last + 3), ("along", last + 2), ("corner", last)]


def forward_kernel(units, *refs):
    masters, block, frames = refs[:5], refs[5], refs[6]
    full = list(refs[7:12])
    affine, patch, normed_t, merged_t, mixed_t, first_t = refs[12:18]
    after_t, normed_s, merged_s, mixed_s, after_s, lowered = refs[18:24]
    owned, gathered = list(refs[24:29]), refs[29]
    entry_w, temporal_w, spatial_w, outbox, sent, inbox, load_sem = refs[30:37]
    there_sems, back_sems = refs[37:40], refs[40:43]
    sems = refs[43:]
    greet()
    full.append(gathered)
    owned.append(block)
    flight = Flight()
    begin, along, crossing, corner, settle, drain = gather_steps(units, owned, full, sems)
    count = len(units)
    place = {k: [n for n in range(count) if units[n][0] == k] for k in range(6)}
    there = Exchange(lambda s: outbox.at[s], lambda s: patch.at[:, s], there_sems, flight)
    back = Exchange(lambda s: sent.at[:, s], lambda s: inbox.at[s], back_sems, flight)
    def settle_all(k):
        for n in place[k]:
            settle(n)

    ready = set()
    original = begin

    def begin(n):
        k = units[n][0]
        if k not in ready and k != AFFINE:
            rows_from(masters[k], owned[k])
            ready.add(k)
        original(n)

    steps = {"begin": begin, "along": along, "crossing": crossing, "corner": corner}
    head = [functools.partial(steps[name], n) for name, n in gather_head(units)]
    step = lambda name, n: [functools.partial(steps[name], n)]
    for call in head[:A2A_AT]:
        call()
    pack(outbox, lambda f, start, size: up(frames[f, start : start + size, :]))
    there.start()
    for call in head[A2A_AT:]:
        call()

    def load(part, source, target):
        return pltpu.make_async_copy(source, target, load_sem.at[part])

    loads = {
        "entry": load(0, full[0].at[pl.ds(0, 16)], entry_w),
        "temporal": load(1, full[1], temporal_w),
        "later": load(2, full[0].at[pl.ds(16, 16)], entry_w),
        "spatial": load(3, full[2], spatial_w),
    }
    settle_all(AFFINE)
    join_affine(gathered, affine)
    there.wait()

    def norm_t(b):
        unit, unused = center_rows(up(patch[b].reshape(64, D)))
        normed_t[rows_of(b, 64), :] = low(unit * affine[0:1, :] + affine[3:4, :])

    def heads_t(p):
        found = []
        for start, size in T_BLOCKS:
            rows = pl.ds(start, size)
            query, keys, values = (merged_t[rows, columns(p + 6 * i, 128)] for i in range(3))
            found.append(attend(query, keys, values, frame_mask(size)))
        for (start, size), value in zip(T_BLOCKS, found):
            mixed_t[pl.ds(start, size), columns(p, 128)] = value

    entry_m = lambda at: entry_w[:, :, at].reshape(D, CHUNK)

    def merge(out, left):
        def step(j):
            at = columns(j, CHUNK)
            out[:, at] = low(dot(left[...], entry_m(at)))

        return step

    def first_step(j):
        at = columns(j, CHUNK)
        first_t[:, at] = low(dot(mixed_t[...], temporal_w[0:16, :, at].reshape(D, CHUNK)))

    def branch_step(j):
        at = columns(j, CHUNK)
        value = low(dot(first_t[...], temporal_w[16:32, :, at].reshape(D, CHUNK)))
        sent[:, :, :, at] = value.reshape(GROUPS, TOK, 16, CHUNK)

    def start_temporal():
        settle_all(0)
        settle_all(1)
        loads["entry"].start()
        loads["temporal"].start()
        for call in pieces(GROUPS, norm_t, GROUPS):
            call()
        loads["entry"].wait()
        loads["temporal"].wait()

    def start_spatial():
        settle_all(2)
        loads["later"].start()
        loads["spatial"].start()
        back.wait()
        for f in range(2):

            def put(start, size, rows, f=f):
                after_t[f * S_PAD + start : f * S_PAD + start + size, :] = (
                    up(frames[f, start : start + size, :]) + rows
                )

            unpack(inbox, f, put)
            tail = f * S_PAD + PATCHES
            after_t[tail : (f + 1) * S_PAD, :] = jnp.zeros((S_PAD - PATCHES, D), jnp.float32)

    def norm_s(b):
        unit, unused = center_rows(after_t[rows_of(b, 32), :])
        normed_s[rows_of(b, 32), :] = low(unit * affine[1:2, :] + affine[4:5, :])

    def wait_spatial():
        loads["later"].wait()
        loads["spatial"].wait()

    def heads_s(p):
        found = []
        for f in range(2):
            rows = pl.ds(f * S_PAD, S_PAD)
            query, keys, values = (merged_s[rows, columns(p + 6 * i, 128)] for i in range(3))
            found.append(attend(query, keys, values, patch_mask()))
        for f in range(2):
            mixed_s[pl.ds(f * S_PAD, S_PAD), columns(p, 128)] = found[f]

    def out_s(j):
        at = columns(j, CHUNK)
        weight = low(up(spatial_w[:, :, at]).reshape(D, CHUNK))
        after_s[:, at] = after_t[:, at] + dot(mixed_s[...], weight)

    def norm_m(b):
        unit, unused = center_rows(after_s[rows_of(b, 32), :])
        lowered[rows_of(b, 32), :] = low(unit * affine[2:3, :] + affine[5:6, :])

    order = (
        [start_temporal]
        + step("crossing", 3)
        + pieces(3, merge(merged_t, normed_t), 1)
        + step("corner", 3)
        + step("along", 5)
        + pieces(6, heads_t, 2)
        + step("crossing", 4)
        + pieces(1, first_step, 1)
        + pieces(1, branch_step, 1)
        + [back.start]
        + step("corner", 4)
        + step("crossing", 5)
        + [start_spatial]
        + pieces(13, norm_s, 13)
        + [wait_spatial]
        + pieces(3, merge(merged_s, normed_s), 1)
        + pieces(6, heads_s, 3)
        + step("corner", 5)
        + pieces(1, out_s, 1)
        + pieces(13, norm_m, 13)
    )
    for call in order:
        call()
    for k in (3, 4):
        settle_all(k)
    drain()
    flight.drain()


def forward(masters, block, frames):
    units = units_of(ORDER_IN, HID)
    vmem = pl.BlockSpec(memory_space=pltpu.VMEM)
    anywhere = pl.BlockSpec(memory_space=pl.ANY)
    bf16, f32 = jnp.bfloat16, jnp.float32
    slab = (TOK, GROUPS, 16, D)
    group = (GROUPS, TOK, 16, D)
    saved = [
        ((16, D), f32),
        (group, bf16),
        ((T_ROWS, D), bf16),
        ((T_ROWS, 3 * D), bf16),
        ((T_ROWS, D), bf16),
        ((T_ROWS, D), bf16),
        ((S_ROWS, D), f32),
        ((S_ROWS, D), bf16),
        ((S_ROWS, 3 * D), bf16),
        ((S_ROWS, D), bf16),
        ((S_ROWS, D), f32),
        ((S_ROWS, D), bf16),
    ]
    return pl.pallas_call(
        functools.partial(forward_kernel, units),
        out_shape=[jax.ShapeDtypeStruct((32, r, w), bf16) for r, w in zip(ROWS, WIDTHS)]
        + [jax.ShapeDtypeStruct(s, t) for s, t in saved],
        in_specs=[vmem] * 7,
        out_specs=[anywhere] * 5 + [vmem] * 12,
        scratch_shapes=[pltpu.VMEM((r, w), bf16) for r, w in zip(ROWS, WIDTHS)]
        + [
            pltpu.VMEM((32, 16, 128), bf16),
            pltpu.VMEM((16, 48, 3 * D), bf16),
            pltpu.VMEM((32, 48, D), bf16),
            pltpu.VMEM((32, 24, D), bf16),
            pltpu.VMEM(slab, bf16),
            pltpu.VMEM(group, bf16),
            pltpu.VMEM(slab, bf16),
            pltpu.SemaphoreType.DMA((4,)),
        ]
        + exchange_sems()
        + exchange_sems()
        + gather_sems(len(units)),
        compiler_params=pltpu.CompilerParams(
            collective_id=0, has_side_effects=True, vmem_limit_bytes=VMEM_LIMIT
        ),
    )(*masters, block, frames)


def finals_of(grads, affine_out=None):
    def finals(unit, total):
        k, c, width = unit
        if k == AFFINE:
            affine_out[...] = total
            return
        n, rows = WIDTHS[k] // 128, ROWS[k]
        for i in range(width // 128):
            grads[k][pl.ds(c // 128 + i, rows, stride=n), :] = total[:, i * 128 : (i + 1) * 128]

    return finals


def back_kernel(units, *refs):
    parts = dict(zip((3, 4), refs[:2]))
    d_after_s, after_t, affine, spatial = refs[2:6]
    normed_s_in, merged_s_in, mixed_s_in, entry_in = refs[6:10]
    patch_in, normed_t_in, merged_t_in, mixed_t_in, first_t_in, temporal_in = refs[10:16]
    grads = dict(zip((2, 3, 4), refs[16:19]))
    sent, d_after_t, d_entry_out, d_temporal, norm_s_out, norm_t_out = refs[19:25]
    pos = 25
    pools = []
    for i in range(5):
        pools.append(refs[pos : pos + len(units)])
        pos += len(units)
    parts[2] = refs[pos]
    pos += 1
    normed_s, merged_s, mixed_s, entry_w = refs[pos : pos + 4]
    patch, normed_t, merged_t, mixed_t, first_t, temporal_w = refs[pos + 4 : pos + 10]
    d_entry, lowered, d_mixed, d_first, d_merged, turned_s, turned_t, back, outbox, grouped, load_sem = refs[
        pos + 10 : pos + 21
    ]
    pos += 21
    there_sems = refs[pos : pos + 3]
    sems = refs[pos + 3 :]
    sources = (normed_s_in, merged_s_in, mixed_s_in, entry_in.at[1])
    targets = (normed_s, merged_s, mixed_s, entry_w)
    sources += (patch_in, normed_t_in, merged_t_in, mixed_t_in, first_t_in, temporal_in)
    targets += (patch, normed_t, merged_t, mixed_t, first_t, temporal_w)
    loads = [pltpu.make_async_copy(a, b, load_sem.at[i]) for i, (a, b) in enumerate(zip(sources, targets))]
    for copy in loads:
        copy.start()
    entry_load = pltpu.make_async_copy(entry_in.at[0], entry_w, load_sem.at[10])
    entry_stores = [pltpu.make_async_copy(d_entry, d_entry_out.at[i], load_sem.at[12 - i]) for i in range(2)]
    greet()
    flight = Flight()
    finals = finals_of(grads)
    steps = scatter_steps(
        units, parts, *pools, sems, flight, lambda u, total: finals(units[u], total)
    )
    there = Exchange(lambda s: outbox.at[s], lambda s: grouped.at[:, s], there_sems, flight)
    zero = jnp.zeros((8, D), jnp.float32)

    def begin_s():
        lowered[...] = low(d_after_s[...])
        for copy in loads[:3]:
            copy.wait()
        turned_s[...] = mixed_s[...].T

    def turn_s():
        turned_s[...] = normed_s[...].T

    def heads_s(p):
        found = []
        for f in range(2):
            rows = pl.ds(f * S_PAD, S_PAD)
            query, keys, values = (merged_s[rows, columns(p + 6 * i, 128)] for i in range(3))
            found.append(
                attend_back(query, keys, values, d_mixed[rows, columns(p, 128)], patch_mask())
            )
        for f in range(2):
            for i in range(3):
                d_merged[pl.ds(f * S_PAD, S_PAD), columns(p + 6 * i, 128)] = found[f][i]

    def s_back(j):
        at = columns(j, CHUNK)
        back[0:S_ROWS, at] = dot(d_merged[0:S_ROWS, :], entry_w[at, :], NT)

    def end_s():
        entry_load.start()

        def norm(b, carry):
            rows = rows_of(b, 32)
            unit, inverse = center_rows(after_t[rows, :])
            upstream = back[rows, :]
            d_after_t[rows, :] = d_after_s[rows, :] + back_rows(upstream, unit, inverse, affine[1:2, :])
            return carry[0] + fold(upstream * unit), carry[1] + fold(upstream)

        gain, shift = lax.fori_loop(0, S_ROWS // 32, norm, (zero, zero))
        norm_s_out[0:8, :] = gain
        norm_s_out[8:16, :] = shift
        pack(outbox, lambda f, start, size: d_after_t[f * S_PAD + start : f * S_PAD + start + size, :])
        there.start()

    def wait_entry():
        loads[3].wait()

    def spatial_sum():
        parts[2][...] = low(dot(turned_s[...], lowered[...]).reshape(32, 24, D))
        steps[0](len(units) - 1)

    d_mixed_s = d_mixed.at[0:S_ROWS]
    compute = (
        [begin_s]
        + [spatial_sum]
        + pieces(1, product_back(d_mixed_s, lambda: lowered[...], spatial), 1)
        + [turn_s]
        + pieces(6, heads_s, 1)
        + [wait_entry]
        + pieces(1, s_back, 1)
        + [end_s]
        + pieces(3, gradient(d_entry, turned_s, lambda at: d_merged[0:S_ROWS, at]), 1)
        + [entry_stores[1].start]
    )

    def begin_t():
        for copy in loads[4:]:
            copy.wait()
        turned_t[...] = first_t[...].T
        there.wait()

    group_cols = lambda at: grouped[:, :, :, at].reshape(T_ROWS, CHUNK)

    def turn_mixed():
        turned_t[...] = mixed_t[...].T

    def turn_normed():
        turned_t[...] = normed_t[...].T

    def heads_t(p):
        found = []
        for start, size in T_BLOCKS:
            rows = pl.ds(start, size)
            query, keys, values = (merged_t[rows, columns(p + 6 * i, 128)] for i in range(3))
            found.append(
                attend_back(query, keys, values, d_mixed[rows, columns(p, 128)], frame_mask(size))
            )
        for (start, size), values in zip(T_BLOCKS, found):
            for i in range(3):
                d_merged[pl.ds(start, size), columns(p + 6 * i, 128)] = values[i]

    def t_back(j):
        at = columns(j, CHUNK)
        back[:, at] = dot(d_merged[...], entry_w[at, :], NT)

    def end_t():
        def norm(b, carry):
            rows = rows_of(b, 64)
            unit, inverse = center_rows(up(patch[b].reshape(64, D)))
            upstream = back[rows, :]
            value = back_rows(upstream, unit, inverse, affine[0:1, :])
            sent[b] = low(value).reshape(TOK, 16, D)
            return carry[0] + fold(upstream * unit), carry[1] + fold(upstream)

        gain, shift = lax.fori_loop(0, GROUPS, norm, (zero, zero))
        norm_t_out[0:8, :] = gain
        norm_t_out[8:16, :] = shift

    def free_entry():
        entry_stores[1].wait()
        entry_load.wait()

    compute += (
        [begin_t]
        + pieces(1, gradient(d_temporal.at[1], turned_t, group_cols), 1)
        + pieces(1, product_back(d_first, lambda: grouped[...].reshape(T_ROWS, D), temporal_w.at[1]), 1)
        + [turn_mixed]
        + pieces(1, gradient(d_temporal.at[0], turned_t, lambda at: d_first[:, at]), 1)
        + pieces(1, product_back(d_mixed, lambda: d_first[...], temporal_w.at[0]), 1)
        + [turn_normed]
        + pieces(6, heads_t, 1)
        + [free_entry]
        + pieces(1, t_back, 1)
        + [end_t]
        + pieces(3, gradient(d_entry, turned_t, lambda at: d_merged[:, at]), 1)
        + [entry_stores[0].start]
    )
    for u in range(len(units) - 1):
        steps[0](u)
    rest = full_kernel_steps(units, steps[1:], SUM_SHIFTS, 0, len(units) + SUM_SHIFTS[-1])
    spaced(compute, rest)
    entry_stores[0].wait()
    flight.drain()


def backward(parts, d_after_s, after_t, affine, spatial, entry, temporal, saved_s, saved_t):
    units = units_of(ORDER_MLP)
    vmem = pl.BlockSpec(memory_space=pltpu.VMEM)
    anywhere = pl.BlockSpec(memory_space=pl.ANY)
    bf16, f32 = jnp.bfloat16, jnp.float32
    flat = [(ROWS[k] * WIDTHS[k] // 128, 128) for k in (2, 3, 4)]
    slab = (TOK, GROUPS, 16, D)
    group = (GROUPS, TOK, 16, D)
    outs = [(s, f32) for s in flat] + [
        (group, bf16),
        ((S_ROWS, D), f32),
        ((2, D, 3 * D), bf16),
        ((2, D, D), bf16),
        ((16, D), f32),
        ((16, D), f32),
    ]
    return pl.pallas_call(
        functools.partial(back_kernel, units),
        out_shape=[jax.ShapeDtypeStruct(s, t) for s, t in outs],
        in_specs=[anywhere] * 2 + [vmem] * 4 + [anywhere] * 10,
        out_specs=[vmem] * 5 + [anywhere] + [vmem] * 3,
        scratch_shapes=scatter_scratch(units)
        + [
            pltpu.VMEM((32, 24, D), bf16),
            pltpu.VMEM((S_ROWS, D), bf16),
            pltpu.VMEM((S_ROWS, 3 * D), bf16),
            pltpu.VMEM((S_ROWS, D), bf16),
            pltpu.VMEM((D, 3 * D), bf16),
            pltpu.VMEM(group, bf16),
            pltpu.VMEM((T_ROWS, D), bf16),
            pltpu.VMEM((T_ROWS, 3 * D), bf16),
            pltpu.VMEM((T_ROWS, D), bf16),
            pltpu.VMEM((T_ROWS, D), bf16),
            pltpu.VMEM((2, D, D), bf16),
            pltpu.VMEM((D, 3 * D), bf16),
            pltpu.VMEM((S_ROWS, D), bf16),
            pltpu.VMEM((T_ROWS, D), bf16),
            pltpu.VMEM((T_ROWS, D), bf16),
            pltpu.VMEM((T_ROWS, 3 * D), bf16),
            pltpu.VMEM((D, S_ROWS), bf16),
            pltpu.VMEM((D, T_ROWS), bf16),
            pltpu.VMEM((T_ROWS, D), f32),
            pltpu.VMEM(slab, bf16),
            pltpu.VMEM(group, bf16),
            pltpu.SemaphoreType.DMA((13,)),
        ]
        + exchange_sems()
        + scatter_sems(len(units)),
        compiler_params=pltpu.CompilerParams(
            collective_id=1, has_side_effects=True, vmem_limit_bytes=VMEM_LIMIT
        ),
    )(*parts, d_after_s, after_t, affine, spatial, *saved_s, entry, *saved_t, temporal)


HOME_AT = 4
HOME_END = 24


def rest_kernel(units, *refs):
    parts = dict(zip((0, 1), refs[:2]))
    norms = refs[2:5]
    sent, d_after_t = refs[5:7]
    grads = dict(zip((0, 1), refs[7:9]))
    affine_out, input_gradient = refs[9:11]
    pos = 11
    pools = []
    for i in range(5):
        pools.append(refs[pos : pos + len(units)])
        pos += len(units)
    parts[AFFINE] = refs[pos]
    inbox, home_sems = refs[pos + 1], refs[pos + 2 : pos + 5]
    sems = refs[pos + 5 :]
    greet()
    flight = Flight()
    home = Exchange(lambda s: sent.at[:, s], lambda s: inbox.at[s], home_sems, flight)
    finals = finals_of(grads, affine_out)
    steps = scatter_steps(
        units, parts, *pools, sems, flight, lambda u, total: finals(units[u], total)
    )
    begin = steps[0]

    def begin_after(u):
        if units[u][0] == AFFINE:
            part_affine(norms, parts[AFFINE])
        begin(u)

    def receive():
        home.wait()
        for f in range(2):

            def put(start, size, rows, f=f):
                at = f * S_PAD + start
                input_gradient[f, start : start + size, :] = d_after_t[at : at + size, :] + rows

            unpack(inbox, f, put)

    calls = full_kernel_steps(units, (begin_after,) + steps[1:], (0, 2, 3, 4, 5), 0, len(units) + 5)
    calls.insert(HOME_AT, home.start)
    calls.insert(HOME_END, receive)
    for call in calls:
        call()
    flight.drain()


def scatter_rest(parts, norms, sent, d_after_t):
    units = units_of(ORDER_REST)
    vmem = pl.BlockSpec(memory_space=pltpu.VMEM)
    flat = [(ROWS[k] * WIDTHS[k] // 128, 128) for k in (0, 1)]
    return pl.pallas_call(
        functools.partial(rest_kernel, units),
        out_shape=[jax.ShapeDtypeStruct(s, jnp.float32) for s in flat]
        + [
            jax.ShapeDtypeStruct((16, 128), jnp.float32),
            jax.ShapeDtypeStruct((2, PATCHES, D), jnp.float32),
        ],
        in_specs=[pl.BlockSpec(memory_space=pl.ANY)] * 2 + [vmem] * 5,
        out_specs=[vmem] * 4,
        scratch_shapes=scatter_scratch(units)
        + [pltpu.VMEM((32, 16, 128), jnp.bfloat16)]
        + [pltpu.VMEM((TOK, GROUPS, 16, D), jnp.bfloat16)]
        + exchange_sems()
        + scatter_sems(len(units)),
        compiler_params=pltpu.CompilerParams(
            collective_id=2, has_side_effects=True, vmem_limit_bytes=VMEM_LIMIT
        ),
    )(*parts, *norms, sent, d_after_t)


def update_kernel(*refs):
    for k in range(5):
        weights, moment, square = (refs[5 + 3 * k + i][...] for i in range(3))
        adamw_rows(RATES[k], weights, moment, square, refs[k][...], refs[20 + 3 * k : 23 + 3 * k])


def update(grads, states):
    steps = 6
    blocks = [pl.BlockSpec((g.shape[0] // steps, 128), lambda i: (i, 0)) for g in grads]
    triples = [b for b in blocks for _ in range(3)]
    return pl.pallas_call(
        update_kernel,
        grid=(steps,),
        out_shape=[jax.ShapeDtypeStruct(s.shape, jnp.float32) for s in states],
        in_specs=blocks + triples,
        out_specs=triples,
    )(*grads, *states)


def on_device(
    frames,
    cotangent,
    entry_weights,
    entry_momentum,
    entry_variance,
    temporal_weights,
    temporal_momentum,
    temporal_variance,
    spatial_weights,
    spatial_momentum,
    spatial_variance,
    widen_weights,
    widen_momentum,
    widen_variance,
    narrow_weights,
    narrow_momentum,
    narrow_variance,
    norm_affine,
    affine_momentum,
    affine_variance,
):
    masters = (entry_weights, temporal_weights, spatial_weights, widen_weights, narrow_weights)
    block = jnp.pad(low(norm_affine).reshape(6, EACH), ((0, 10), (0, 128 - EACH)))
    found = forward(masters, block, frames[0])
    entry, temporal, spatial, widen, narrow = found[:5]
    entry = entry.reshape(2, D, 3 * D)
    temporal = temporal.reshape(2, D, D)
    spatial = spatial.reshape(D, D)
    widen = widen.reshape(D, HID)
    narrow = narrow.reshape(HID, D)
    affine, patch, normed_t, merged_t, mixed_t, first_t = found[5:11]
    after_t, normed_s, merged_s, mixed_s, after_s, lowered = found[11:17]
    result, narrow_grad, widen_grad, d_after_s, norm_m = mlp(
        lowered, after_s, cotangent[0], widen, narrow, affine
    )
    found = backward(
        (widen_grad.reshape(32, -1, HID), narrow_grad.reshape(32, -1, D)),
        d_after_s,
        after_t,
        affine,
        spatial,
        entry,
        temporal,
        (normed_s, merged_s, mixed_s),
        (patch, normed_t, merged_t, mixed_t, first_t),
    )
    spatial_sum, widen_sum, narrow_sum = found[:3]
    sent, d_after_t, d_entry, d_temporal, norm_s, norm_t = found[3:9]
    entry_sum, temporal_sum, affine_sum, input_gradient = scatter_rest(
        (d_entry.reshape(32, -1, 3 * D), d_temporal.reshape(32, -1, D)),
        (norm_t, norm_s, norm_m),
        sent,
        d_after_t,
    )
    updated = update(
        (entry_sum, temporal_sum, spatial_sum, widen_sum, narrow_sum),
        (
            entry_weights,
            entry_momentum,
            entry_variance,
            temporal_weights,
            temporal_momentum,
            temporal_variance,
            spatial_weights,
            spatial_momentum,
            spatial_variance,
            widen_weights,
            widen_momentum,
            widen_variance,
            narrow_weights,
            narrow_momentum,
            narrow_variance,
        ),
    )
    affine_sum = affine_sum[:6, :EACH].reshape(2, 3, EACH)
    affine_new = adamw(norm_affine, affine_momentum, affine_variance, affine_sum, 0.5)
    return (
        result[None],
        input_gradient[None],
        *updated,
        affine_new[0],
        affine_new[1],
        affine_new[2][:, 0:2],
        affine_new[2][:, 2],
    )

def solution(mesh):
    return jax.shard_map(
        on_device if mesh.shape["clip"] == 8 and mesh.shape["tok"] == TOK else on_any,
        mesh=mesh,
        in_specs=(
            P("clip", "tok", None, None),
            P("clip", "tok", None, None),
            P(("clip", "tok"), None),
            P(("clip", "tok"), None),
            P(("clip", "tok"), None),
            P(("clip", "tok"), None),
            P(("clip", "tok"), None),
            P(("clip", "tok"), None),
            P(("clip", "tok"), None),
            P(("clip", "tok"), None),
            P(("clip", "tok"), None),
            P(("clip", "tok"), None),
            P(("clip", "tok"), None),
            P(("clip", "tok"), None),
            P(("clip", "tok"), None),
            P(("clip", "tok"), None),
            P(("clip", "tok"), None),
            P(None, None, ("clip", "tok")),
            P(None, None, ("clip", "tok")),
            P(None, None, ("clip", "tok")),
        ),
        out_specs=(
            P("clip", "tok", None, None),
            P("clip", "tok", None, None),
            P(("clip", "tok"), None),
            P(("clip", "tok"), None),
            P(("clip", "tok"), None),
            P(("clip", "tok"), None),
            P(("clip", "tok"), None),
            P(("clip", "tok"), None),
            P(("clip", "tok"), None),
            P(("clip", "tok"), None),
            P(("clip", "tok"), None),
            P(("clip", "tok"), None),
            P(("clip", "tok"), None),
            P(("clip", "tok"), None),
            P(("clip", "tok"), None),
            P(("clip", "tok"), None),
            P(("clip", "tok"), None),
            P(None, None, ("clip", "tok")),
            P(None, None, ("clip", "tok")),
            P(None, None, ("clip", "tok")),
            P(None, ("clip", "tok")),
        ),
        check_vma=False,
    )
```

```python
import functools

import jax
import jax.numpy as jnp
from jax import lax
from jax.experimental import pallas as pl
from jax.experimental.pallas import tpu as pltpu
from jax.sharding import PartitionSpec as P

D = 768
HEADS = 12
HEAD_DIM = 64
HID = 3072
PATCHES = 196
STEP = 5

time_scores = "cfphe,cgphe->cphfg"
time_mixed = "cphfg,cgphe->cfphe"
time_flip = "cphfg,cfphe->cgphe"
space_scores = "cfphe,cfqhe->cfhpq"
space_mixed = "cfhpq,cfqhe->cfphe"
space_flip = "cfhpq,cfphe->cfqhe"


def project(inputs, weight):
    return jnp.einsum("cfpa,ab->cfpb", inputs, weight, preferred_element_type=jnp.float32)


def project_back(upstream, weight):
    return jnp.einsum("cfpb,ab->cfpa", upstream, weight, preferred_element_type=jnp.float32)


def weight_sum(inputs, upstream):
    return jnp.einsum("cfpa,cfpb->ab", inputs, upstream, preferred_element_type=jnp.float32)


def layer_norm(values, gain, shift):
    center = values - jnp.mean(values, axis=-1, keepdims=True)
    inverse = lax.rsqrt(jnp.mean(center * center, axis=-1, keepdims=True) + 1e-06)
    unit = center * inverse
    return (unit * gain + shift, unit, inverse)


def norm_back(upstream, unit, inverse, gain):
    scaled = upstream * gain
    inner = (
        scaled
        - jnp.mean(scaled, axis=-1, keepdims=True)
        - unit * jnp.mean(scaled * unit, axis=-1, keepdims=True)
    )
    return (
        inner * inverse,
        jnp.sum(upstream * unit, axis=(0, 1, 2)),
        jnp.sum(upstream, axis=(0, 1, 2)),
    )


def split_heads(merged):
    lowered = merged.astype(jnp.bfloat16)
    parts = lowered.reshape(lowered.shape[:-1] + (3, HEADS, HEAD_DIM))
    return (parts[..., 0, :, :], parts[..., 1, :, :], parts[..., 2, :, :])


def attend_forward(heads, score_form, mixed_form):
    query, keys, values = heads
    scores = jnp.einsum(score_form, query, keys, preferred_element_type=jnp.float32) * HEAD_DIM ** (
        -0.5
    )
    top = jnp.max(scores, axis=-1, keepdims=True)
    expo = jnp.exp(scores - top)
    total = jnp.sum(expo, axis=-1, keepdims=True)
    probs = (expo / total).astype(jnp.bfloat16)
    mixed = jnp.einsum(mixed_form, probs, values, preferred_element_type=jnp.float32)
    joined = mixed.reshape(mixed.shape[:-2] + (HEADS * HEAD_DIM,)).astype(jnp.bfloat16)
    return (joined, top + jnp.log(total))


def attend_backward(heads, logsum, upstream_joined, score_form, mixed_form, flip_form):
    query, keys, values = heads
    upstream = upstream_joined.reshape(upstream_joined.shape[:-1] + (HEADS, HEAD_DIM))
    scale = HEAD_DIM ** (-0.5)
    scores = jnp.einsum(score_form, query, keys, preferred_element_type=jnp.float32) * scale
    probs = jnp.exp(scores - logsum)
    dprobs = jnp.einsum(score_form, upstream, values, preferred_element_type=jnp.float32)
    dscores = (probs * (dprobs - jnp.sum(dprobs * probs, axis=-1, keepdims=True))).astype(
        jnp.bfloat16
    )
    dquery = jnp.einsum(mixed_form, dscores, keys, preferred_element_type=jnp.float32) * scale
    dkeys = jnp.einsum(flip_form, dscores, query, preferred_element_type=jnp.float32) * scale
    dvalues = jnp.einsum(
        flip_form, probs.astype(jnp.bfloat16), upstream, preferred_element_type=jnp.float32
    )
    stacked = jnp.stack([dquery, dkeys, dvalues], axis=-3)
    return stacked.reshape(stacked.shape[:-3] + (3 * HEADS * HEAD_DIM,)).astype(jnp.bfloat16)


def collect(masters):
    gathered = (
        lax.all_gather(masters[0].astype(jnp.bfloat16), ("clip", "tok"), axis=0, tiled=True),
        lax.all_gather(masters[1].astype(jnp.bfloat16), ("clip", "tok"), axis=0, tiled=True),
        lax.all_gather(masters[2].astype(jnp.bfloat16), ("clip", "tok"), axis=0, tiled=True),
        lax.all_gather(masters[3].astype(jnp.bfloat16), ("clip", "tok"), axis=0, tiled=True),
        lax.all_gather(masters[4].astype(jnp.bfloat16), ("clip", "tok"), axis=0, tiled=True),
        lax.all_gather(masters[5].astype(jnp.bfloat16), ("clip", "tok"), axis=2, tiled=True),
    )
    return (
        gathered[0].reshape(2, D, 3 * D),
        gathered[1].reshape(2, D, D),
        gathered[2].reshape(D, D),
        gathered[3].reshape(D, HID),
        gathered[4].reshape(HID, D),
        gathered[5],
    )


def plain_forward(frames, masters):
    weights = collect(masters)
    entry, temporal, spatial, widen, narrow, affine = weights
    gains = affine.astype(jnp.float32)
    patchwise = lax.all_to_all(frames, "tok", split_axis=2, concat_axis=1, tiled=True)
    normed_t, unit_t, inverse_t = layer_norm(
        patchwise.astype(jnp.float32), gains[0, 0], gains[1, 0]
    )
    lowered_t = normed_t.astype(jnp.bfloat16)
    heads_t = split_heads(project(lowered_t, entry[0]))
    mixed_t, lse_t = attend_forward(heads_t, time_scores, time_mixed)
    first_t = project(mixed_t, temporal[0]).astype(jnp.bfloat16)
    branch = project(first_t, temporal[1]).astype(jnp.bfloat16)
    returned = lax.all_to_all(branch, "tok", split_axis=1, concat_axis=2, tiled=True)
    after_t = frames.astype(jnp.float32) + returned.astype(jnp.float32)
    normed_s, unit_s, inverse_s = layer_norm(after_t, gains[0, 1], gains[1, 1])
    lowered_s = normed_s.astype(jnp.bfloat16)
    heads_s = split_heads(project(lowered_s, entry[1]))
    mixed_s, lse_s = attend_forward(heads_s, space_scores, space_mixed)
    after_s = after_t + project(mixed_s, spatial)
    normed_m, unit_m, inverse_m = layer_norm(after_s, gains[0, 2], gains[1, 2])
    lowered_m = normed_m.astype(jnp.bfloat16)
    widened = project(lowered_m, widen)
    activated = jax.nn.gelu(widened, approximate=False).astype(jnp.bfloat16)
    result = (after_s + project(activated, narrow)).astype(jnp.bfloat16)
    saved = {
        "weights": weights,
        "unit_t": unit_t,
        "inverse_t": inverse_t,
        "lowered_t": lowered_t,
        "heads_t": heads_t,
        "lse_t": lse_t,
        "mixed_t": mixed_t,
        "first_t": first_t,
        "unit_s": unit_s,
        "inverse_s": inverse_s,
        "lowered_s": lowered_s,
        "heads_s": heads_s,
        "lse_s": lse_s,
        "mixed_s": mixed_s,
        "unit_m": unit_m,
        "inverse_m": inverse_m,
        "lowered_m": lowered_m,
        "widened": widened,
        "activated": activated,
    }
    return (result, saved)


def adamw(master, moment, square, grad, rate):
    fix = 1.0 - 0.5**STEP
    averaged = 0.5 * moment + 0.5 * grad
    squared = 0.5 * square + 0.5 * grad * grad
    updated = master - rate * (averaged / fix / (jnp.sqrt(squared / fix) + 1e-08) + 0.1 * master)
    return (updated, averaged, squared)

def on_any(
    frames,
    cotangent,
    entry_weights,
    entry_momentum,
    entry_variance,
    temporal_weights,
    temporal_momentum,
    temporal_variance,
    spatial_weights,
    spatial_momentum,
    spatial_variance,
    widen_weights,
    widen_momentum,
    widen_variance,
    narrow_weights,
    narrow_momentum,
    narrow_variance,
    norm_affine,
    affine_momentum,
    affine_variance,
):
    masters = (
        entry_weights,
        temporal_weights,
        spatial_weights,
        widen_weights,
        narrow_weights,
        norm_affine,
    )
    result, saved = plain_forward(frames, masters)
    entry, temporal, spatial, widen, narrow, affine = saved["weights"]
    gains = affine.astype(jnp.float32)
    narrow_grad = weight_sum(saved["activated"], cotangent)
    widened = saved["widened"]
    slope = (
        0.5 * (1.0 + lax.erf(widened * 0.7071067811865476))
        + widened * jnp.exp(-0.5 * widened * widened) * 0.3989422804014327
    )
    dwidened = (project_back(cotangent, narrow) * slope).astype(jnp.bfloat16)
    widen_grad = weight_sum(saved["lowered_m"], dwidened)
    dpart_m, gain_m, shift_m = norm_back(
        project_back(dwidened, widen), saved["unit_m"], saved["inverse_m"], gains[0, 2]
    )
    dafter_s = cotangent.astype(jnp.float32) + dpart_m
    dspatial = dafter_s.astype(jnp.bfloat16)
    spatial_grad = weight_sum(saved["mixed_s"], dspatial)
    dmixed_s = project_back(dspatial, spatial).astype(jnp.bfloat16)
    dfused_s = attend_backward(
        saved["heads_s"], saved["lse_s"], dmixed_s, space_scores, space_mixed, space_flip
    )
    entry_grad_s = weight_sum(saved["lowered_s"], dfused_s)
    dpart_s, gain_s, shift_s = norm_back(
        project_back(dfused_s, entry[1]), saved["unit_s"], saved["inverse_s"], gains[0, 1]
    )
    dafter_t = dafter_s + dpart_s
    dbranch = lax.all_to_all(
        dafter_t.astype(jnp.bfloat16), "tok", split_axis=2, concat_axis=1, tiled=True
    )
    temporal_grad_b = weight_sum(saved["first_t"], dbranch)
    dfirst = project_back(dbranch, temporal[1]).astype(jnp.bfloat16)
    temporal_grad_a = weight_sum(saved["mixed_t"], dfirst)
    dmixed_t = project_back(dfirst, temporal[0]).astype(jnp.bfloat16)
    dfused_t = attend_backward(
        saved["heads_t"], saved["lse_t"], dmixed_t, time_scores, time_mixed, time_flip
    )
    entry_grad_t = weight_sum(saved["lowered_t"], dfused_t)
    dsent, gain_t, shift_t = norm_back(
        project_back(dfused_t, entry[0]), saved["unit_t"], saved["inverse_t"], gains[0, 0]
    )
    dreturned = lax.all_to_all(
        dsent.astype(jnp.bfloat16), "tok", split_axis=1, concat_axis=2, tiled=True
    )
    input_gradient = dafter_t + dreturned.astype(jnp.float32)
    members = (
        jnp.stack([entry_grad_t, entry_grad_s]).reshape(-1, 128),
        jnp.stack([temporal_grad_a, temporal_grad_b]).reshape(-1, 128),
        spatial_grad.reshape(-1, 128),
        widen_grad.reshape(-1, 128),
        narrow_grad.reshape(-1, 128),
        jnp.stack([jnp.stack([gain_t, gain_s, gain_m]), jnp.stack([shift_t, shift_s, shift_m])]),
    )
    totals = (
        lax.psum_scatter(members[0], ("clip", "tok"), scatter_dimension=0, tiled=True),
        lax.psum_scatter(members[1], ("clip", "tok"), scatter_dimension=0, tiled=True),
        lax.psum_scatter(members[2], ("clip", "tok"), scatter_dimension=0, tiled=True),
        lax.psum_scatter(members[3], ("clip", "tok"), scatter_dimension=0, tiled=True),
        lax.psum_scatter(members[4], ("clip", "tok"), scatter_dimension=0, tiled=True),
        lax.psum_scatter(members[5], ("clip", "tok"), scatter_dimension=2, tiled=True),
    )
    entry_sum, temporal_sum, spatial_sum, widen_sum, narrow_sum, affine_sum = totals
    entry_new = adamw(entry_weights, entry_momentum, entry_variance, entry_sum, D ** (-0.5))
    temporal_new = adamw(
        temporal_weights, temporal_momentum, temporal_variance, temporal_sum, (D // 2) ** (-0.5)
    )
    spatial_new = adamw(
        spatial_weights,
        spatial_momentum,
        spatial_variance,
        spatial_sum,
        (3 * D // PATCHES) ** (-0.5),
    )
    widen_new = adamw(widen_weights, widen_momentum, widen_variance, widen_sum, D ** (-0.5))
    narrow_new = adamw(narrow_weights, narrow_momentum, narrow_variance, narrow_sum, HID ** (-0.5))
    affine_new = adamw(norm_affine, affine_momentum, affine_variance, affine_sum, 0.5)
    return (
        result,
        input_gradient,
        entry_new[0],
        entry_new[1],
        entry_new[2],
        temporal_new[0],
        temporal_new[1],
        temporal_new[2],
        spatial_new[0],
        spatial_new[1],
        spatial_new[2],
        widen_new[0],
        widen_new[1],
        widen_new[2],
        narrow_new[0],
        narrow_new[1],
        narrow_new[2],
        affine_new[0],
        affine_new[1],
        affine_new[2][:, 0:2],
        affine_new[2][:, 2],
    )

MESH = pl.DeviceIdType.MESH
TOK = 4
UNIT = 768
ROWS = (48, 48, 24, 24, 96)
WIDTHS = (2304, 768, 768, 3072, 768)
AFFINE = 5
EACH = 24
ORDER_IN = (5, 0, 1, 2, 3, 4)
ORDER_MLP = (4, 3, 2)
ORDER_REST = (0, 1, 5)
VMEM_LIMIT = 60 * 1024 * 1024


def units_of(order, unit=UNIT):
    units = []
    for k in order:
        if k == AFFINE:
            units.append((k, 0, 128))
        else:
            wide = unit if ROWS[k] < 96 or unit > UNIT else unit // 2
            units += [(k, c, min(wide, WIDTHS[k] - c)) for c in range(0, WIDTHS[k], wide)]
    return units


def spot():
    clip = lax.axis_index("clip")
    return clip // 4, (clip // 2) % 2, clip % 2, lax.axis_index("tok")


def clip_of(y, x, core):
    return (y * 2 + x) * 2 + core


def greet():
    y, x, core, t = spot()
    barrier = pltpu.get_barrier_semaphore()

    def tell(clip, tok):
        pl.semaphore_signal(barrier, inc=1, device_id=(clip, tok), device_id_type=MESH)

    tell(clip_of(y, x, 1 - core), t)
    tell(clip_of(y, 1 - x, core), t)
    tell(clip_of(1 - y, x, core), t)
    for far in range(1, TOK):
        tell(clip_of(y, x, core), (t + far) % TOK)
    pl.semaphore_wait(barrier, 3 + (TOK - 1))


class Flight:
    def __init__(self):
        self.started = []

    def go(self, copy, when=None):
        if when is None:
            copy.start()
        else:
            pl.when(when)(copy.start)
        self.started.append((copy, when))
        return copy

    def drain(self):
        for copy, when in self.started:
            if when is None:
                copy.wait_send()
            else:
                pl.when(when)(copy.wait_send)


def gather_steps(units, owned, full, sems):
    local, got, core_got, out_sem, z_sem = sems
    y, x, core, t = spot()
    here, by_x, by_y = clip_of(y, x, core), clip_of(y, 1 - x, core), clip_of(1 - y, x, core)
    mate = clip_of(y, x, 1 - core)
    corner_clip = clip_of(1 - y, 1 - x, core)
    local_copies = []

    def place(u, at):
        k, c, width = units[u]
        return full[k].at[at, :, pl.ds(c, width)]

    def send(u, at, to, tok=None, own=False, along_z=False, when=None):
        k, c, width = units[u]
        there = place(u, at)
        copy = pltpu.make_async_remote_copy(
            src_ref=owned[k].at[:, pl.ds(c, width)] if own else there,
            dst_ref=there,
            send_sem=(z_sem if along_z else out_sem).at[u],
            recv_sem=got.at[u, at],
            device_id=(to, t if tok is None else tok),
            device_id_type=MESH,
        )
        if when is None:
            copy.start()
        else:
            pl.when(when)(copy.start)

    def many(u, count):
        k, c, width = units[u]
        return full[k].at[pl.ds(0, count), :, pl.ds(c, width)]

    def took(u, count, sem):
        there = many(u, count)
        pltpu.make_async_copy(there, there, sem.at[u]).wait()

    def arrive(u, at):
        there = place(u, at)
        pltpu.make_async_copy(there, there, got.at[u, at]).wait()

    def spread(u, at, own=False, when=None):
        def both():
            send(u, at, by_x, own=own)
            send(u, at, by_y, own=own)

        if when is None:
            both()
        else:
            pl.when(when)(both)

    def begin(u):
        k, c, width = units[u]
        me = here * TOK + t
        copy = pltpu.make_async_copy(owned[k].at[:, pl.ds(c, width)], place(u, me), local.at[u])
        copy.start()
        local_copies.append(copy)
        send(u, me, here, t + 1, own=True, along_z=True, when=t < TOK - 1)
        send(u, me, here, t - 1, own=True, along_z=True, when=t > 0)
        spread(u, me, own=True)

    hops = [(far, way) for far in range(1, TOK) for way in (1, -1)]

    def guard(far, way):
        return t + far <= TOK - 1 if way == 1 else t - far >= 0

    def to_mate(u, clip):
        k, c, width = units[u]
        there = full[k].at[pl.ds(clip * TOK, TOK), :, pl.ds(c, width)]
        pltpu.make_async_remote_copy(
            src_ref=there,
            dst_ref=there,
            send_sem=out_sem.at[u],
            recv_sem=core_got.at[u],
            device_id=(mate, t),
            device_id_type=MESH,
        ).start()

    def along(u):
        for far, way in hops:
            at = here * TOK + t + far * way

            def passing(at=at, way=way):
                arrive(u, at)
                onward = t > 0 if way == 1 else t < TOK - 1
                send(u, at, here, t - way, along_z=True, when=onward)
                spread(u, at)

            pl.when(guard(far, way))(passing)
        local_copies[u].wait()
        to_mate(u, here)

    def crossing(u):
        for far in range(TOK):
            tok = (t + far) % TOK
            from_x, from_y = by_x * TOK + tok, by_y * TOK + tok
            arrive(u, from_x)
            if far % 2 == 1:
                send(u, from_x, by_y)
            arrive(u, from_y)
            if far % 2 == 0:
                send(u, from_y, by_x)
        to_mate(u, by_x)
        to_mate(u, by_y)

    def corner(u):
        for far in range(TOK):
            arrive(u, corner_clip * TOK + (t + far) % TOK)
        to_mate(u, corner_clip)

    def settle(u):
        took(u, 16, core_got)

    def drain():
        edge = jnp.logical_or(t == 0, t == TOK - 1)
        for u in range(len(units)):
            took(u, 28, out_sem)

        def wait_z(count):
            for u in range(len(units)):
                took(u, count, z_sem)

        pl.when(edge)(functools.partial(wait_z, 1))
        pl.when(jnp.logical_not(edge))(functools.partial(wait_z, 5))

    return begin, along, crossing, corner, settle, drain


def gather_sems(count):
    dma = pltpu.SemaphoreType.DMA
    return [
        dma((count,)),
        dma((count, 32)),
        dma((count,)),
        dma((count,)),
        dma((count,)),
    ]


def rows_from(flat, out):
    rows, n = out.shape[0], out.shape[1] // 128
    for c in range(n):
        out[:, c * 128 : (c + 1) * 128] = flat[pl.ds(c, rows, stride=n), :].astype(out.dtype)


def join_affine(blocks, out):
    lane = lax.broadcasted_iota(jnp.int32, (16, 128), 1)
    tiles = [jnp.zeros((16, 128), jnp.float32) for _ in range(6)]
    for i in range(32):
        block = jnp.where(lane < EACH, blocks[i].astype(jnp.float32), 0.0)
        tile, shift = (i * EACH) // 128, (i * EACH) % 128
        turned = pltpu.roll(block, shift, 1) if shift else block
        tiles[tile] = tiles[tile] + jnp.where(lane >= shift, turned, 0.0)
        if shift + EACH > 128:
            tiles[tile + 1] = tiles[tile + 1] + jnp.where(lane < shift, turned, 0.0)
    for i in range(6):
        out[:, i * 128 : (i + 1) * 128] = tiles[i]


def scatter_steps(units, parts, held, core_in, side_in, part_in, z_in, sems, finals):
    load_sem, c_send, c_recv, d_send, d_recv, s_send, s_recv, z_send, z_recv = sems
    y, x, core, t = spot()
    here, by_x, by_y = clip_of(y, x, core), clip_of(y, 1 - x, core), clip_of(1 - y, x, core)
    mate = clip_of(y, x, 1 - core)
    homes = [(1 - y, 1 - x), (y, 1 - x), (1 - y, x), (y, x)]

    def cols(u):
        k, c, width = units[u]
        return pl.ds(c, width)

    def remote(src, dst, send_sem, recv_sem, to, tok=None):
        return pltpu.make_async_remote_copy(
            src_ref=src,
            dst_ref=dst,
            send_sem=send_sem,
            recv_sem=recv_sem,
            device_id=(to, t if tok is None else tok),
            device_id_type=MESH,
        )

    def load(u, g):
        k = units[u][0]
        ya, xa = homes[g]
        return pltpu.make_async_copy(
            parts[k].at[pl.ds(clip_of(ya, xa, core) * TOK, TOK), :, cols(u)],
            held[u].at[g],
            load_sem.at[u, g],
        )

    def to_mate(u, g):
        k = units[u][0]
        ya, xa = homes[g]
        return remote(
            parts[k].at[pl.ds(clip_of(ya, xa, 1 - core) * TOK, TOK), :, cols(u)],
            core_in[u].at[g],
            c_send.at[u],
            c_recv.at[u, g],
            mate,
        )

    def begin(u):
        for g in range(4):
            load(u, g).start()
            to_mate(u, g).start()

    def ready(u, g):
        load(u, g).wait()
        to_mate(u, g).wait_recv()

    def add_into(u, g, lo, hi, pieces):
        def one(j, carry):
            total = up(held[u][g, j])
            for piece in pieces:
                total = total + up(piece[j])
            held[u][g, j] = low(total)
            return carry

        lax.fori_loop(lo, hi, one, 0)

    def first(u, half):
        return remote(
            held[u].at[0, pl.ds(2 * half, 2)],
            side_in[u].at[pl.ds(2 * half, 2)],
            d_send.at[u],
            d_recv.at[u, half],
            by_y if half else by_x,
        )

    def second(u, across):
        return remote(
            held[u].at[1 if across == 0 else 2],
            part_in[u].at[across],
            s_send.at[u],
            s_recv.at[u, across],
            by_x if across == 0 else by_y,
        )

    def last(u, far):
        tok = (t + far) % TOK
        return remote(
            held[u].at[3, tok],
            z_in[u].at[far - 1],
            z_send.at[u],
            z_recv.at[u, far - 1],
            here,
            tok,
        )

    def step1(u):
        ready(u, 0)
        add_into(u, 0, 0, TOK, [core_in[u].at[0]])
        first(u, 0).start()
        first(u, 1).start()

    def step2(u):
        ready(u, 2)
        first(u, 0).wait_recv()
        add_into(u, 2, 0, 2, [core_in[u].at[2], side_in[u]])
        add_into(u, 2, 2, TOK, [core_in[u].at[2]])
        second(u, 1).start()
        ready(u, 1)
        first(u, 1).wait_recv()
        add_into(u, 1, 0, 2, [core_in[u].at[1]])
        add_into(u, 1, 2, TOK, [core_in[u].at[1], side_in[u]])
        second(u, 0).start()

    def step3(u):
        ready(u, 3)
        second(u, 0).wait_recv()
        second(u, 1).wait_recv()
        add_into(u, 3, 0, TOK, [core_in[u].at[3], part_in[u].at[0], part_in[u].at[1]])
        for far in range(1, TOK):
            last(u, far).start()

    def step4(u):
        total = up(held[u][3, t])
        for far in range(1, TOK):
            last(u, far).wait_recv()
            total = total + up(z_in[u][far - 1])
        finals(u, total)

    def drain():
        for u in range(len(units)):
            for place, sem in ((held, c_send), (side_in, d_send), (part_in, s_send), (z_in, z_send)):
                pltpu.make_async_copy(place[u], place[u], sem.at[u]).wait()

    return begin, step1, step2, step3, step4, drain


def scatter_scratch(units):
    bf16 = jnp.bfloat16
    shapes = [(16 if k == AFFINE else ROWS[k], width) for k, c, width in units]
    held = [pltpu.VMEM((4, TOK) + s, bf16) for s in shapes]
    side = [pltpu.VMEM((TOK,) + s, bf16) for s in shapes]
    part = [pltpu.VMEM((2, TOK) + s, bf16) for s in shapes]
    last = [pltpu.VMEM((TOK - 1,) + s, bf16) for s in shapes]
    return held + held + side + part + last


def scatter_sems(count):
    dma = pltpu.SemaphoreType.DMA
    return [
        dma((count, 4)),
        dma((count,)),
        dma((count, 4)),
        dma((count,)),
        dma((count, 2)),
        dma((count,)),
        dma((count, 2)),
        dma((count,)),
        dma((count, TOK - 1)),
    ]


STEP_FIX = 1.0 - 0.5**STEP


def adamw_rows(rate, weights, moment, square, grad, out):
    averaged = 0.5 * moment + 0.5 * grad
    squared = 0.5 * square + 0.5 * grad * grad
    out[0][...] = weights - rate * (
        averaged / STEP_FIX / (jnp.sqrt(squared / STEP_FIX) + 1e-08) + 0.1 * weights
    )
    out[1][...] = averaged
    out[2][...] = squared


RATES = (768 ** (-0.5), 384 ** (-0.5), 11 ** (-0.5), 768 ** (-0.5), 3072 ** (-0.5))


def part_affine(norms, out):
    rows = [jnp.sum(n[0:8, :], axis=0, keepdims=True) for n in norms]
    rows += [jnp.sum(n[8:16, :], axis=0, keepdims=True) for n in norms]
    table = jnp.concatenate(rows + [jnp.zeros((10, 768), jnp.float32)], axis=0)
    lane = lax.broadcasted_iota(jnp.int32, (16, 128), 1)
    for i in range(32):
        tile, shift = (i * EACH) // 128, (i * EACH) % 128
        block = table[:, tile * 128 : (tile + 1) * 128]
        block = pltpu.roll(block, (128 - shift) % 128, 1) if shift else block
        if shift + EACH > 128:
            after = pltpu.roll(table[:, (tile + 1) * 128 : (tile + 2) * 128], 128 - shift, 1)
            block = jnp.where(lane < 128 - shift, block, after)
        out[i] = jnp.where(lane < EACH, block, 0.0).astype(jnp.bfloat16)

GROUPS = 7
T_ROWS = 448
S_PAD = 208
S_ROWS = 416
CHUNK = 768
MLP_CHUNK = 512
SCALE = HEAD_DIM ** (-0.5)
BIG = -1e30
NT = (((1,), (1,)), ((), ()))
TN = (((0,), (0,)), ((), ()))


def dot(left, right, dims=(((1,), (0,)), ((), ()))):
    return lax.dot_general(left, right, dims, preferred_element_type=jnp.float32)


def low(values):
    return values.astype(jnp.bfloat16)


def up(values):
    return values.astype(jnp.float32)


def center_rows(values):
    center = values - jnp.mean(values, axis=-1, keepdims=True)
    inverse = lax.rsqrt(jnp.mean(center * center, axis=-1, keepdims=True) + 1e-06)
    return center * inverse, inverse


def back_rows(upstream, unit, inverse, gain):
    scaled = upstream * gain
    inner = (
        scaled
        - jnp.mean(scaled, axis=-1, keepdims=True)
        - unit * jnp.mean(scaled * unit, axis=-1, keepdims=True)
    )
    return inner * inverse


def fold(values):
    return jnp.sum(values.reshape(-1, 8, values.shape[-1]), axis=0)


def columns(j, width):
    return pl.ds(pl.multiple_of(j * width, 128), width)


def rows_of(i, height):
    return pl.ds(pl.multiple_of(i * height, 8), height)


def times(out, left, weight, width=CHUNK):
    def step(j, carry):
        at = columns(j, width)
        out[:, at] = dot(left[...], weight[:, at]).astype(out.dtype)
        return carry

    lax.fori_loop(0, out.shape[1] // width, step, 0)


def lane_half(shape):
    return lax.broadcasted_iota(jnp.int32, shape, 1) < HEAD_DIM


def soft(query, keys, mask):
    scores = jnp.where(mask, dot(keys, query, NT), BIG)
    expo = jnp.exp(scores - jnp.max(scores, axis=0, keepdims=True))
    return expo * (1.0 / jnp.sum(expo, axis=0, keepdims=True))


def attend(query, keys, values, mask):
    half = lane_half(query.shape)
    zero = jnp.zeros_like(query)
    query = query * jnp.bfloat16(SCALE)
    first = dot(low(soft(jnp.where(half, query, zero), keys, mask)), values, TN)
    second = dot(low(soft(jnp.where(half, zero, query), keys, mask)), values, TN)
    return low(jnp.where(half, first, second))


def attend_back(query, keys, values, upstream, mask):
    half = lane_half(query.shape)
    zero = jnp.zeros_like(query)
    query = query * jnp.bfloat16(SCALE)
    scaled = keys * jnp.bfloat16(SCALE)

    def one(pick):
        probs = soft(pick(query, zero), keys, mask)
        dprobs = dot(values, pick(upstream, zero), NT)
        dscores = low(probs * (dprobs - jnp.sum(dprobs * probs, axis=0, keepdims=True)))
        return dot(dscores, scaled, TN), dot(dscores, query), dot(low(probs), upstream)

    first = one(lambda a, b: jnp.where(half, a, b))
    second = one(lambda a, b: jnp.where(half, b, a))
    return tuple(low(jnp.where(half, a, b)) for a, b in zip(first, second))


def frame_mask(size):
    patch = lambda axis: (lambda i: (i // 64) * 8 + i % 8)(
        lax.broadcasted_iota(jnp.int32, (size, size), axis)
    )
    return patch(0) == patch(1)


def patch_mask():
    return lax.broadcasted_iota(jnp.int32, (S_PAD, S_PAD), 0) < PATCHES


T_BLOCKS = ((0, 192), (192, 256))


def mlp_kernel(lowered, after_s, cotangent, widen, narrow, affine, result, d_narrow, d_widen, d_after, d_norm, cot, turned, total, back):
    j = pl.program_id(0)

    @pl.when(j == 0)
    def start():
        cot[...] = jnp.zeros_like(cot)
        for f in range(2):
            back[pl.ds(f * S_PAD, PATCHES), :] = up(cotangent[f])
            back[pl.ds(f * S_PAD + PATCHES, S_PAD - PATCHES), :] = jnp.zeros((S_PAD - PATCHES, D), jnp.float32)
        cot[...] = low(back[...])
        turned[...] = lowered[...].T
        total[...] = after_s[...]
        back[...] = jnp.zeros_like(back)

    wide = dot(lowered[...], widen[...])
    phi = 0.5 * (1.0 + lax.erf(wide * 0.7071067811865476))
    active = low(wide * phi)
    slope = phi + wide * jnp.exp(-0.5 * wide * wide) * 0.3989422804014327
    d_wide = low(dot(cot[...], narrow[...], NT) * slope)
    total[...] += dot(active, narrow[...])
    d_narrow[...] = low(dot(active, cot[...], TN))
    d_widen[...] = low(dot(turned[...], d_wide))
    back[...] += dot(d_wide, widen[...], NT)

    @pl.when(j == pl.num_programs(0) - 1)
    def finish():
        for f in range(2):
            result[f] = low(total[pl.ds(f * S_PAD, PATCHES), :])

        def norm(b, carry):
            rows = rows_of(b, 32)
            unit, inverse = center_rows(after_s[rows, :])
            upstream = back[rows, :]
            d_after[rows, :] = up(cot[rows, :]) + back_rows(upstream, unit, inverse, affine[2:3, :])
            return carry[0] + fold(upstream * unit), carry[1] + fold(upstream)

        zero = jnp.zeros((8, D), jnp.float32)
        gain, shift = lax.fori_loop(0, S_ROWS // 32, norm, (zero, zero))
        d_norm[0:8, :] = gain
        d_norm[8:16, :] = shift


def mlp(lowered, after_s, cotangent, widen, narrow, affine):
    whole = lambda shape: pl.BlockSpec(shape, lambda j: (0,) * len(shape))
    steps = HID // MLP_CHUNK
    return pl.pallas_call(
        mlp_kernel,
        grid=(steps,),
        in_specs=[
            whole((S_ROWS, D)),
            whole((S_ROWS, D)),
            whole((2, PATCHES, D)),
            pl.BlockSpec((D, MLP_CHUNK), lambda j: (0, j)),
            pl.BlockSpec((MLP_CHUNK, D), lambda j: (j, 0)),
            whole((16, D)),
        ],
        out_specs=[
            whole((2, PATCHES, D)),
            pl.BlockSpec((MLP_CHUNK, D), lambda j: (j, 0)),
            pl.BlockSpec((D, MLP_CHUNK), lambda j: (0, j)),
            whole((S_ROWS, D)),
            whole((16, D)),
        ],
        out_shape=[
            jax.ShapeDtypeStruct((2, PATCHES, D), jnp.bfloat16),
            jax.ShapeDtypeStruct((HID, D), jnp.bfloat16),
            jax.ShapeDtypeStruct((D, HID), jnp.bfloat16),
            jax.ShapeDtypeStruct((S_ROWS, D), jnp.float32),
            jax.ShapeDtypeStruct((16, D), jnp.float32),
        ],
        scratch_shapes=[
            pltpu.VMEM((S_ROWS, D), jnp.bfloat16),
            pltpu.VMEM((D, S_ROWS), jnp.bfloat16),
            pltpu.VMEM((S_ROWS, D), jnp.float32),
            pltpu.VMEM((S_ROWS, D), jnp.float32),
        ],
        compiler_params=pltpu.CompilerParams(vmem_limit_bytes=56 * 1024 * 1024),
        cost_estimate=pl.CostEstimate(flops=12000000000, bytes_accessed=30000000, transcendentals=0),
    )(lowered, after_s, cotangent, widen, narrow, affine)

def pack(box, rows):
    extra = [rows(f, 192, 4) for f in range(2)]
    line = lax.broadcasted_iota(jnp.int32, (16, D), 0)
    for s in range(TOK):
        wide = [rows(f, 48 * s, 48) for f in range(2)]
        for b in range(6):
            pair = [w[8 * b : 8 * b + 8, :] for w in wide]
            box[s, b] = low(jnp.concatenate(pair, axis=0))
        one = [jnp.broadcast_to(e[s : s + 1, :], (16, D)) for e in extra]
        box[s, 6] = low(jnp.where(line == 0, one[0], jnp.where(line == 8, one[1], 0.0)))


def unpack(box, f, put):
    for s in range(TOK):
        for b in range(6):
            slab = up(box[s, b])
            put(48 * s + 8 * b, 8, slab[8 * f : 8 * f + 8, :])
    last = [up(box[s, 6])[8 * f : 8 * f + 1, :] for s in range(TOK)]
    put(192, TOK, jnp.concatenate(last, axis=0))


class Exchange:
    def __init__(self, source, target, sems, flight):
        self.source, self.target, self.flight = source, target, flight
        self.local, self.sent, self.got = sems
        self.clip, self.t = lax.axis_index("clip"), lax.axis_index("tok")

    def copy(self, far):
        return pltpu.make_async_remote_copy(
            src_ref=self.source((self.t + far) % TOK),
            dst_ref=self.target(self.t),
            send_sem=self.sent.at[far - 1],
            recv_sem=self.got.at[far - 1],
            device_id=(self.clip, (self.t + far) % TOK),
            device_id_type=MESH,
        )

    def own(self):
        return pltpu.make_async_copy(self.source(self.t), self.target(self.t), self.local.at[0])

    def start(self):
        for far in range(1, TOK):
            self.flight.go(self.copy(far))
        self.own().start()

    def wait(self):
        for far in range(1, TOK):
            there = self.target((self.t - far + TOK) % TOK)
            pltpu.make_async_copy(there, there, self.got.at[far - 1]).wait()
        self.own().wait()


def exchange_sems():
    dma = pltpu.SemaphoreType.DMA
    return [dma((1,)), dma((TOK - 1,)), dma((TOK - 1,))]


def pieces(count, step, size):
    def run(lo, hi):
        def one(j, carry):
            step(j)
            return carry

        lax.fori_loop(lo, hi, one, 0)

    return [functools.partial(run, lo, min(lo + size, count)) for lo in range(0, count, size)]


def product(out, left, weight, width=CHUNK):
    def step(j):
        at = columns(j, width)
        out[:, at] = dot(left(), weight[:, at]).astype(out.dtype)

    return step


def product_back(out, left, weight, width=CHUNK):
    def step(j):
        at = columns(j, width)
        out[:, at] = dot(left(), weight[at, :], NT).astype(out.dtype)

    return step


def gradient(out, turned, upstream, width=CHUNK):
    def step(j):
        at = columns(j, width)
        out[:, at] = low(dot(turned[...], upstream(at)))

    return step


SUM_START = 6
SUM_RATE = 1.0
SUM_SHIFTS = (0, 1, 2, 3)


def spaced(compute, rest):
    done = 0
    for i, call in enumerate(compute):
        call()
        while done < len(rest) and SUM_START + done * SUM_RATE <= i + 1:
            rest[done]()
            done += 1
    for call in rest[done:]:
        call()


def full_kernel_steps(units, steps, shifts, lo, hi):
    calls = []
    for n in range(lo, hi):
        for shift, step in zip(shifts, steps):
            if 0 <= n - shift < len(units):
                calls.append(functools.partial(step, n - shift))
    return calls


A2A_AT = 10


def gather_head(units):
    count = len(units)
    last = [n for n in range(count) if units[n][0] == 1][-1]
    names = ("begin", "along", "crossing", "corner")
    calls = []
    for n in range(last + 3):
        calls += [(name, n - shift) for shift, name in enumerate(names) if 0 <= n - shift < count]
    return calls + [("begin", last + 3), ("along", last + 2), ("corner", last)]


def forward_kernel(units, *refs):
    masters, block, frames = refs[:5], refs[5], refs[6]
    full = list(refs[7:12])
    affine, early_out, mixed_s, after_s, lowered = refs[12], refs[13:21], refs[21], refs[22], refs[23]
    owned, gathered = list(refs[24:29]), refs[29]
    entry_w, temporal_w, spatial_w, outbox, sent, inbox, load_sem = refs[30:37]
    early = refs[37:45]
    patch, normed_t, merged_t, mixed_t, first_t, after_t, normed_s, merged_s = early
    there_sems, back_sems = refs[45:48], refs[48:51]
    sems = refs[51:]
    stores = [
        pltpu.make_async_copy(a, b, load_sem.at[4 + i]) for i, (a, b) in enumerate(zip(early, early_out))
    ]

    def store(lo, hi):
        def begin_stores():
            for copy in stores[lo:hi]:
                copy.start()

        return [begin_stores]

    greet()
    full.append(gathered)
    owned.append(block)
    flight = Flight()
    begin, along, crossing, corner, settle, drain = gather_steps(units, owned, full, sems)
    count = len(units)
    place = {k: [n for n in range(count) if units[n][0] == k] for k in range(6)}
    there = Exchange(lambda s: outbox.at[s], lambda s: patch.at[:, s], there_sems, flight)
    back = Exchange(lambda s: sent.at[:, s], lambda s: inbox.at[s], back_sems, flight)
    def settle_all(k):
        for n in place[k]:
            settle(n)

    ready = set()
    original = begin

    def begin(n):
        k = units[n][0]
        if k not in ready and k != AFFINE:
            rows_from(masters[k], owned[k])
            ready.add(k)
        original(n)

    steps = {"begin": begin, "along": along, "crossing": crossing, "corner": corner}
    head = [functools.partial(steps[name], n) for name, n in gather_head(units)]
    step = lambda name, n: [functools.partial(steps[name], n)]
    for call in head[:A2A_AT]:
        call()
    pack(outbox, lambda f, start, size: up(frames[f, start : start + size, :]))
    there.start()
    for call in head[A2A_AT:]:
        call()

    def load(part, source, target):
        return pltpu.make_async_copy(source, target, load_sem.at[part])

    loads = {
        "entry": load(0, full[0].at[pl.ds(0, 16)], entry_w),
        "temporal": load(1, full[1], temporal_w),
        "later": load(2, full[0].at[pl.ds(16, 16)], entry_w),
        "spatial": load(3, full[2], spatial_w),
    }
    settle_all(AFFINE)
    join_affine(gathered, affine)
    there.wait()

    def norm_t(b):
        unit, unused = center_rows(up(patch[b].reshape(64, D)))
        normed_t[rows_of(b, 64), :] = low(unit * affine[0:1, :] + affine[3:4, :])

    def heads_t(p):
        found = []
        for start, size in T_BLOCKS:
            rows = pl.ds(start, size)
            query, keys, values = (merged_t[rows, columns(p + 6 * i, 128)] for i in range(3))
            found.append(attend(query, keys, values, frame_mask(size)))
        for (start, size), value in zip(T_BLOCKS, found):
            mixed_t[pl.ds(start, size), columns(p, 128)] = value

    entry_m = lambda at: entry_w[:, :, at].reshape(D, CHUNK)

    def merge(out, left):
        def step(j):
            at = columns(j, CHUNK)
            out[:, at] = low(dot(left[...], entry_m(at)))

        return step

    def first_step(j):
        at = columns(j, CHUNK)
        first_t[:, at] = low(dot(mixed_t[...], temporal_w[0:16, :, at].reshape(D, CHUNK)))

    def branch_step(j):
        at = columns(j, CHUNK)
        value = low(dot(first_t[...], temporal_w[16:32, :, at].reshape(D, CHUNK)))
        sent[:, :, :, at] = value.reshape(GROUPS, TOK, 16, CHUNK)

    def start_temporal():
        settle_all(0)
        settle_all(1)
        loads["entry"].start()
        loads["temporal"].start()
        for call in pieces(GROUPS, norm_t, GROUPS):
            call()
        loads["entry"].wait()
        loads["temporal"].wait()

    def start_spatial():
        settle_all(2)
        loads["later"].start()
        loads["spatial"].start()
        back.wait()
        for f in range(2):

            def put(start, size, rows, f=f):
                after_t[f * S_PAD + start : f * S_PAD + start + size, :] = (
                    up(frames[f, start : start + size, :]) + rows
                )

            unpack(inbox, f, put)
            tail = f * S_PAD + PATCHES
            after_t[tail : (f + 1) * S_PAD, :] = jnp.zeros((S_PAD - PATCHES, D), jnp.float32)

    def norm_s(b):
        unit, unused = center_rows(after_t[rows_of(b, 32), :])
        normed_s[rows_of(b, 32), :] = low(unit * affine[1:2, :] + affine[4:5, :])

    def wait_spatial():
        loads["later"].wait()
        loads["spatial"].wait()

    def heads_s(p):
        found = []
        for f in range(2):
            rows = pl.ds(f * S_PAD, S_PAD)
            query, keys, values = (merged_s[rows, columns(p + 6 * i, 128)] for i in range(3))
            found.append(attend(query, keys, values, patch_mask()))
        for f in range(2):
            mixed_s[pl.ds(f * S_PAD, S_PAD), columns(p, 128)] = found[f]

    def out_s(j):
        at = columns(j, CHUNK)
        weight = low(up(spatial_w[:, :, at]).reshape(D, CHUNK))
        after_s[:, at] = after_t[:, at] + dot(mixed_s[...], weight)

    def norm_m(b):
        unit, unused = center_rows(after_s[rows_of(b, 32), :])
        lowered[rows_of(b, 32), :] = low(unit * affine[2:3, :] + affine[5:6, :])

    order = (
        [start_temporal]
        + pieces(3, merge(merged_t, normed_t), 1)
        + step("crossing", 3)
        + step("along", 5)
        + step("corner", 3)
        + pieces(6, heads_t, 2)
        + step("crossing", 4)
        + pieces(1, first_step, 1)
        + pieces(1, branch_step, 1)
        + [back.start]
        + store(0, 5)
        + step("corner", 4)
        + step("crossing", 5)
        + [start_spatial]
        + pieces(13, norm_s, 13)
        + [wait_spatial]
        + pieces(3, merge(merged_s, normed_s), 1)
        + pieces(6, heads_s, 3)
        + store(5, 8)
        + step("corner", 5)
        + pieces(1, out_s, 1)
        + pieces(13, norm_m, 13)
    )
    for call in order:
        call()
    for k in (3, 4):
        settle_all(k)
    drain()
    flight.drain()
    for copy in stores:
        copy.wait()


def forward(masters, block, frames):
    units = units_of(ORDER_IN, HID)
    vmem = pl.BlockSpec(memory_space=pltpu.VMEM)
    anywhere = pl.BlockSpec(memory_space=pl.ANY)
    bf16, f32 = jnp.bfloat16, jnp.float32
    slab = (TOK, GROUPS, 16, D)
    group = (GROUPS, TOK, 16, D)
    saved = [
        ((16, D), f32),
        (group, bf16),
        ((T_ROWS, D), bf16),
        ((T_ROWS, 3 * D), bf16),
        ((T_ROWS, D), bf16),
        ((T_ROWS, D), bf16),
        ((S_ROWS, D), f32),
        ((S_ROWS, D), bf16),
        ((S_ROWS, 3 * D), bf16),
        ((S_ROWS, D), bf16),
        ((S_ROWS, D), f32),
        ((S_ROWS, D), bf16),
    ]
    early = [pltpu.VMEM(s, t) for s, t in saved[1:9]]
    return pl.pallas_call(
        functools.partial(forward_kernel, units),
        out_shape=[jax.ShapeDtypeStruct((32, r, w), bf16) for r, w in zip(ROWS, WIDTHS)]
        + [jax.ShapeDtypeStruct(s, t) for s, t in saved],
        in_specs=[vmem] * 7,
        out_specs=[anywhere] * 5 + [vmem] + [anywhere] * 8 + [vmem] * 3,
        scratch_shapes=[pltpu.VMEM((r, w), bf16) for r, w in zip(ROWS, WIDTHS)]
        + [
            pltpu.VMEM((32, 16, 128), bf16),
            pltpu.VMEM((16, 48, 3 * D), bf16),
            pltpu.VMEM((32, 48, D), bf16),
            pltpu.VMEM((32, 24, D), bf16),
            pltpu.VMEM(slab, bf16),
            pltpu.VMEM(group, bf16),
            pltpu.VMEM(slab, bf16),
            pltpu.SemaphoreType.DMA((12,)),
        ]
        + early
        + exchange_sems()
        + exchange_sems()
        + gather_sems(len(units)),
        compiler_params=pltpu.CompilerParams(
            collective_id=0, has_side_effects=True, vmem_limit_bytes=VMEM_LIMIT
        ),
    )(*masters, block, frames)


def finals_of(grads, affine_out=None):
    def finals(unit, total):
        k, c, width = unit
        if k == AFFINE:
            affine_out[...] = total
            return
        n, rows = WIDTHS[k] // 128, ROWS[k]
        for i in range(width // 128):
            grads[k][pl.ds(c // 128 + i, rows, stride=n), :] = total[:, i * 128 : (i + 1) * 128]

    return finals


def back_kernel(units, *refs):
    parts = dict(zip((3, 4), refs[:2]))
    d_after_s, after_t, affine, spatial = refs[2:6]
    normed_s_in, merged_s_in, mixed_s_in, entry_in = refs[6:10]
    patch_in, normed_t_in, merged_t_in, mixed_t_in, first_t_in, temporal_in = refs[10:16]
    grads = dict(zip((2, 3, 4), refs[16:19]))
    sent, d_after_t, d_entry_out, d_temporal, norm_s_out, norm_t_out = refs[19:25]
    pos = 25
    pools = []
    for i in range(5):
        pools.append(refs[pos : pos + len(units)])
        pos += len(units)
    parts[2] = refs[pos]
    pos += 1
    normed_s, merged_s, mixed_s, entry_w = refs[pos : pos + 4]
    patch, normed_t, merged_t, mixed_t, first_t, temporal_w = refs[pos + 4 : pos + 10]
    d_entry, lowered, d_mixed, d_first, d_merged, turned_s, turned_t, back, outbox, grouped, load_sem = refs[
        pos + 10 : pos + 21
    ]
    pos += 21
    there_sems = refs[pos : pos + 3]
    sems = refs[pos + 3 :]
    sources = (normed_s_in, merged_s_in, mixed_s_in, entry_in.at[1])
    targets = (normed_s, merged_s, mixed_s, entry_w)
    sources += (patch_in, normed_t_in, merged_t_in, mixed_t_in, first_t_in, temporal_in)
    targets += (patch, normed_t, merged_t, mixed_t, first_t, temporal_w)
    loads = [pltpu.make_async_copy(a, b, load_sem.at[i]) for i, (a, b) in enumerate(zip(sources, targets))]
    for copy in loads:
        copy.start()
    entry_load = pltpu.make_async_copy(entry_in.at[0], entry_w, load_sem.at[10])
    entry_stores = [pltpu.make_async_copy(d_entry, d_entry_out.at[i], load_sem.at[12 - i]) for i in range(2)]
    greet()
    flight = Flight()
    finals = finals_of(grads)
    steps = scatter_steps(
        units, parts, *pools, sems, lambda u, total: finals(units[u], total)
    )
    there = Exchange(lambda s: outbox.at[s], lambda s: grouped.at[:, s], there_sems, flight)
    zero = jnp.zeros((8, D), jnp.float32)

    def begin_s():
        lowered[...] = low(d_after_s[...])
        for copy in loads[:3]:
            copy.wait()
        turned_s[...] = mixed_s[...].T

    def turn_s():
        turned_s[...] = normed_s[...].T

    def heads_s(p):
        found = []
        for f in range(2):
            rows = pl.ds(f * S_PAD, S_PAD)
            query, keys, values = (merged_s[rows, columns(p + 6 * i, 128)] for i in range(3))
            found.append(
                attend_back(query, keys, values, d_mixed[rows, columns(p, 128)], patch_mask())
            )
        for f in range(2):
            for i in range(3):
                d_merged[pl.ds(f * S_PAD, S_PAD), columns(p + 6 * i, 128)] = found[f][i]

    def s_back(j):
        at = columns(j, CHUNK)
        back[0:S_ROWS, at] = dot(d_merged[0:S_ROWS, :], entry_w[at, :], NT)

    def end_s():
        entry_load.start()

        def norm(b, carry):
            rows = rows_of(b, 32)
            unit, inverse = center_rows(after_t[rows, :])
            upstream = back[rows, :]
            d_after_t[rows, :] = d_after_s[rows, :] + back_rows(upstream, unit, inverse, affine[1:2, :])
            return carry[0] + fold(upstream * unit), carry[1] + fold(upstream)

        gain, shift = lax.fori_loop(0, S_ROWS // 32, norm, (zero, zero))
        norm_s_out[0:8, :] = gain
        norm_s_out[8:16, :] = shift
        pack(outbox, lambda f, start, size: d_after_t[f * S_PAD + start : f * S_PAD + start + size, :])
        there.start()

    def wait_entry():
        loads[3].wait()

    def spatial_sum():
        parts[2][...] = low(dot(turned_s[...], lowered[...]).reshape(32, 24, D))
        steps[0](len(units) - 1)

    d_mixed_s = d_mixed.at[0:S_ROWS]
    compute = (
        [begin_s]
        + [spatial_sum]
        + pieces(1, product_back(d_mixed_s, lambda: lowered[...], spatial), 1)
        + [turn_s]
        + pieces(6, heads_s, 1)
        + [wait_entry]
        + pieces(1, s_back, 1)
        + [end_s]
        + pieces(3, gradient(d_entry, turned_s, lambda at: d_merged[0:S_ROWS, at]), 1)
        + [entry_stores[1].start]
    )

    def begin_t():
        for copy in loads[4:]:
            copy.wait()
        turned_t[...] = first_t[...].T
        there.wait()

    group_cols = lambda at: grouped[:, :, :, at].reshape(T_ROWS, CHUNK)

    def turn_mixed():
        turned_t[...] = mixed_t[...].T

    def turn_normed():
        turned_t[...] = normed_t[...].T

    def heads_t(p):
        found = []
        for start, size in T_BLOCKS:
            rows = pl.ds(start, size)
            query, keys, values = (merged_t[rows, columns(p + 6 * i, 128)] for i in range(3))
            found.append(
                attend_back(query, keys, values, d_mixed[rows, columns(p, 128)], frame_mask(size))
            )
        for (start, size), values in zip(T_BLOCKS, found):
            for i in range(3):
                d_merged[pl.ds(start, size), columns(p + 6 * i, 128)] = values[i]

    def t_back(j):
        at = columns(j, CHUNK)
        back[:, at] = dot(d_merged[...], entry_w[at, :], NT)

    def end_t():
        def norm(b, carry):
            rows = rows_of(b, 64)
            unit, inverse = center_rows(up(patch[b].reshape(64, D)))
            upstream = back[rows, :]
            value = back_rows(upstream, unit, inverse, affine[0:1, :])
            sent[b] = low(value).reshape(TOK, 16, D)
            return carry[0] + fold(upstream * unit), carry[1] + fold(upstream)

        gain, shift = lax.fori_loop(0, GROUPS, norm, (zero, zero))
        norm_t_out[0:8, :] = gain
        norm_t_out[8:16, :] = shift

    def free_entry():
        entry_stores[1].wait()
        entry_load.wait()

    compute += (
        [begin_t]
        + pieces(1, gradient(d_temporal.at[1], turned_t, group_cols), 1)
        + pieces(1, product_back(d_first, lambda: grouped[...].reshape(T_ROWS, D), temporal_w.at[1]), 1)
        + [turn_mixed]
        + pieces(1, gradient(d_temporal.at[0], turned_t, lambda at: d_first[:, at]), 1)
        + pieces(1, product_back(d_mixed, lambda: d_first[...], temporal_w.at[0]), 1)
        + [turn_normed]
        + pieces(6, heads_t, 1)
        + [free_entry]
        + pieces(1, t_back, 1)
        + [end_t]
        + pieces(3, gradient(d_entry, turned_t, lambda at: d_merged[:, at]), 1)
        + [entry_stores[0].start]
    )
    for u in range(len(units) - 1):
        steps[0](u)
    rest = full_kernel_steps(units, steps[1:5], SUM_SHIFTS, 0, len(units) + SUM_SHIFTS[-1])
    spaced(compute, rest)
    entry_stores[0].wait()
    steps[5]()
    flight.drain()


def backward(parts, d_after_s, after_t, affine, spatial, entry, temporal, saved_s, saved_t):
    units = units_of(ORDER_MLP)
    vmem = pl.BlockSpec(memory_space=pltpu.VMEM)
    anywhere = pl.BlockSpec(memory_space=pl.ANY)
    bf16, f32 = jnp.bfloat16, jnp.float32
    flat = [(ROWS[k] * WIDTHS[k] // 128, 128) for k in (2, 3, 4)]
    slab = (TOK, GROUPS, 16, D)
    group = (GROUPS, TOK, 16, D)
    outs = [(s, f32) for s in flat] + [
        (group, bf16),
        ((S_ROWS, D), f32),
        ((2, D, 3 * D), bf16),
        ((2, D, D), bf16),
        ((16, D), f32),
        ((16, D), f32),
    ]
    return pl.pallas_call(
        functools.partial(back_kernel, units),
        out_shape=[jax.ShapeDtypeStruct(s, t) for s, t in outs],
        in_specs=[anywhere] * 2 + [vmem] * 4 + [anywhere] * 10,
        out_specs=[vmem] * 5 + [anywhere] + [vmem] * 3,
        scratch_shapes=scatter_scratch(units)
        + [
            pltpu.VMEM((32, 24, D), bf16),
            pltpu.VMEM((S_ROWS, D), bf16),
            pltpu.VMEM((S_ROWS, 3 * D), bf16),
            pltpu.VMEM((S_ROWS, D), bf16),
            pltpu.VMEM((D, 3 * D), bf16),
            pltpu.VMEM(group, bf16),
            pltpu.VMEM((T_ROWS, D), bf16),
            pltpu.VMEM((T_ROWS, 3 * D), bf16),
            pltpu.VMEM((T_ROWS, D), bf16),
            pltpu.VMEM((T_ROWS, D), bf16),
            pltpu.VMEM((2, D, D), bf16),
            pltpu.VMEM((D, 3 * D), bf16),
            pltpu.VMEM((S_ROWS, D), bf16),
            pltpu.VMEM((T_ROWS, D), bf16),
            pltpu.VMEM((T_ROWS, D), bf16),
            pltpu.VMEM((T_ROWS, 3 * D), bf16),
            pltpu.VMEM((D, S_ROWS), bf16),
            pltpu.VMEM((D, T_ROWS), bf16),
            pltpu.VMEM((T_ROWS, D), f32),
            pltpu.VMEM(slab, bf16),
            pltpu.VMEM(group, bf16),
            pltpu.SemaphoreType.DMA((13,)),
        ]
        + exchange_sems()
        + scatter_sems(len(units)),
        compiler_params=pltpu.CompilerParams(
            collective_id=1, has_side_effects=True, vmem_limit_bytes=VMEM_LIMIT
        ),
    )(*parts, d_after_s, after_t, affine, spatial, *saved_s, entry, *saved_t, temporal)


HOME_AT = 4
HOME_END = 24


def rest_kernel(units, *refs):
    parts = dict(zip((0, 1), refs[:2]))
    norms = refs[2:5]
    sent, d_after_t = refs[5:7]
    grads = dict(zip((0, 1), refs[7:9]))
    affine_out, input_gradient = refs[9:11]
    pos = 11
    pools = []
    for i in range(5):
        pools.append(refs[pos : pos + len(units)])
        pos += len(units)
    parts[AFFINE] = refs[pos]
    inbox, home_sems = refs[pos + 1], refs[pos + 2 : pos + 5]
    sems = refs[pos + 5 :]
    greet()
    flight = Flight()
    home = Exchange(lambda s: sent.at[:, s], lambda s: inbox.at[s], home_sems, flight)
    finals = finals_of(grads, affine_out)
    steps = scatter_steps(
        units, parts, *pools, sems, lambda u, total: finals(units[u], total)
    )
    begin = steps[0]

    def begin_after(u):
        if units[u][0] == AFFINE:
            part_affine(norms, parts[AFFINE])
        begin(u)

    def receive():
        home.wait()
        for f in range(2):

            def put(start, size, rows, f=f):
                at = f * S_PAD + start
                input_gradient[f, start : start + size, :] = d_after_t[at : at + size, :] + rows

            unpack(inbox, f, put)

    calls = full_kernel_steps(units, (begin_after,) + steps[1:5], (0, 2, 3, 4, 5), 0, len(units) + 5)
    calls.insert(HOME_AT, home.start)
    calls.insert(HOME_END, receive)
    for call in calls:
        call()
    steps[5]()
    flight.drain()


def scatter_rest(parts, norms, sent, d_after_t):
    units = units_of(ORDER_REST)
    vmem = pl.BlockSpec(memory_space=pltpu.VMEM)
    flat = [(ROWS[k] * WIDTHS[k] // 128, 128) for k in (0, 1)]
    return pl.pallas_call(
        functools.partial(rest_kernel, units),
        out_shape=[jax.ShapeDtypeStruct(s, jnp.float32) for s in flat]
        + [
            jax.ShapeDtypeStruct((16, 128), jnp.float32),
            jax.ShapeDtypeStruct((2, PATCHES, D), jnp.float32),
        ],
        in_specs=[pl.BlockSpec(memory_space=pl.ANY)] * 2 + [vmem] * 5,
        out_specs=[vmem] * 4,
        scratch_shapes=scatter_scratch(units)
        + [pltpu.VMEM((32, 16, 128), jnp.bfloat16)]
        + [pltpu.VMEM((TOK, GROUPS, 16, D), jnp.bfloat16)]
        + exchange_sems()
        + scatter_sems(len(units)),
        compiler_params=pltpu.CompilerParams(
            collective_id=2, has_side_effects=True, vmem_limit_bytes=VMEM_LIMIT
        ),
    )(*parts, *norms, sent, d_after_t)


def update_kernel(*refs):
    for k in range(5):
        weights, moment, square = (refs[5 + 3 * k + i][...] for i in range(3))
        adamw_rows(RATES[k], weights, moment, square, refs[k][...], refs[20 + 3 * k : 23 + 3 * k])


def update(grads, states):
    steps = 6
    blocks = [pl.BlockSpec((g.shape[0] // steps, 128), lambda i: (i, 0)) for g in grads]
    triples = [b for b in blocks for _ in range(3)]
    return pl.pallas_call(
        update_kernel,
        grid=(steps,),
        out_shape=[jax.ShapeDtypeStruct(s.shape, jnp.float32) for s in states],
        in_specs=blocks + triples,
        out_specs=triples,
    )(*grads, *states)


def on_device(
    frames,
    cotangent,
    entry_weights,
    entry_momentum,
    entry_variance,
    temporal_weights,
    temporal_momentum,
    temporal_variance,
    spatial_weights,
    spatial_momentum,
    spatial_variance,
    widen_weights,
    widen_momentum,
    widen_variance,
    narrow_weights,
    narrow_momentum,
    narrow_variance,
    norm_affine,
    affine_momentum,
    affine_variance,
):
    masters = (entry_weights, temporal_weights, spatial_weights, widen_weights, narrow_weights)
    block = jnp.pad(low(norm_affine).reshape(6, EACH), ((0, 10), (0, 128 - EACH)))
    found = forward(masters, block, frames[0])
    entry, temporal, spatial, widen, narrow = found[:5]
    entry = entry.reshape(2, D, 3 * D)
    temporal = temporal.reshape(2, D, D)
    spatial = spatial.reshape(D, D)
    widen = widen.reshape(D, HID)
    narrow = narrow.reshape(HID, D)
    affine, patch, normed_t, merged_t, mixed_t, first_t = found[5:11]
    after_t, normed_s, merged_s, mixed_s, after_s, lowered = found[11:17]
    result, narrow_grad, widen_grad, d_after_s, norm_m = mlp(
        lowered, after_s, cotangent[0], widen, narrow, affine
    )
    found = backward(
        (widen_grad.reshape(32, -1, HID), narrow_grad.reshape(32, -1, D)),
        d_after_s,
        after_t,
        affine,
        spatial,
        entry,
        temporal,
        (normed_s, merged_s, mixed_s),
        (patch, normed_t, merged_t, mixed_t, first_t),
    )
    spatial_sum, widen_sum, narrow_sum = found[:3]
    sent, d_after_t, d_entry, d_temporal, norm_s, norm_t = found[3:9]
    entry_sum, temporal_sum, affine_sum, input_gradient = scatter_rest(
        (d_entry.reshape(32, -1, 3 * D), d_temporal.reshape(32, -1, D)),
        (norm_t, norm_s, norm_m),
        sent,
        d_after_t,
    )
    updated = update(
        (entry_sum, temporal_sum, spatial_sum, widen_sum, narrow_sum),
        (
            entry_weights,
            entry_momentum,
            entry_variance,
            temporal_weights,
            temporal_momentum,
            temporal_variance,
            spatial_weights,
            spatial_momentum,
            spatial_variance,
            widen_weights,
            widen_momentum,
            widen_variance,
            narrow_weights,
            narrow_momentum,
            narrow_variance,
        ),
    )
    affine_sum = affine_sum[:6, :EACH].reshape(2, 3, EACH)
    affine_new = adamw(norm_affine, affine_momentum, affine_variance, affine_sum, 0.5)
    return (
        result[None],
        input_gradient[None],
        *updated,
        affine_new[0],
        affine_new[1],
        affine_new[2][:, 0:2],
        affine_new[2][:, 2],
    )

def solution(mesh):
    return jax.shard_map(
        on_device if mesh.shape["clip"] == 8 and mesh.shape["tok"] == TOK else on_any,
        mesh=mesh,
        in_specs=(
            P("clip", "tok", None, None),
            P("clip", "tok", None, None),
            P(("clip", "tok"), None),
            P(("clip", "tok"), None),
            P(("clip", "tok"), None),
            P(("clip", "tok"), None),
            P(("clip", "tok"), None),
            P(("clip", "tok"), None),
            P(("clip", "tok"), None),
            P(("clip", "tok"), None),
            P(("clip", "tok"), None),
            P(("clip", "tok"), None),
            P(("clip", "tok"), None),
            P(("clip", "tok"), None),
            P(("clip", "tok"), None),
            P(("clip", "tok"), None),
            P(("clip", "tok"), None),
            P(None, None, ("clip", "tok")),
            P(None, None, ("clip", "tok")),
            P(None, None, ("clip", "tok")),
        ),
        out_specs=(
            P("clip", "tok", None, None),
            P("clip", "tok", None, None),
            P(("clip", "tok"), None),
            P(("clip", "tok"), None),
            P(("clip", "tok"), None),
            P(("clip", "tok"), None),
            P(("clip", "tok"), None),
            P(("clip", "tok"), None),
            P(("clip", "tok"), None),
            P(("clip", "tok"), None),
            P(("clip", "tok"), None),
            P(("clip", "tok"), None),
            P(("clip", "tok"), None),
            P(("clip", "tok"), None),
            P(("clip", "tok"), None),
            P(("clip", "tok"), None),
            P(("clip", "tok"), None),
            P(None, None, ("clip", "tok")),
            P(None, None, ("clip", "tok")),
            P(None, None, ("clip", "tok")),
            P(None, ("clip", "tok")),
        ),
        check_vma=False,
    )
```

```python
import functools

import jax
import jax.numpy as jnp
from jax import lax
from jax.experimental import pallas as pl
from jax.experimental.pallas import tpu as pltpu
from jax.sharding import PartitionSpec as P

D = 768
HEADS = 12
HEAD_DIM = 64
HID = 3072
PATCHES = 196
STEP = 5

time_scores = "cfphe,cgphe->cphfg"
time_mixed = "cphfg,cgphe->cfphe"
time_flip = "cphfg,cfphe->cgphe"
space_scores = "cfphe,cfqhe->cfhpq"
space_mixed = "cfhpq,cfqhe->cfphe"
space_flip = "cfhpq,cfphe->cfqhe"


def project(inputs, weight):
    return jnp.einsum("cfpa,ab->cfpb", inputs, weight, preferred_element_type=jnp.float32)


def project_back(upstream, weight):
    return jnp.einsum("cfpb,ab->cfpa", upstream, weight, preferred_element_type=jnp.float32)


def weight_sum(inputs, upstream):
    return jnp.einsum("cfpa,cfpb->ab", inputs, upstream, preferred_element_type=jnp.float32)


def layer_norm(values, gain, shift):
    center = values - jnp.mean(values, axis=-1, keepdims=True)
    inverse = lax.rsqrt(jnp.mean(center * center, axis=-1, keepdims=True) + 1e-06)
    unit = center * inverse
    return (unit * gain + shift, unit, inverse)


def norm_back(upstream, unit, inverse, gain):
    scaled = upstream * gain
    inner = (
        scaled
        - jnp.mean(scaled, axis=-1, keepdims=True)
        - unit * jnp.mean(scaled * unit, axis=-1, keepdims=True)
    )
    return (
        inner * inverse,
        jnp.sum(upstream * unit, axis=(0, 1, 2)),
        jnp.sum(upstream, axis=(0, 1, 2)),
    )


def split_heads(merged):
    lowered = merged.astype(jnp.bfloat16)
    parts = lowered.reshape(lowered.shape[:-1] + (3, HEADS, HEAD_DIM))
    return (parts[..., 0, :, :], parts[..., 1, :, :], parts[..., 2, :, :])


def attend_forward(heads, score_form, mixed_form):
    query, keys, values = heads
    scores = jnp.einsum(score_form, query, keys, preferred_element_type=jnp.float32) * HEAD_DIM ** (
        -0.5
    )
    top = jnp.max(scores, axis=-1, keepdims=True)
    expo = jnp.exp(scores - top)
    total = jnp.sum(expo, axis=-1, keepdims=True)
    probs = (expo / total).astype(jnp.bfloat16)
    mixed = jnp.einsum(mixed_form, probs, values, preferred_element_type=jnp.float32)
    joined = mixed.reshape(mixed.shape[:-2] + (HEADS * HEAD_DIM,)).astype(jnp.bfloat16)
    return (joined, top + jnp.log(total))


def attend_backward(heads, logsum, upstream_joined, score_form, mixed_form, flip_form):
    query, keys, values = heads
    upstream = upstream_joined.reshape(upstream_joined.shape[:-1] + (HEADS, HEAD_DIM))
    scale = HEAD_DIM ** (-0.5)
    scores = jnp.einsum(score_form, query, keys, preferred_element_type=jnp.float32) * scale
    probs = jnp.exp(scores - logsum)
    dprobs = jnp.einsum(score_form, upstream, values, preferred_element_type=jnp.float32)
    dscores = (probs * (dprobs - jnp.sum(dprobs * probs, axis=-1, keepdims=True))).astype(
        jnp.bfloat16
    )
    dquery = jnp.einsum(mixed_form, dscores, keys, preferred_element_type=jnp.float32) * scale
    dkeys = jnp.einsum(flip_form, dscores, query, preferred_element_type=jnp.float32) * scale
    dvalues = jnp.einsum(
        flip_form, probs.astype(jnp.bfloat16), upstream, preferred_element_type=jnp.float32
    )
    stacked = jnp.stack([dquery, dkeys, dvalues], axis=-3)
    return stacked.reshape(stacked.shape[:-3] + (3 * HEADS * HEAD_DIM,)).astype(jnp.bfloat16)


def collect(masters):
    gathered = (
        lax.all_gather(masters[0].astype(jnp.bfloat16), ("clip", "tok"), axis=0, tiled=True),
        lax.all_gather(masters[1].astype(jnp.bfloat16), ("clip", "tok"), axis=0, tiled=True),
        lax.all_gather(masters[2].astype(jnp.bfloat16), ("clip", "tok"), axis=0, tiled=True),
        lax.all_gather(masters[3].astype(jnp.bfloat16), ("clip", "tok"), axis=0, tiled=True),
        lax.all_gather(masters[4].astype(jnp.bfloat16), ("clip", "tok"), axis=0, tiled=True),
        lax.all_gather(masters[5].astype(jnp.bfloat16), ("clip", "tok"), axis=2, tiled=True),
    )
    return (
        gathered[0].reshape(2, D, 3 * D),
        gathered[1].reshape(2, D, D),
        gathered[2].reshape(D, D),
        gathered[3].reshape(D, HID),
        gathered[4].reshape(HID, D),
        gathered[5],
    )


def plain_forward(frames, masters):
    weights = collect(masters)
    entry, temporal, spatial, widen, narrow, affine = weights
    gains = affine.astype(jnp.float32)
    patchwise = lax.all_to_all(frames, "tok", split_axis=2, concat_axis=1, tiled=True)
    normed_t, unit_t, inverse_t = layer_norm(
        patchwise.astype(jnp.float32), gains[0, 0], gains[1, 0]
    )
    lowered_t = normed_t.astype(jnp.bfloat16)
    heads_t = split_heads(project(lowered_t, entry[0]))
    mixed_t, lse_t = attend_forward(heads_t, time_scores, time_mixed)
    first_t = project(mixed_t, temporal[0]).astype(jnp.bfloat16)
    branch = project(first_t, temporal[1]).astype(jnp.bfloat16)
    returned = lax.all_to_all(branch, "tok", split_axis=1, concat_axis=2, tiled=True)
    after_t = frames.astype(jnp.float32) + returned.astype(jnp.float32)
    normed_s, unit_s, inverse_s = layer_norm(after_t, gains[0, 1], gains[1, 1])
    lowered_s = normed_s.astype(jnp.bfloat16)
    heads_s = split_heads(project(lowered_s, entry[1]))
    mixed_s, lse_s = attend_forward(heads_s, space_scores, space_mixed)
    after_s = after_t + project(mixed_s, spatial)
    normed_m, unit_m, inverse_m = layer_norm(after_s, gains[0, 2], gains[1, 2])
    lowered_m = normed_m.astype(jnp.bfloat16)
    widened = project(lowered_m, widen)
    activated = jax.nn.gelu(widened, approximate=False).astype(jnp.bfloat16)
    result = (after_s + project(activated, narrow)).astype(jnp.bfloat16)
    saved = {
        "weights": weights,
        "unit_t": unit_t,
        "inverse_t": inverse_t,
        "lowered_t": lowered_t,
        "heads_t": heads_t,
        "lse_t": lse_t,
        "mixed_t": mixed_t,
        "first_t": first_t,
        "unit_s": unit_s,
        "inverse_s": inverse_s,
        "lowered_s": lowered_s,
        "heads_s": heads_s,
        "lse_s": lse_s,
        "mixed_s": mixed_s,
        "unit_m": unit_m,
        "inverse_m": inverse_m,
        "lowered_m": lowered_m,
        "widened": widened,
        "activated": activated,
    }
    return (result, saved)


def adamw(master, moment, square, grad, rate):
    fix = 1.0 - 0.5**STEP
    averaged = 0.5 * moment + 0.5 * grad
    squared = 0.5 * square + 0.5 * grad * grad
    updated = master - rate * (averaged / fix / (jnp.sqrt(squared / fix) + 1e-08) + 0.1 * master)
    return (updated, averaged, squared)

def on_any(
    frames,
    cotangent,
    entry_weights,
    entry_momentum,
    entry_variance,
    temporal_weights,
    temporal_momentum,
    temporal_variance,
    spatial_weights,
    spatial_momentum,
    spatial_variance,
    widen_weights,
    widen_momentum,
    widen_variance,
    narrow_weights,
    narrow_momentum,
    narrow_variance,
    norm_affine,
    affine_momentum,
    affine_variance,
):
    masters = (
        entry_weights,
        temporal_weights,
        spatial_weights,
        widen_weights,
        narrow_weights,
        norm_affine,
    )
    result, saved = plain_forward(frames, masters)
    entry, temporal, spatial, widen, narrow, affine = saved["weights"]
    gains = affine.astype(jnp.float32)
    narrow_grad = weight_sum(saved["activated"], cotangent)
    widened = saved["widened"]
    slope = (
        0.5 * (1.0 + lax.erf(widened * 0.7071067811865476))
        + widened * jnp.exp(-0.5 * widened * widened) * 0.3989422804014327
    )
    dwidened = (project_back(cotangent, narrow) * slope).astype(jnp.bfloat16)
    widen_grad = weight_sum(saved["lowered_m"], dwidened)
    dpart_m, gain_m, shift_m = norm_back(
        project_back(dwidened, widen), saved["unit_m"], saved["inverse_m"], gains[0, 2]
    )
    dafter_s = cotangent.astype(jnp.float32) + dpart_m
    dspatial = dafter_s.astype(jnp.bfloat16)
    spatial_grad = weight_sum(saved["mixed_s"], dspatial)
    dmixed_s = project_back(dspatial, spatial).astype(jnp.bfloat16)
    dfused_s = attend_backward(
        saved["heads_s"], saved["lse_s"], dmixed_s, space_scores, space_mixed, space_flip
    )
    entry_grad_s = weight_sum(saved["lowered_s"], dfused_s)
    dpart_s, gain_s, shift_s = norm_back(
        project_back(dfused_s, entry[1]), saved["unit_s"], saved["inverse_s"], gains[0, 1]
    )
    dafter_t = dafter_s + dpart_s
    dbranch = lax.all_to_all(
        dafter_t.astype(jnp.bfloat16), "tok", split_axis=2, concat_axis=1, tiled=True
    )
    temporal_grad_b = weight_sum(saved["first_t"], dbranch)
    dfirst = project_back(dbranch, temporal[1]).astype(jnp.bfloat16)
    temporal_grad_a = weight_sum(saved["mixed_t"], dfirst)
    dmixed_t = project_back(dfirst, temporal[0]).astype(jnp.bfloat16)
    dfused_t = attend_backward(
        saved["heads_t"], saved["lse_t"], dmixed_t, time_scores, time_mixed, time_flip
    )
    entry_grad_t = weight_sum(saved["lowered_t"], dfused_t)
    dsent, gain_t, shift_t = norm_back(
        project_back(dfused_t, entry[0]), saved["unit_t"], saved["inverse_t"], gains[0, 0]
    )
    dreturned = lax.all_to_all(
        dsent.astype(jnp.bfloat16), "tok", split_axis=1, concat_axis=2, tiled=True
    )
    input_gradient = dafter_t + dreturned.astype(jnp.float32)
    members = (
        jnp.stack([entry_grad_t, entry_grad_s]).reshape(-1, 128),
        jnp.stack([temporal_grad_a, temporal_grad_b]).reshape(-1, 128),
        spatial_grad.reshape(-1, 128),
        widen_grad.reshape(-1, 128),
        narrow_grad.reshape(-1, 128),
        jnp.stack([jnp.stack([gain_t, gain_s, gain_m]), jnp.stack([shift_t, shift_s, shift_m])]),
    )
    totals = (
        lax.psum_scatter(members[0], ("clip", "tok"), scatter_dimension=0, tiled=True),
        lax.psum_scatter(members[1], ("clip", "tok"), scatter_dimension=0, tiled=True),
        lax.psum_scatter(members[2], ("clip", "tok"), scatter_dimension=0, tiled=True),
        lax.psum_scatter(members[3], ("clip", "tok"), scatter_dimension=0, tiled=True),
        lax.psum_scatter(members[4], ("clip", "tok"), scatter_dimension=0, tiled=True),
        lax.psum_scatter(members[5], ("clip", "tok"), scatter_dimension=2, tiled=True),
    )
    entry_sum, temporal_sum, spatial_sum, widen_sum, narrow_sum, affine_sum = totals
    entry_new = adamw(entry_weights, entry_momentum, entry_variance, entry_sum, D ** (-0.5))
    temporal_new = adamw(
        temporal_weights, temporal_momentum, temporal_variance, temporal_sum, (D // 2) ** (-0.5)
    )
    spatial_new = adamw(
        spatial_weights,
        spatial_momentum,
        spatial_variance,
        spatial_sum,
        (3 * D // PATCHES) ** (-0.5),
    )
    widen_new = adamw(widen_weights, widen_momentum, widen_variance, widen_sum, D ** (-0.5))
    narrow_new = adamw(narrow_weights, narrow_momentum, narrow_variance, narrow_sum, HID ** (-0.5))
    affine_new = adamw(norm_affine, affine_momentum, affine_variance, affine_sum, 0.5)
    return (
        result,
        input_gradient,
        entry_new[0],
        entry_new[1],
        entry_new[2],
        temporal_new[0],
        temporal_new[1],
        temporal_new[2],
        spatial_new[0],
        spatial_new[1],
        spatial_new[2],
        widen_new[0],
        widen_new[1],
        widen_new[2],
        narrow_new[0],
        narrow_new[1],
        narrow_new[2],
        affine_new[0],
        affine_new[1],
        affine_new[2][:, 0:2],
        affine_new[2][:, 2],
    )

MESH = pl.DeviceIdType.MESH
TOK = 4
UNIT = 768
ROWS = (48, 48, 24, 24, 96)
WIDTHS = (2304, 768, 768, 3072, 768)
AFFINE = 5
EACH = 24
ORDER_IN = (5, 0, 1, 2, 3, 4)
ORDER_MLP = (4, 3, 2)
ORDER_REST = (0, 1, 5)
VMEM_LIMIT = 60 * 1024 * 1024


def units_of(order, unit=UNIT):
    units = []
    for k in order:
        if k == AFFINE:
            units.append((k, 0, 128))
        else:
            wide = unit if ROWS[k] < 96 or unit > UNIT else unit // 2
            units += [(k, c, min(wide, WIDTHS[k] - c)) for c in range(0, WIDTHS[k], wide)]
    return units


def spot():
    clip = lax.axis_index("clip")
    return clip // 4, (clip // 2) % 2, clip % 2, lax.axis_index("tok")


def clip_of(y, x, core):
    return (y * 2 + x) * 2 + core


def greet():
    y, x, core, t = spot()
    barrier = pltpu.get_barrier_semaphore()

    def tell(clip, tok):
        pl.semaphore_signal(barrier, inc=1, device_id=(clip, tok), device_id_type=MESH)

    tell(clip_of(y, x, 1 - core), t)
    tell(clip_of(y, 1 - x, core), t)
    tell(clip_of(1 - y, x, core), t)
    for far in range(1, TOK):
        tell(clip_of(y, x, core), (t + far) % TOK)
    pl.semaphore_wait(barrier, 3 + (TOK - 1))


class Flight:
    def __init__(self):
        self.started = []

    def go(self, copy, when=None):
        if when is None:
            copy.start()
        else:
            pl.when(when)(copy.start)
        self.started.append((copy, when))
        return copy

    def drain(self):
        for copy, when in self.started:
            if when is None:
                copy.wait_send()
            else:
                pl.when(when)(copy.wait_send)


def gather_steps(units, owned, full, sems):
    local, got, core_got, out_sem, z_sem = sems
    y, x, core, t = spot()
    here, by_x, by_y = clip_of(y, x, core), clip_of(y, 1 - x, core), clip_of(1 - y, x, core)
    mate = clip_of(y, x, 1 - core)
    corner_clip = clip_of(1 - y, 1 - x, core)
    local_copies = []

    def place(u, at):
        k, c, width = units[u]
        return full[k].at[at, :, pl.ds(c, width)]

    def send(u, at, to, tok=None, own=False, along_z=False, when=None):
        k, c, width = units[u]
        there = place(u, at)
        copy = pltpu.make_async_remote_copy(
            src_ref=owned[k].at[:, pl.ds(c, width)] if own else there,
            dst_ref=there,
            send_sem=(z_sem if along_z else out_sem).at[u],
            recv_sem=got.at[u, at],
            device_id=(to, t if tok is None else tok),
            device_id_type=MESH,
        )
        if when is None:
            copy.start()
        else:
            pl.when(when)(copy.start)

    def many(u, count):
        k, c, width = units[u]
        return full[k].at[pl.ds(0, count), :, pl.ds(c, width)]

    def took(u, count, sem):
        there = many(u, count)
        pltpu.make_async_copy(there, there, sem.at[u]).wait()

    def arrive(u, at):
        there = place(u, at)
        pltpu.make_async_copy(there, there, got.at[u, at]).wait()

    def spread(u, at, own=False, when=None):
        def both():
            send(u, at, by_x, own=own)
            send(u, at, by_y, own=own)

        if when is None:
            both()
        else:
            pl.when(when)(both)

    def begin(u):
        k, c, width = units[u]
        me = here * TOK + t
        copy = pltpu.make_async_copy(owned[k].at[:, pl.ds(c, width)], place(u, me), local.at[u])
        copy.start()
        local_copies.append(copy)
        send(u, me, here, t + 1, own=True, along_z=True, when=t < TOK - 1)
        send(u, me, here, t - 1, own=True, along_z=True, when=t > 0)
        spread(u, me, own=True)

    hops = [(far, way) for far in range(1, TOK) for way in (1, -1)]

    def guard(far, way):
        return t + far <= TOK - 1 if way == 1 else t - far >= 0

    def to_mate(u, clip):
        k, c, width = units[u]
        there = full[k].at[pl.ds(clip * TOK, TOK), :, pl.ds(c, width)]
        pltpu.make_async_remote_copy(
            src_ref=there,
            dst_ref=there,
            send_sem=out_sem.at[u],
            recv_sem=core_got.at[u],
            device_id=(mate, t),
            device_id_type=MESH,
        ).start()

    def along(u):
        for far, way in hops:
            at = here * TOK + t + far * way

            def passing(at=at, way=way):
                arrive(u, at)
                onward = t > 0 if way == 1 else t < TOK - 1
                send(u, at, here, t - way, along_z=True, when=onward)
                spread(u, at)

            pl.when(guard(far, way))(passing)
        local_copies[u].wait()
        to_mate(u, here)

    def crossing(u):
        for far in range(TOK):
            tok = (t + far) % TOK
            from_x, from_y = by_x * TOK + tok, by_y * TOK + tok
            arrive(u, from_x)
            if far % 2 == 1:
                send(u, from_x, by_y)
            arrive(u, from_y)
            if far % 2 == 0:
                send(u, from_y, by_x)
        to_mate(u, by_x)
        to_mate(u, by_y)

    def corner(u):
        for far in range(TOK):
            arrive(u, corner_clip * TOK + (t + far) % TOK)
        to_mate(u, corner_clip)

    def settle(u):
        took(u, 16, core_got)

    def drain():
        edge = jnp.logical_or(t == 0, t == TOK - 1)
        for u in range(len(units)):
            took(u, 28, out_sem)

        def wait_z(count):
            for u in range(len(units)):
                took(u, count, z_sem)

        pl.when(edge)(functools.partial(wait_z, 1))
        pl.when(jnp.logical_not(edge))(functools.partial(wait_z, 5))

    return begin, along, crossing, corner, settle, drain


def gather_sems(count):
    dma = pltpu.SemaphoreType.DMA
    return [
        dma((count,)),
        dma((count, 32)),
        dma((count,)),
        dma((count,)),
        dma((count,)),
    ]


def rows_from(flat, out):
    rows, n = out.shape[0], out.shape[1] // 128
    for c in range(n):
        out[:, c * 128 : (c + 1) * 128] = flat[pl.ds(c, rows, stride=n), :].astype(out.dtype)


def join_affine(blocks, out):
    lane = lax.broadcasted_iota(jnp.int32, (16, 128), 1)
    tiles = [jnp.zeros((16, 128), jnp.float32) for _ in range(6)]
    for i in range(32):
        block = jnp.where(lane < EACH, blocks[i].astype(jnp.float32), 0.0)
        tile, shift = (i * EACH) // 128, (i * EACH) % 128
        turned = pltpu.roll(block, shift, 1) if shift else block
        tiles[tile] = tiles[tile] + jnp.where(lane >= shift, turned, 0.0)
        if shift + EACH > 128:
            tiles[tile + 1] = tiles[tile + 1] + jnp.where(lane < shift, turned, 0.0)
    for i in range(6):
        out[:, i * 128 : (i + 1) * 128] = tiles[i]


def scatter_steps(units, parts, held, core_in, side_in, part_in, z_in, sems, finals):
    load_sem, c_send, c_recv, d_send, d_recv, s_send, s_recv, z_send, z_recv = sems
    y, x, core, t = spot()
    here, by_x, by_y = clip_of(y, x, core), clip_of(y, 1 - x, core), clip_of(1 - y, x, core)
    mate = clip_of(y, x, 1 - core)
    homes = [(1 - y, 1 - x), (y, 1 - x), (1 - y, x), (y, x)]

    def cols(u):
        k, c, width = units[u]
        return pl.ds(c, width)

    def remote(src, dst, send_sem, recv_sem, to, tok=None):
        return pltpu.make_async_remote_copy(
            src_ref=src,
            dst_ref=dst,
            send_sem=send_sem,
            recv_sem=recv_sem,
            device_id=(to, t if tok is None else tok),
            device_id_type=MESH,
        )

    def load(u, g):
        k = units[u][0]
        ya, xa = homes[g]
        return pltpu.make_async_copy(
            parts[k].at[pl.ds(clip_of(ya, xa, core) * TOK, TOK), :, cols(u)],
            held[u].at[g],
            load_sem.at[u, g],
        )

    def to_mate(u, g):
        k = units[u][0]
        ya, xa = homes[g]
        return remote(
            parts[k].at[pl.ds(clip_of(ya, xa, 1 - core) * TOK, TOK), :, cols(u)],
            core_in[u].at[g],
            c_send.at[u],
            c_recv.at[u, g],
            mate,
        )

    def begin(u):
        for g in range(4):
            load(u, g).start()
            to_mate(u, g).start()

    def ready(u, g):
        load(u, g).wait()
        to_mate(u, g).wait_recv()

    def add_into(u, g, lo, hi, pieces):
        def one(j, carry):
            total = up(held[u][g, j])
            for piece in pieces:
                total = total + up(piece[j])
            held[u][g, j] = low(total)
            return carry

        lax.fori_loop(lo, hi, one, 0)

    def first(u, half):
        return remote(
            held[u].at[0, pl.ds(2 * half, 2)],
            side_in[u].at[pl.ds(2 * half, 2)],
            d_send.at[u],
            d_recv.at[u, half],
            by_y if half else by_x,
        )

    def second(u, across):
        return remote(
            held[u].at[1 if across == 0 else 2],
            part_in[u].at[across],
            s_send.at[u],
            s_recv.at[u, across],
            by_x if across == 0 else by_y,
        )

    def last(u, far):
        tok = (t + far) % TOK
        return remote(
            held[u].at[3, tok],
            z_in[u].at[far - 1],
            z_send.at[u],
            z_recv.at[u, far - 1],
            here,
            tok,
        )

    def step1(u):
        ready(u, 0)
        add_into(u, 0, 0, TOK, [core_in[u].at[0]])
        first(u, 0).start()
        first(u, 1).start()

    def step2(u):
        ready(u, 2)
        first(u, 0).wait_recv()
        add_into(u, 2, 0, 2, [core_in[u].at[2], side_in[u]])
        add_into(u, 2, 2, TOK, [core_in[u].at[2]])
        second(u, 1).start()
        ready(u, 1)
        first(u, 1).wait_recv()
        add_into(u, 1, 0, 2, [core_in[u].at[1]])
        add_into(u, 1, 2, TOK, [core_in[u].at[1], side_in[u]])
        second(u, 0).start()

    def step3(u):
        ready(u, 3)
        second(u, 0).wait_recv()
        second(u, 1).wait_recv()
        add_into(u, 3, 0, TOK, [core_in[u].at[3], part_in[u].at[0], part_in[u].at[1]])
        for far in range(1, TOK):
            last(u, far).start()

    def step4(u):
        total = up(held[u][3, t])
        for far in range(1, TOK):
            last(u, far).wait_recv()
            total = total + up(z_in[u][far - 1])
        finals(u, total)

    def drain():
        for u in range(len(units)):
            for place, sem in ((held, c_send), (side_in, d_send), (part_in, s_send), (z_in, z_send)):
                pltpu.make_async_copy(place[u], place[u], sem.at[u]).wait()

    return begin, step1, step2, step3, step4, drain


def scatter_scratch(units):
    bf16 = jnp.bfloat16
    shapes = [(16 if k == AFFINE else ROWS[k], width) for k, c, width in units]
    held = [pltpu.VMEM((4, TOK) + s, bf16) for s in shapes]
    side = [pltpu.VMEM((TOK,) + s, bf16) for s in shapes]
    part = [pltpu.VMEM((2, TOK) + s, bf16) for s in shapes]
    last = [pltpu.VMEM((TOK - 1,) + s, bf16) for s in shapes]
    return held + held + side + part + last


def scatter_sems(count):
    dma = pltpu.SemaphoreType.DMA
    return [
        dma((count, 4)),
        dma((count,)),
        dma((count, 4)),
        dma((count,)),
        dma((count, 2)),
        dma((count,)),
        dma((count, 2)),
        dma((count,)),
        dma((count, TOK - 1)),
    ]


STEP_FIX = 1.0 - 0.5**STEP


def adamw_rows(rate, weights, moment, square, grad, out):
    averaged = 0.5 * moment + 0.5 * grad
    squared = 0.5 * square + 0.5 * grad * grad
    out[0][...] = weights - rate * (
        averaged / STEP_FIX / (jnp.sqrt(squared / STEP_FIX) + 1e-08) + 0.1 * weights
    )
    out[1][...] = averaged
    out[2][...] = squared


RATES = (768 ** (-0.5), 384 ** (-0.5), 11 ** (-0.5), 768 ** (-0.5), 3072 ** (-0.5))


def part_affine(norms, out):
    rows = [jnp.sum(n[0:8, :], axis=0, keepdims=True) for n in norms]
    rows += [jnp.sum(n[8:16, :], axis=0, keepdims=True) for n in norms]
    table = jnp.concatenate(rows + [jnp.zeros((10, 768), jnp.float32)], axis=0)
    lane = lax.broadcasted_iota(jnp.int32, (16, 128), 1)
    for i in range(32):
        tile, shift = (i * EACH) // 128, (i * EACH) % 128
        block = table[:, tile * 128 : (tile + 1) * 128]
        block = pltpu.roll(block, (128 - shift) % 128, 1) if shift else block
        if shift + EACH > 128:
            after = pltpu.roll(table[:, (tile + 1) * 128 : (tile + 2) * 128], 128 - shift, 1)
            block = jnp.where(lane < 128 - shift, block, after)
        out[i] = jnp.where(lane < EACH, block, 0.0).astype(jnp.bfloat16)

GROUPS = 7
T_ROWS = 448
S_PAD = 208
S_ROWS = 416
CHUNK = 768
MLP_CHUNK = 512
SCALE = HEAD_DIM ** (-0.5)
BIG = -1e30
NT = (((1,), (1,)), ((), ()))
TN = (((0,), (0,)), ((), ()))


def dot(left, right, dims=(((1,), (0,)), ((), ()))):
    return lax.dot_general(left, right, dims, preferred_element_type=jnp.float32)


def low(values):
    return values.astype(jnp.bfloat16)


def up(values):
    return values.astype(jnp.float32)


def center_rows(values):
    center = values - jnp.mean(values, axis=-1, keepdims=True)
    inverse = lax.rsqrt(jnp.mean(center * center, axis=-1, keepdims=True) + 1e-06)
    return center * inverse, inverse


def back_rows(upstream, unit, inverse, gain):
    scaled = upstream * gain
    inner = (
        scaled
        - jnp.mean(scaled, axis=-1, keepdims=True)
        - unit * jnp.mean(scaled * unit, axis=-1, keepdims=True)
    )
    return inner * inverse


def fold(values):
    return jnp.sum(values.reshape(-1, 8, values.shape[-1]), axis=0)


def columns(j, width):
    return pl.ds(pl.multiple_of(j * width, 128), width)


def rows_of(i, height):
    return pl.ds(pl.multiple_of(i * height, 8), height)


def times(out, left, weight, width=CHUNK):
    def step(j, carry):
        at = columns(j, width)
        out[:, at] = dot(left[...], weight[:, at]).astype(out.dtype)
        return carry

    lax.fori_loop(0, out.shape[1] // width, step, 0)


def lane_half(shape):
    return lax.broadcasted_iota(jnp.int32, shape, 1) < HEAD_DIM


def soft(query, keys, mask):
    scores = jnp.where(mask, dot(keys, query, NT), BIG)
    expo = jnp.exp(scores - jnp.max(scores, axis=0, keepdims=True))
    return expo * (1.0 / jnp.sum(expo, axis=0, keepdims=True))


def attend(query, keys, values, mask):
    half = lane_half(query.shape)
    zero = jnp.zeros_like(query)
    query = query * jnp.bfloat16(SCALE)
    first = dot(low(soft(jnp.where(half, query, zero), keys, mask)), values, TN)
    second = dot(low(soft(jnp.where(half, zero, query), keys, mask)), values, TN)
    return low(jnp.where(half, first, second))


def attend_back(query, keys, values, upstream, mask):
    half = lane_half(query.shape)
    zero = jnp.zeros_like(query)
    query = query * jnp.bfloat16(SCALE)
    scaled = keys * jnp.bfloat16(SCALE)

    def one(pick):
        probs = soft(pick(query, zero), keys, mask)
        dprobs = dot(values, pick(upstream, zero), NT)
        dscores = low(probs * (dprobs - jnp.sum(dprobs * probs, axis=0, keepdims=True)))
        return dot(dscores, scaled, TN), dot(dscores, query), dot(low(probs), upstream)

    first = one(lambda a, b: jnp.where(half, a, b))
    second = one(lambda a, b: jnp.where(half, b, a))
    return tuple(low(jnp.where(half, a, b)) for a, b in zip(first, second))


def frame_mask(size):
    patch = lambda axis: (lambda i: (i // 64) * 8 + i % 8)(
        lax.broadcasted_iota(jnp.int32, (size, size), axis)
    )
    return patch(0) == patch(1)


def patch_mask():
    return lax.broadcasted_iota(jnp.int32, (S_PAD, S_PAD), 0) < PATCHES


T_BLOCKS = ((0, 192), (192, 256))


def mlp_kernel(lowered, after_s, cotangent, widen, narrow, affine, result, d_narrow, d_widen, d_after, d_norm, cot, turned, total, back):
    j = pl.program_id(0)

    @pl.when(j == 0)
    def start():
        cot[...] = jnp.zeros_like(cot)
        for f in range(2):
            back[pl.ds(f * S_PAD, PATCHES), :] = up(cotangent[f])
            back[pl.ds(f * S_PAD + PATCHES, S_PAD - PATCHES), :] = jnp.zeros((S_PAD - PATCHES, D), jnp.float32)
        cot[...] = low(back[...])
        turned[...] = lowered[...].T
        total[...] = after_s[...]
        back[...] = jnp.zeros_like(back)

    wide = dot(lowered[...], widen[...])
    phi = 0.5 * (1.0 + lax.erf(wide * 0.7071067811865476))
    active = low(wide * phi)
    slope = phi + wide * jnp.exp(-0.5 * wide * wide) * 0.3989422804014327
    d_wide = low(dot(cot[...], narrow[...], NT) * slope)
    total[...] += dot(active, narrow[...])
    d_narrow[...] = low(dot(active, cot[...], TN))
    d_widen[...] = low(dot(turned[...], d_wide))
    back[...] += dot(d_wide, widen[...], NT)

    @pl.when(j == pl.num_programs(0) - 1)
    def finish():
        for f in range(2):
            result[f] = low(total[pl.ds(f * S_PAD, PATCHES), :])

        def norm(b, carry):
            rows = rows_of(b, 32)
            unit, inverse = center_rows(after_s[rows, :])
            upstream = back[rows, :]
            d_after[rows, :] = up(cot[rows, :]) + back_rows(upstream, unit, inverse, affine[2:3, :])
            return carry[0] + fold(upstream * unit), carry[1] + fold(upstream)

        zero = jnp.zeros((8, D), jnp.float32)
        gain, shift = lax.fori_loop(0, S_ROWS // 32, norm, (zero, zero))
        d_norm[0:8, :] = gain
        d_norm[8:16, :] = shift


def mlp(lowered, after_s, cotangent, widen, narrow, affine):
    whole = lambda shape: pl.BlockSpec(shape, lambda j: (0,) * len(shape))
    steps = HID // MLP_CHUNK
    return pl.pallas_call(
        mlp_kernel,
        grid=(steps,),
        in_specs=[
            whole((S_ROWS, D)),
            whole((S_ROWS, D)),
            whole((2, PATCHES, D)),
            pl.BlockSpec((D, MLP_CHUNK), lambda j: (0, j)),
            pl.BlockSpec((MLP_CHUNK, D), lambda j: (j, 0)),
            whole((16, D)),
        ],
        out_specs=[
            whole((2, PATCHES, D)),
            pl.BlockSpec((MLP_CHUNK, D), lambda j: (j, 0)),
            pl.BlockSpec((D, MLP_CHUNK), lambda j: (0, j)),
            whole((S_ROWS, D)),
            whole((16, D)),
        ],
        out_shape=[
            jax.ShapeDtypeStruct((2, PATCHES, D), jnp.bfloat16),
            jax.ShapeDtypeStruct((HID, D), jnp.bfloat16),
            jax.ShapeDtypeStruct((D, HID), jnp.bfloat16),
            jax.ShapeDtypeStruct((S_ROWS, D), jnp.float32),
            jax.ShapeDtypeStruct((16, D), jnp.float32),
        ],
        scratch_shapes=[
            pltpu.VMEM((S_ROWS, D), jnp.bfloat16),
            pltpu.VMEM((D, S_ROWS), jnp.bfloat16),
            pltpu.VMEM((S_ROWS, D), jnp.float32),
            pltpu.VMEM((S_ROWS, D), jnp.float32),
        ],
        compiler_params=pltpu.CompilerParams(vmem_limit_bytes=56 * 1024 * 1024),
        cost_estimate=pl.CostEstimate(flops=12000000000, bytes_accessed=30000000, transcendentals=0),
    )(lowered, after_s, cotangent, widen, narrow, affine)

def pack(box, rows):
    extra = [rows(f, 192, 4) for f in range(2)]
    line = lax.broadcasted_iota(jnp.int32, (16, D), 0)
    for s in range(TOK):
        wide = [rows(f, 48 * s, 48) for f in range(2)]
        for b in range(6):
            pair = [w[8 * b : 8 * b + 8, :] for w in wide]
            box[s, b] = low(jnp.concatenate(pair, axis=0))
        one = [jnp.broadcast_to(e[s : s + 1, :], (16, D)) for e in extra]
        box[s, 6] = low(jnp.where(line == 0, one[0], jnp.where(line == 8, one[1], 0.0)))


def unpack(box, f, put):
    for s in range(TOK):
        for b in range(6):
            slab = up(box[s, b])
            put(48 * s + 8 * b, 8, slab[8 * f : 8 * f + 8, :])
    last = [up(box[s, 6])[8 * f : 8 * f + 1, :] for s in range(TOK)]
    put(192, TOK, jnp.concatenate(last, axis=0))


class Exchange:
    def __init__(self, source, target, sems, flight):
        self.source, self.target, self.flight = source, target, flight
        self.local, self.sent, self.got = sems
        self.clip, self.t = lax.axis_index("clip"), lax.axis_index("tok")

    def copy(self, far):
        return pltpu.make_async_remote_copy(
            src_ref=self.source((self.t + far) % TOK),
            dst_ref=self.target(self.t),
            send_sem=self.sent.at[far - 1],
            recv_sem=self.got.at[far - 1],
            device_id=(self.clip, (self.t + far) % TOK),
            device_id_type=MESH,
        )

    def own(self):
        return pltpu.make_async_copy(self.source(self.t), self.target(self.t), self.local.at[0])

    def start(self):
        for far in range(1, TOK):
            self.flight.go(self.copy(far))
        self.own().start()

    def wait(self):
        for far in range(1, TOK):
            there = self.target((self.t - far + TOK) % TOK)
            pltpu.make_async_copy(there, there, self.got.at[far - 1]).wait()
        self.own().wait()


def exchange_sems():
    dma = pltpu.SemaphoreType.DMA
    return [dma((1,)), dma((TOK - 1,)), dma((TOK - 1,))]


def pieces(count, step, size):
    def run(lo, hi):
        def one(j, carry):
            step(j)
            return carry

        lax.fori_loop(lo, hi, one, 0)

    return [functools.partial(run, lo, min(lo + size, count)) for lo in range(0, count, size)]


def product(out, left, weight, width=CHUNK):
    def step(j):
        at = columns(j, width)
        out[:, at] = dot(left(), weight[:, at]).astype(out.dtype)

    return step


def product_back(out, left, weight, width=CHUNK):
    def step(j):
        at = columns(j, width)
        out[:, at] = dot(left(), weight[at, :], NT).astype(out.dtype)

    return step


def gradient(out, turned, upstream, width=CHUNK):
    def step(j):
        at = columns(j, width)
        out[:, at] = low(dot(turned[...], upstream(at)))

    return step


SUM_START = 5
SUM_RATE = 1.15
SUM_SHIFTS = (0, 1, 2, 3)


def spaced(compute, rest):
    done = 0
    for i, call in enumerate(compute):
        call()
        while done < len(rest) and SUM_START + done * SUM_RATE <= i + 1:
            rest[done]()
            done += 1
    for call in rest[done:]:
        call()


def full_kernel_steps(units, steps, shifts, lo, hi):
    calls = []
    for n in range(lo, hi):
        for shift, step in zip(shifts, steps):
            if 0 <= n - shift < len(units):
                calls.append(functools.partial(step, n - shift))
    return calls


A2A_AT = 10


def gather_head(units):
    count = len(units)
    last = [n for n in range(count) if units[n][0] == 1][-1]
    names = ("begin", "along", "crossing", "corner")
    calls = []
    for n in range(last + 3):
        calls += [(name, n - shift) for shift, name in enumerate(names) if 0 <= n - shift < count]
    return calls + [("begin", last + 3), ("along", last + 2), ("corner", last)]


def forward_kernel(units, *refs):
    masters, block, frames = refs[:5], refs[5], refs[6]
    full = list(refs[7:12])
    affine, early_out, mixed_s, after_s, lowered = refs[12], refs[13:21], refs[21], refs[22], refs[23]
    owned, gathered = list(refs[24:29]), refs[29]
    entry_w, temporal_w, spatial_w, outbox, sent, inbox, load_sem = refs[30:37]
    early = refs[37:45]
    patch, normed_t, merged_t, mixed_t, first_t, after_t, normed_s, merged_s = early
    there_sems, back_sems = refs[45:48], refs[48:51]
    sems = refs[51:]
    stores = [
        pltpu.make_async_copy(a, b, load_sem.at[4 + i]) for i, (a, b) in enumerate(zip(early, early_out))
    ]

    def store(lo, hi):
        def begin_stores():
            for copy in stores[lo:hi]:
                copy.start()

        return [begin_stores]

    greet()
    full.append(gathered)
    owned.append(block)
    flight = Flight()
    begin, along, crossing, corner, settle, drain = gather_steps(units, owned, full, sems)
    count = len(units)
    place = {k: [n for n in range(count) if units[n][0] == k] for k in range(6)}
    there = Exchange(lambda s: outbox.at[s], lambda s: patch.at[:, s], there_sems, flight)
    back = Exchange(lambda s: sent.at[:, s], lambda s: inbox.at[s], back_sems, flight)
    def settle_all(k):
        for n in place[k]:
            settle(n)

    ready = set()
    original = begin

    def begin(n):
        k = units[n][0]
        if k not in ready and k != AFFINE:
            rows_from(masters[k], owned[k])
            ready.add(k)
        original(n)

    steps = {"begin": begin, "along": along, "crossing": crossing, "corner": corner}
    head = [functools.partial(steps[name], n) for name, n in gather_head(units)]
    step = lambda name, n: [functools.partial(steps[name], n)]
    for call in head[:A2A_AT]:
        call()
    pack(outbox, lambda f, start, size: up(frames[f, start : start + size, :]))
    there.start()
    for call in head[A2A_AT:]:
        call()

    def load(part, source, target):
        return pltpu.make_async_copy(source, target, load_sem.at[part])

    loads = {
        "entry": load(0, full[0].at[pl.ds(0, 16)], entry_w),
        "temporal": load(1, full[1], temporal_w),
        "later": load(2, full[0].at[pl.ds(16, 16)], entry_w),
        "spatial": load(3, full[2], spatial_w),
    }
    settle_all(AFFINE)
    join_affine(gathered, affine)
    there.wait()

    def norm_t(b):
        unit, unused = center_rows(up(patch[b].reshape(64, D)))
        normed_t[rows_of(b, 64), :] = low(unit * affine[0:1, :] + affine[3:4, :])

    def heads_t(p):
        found = []
        for start, size in T_BLOCKS:
            rows = pl.ds(start, size)
            query, keys, values = (merged_t[rows, columns(p + 6 * i, 128)] for i in range(3))
            found.append(attend(query, keys, values, frame_mask(size)))
        for (start, size), value in zip(T_BLOCKS, found):
            mixed_t[pl.ds(start, size), columns(p, 128)] = value

    entry_m = lambda at: entry_w[:, :, at].reshape(D, CHUNK)

    def merge(out, left):
        def step(j):
            at = columns(j, CHUNK)
            out[:, at] = low(dot(left[...], entry_m(at)))

        return step

    def first_step(j):
        at = columns(j, CHUNK)
        first_t[:, at] = low(dot(mixed_t[...], temporal_w[0:16, :, at].reshape(D, CHUNK)))

    def branch_step(j):
        at = columns(j, CHUNK)
        value = low(dot(first_t[...], temporal_w[16:32, :, at].reshape(D, CHUNK)))
        sent[:, :, :, at] = value.reshape(GROUPS, TOK, 16, CHUNK)

    def start_temporal():
        settle_all(0)
        settle_all(1)
        loads["entry"].start()
        loads["temporal"].start()
        for call in pieces(GROUPS, norm_t, GROUPS):
            call()
        loads["entry"].wait()
        loads["temporal"].wait()

    def start_spatial():
        settle_all(2)
        loads["later"].start()
        loads["spatial"].start()
        back.wait()
        for f in range(2):

            def put(start, size, rows, f=f):
                after_t[f * S_PAD + start : f * S_PAD + start + size, :] = (
                    up(frames[f, start : start + size, :]) + rows
                )

            unpack(inbox, f, put)
            tail = f * S_PAD + PATCHES
            after_t[tail : (f + 1) * S_PAD, :] = jnp.zeros((S_PAD - PATCHES, D), jnp.float32)

    def norm_s(b):
        unit, unused = center_rows(after_t[rows_of(b, 32), :])
        normed_s[rows_of(b, 32), :] = low(unit * affine[1:2, :] + affine[4:5, :])

    def wait_spatial():
        loads["later"].wait()
        loads["spatial"].wait()

    def heads_s(p):
        found = []
        for f in range(2):
            rows = pl.ds(f * S_PAD, S_PAD)
            query, keys, values = (merged_s[rows, columns(p + 6 * i, 128)] for i in range(3))
            found.append(attend(query, keys, values, patch_mask()))
        for f in range(2):
            mixed_s[pl.ds(f * S_PAD, S_PAD), columns(p, 128)] = found[f]

    def out_s(j):
        at = columns(j, CHUNK)
        weight = low(up(spatial_w[:, :, at]).reshape(D, CHUNK))
        after_s[:, at] = after_t[:, at] + dot(mixed_s[...], weight)

    def norm_m(b):
        unit, unused = center_rows(after_s[rows_of(b, 32), :])
        lowered[rows_of(b, 32), :] = low(unit * affine[2:3, :] + affine[5:6, :])

    order = (
        [start_temporal]
        + pieces(3, merge(merged_t, normed_t), 1)
        + step("crossing", 3)
        + step("along", 5)
        + step("corner", 3)
        + pieces(6, heads_t, 2)
        + step("crossing", 4)
        + pieces(1, first_step, 1)
        + pieces(1, branch_step, 1)
        + [back.start]
        + store(0, 5)
        + step("corner", 4)
        + step("crossing", 5)
        + [start_spatial]
        + pieces(13, norm_s, 13)
        + [wait_spatial]
        + pieces(3, merge(merged_s, normed_s), 1)
        + pieces(6, heads_s, 3)
        + store(5, 8)
        + step("corner", 5)
        + pieces(1, out_s, 1)
        + pieces(13, norm_m, 13)
    )
    for call in order:
        call()
    for k in (3, 4):
        settle_all(k)
    drain()
    flight.drain()
    for copy in stores:
        copy.wait()


def forward(masters, block, frames):
    units = units_of(ORDER_IN, HID)
    vmem = pl.BlockSpec(memory_space=pltpu.VMEM)
    anywhere = pl.BlockSpec(memory_space=pl.ANY)
    bf16, f32 = jnp.bfloat16, jnp.float32
    slab = (TOK, GROUPS, 16, D)
    group = (GROUPS, TOK, 16, D)
    saved = [
        ((16, D), f32),
        (group, bf16),
        ((T_ROWS, D), bf16),
        ((T_ROWS, 3 * D), bf16),
        ((T_ROWS, D), bf16),
        ((T_ROWS, D), bf16),
        ((S_ROWS, D), f32),
        ((S_ROWS, D), bf16),
        ((S_ROWS, 3 * D), bf16),
        ((S_ROWS, D), bf16),
        ((S_ROWS, D), f32),
        ((S_ROWS, D), bf16),
    ]
    early = [pltpu.VMEM(s, t) for s, t in saved[1:9]]
    return pl.pallas_call(
        functools.partial(forward_kernel, units),
        out_shape=[jax.ShapeDtypeStruct((32, r, w), bf16) for r, w in zip(ROWS, WIDTHS)]
        + [jax.ShapeDtypeStruct(s, t) for s, t in saved],
        in_specs=[vmem] * 7,
        out_specs=[anywhere] * 5 + [vmem] + [anywhere] * 8 + [vmem] * 3,
        scratch_shapes=[pltpu.VMEM((r, w), bf16) for r, w in zip(ROWS, WIDTHS)]
        + [
            pltpu.VMEM((32, 16, 128), bf16),
            pltpu.VMEM((16, 48, 3 * D), bf16),
            pltpu.VMEM((32, 48, D), bf16),
            pltpu.VMEM((32, 24, D), bf16),
            pltpu.VMEM(slab, bf16),
            pltpu.VMEM(group, bf16),
            pltpu.VMEM(slab, bf16),
            pltpu.SemaphoreType.DMA((12,)),
        ]
        + early
        + exchange_sems()
        + exchange_sems()
        + gather_sems(len(units)),
        compiler_params=pltpu.CompilerParams(
            collective_id=0, has_side_effects=True, vmem_limit_bytes=VMEM_LIMIT
        ),
    )(*masters, block, frames)


def finals_of(grads, affine_out=None):
    def finals(unit, total):
        k, c, width = unit
        if k == AFFINE:
            affine_out[...] = total
            return
        n, rows = WIDTHS[k] // 128, ROWS[k]
        for i in range(width // 128):
            grads[k][pl.ds(c // 128 + i, rows, stride=n), :] = total[:, i * 128 : (i + 1) * 128]

    return finals


def back_kernel(units, *refs):
    parts = dict(zip((3, 4), refs[:2]))
    d_after_s, after_t, affine, spatial = refs[2:6]
    normed_s_in, merged_s_in, mixed_s_in, entry_in = refs[6:10]
    patch_in, normed_t_in, merged_t_in, mixed_t_in, first_t_in, temporal_in = refs[10:16]
    grads = dict(zip((2, 3, 4), refs[16:19]))
    sent, d_after_t, d_entry_out, d_temporal, norm_s_out, norm_t_out = refs[19:25]
    pos = 25
    pools = []
    for i in range(5):
        pools.append(refs[pos : pos + len(units)])
        pos += len(units)
    parts[2] = refs[pos]
    pos += 1
    normed_s, merged_s, mixed_s, entry_w = refs[pos : pos + 4]
    patch, normed_t, merged_t, mixed_t, first_t, temporal_w = refs[pos + 4 : pos + 10]
    d_entry, lowered, d_mixed, d_first, d_merged, turned_s, turned_t, back, outbox, grouped, load_sem = refs[
        pos + 10 : pos + 21
    ]
    pos += 21
    there_sems = refs[pos : pos + 3]
    sems = refs[pos + 3 :]
    sources = (normed_s_in, merged_s_in, mixed_s_in, entry_in.at[1])
    targets = (normed_s, merged_s, mixed_s, entry_w)
    sources += (patch_in, normed_t_in, merged_t_in, mixed_t_in, first_t_in, temporal_in)
    targets += (patch, normed_t, merged_t, mixed_t, first_t, temporal_w)
    loads = [pltpu.make_async_copy(a, b, load_sem.at[i]) for i, (a, b) in enumerate(zip(sources, targets))]
    for copy in loads:
        copy.start()
    entry_load = pltpu.make_async_copy(entry_in.at[0], entry_w, load_sem.at[10])
    entry_stores = [pltpu.make_async_copy(d_entry, d_entry_out.at[i], load_sem.at[12 - i]) for i in range(2)]
    greet()
    flight = Flight()
    finals = finals_of(grads)
    steps = scatter_steps(
        units, parts, *pools, sems, lambda u, total: finals(units[u], total)
    )
    there = Exchange(lambda s: outbox.at[s], lambda s: grouped.at[:, s], there_sems, flight)
    zero = jnp.zeros((8, D), jnp.float32)

    def begin_s():
        lowered[...] = low(d_after_s[...])
        for copy in loads[:3]:
            copy.wait()
        turned_s[...] = mixed_s[...].T

    def turn_s():
        turned_s[...] = normed_s[...].T

    def heads_s(p):
        found = []
        for f in range(2):
            rows = pl.ds(f * S_PAD, S_PAD)
            query, keys, values = (merged_s[rows, columns(p + 6 * i, 128)] for i in range(3))
            found.append(
                attend_back(query, keys, values, d_mixed[rows, columns(p, 128)], patch_mask())
            )
        for f in range(2):
            for i in range(3):
                d_merged[pl.ds(f * S_PAD, S_PAD), columns(p + 6 * i, 128)] = found[f][i]

    def s_back(j):
        at = columns(j, CHUNK)
        back[0:S_ROWS, at] = dot(d_merged[0:S_ROWS, :], entry_w[at, :], NT)

    def end_s():
        entry_load.start()

        def norm(b, carry):
            rows = rows_of(b, 32)
            unit, inverse = center_rows(after_t[rows, :])
            upstream = back[rows, :]
            d_after_t[rows, :] = d_after_s[rows, :] + back_rows(upstream, unit, inverse, affine[1:2, :])
            return carry[0] + fold(upstream * unit), carry[1] + fold(upstream)

        gain, shift = lax.fori_loop(0, S_ROWS // 32, norm, (zero, zero))
        norm_s_out[0:8, :] = gain
        norm_s_out[8:16, :] = shift
        pack(outbox, lambda f, start, size: d_after_t[f * S_PAD + start : f * S_PAD + start + size, :])
        there.start()

    def wait_entry():
        loads[3].wait()

    def spatial_sum():
        parts[2][...] = low(dot(turned_s[...], lowered[...]).reshape(32, 24, D))
        steps[0](len(units) - 1)

    d_mixed_s = d_mixed.at[0:S_ROWS]
    compute = (
        [begin_s]
        + [spatial_sum]
        + pieces(1, product_back(d_mixed_s, lambda: lowered[...], spatial), 1)
        + [turn_s]
        + pieces(6, heads_s, 1)
        + [wait_entry]
        + pieces(1, s_back, 1)
        + [end_s]
        + pieces(3, gradient(d_entry, turned_s, lambda at: d_merged[0:S_ROWS, at]), 1)
        + [entry_stores[1].start]
    )

    def begin_t():
        for copy in loads[4:]:
            copy.wait()
        turned_t[...] = first_t[...].T
        there.wait()

    group_cols = lambda at: grouped[:, :, :, at].reshape(T_ROWS, CHUNK)

    def turn_mixed():
        turned_t[...] = mixed_t[...].T

    def turn_normed():
        turned_t[...] = normed_t[...].T

    def heads_t(p):
        found = []
        for start, size in T_BLOCKS:
            rows = pl.ds(start, size)
            query, keys, values = (merged_t[rows, columns(p + 6 * i, 128)] for i in range(3))
            found.append(
                attend_back(query, keys, values, d_mixed[rows, columns(p, 128)], frame_mask(size))
            )
        for (start, size), values in zip(T_BLOCKS, found):
            for i in range(3):
                d_merged[pl.ds(start, size), columns(p + 6 * i, 128)] = values[i]

    def t_back(j):
        at = columns(j, CHUNK)
        back[:, at] = dot(d_merged[...], entry_w[at, :], NT)

    def end_t():
        def norm(b, carry):
            rows = rows_of(b, 64)
            unit, inverse = center_rows(up(patch[b].reshape(64, D)))
            upstream = back[rows, :]
            value = back_rows(upstream, unit, inverse, affine[0:1, :])
            sent[b] = low(value).reshape(TOK, 16, D)
            return carry[0] + fold(upstream * unit), carry[1] + fold(upstream)

        gain, shift = lax.fori_loop(0, GROUPS, norm, (zero, zero))
        norm_t_out[0:8, :] = gain
        norm_t_out[8:16, :] = shift

    def free_entry():
        entry_stores[1].wait()
        entry_load.wait()

    compute += (
        [begin_t]
        + pieces(1, gradient(d_temporal.at[1], turned_t, group_cols), 1)
        + pieces(1, product_back(d_first, lambda: grouped[...].reshape(T_ROWS, D), temporal_w.at[1]), 1)
        + [turn_mixed]
        + pieces(1, gradient(d_temporal.at[0], turned_t, lambda at: d_first[:, at]), 1)
        + pieces(1, product_back(d_mixed, lambda: d_first[...], temporal_w.at[0]), 1)
        + [turn_normed]
        + pieces(6, heads_t, 1)
        + [free_entry]
        + pieces(1, t_back, 1)
        + [end_t]
        + pieces(3, gradient(d_entry, turned_t, lambda at: d_merged[:, at]), 1)
        + [entry_stores[0].start]
    )
    for u in range(len(units) - 1):
        steps[0](u)
    rest = full_kernel_steps(units, steps[1:5], SUM_SHIFTS, 0, len(units) + SUM_SHIFTS[-1])
    spaced(compute, rest)
    entry_stores[0].wait()
    steps[5]()
    flight.drain()


def backward(parts, d_after_s, after_t, affine, spatial, entry, temporal, saved_s, saved_t):
    units = units_of(ORDER_MLP)
    vmem = pl.BlockSpec(memory_space=pltpu.VMEM)
    anywhere = pl.BlockSpec(memory_space=pl.ANY)
    bf16, f32 = jnp.bfloat16, jnp.float32
    flat = [(ROWS[k] * WIDTHS[k] // 128, 128) for k in (2, 3, 4)]
    slab = (TOK, GROUPS, 16, D)
    group = (GROUPS, TOK, 16, D)
    outs = [(s, f32) for s in flat] + [
        (group, bf16),
        ((S_ROWS, D), f32),
        ((2, D, 3 * D), bf16),
        ((2, D, D), bf16),
        ((16, D), f32),
        ((16, D), f32),
    ]
    return pl.pallas_call(
        functools.partial(back_kernel, units),
        out_shape=[jax.ShapeDtypeStruct(s, t) for s, t in outs],
        in_specs=[anywhere] * 2 + [vmem] * 4 + [anywhere] * 10,
        out_specs=[vmem] * 5 + [anywhere] + [vmem] * 3,
        scratch_shapes=scatter_scratch(units)
        + [
            pltpu.VMEM((32, 24, D), bf16),
            pltpu.VMEM((S_ROWS, D), bf16),
            pltpu.VMEM((S_ROWS, 3 * D), bf16),
            pltpu.VMEM((S_ROWS, D), bf16),
            pltpu.VMEM((D, 3 * D), bf16),
            pltpu.VMEM(group, bf16),
            pltpu.VMEM((T_ROWS, D), bf16),
            pltpu.VMEM((T_ROWS, 3 * D), bf16),
            pltpu.VMEM((T_ROWS, D), bf16),
            pltpu.VMEM((T_ROWS, D), bf16),
            pltpu.VMEM((2, D, D), bf16),
            pltpu.VMEM((D, 3 * D), bf16),
            pltpu.VMEM((S_ROWS, D), bf16),
            pltpu.VMEM((T_ROWS, D), bf16),
            pltpu.VMEM((T_ROWS, D), bf16),
            pltpu.VMEM((T_ROWS, 3 * D), bf16),
            pltpu.VMEM((D, S_ROWS), bf16),
            pltpu.VMEM((D, T_ROWS), bf16),
            pltpu.VMEM((T_ROWS, D), f32),
            pltpu.VMEM(slab, bf16),
            pltpu.VMEM(group, bf16),
            pltpu.SemaphoreType.DMA((13,)),
        ]
        + exchange_sems()
        + scatter_sems(len(units)),
        compiler_params=pltpu.CompilerParams(
            collective_id=1, has_side_effects=True, vmem_limit_bytes=VMEM_LIMIT
        ),
    )(*parts, d_after_s, after_t, affine, spatial, *saved_s, entry, *saved_t, temporal)


HOME_AT = 4
HOME_END = 24


def rest_kernel(units, *refs):
    parts = dict(zip((0, 1), refs[:2]))
    norms = refs[2:5]
    sent, d_after_t = refs[5:7]
    grads = dict(zip((0, 1), refs[7:9]))
    affine_out, input_gradient = refs[9:11]
    pos = 11
    pools = []
    for i in range(5):
        pools.append(refs[pos : pos + len(units)])
        pos += len(units)
    parts[AFFINE] = refs[pos]
    inbox, home_sems = refs[pos + 1], refs[pos + 2 : pos + 5]
    sems = refs[pos + 5 :]
    greet()
    flight = Flight()
    home = Exchange(lambda s: sent.at[:, s], lambda s: inbox.at[s], home_sems, flight)
    finals = finals_of(grads, affine_out)
    steps = scatter_steps(
        units, parts, *pools, sems, lambda u, total: finals(units[u], total)
    )
    begin = steps[0]

    def begin_after(u):
        if units[u][0] == AFFINE:
            part_affine(norms, parts[AFFINE])
        begin(u)

    def receive():
        home.wait()
        for f in range(2):

            def put(start, size, rows, f=f):
                at = f * S_PAD + start
                input_gradient[f, start : start + size, :] = d_after_t[at : at + size, :] + rows

            unpack(inbox, f, put)

    calls = full_kernel_steps(units, (begin_after,) + steps[1:5], (0, 2, 3, 4, 5), 0, len(units) + 5)
    calls.insert(HOME_AT, home.start)
    calls.insert(HOME_END, receive)
    for call in calls:
        call()
    steps[5]()
    flight.drain()


def scatter_rest(parts, norms, sent, d_after_t):
    units = units_of(ORDER_REST)
    vmem = pl.BlockSpec(memory_space=pltpu.VMEM)
    flat = [(ROWS[k] * WIDTHS[k] // 128, 128) for k in (0, 1)]
    return pl.pallas_call(
        functools.partial(rest_kernel, units),
        out_shape=[jax.ShapeDtypeStruct(s, jnp.float32) for s in flat]
        + [
            jax.ShapeDtypeStruct((16, 128), jnp.float32),
            jax.ShapeDtypeStruct((2, PATCHES, D), jnp.float32),
        ],
        in_specs=[pl.BlockSpec(memory_space=pl.ANY)] * 2 + [vmem] * 5,
        out_specs=[vmem] * 4,
        scratch_shapes=scatter_scratch(units)
        + [pltpu.VMEM((32, 16, 128), jnp.bfloat16)]
        + [pltpu.VMEM((TOK, GROUPS, 16, D), jnp.bfloat16)]
        + exchange_sems()
        + scatter_sems(len(units)),
        compiler_params=pltpu.CompilerParams(
            collective_id=2, has_side_effects=True, vmem_limit_bytes=VMEM_LIMIT
        ),
    )(*parts, *norms, sent, d_after_t)


def update_kernel(*refs):
    for k in range(5):
        weights, moment, square = (refs[5 + 3 * k + i][...] for i in range(3))
        adamw_rows(RATES[k], weights, moment, square, refs[k][...], refs[20 + 3 * k : 23 + 3 * k])


def update(grads, states):
    steps = 6
    blocks = [pl.BlockSpec((g.shape[0] // steps, 128), lambda i: (i, 0)) for g in grads]
    triples = [b for b in blocks for _ in range(3)]
    return pl.pallas_call(
        update_kernel,
        grid=(steps,),
        out_shape=[jax.ShapeDtypeStruct(s.shape, jnp.float32) for s in states],
        in_specs=blocks + triples,
        out_specs=triples,
    )(*grads, *states)


def on_device(
    frames,
    cotangent,
    entry_weights,
    entry_momentum,
    entry_variance,
    temporal_weights,
    temporal_momentum,
    temporal_variance,
    spatial_weights,
    spatial_momentum,
    spatial_variance,
    widen_weights,
    widen_momentum,
    widen_variance,
    narrow_weights,
    narrow_momentum,
    narrow_variance,
    norm_affine,
    affine_momentum,
    affine_variance,
):
    masters = (entry_weights, temporal_weights, spatial_weights, widen_weights, narrow_weights)
    block = jnp.pad(low(norm_affine).reshape(6, EACH), ((0, 10), (0, 128 - EACH)))
    found = forward(masters, block, frames[0])
    entry, temporal, spatial, widen, narrow = found[:5]
    entry = entry.reshape(2, D, 3 * D)
    temporal = temporal.reshape(2, D, D)
    spatial = spatial.reshape(D, D)
    widen = widen.reshape(D, HID)
    narrow = narrow.reshape(HID, D)
    affine, patch, normed_t, merged_t, mixed_t, first_t = found[5:11]
    after_t, normed_s, merged_s, mixed_s, after_s, lowered = found[11:17]
    result, narrow_grad, widen_grad, d_after_s, norm_m = mlp(
        lowered, after_s, cotangent[0], widen, narrow, affine
    )
    found = backward(
        (widen_grad.reshape(32, -1, HID), narrow_grad.reshape(32, -1, D)),
        d_after_s,
        after_t,
        affine,
        spatial,
        entry,
        temporal,
        (normed_s, merged_s, mixed_s),
        (patch, normed_t, merged_t, mixed_t, first_t),
    )
    spatial_sum, widen_sum, narrow_sum = found[:3]
    sent, d_after_t, d_entry, d_temporal, norm_s, norm_t = found[3:9]
    entry_sum, temporal_sum, affine_sum, input_gradient = scatter_rest(
        (d_entry.reshape(32, -1, 3 * D), d_temporal.reshape(32, -1, D)),
        (norm_t, norm_s, norm_m),
        sent,
        d_after_t,
    )
    updated = update(
        (entry_sum, temporal_sum, spatial_sum, widen_sum, narrow_sum),
        (
            entry_weights,
            entry_momentum,
            entry_variance,
            temporal_weights,
            temporal_momentum,
            temporal_variance,
            spatial_weights,
            spatial_momentum,
            spatial_variance,
            widen_weights,
            widen_momentum,
            widen_variance,
            narrow_weights,
            narrow_momentum,
            narrow_variance,
        ),
    )
    affine_sum = affine_sum[:6, :EACH].reshape(2, 3, EACH)
    affine_new = adamw(norm_affine, affine_momentum, affine_variance, affine_sum, 0.5)
    return (
        result[None],
        input_gradient[None],
        *updated,
        affine_new[0],
        affine_new[1],
        affine_new[2][:, 0:2],
        affine_new[2][:, 2],
    )

def solution(mesh):
    return jax.shard_map(
        on_device if mesh.shape["clip"] == 8 and mesh.shape["tok"] == TOK else on_any,
        mesh=mesh,
        in_specs=(
            P("clip", "tok", None, None),
            P("clip", "tok", None, None),
            P(("clip", "tok"), None),
            P(("clip", "tok"), None),
            P(("clip", "tok"), None),
            P(("clip", "tok"), None),
            P(("clip", "tok"), None),
            P(("clip", "tok"), None),
            P(("clip", "tok"), None),
            P(("clip", "tok"), None),
            P(("clip", "tok"), None),
            P(("clip", "tok"), None),
            P(("clip", "tok"), None),
            P(("clip", "tok"), None),
            P(("clip", "tok"), None),
            P(("clip", "tok"), None),
            P(("clip", "tok"), None),
            P(None, None, ("clip", "tok")),
            P(None, None, ("clip", "tok")),
            P(None, None, ("clip", "tok")),
        ),
        out_specs=(
            P("clip", "tok", None, None),
            P("clip", "tok", None, None),
            P(("clip", "tok"), None),
            P(("clip", "tok"), None),
            P(("clip", "tok"), None),
            P(("clip", "tok"), None),
            P(("clip", "tok"), None),
            P(("clip", "tok"), None),
            P(("clip", "tok"), None),
            P(("clip", "tok"), None),
            P(("clip", "tok"), None),
            P(("clip", "tok"), None),
            P(("clip", "tok"), None),
            P(("clip", "tok"), None),
            P(("clip", "tok"), None),
            P(("clip", "tok"), None),
            P(("clip", "tok"), None),
            P(None, None, ("clip", "tok")),
            P(None, None, ("clip", "tok")),
            P(None, None, ("clip", "tok")),
            P(None, ("clip", "tok")),
        ),
        check_vma=False,
    )
```

```python
import functools

import jax
import jax.numpy as jnp
from jax import lax
from jax.experimental import pallas as pl
from jax.experimental.pallas import tpu as pltpu
from jax.sharding import PartitionSpec as P

D = 768
HEADS = 12
HEAD_DIM = 64
HID = 3072
PATCHES = 196
STEP = 5

time_scores = "cfphe,cgphe->cphfg"
time_mixed = "cphfg,cgphe->cfphe"
time_flip = "cphfg,cfphe->cgphe"
space_scores = "cfphe,cfqhe->cfhpq"
space_mixed = "cfhpq,cfqhe->cfphe"
space_flip = "cfhpq,cfphe->cfqhe"


def project(inputs, weight):
    return jnp.einsum("cfpa,ab->cfpb", inputs, weight, preferred_element_type=jnp.float32)


def project_back(upstream, weight):
    return jnp.einsum("cfpb,ab->cfpa", upstream, weight, preferred_element_type=jnp.float32)


def weight_sum(inputs, upstream):
    return jnp.einsum("cfpa,cfpb->ab", inputs, upstream, preferred_element_type=jnp.float32)


def layer_norm(values, gain, shift):
    center = values - jnp.mean(values, axis=-1, keepdims=True)
    inverse = lax.rsqrt(jnp.mean(center * center, axis=-1, keepdims=True) + 1e-06)
    unit = center * inverse
    return (unit * gain + shift, unit, inverse)


def norm_back(upstream, unit, inverse, gain):
    scaled = upstream * gain
    inner = (
        scaled
        - jnp.mean(scaled, axis=-1, keepdims=True)
        - unit * jnp.mean(scaled * unit, axis=-1, keepdims=True)
    )
    return (
        inner * inverse,
        jnp.sum(upstream * unit, axis=(0, 1, 2)),
        jnp.sum(upstream, axis=(0, 1, 2)),
    )


def split_heads(merged):
    lowered = merged.astype(jnp.bfloat16)
    parts = lowered.reshape(lowered.shape[:-1] + (3, HEADS, HEAD_DIM))
    return (parts[..., 0, :, :], parts[..., 1, :, :], parts[..., 2, :, :])


def attend_forward(heads, score_form, mixed_form):
    query, keys, values = heads
    scores = jnp.einsum(score_form, query, keys, preferred_element_type=jnp.float32) * HEAD_DIM ** (
        -0.5
    )
    top = jnp.max(scores, axis=-1, keepdims=True)
    expo = jnp.exp(scores - top)
    total = jnp.sum(expo, axis=-1, keepdims=True)
    probs = (expo / total).astype(jnp.bfloat16)
    mixed = jnp.einsum(mixed_form, probs, values, preferred_element_type=jnp.float32)
    joined = mixed.reshape(mixed.shape[:-2] + (HEADS * HEAD_DIM,)).astype(jnp.bfloat16)
    return (joined, top + jnp.log(total))


def attend_backward(heads, logsum, upstream_joined, score_form, mixed_form, flip_form):
    query, keys, values = heads
    upstream = upstream_joined.reshape(upstream_joined.shape[:-1] + (HEADS, HEAD_DIM))
    scale = HEAD_DIM ** (-0.5)
    scores = jnp.einsum(score_form, query, keys, preferred_element_type=jnp.float32) * scale
    probs = jnp.exp(scores - logsum)
    dprobs = jnp.einsum(score_form, upstream, values, preferred_element_type=jnp.float32)
    dscores = (probs * (dprobs - jnp.sum(dprobs * probs, axis=-1, keepdims=True))).astype(
        jnp.bfloat16
    )
    dquery = jnp.einsum(mixed_form, dscores, keys, preferred_element_type=jnp.float32) * scale
    dkeys = jnp.einsum(flip_form, dscores, query, preferred_element_type=jnp.float32) * scale
    dvalues = jnp.einsum(
        flip_form, probs.astype(jnp.bfloat16), upstream, preferred_element_type=jnp.float32
    )
    stacked = jnp.stack([dquery, dkeys, dvalues], axis=-3)
    return stacked.reshape(stacked.shape[:-3] + (3 * HEADS * HEAD_DIM,)).astype(jnp.bfloat16)


def collect(masters):
    gathered = (
        lax.all_gather(masters[0].astype(jnp.bfloat16), ("clip", "tok"), axis=0, tiled=True),
        lax.all_gather(masters[1].astype(jnp.bfloat16), ("clip", "tok"), axis=0, tiled=True),
        lax.all_gather(masters[2].astype(jnp.bfloat16), ("clip", "tok"), axis=0, tiled=True),
        lax.all_gather(masters[3].astype(jnp.bfloat16), ("clip", "tok"), axis=0, tiled=True),
        lax.all_gather(masters[4].astype(jnp.bfloat16), ("clip", "tok"), axis=0, tiled=True),
        lax.all_gather(masters[5].astype(jnp.bfloat16), ("clip", "tok"), axis=2, tiled=True),
    )
    return (
        gathered[0].reshape(2, D, 3 * D),
        gathered[1].reshape(2, D, D),
        gathered[2].reshape(D, D),
        gathered[3].reshape(D, HID),
        gathered[4].reshape(HID, D),
        gathered[5],
    )


def plain_forward(frames, masters):
    weights = collect(masters)
    entry, temporal, spatial, widen, narrow, affine = weights
    gains = affine.astype(jnp.float32)
    patchwise = lax.all_to_all(frames, "tok", split_axis=2, concat_axis=1, tiled=True)
    normed_t, unit_t, inverse_t = layer_norm(
        patchwise.astype(jnp.float32), gains[0, 0], gains[1, 0]
    )
    lowered_t = normed_t.astype(jnp.bfloat16)
    heads_t = split_heads(project(lowered_t, entry[0]))
    mixed_t, lse_t = attend_forward(heads_t, time_scores, time_mixed)
    first_t = project(mixed_t, temporal[0]).astype(jnp.bfloat16)
    branch = project(first_t, temporal[1]).astype(jnp.bfloat16)
    returned = lax.all_to_all(branch, "tok", split_axis=1, concat_axis=2, tiled=True)
    after_t = frames.astype(jnp.float32) + returned.astype(jnp.float32)
    normed_s, unit_s, inverse_s = layer_norm(after_t, gains[0, 1], gains[1, 1])
    lowered_s = normed_s.astype(jnp.bfloat16)
    heads_s = split_heads(project(lowered_s, entry[1]))
    mixed_s, lse_s = attend_forward(heads_s, space_scores, space_mixed)
    after_s = after_t + project(mixed_s, spatial)
    normed_m, unit_m, inverse_m = layer_norm(after_s, gains[0, 2], gains[1, 2])
    lowered_m = normed_m.astype(jnp.bfloat16)
    widened = project(lowered_m, widen)
    activated = jax.nn.gelu(widened, approximate=False).astype(jnp.bfloat16)
    result = (after_s + project(activated, narrow)).astype(jnp.bfloat16)
    saved = {
        "weights": weights,
        "unit_t": unit_t,
        "inverse_t": inverse_t,
        "lowered_t": lowered_t,
        "heads_t": heads_t,
        "lse_t": lse_t,
        "mixed_t": mixed_t,
        "first_t": first_t,
        "unit_s": unit_s,
        "inverse_s": inverse_s,
        "lowered_s": lowered_s,
        "heads_s": heads_s,
        "lse_s": lse_s,
        "mixed_s": mixed_s,
        "unit_m": unit_m,
        "inverse_m": inverse_m,
        "lowered_m": lowered_m,
        "widened": widened,
        "activated": activated,
    }
    return (result, saved)


def adamw(master, moment, square, grad, rate):
    fix = 1.0 - 0.5**STEP
    averaged = 0.5 * moment + 0.5 * grad
    squared = 0.5 * square + 0.5 * grad * grad
    updated = master - rate * (averaged / fix / (jnp.sqrt(squared / fix) + 1e-08) + 0.1 * master)
    return (updated, averaged, squared)

def on_any(
    frames,
    cotangent,
    entry_weights,
    entry_momentum,
    entry_variance,
    temporal_weights,
    temporal_momentum,
    temporal_variance,
    spatial_weights,
    spatial_momentum,
    spatial_variance,
    widen_weights,
    widen_momentum,
    widen_variance,
    narrow_weights,
    narrow_momentum,
    narrow_variance,
    norm_affine,
    affine_momentum,
    affine_variance,
):
    masters = (
        entry_weights,
        temporal_weights,
        spatial_weights,
        widen_weights,
        narrow_weights,
        norm_affine,
    )
    result, saved = plain_forward(frames, masters)
    entry, temporal, spatial, widen, narrow, affine = saved["weights"]
    gains = affine.astype(jnp.float32)
    narrow_grad = weight_sum(saved["activated"], cotangent)
    widened = saved["widened"]
    slope = (
        0.5 * (1.0 + lax.erf(widened * 0.7071067811865476))
        + widened * jnp.exp(-0.5 * widened * widened) * 0.3989422804014327
    )
    dwidened = (project_back(cotangent, narrow) * slope).astype(jnp.bfloat16)
    widen_grad = weight_sum(saved["lowered_m"], dwidened)
    dpart_m, gain_m, shift_m = norm_back(
        project_back(dwidened, widen), saved["unit_m"], saved["inverse_m"], gains[0, 2]
    )
    dafter_s = cotangent.astype(jnp.float32) + dpart_m
    dspatial = dafter_s.astype(jnp.bfloat16)
    spatial_grad = weight_sum(saved["mixed_s"], dspatial)
    dmixed_s = project_back(dspatial, spatial).astype(jnp.bfloat16)
    dfused_s = attend_backward(
        saved["heads_s"], saved["lse_s"], dmixed_s, space_scores, space_mixed, space_flip
    )
    entry_grad_s = weight_sum(saved["lowered_s"], dfused_s)
    dpart_s, gain_s, shift_s = norm_back(
        project_back(dfused_s, entry[1]), saved["unit_s"], saved["inverse_s"], gains[0, 1]
    )
    dafter_t = dafter_s + dpart_s
    dbranch = lax.all_to_all(
        dafter_t.astype(jnp.bfloat16), "tok", split_axis=2, concat_axis=1, tiled=True
    )
    temporal_grad_b = weight_sum(saved["first_t"], dbranch)
    dfirst = project_back(dbranch, temporal[1]).astype(jnp.bfloat16)
    temporal_grad_a = weight_sum(saved["mixed_t"], dfirst)
    dmixed_t = project_back(dfirst, temporal[0]).astype(jnp.bfloat16)
    dfused_t = attend_backward(
        saved["heads_t"], saved["lse_t"], dmixed_t, time_scores, time_mixed, time_flip
    )
    entry_grad_t = weight_sum(saved["lowered_t"], dfused_t)
    dsent, gain_t, shift_t = norm_back(
        project_back(dfused_t, entry[0]), saved["unit_t"], saved["inverse_t"], gains[0, 0]
    )
    dreturned = lax.all_to_all(
        dsent.astype(jnp.bfloat16), "tok", split_axis=1, concat_axis=2, tiled=True
    )
    input_gradient = dafter_t + dreturned.astype(jnp.float32)
    members = (
        jnp.stack([entry_grad_t, entry_grad_s]).reshape(-1, 128),
        jnp.stack([temporal_grad_a, temporal_grad_b]).reshape(-1, 128),
        spatial_grad.reshape(-1, 128),
        widen_grad.reshape(-1, 128),
        narrow_grad.reshape(-1, 128),
        jnp.stack([jnp.stack([gain_t, gain_s, gain_m]), jnp.stack([shift_t, shift_s, shift_m])]),
    )
    totals = (
        lax.psum_scatter(members[0], ("clip", "tok"), scatter_dimension=0, tiled=True),
        lax.psum_scatter(members[1], ("clip", "tok"), scatter_dimension=0, tiled=True),
        lax.psum_scatter(members[2], ("clip", "tok"), scatter_dimension=0, tiled=True),
        lax.psum_scatter(members[3], ("clip", "tok"), scatter_dimension=0, tiled=True),
        lax.psum_scatter(members[4], ("clip", "tok"), scatter_dimension=0, tiled=True),
        lax.psum_scatter(members[5], ("clip", "tok"), scatter_dimension=2, tiled=True),
    )
    entry_sum, temporal_sum, spatial_sum, widen_sum, narrow_sum, affine_sum = totals
    entry_new = adamw(entry_weights, entry_momentum, entry_variance, entry_sum, D ** (-0.5))
    temporal_new = adamw(
        temporal_weights, temporal_momentum, temporal_variance, temporal_sum, (D // 2) ** (-0.5)
    )
    spatial_new = adamw(
        spatial_weights,
        spatial_momentum,
        spatial_variance,
        spatial_sum,
        (3 * D // PATCHES) ** (-0.5),
    )
    widen_new = adamw(widen_weights, widen_momentum, widen_variance, widen_sum, D ** (-0.5))
    narrow_new = adamw(narrow_weights, narrow_momentum, narrow_variance, narrow_sum, HID ** (-0.5))
    affine_new = adamw(norm_affine, affine_momentum, affine_variance, affine_sum, 0.5)
    return (
        result,
        input_gradient,
        entry_new[0],
        entry_new[1],
        entry_new[2],
        temporal_new[0],
        temporal_new[1],
        temporal_new[2],
        spatial_new[0],
        spatial_new[1],
        spatial_new[2],
        widen_new[0],
        widen_new[1],
        widen_new[2],
        narrow_new[0],
        narrow_new[1],
        narrow_new[2],
        affine_new[0],
        affine_new[1],
        affine_new[2][:, 0:2],
        affine_new[2][:, 2],
    )

MESH = pl.DeviceIdType.MESH
TOK = 4
UNIT = 768
ROWS = (48, 48, 24, 24, 96)
WIDTHS = (2304, 768, 768, 3072, 768)
AFFINE = 5
EACH = 24
ORDER_IN = (5, 0, 1, 2, 3, 4)
ORDER_MLP = (4, 3, 2)
ORDER_REST = (0, 1, 5)
VMEM_LIMIT = 60 * 1024 * 1024


def units_of(order, unit=UNIT):
    units = []
    for k in order:
        if k == AFFINE:
            units.append((k, 0, 128))
        else:
            wide = unit if ROWS[k] < 96 or unit > UNIT else unit // 2
            units += [(k, c, min(wide, WIDTHS[k] - c)) for c in range(0, WIDTHS[k], wide)]
    return units


def spot():
    clip = lax.axis_index("clip")
    return clip // 4, (clip // 2) % 2, clip % 2, lax.axis_index("tok")


def clip_of(y, x, core):
    return (y * 2 + x) * 2 + core


def greet():
    y, x, core, t = spot()
    barrier = pltpu.get_barrier_semaphore()

    def tell(clip, tok):
        pl.semaphore_signal(barrier, inc=1, device_id=(clip, tok), device_id_type=MESH)

    tell(clip_of(y, x, 1 - core), t)
    tell(clip_of(y, 1 - x, core), t)
    tell(clip_of(1 - y, x, core), t)
    for far in range(1, TOK):
        tell(clip_of(y, x, core), (t + far) % TOK)
    pl.semaphore_wait(barrier, 3 + (TOK - 1))


class Flight:
    def __init__(self):
        self.started = []

    def go(self, copy, when=None):
        if when is None:
            copy.start()
        else:
            pl.when(when)(copy.start)
        self.started.append((copy, when))
        return copy

    def drain(self):
        for copy, when in self.started:
            if when is None:
                copy.wait_send()
            else:
                pl.when(when)(copy.wait_send)


def gather_steps(units, owned, full, sems):
    local, got, core_got, out_sem, z_sem = sems
    y, x, core, t = spot()
    here, by_x, by_y = clip_of(y, x, core), clip_of(y, 1 - x, core), clip_of(1 - y, x, core)
    mate = clip_of(y, x, 1 - core)
    corner_clip = clip_of(1 - y, 1 - x, core)
    local_copies = []

    def place(u, at):
        k, c, width = units[u]
        return full[k].at[at, :, pl.ds(c, width)]

    def send(u, at, to, tok=None, own=False, along_z=False, when=None):
        k, c, width = units[u]
        there = place(u, at)
        copy = pltpu.make_async_remote_copy(
            src_ref=owned[k].at[:, pl.ds(c, width)] if own else there,
            dst_ref=there,
            send_sem=(z_sem if along_z else out_sem).at[u],
            recv_sem=got.at[u, at],
            device_id=(to, t if tok is None else tok),
            device_id_type=MESH,
        )
        if when is None:
            copy.start()
        else:
            pl.when(when)(copy.start)

    def many(u, count):
        k, c, width = units[u]
        return full[k].at[pl.ds(0, count), :, pl.ds(c, width)]

    def took(u, count, sem):
        there = many(u, count)
        pltpu.make_async_copy(there, there, sem.at[u]).wait()

    def arrive(u, at):
        there = place(u, at)
        pltpu.make_async_copy(there, there, got.at[u, at]).wait()

    def spread(u, at, own=False, when=None):
        def both():
            send(u, at, by_x, own=own)
            send(u, at, by_y, own=own)

        if when is None:
            both()
        else:
            pl.when(when)(both)

    def begin(u):
        k, c, width = units[u]
        me = here * TOK + t
        copy = pltpu.make_async_copy(owned[k].at[:, pl.ds(c, width)], place(u, me), local.at[u])
        copy.start()
        local_copies.append(copy)
        send(u, me, here, t + 1, own=True, along_z=True, when=t < TOK - 1)
        send(u, me, here, t - 1, own=True, along_z=True, when=t > 0)
        spread(u, me, own=True)

    hops = [(far, way) for far in range(1, TOK) for way in (1, -1)]

    def guard(far, way):
        return t + far <= TOK - 1 if way == 1 else t - far >= 0

    def to_mate(u, clip):
        k, c, width = units[u]
        there = full[k].at[pl.ds(clip * TOK, TOK), :, pl.ds(c, width)]
        pltpu.make_async_remote_copy(
            src_ref=there,
            dst_ref=there,
            send_sem=out_sem.at[u],
            recv_sem=core_got.at[u],
            device_id=(mate, t),
            device_id_type=MESH,
        ).start()

    def along(u):
        for far, way in hops:
            at = here * TOK + t + far * way

            def passing(at=at, way=way):
                arrive(u, at)
                onward = t > 0 if way == 1 else t < TOK - 1
                send(u, at, here, t - way, along_z=True, when=onward)
                spread(u, at)

            pl.when(guard(far, way))(passing)
        local_copies[u].wait()
        to_mate(u, here)

    def crossing(u):
        for far in range(TOK):
            tok = (t + far) % TOK
            from_x, from_y = by_x * TOK + tok, by_y * TOK + tok
            arrive(u, from_x)
            if far % 2 == 1:
                send(u, from_x, by_y)
            arrive(u, from_y)
            if far % 2 == 0:
                send(u, from_y, by_x)
        to_mate(u, by_x)
        to_mate(u, by_y)

    def corner(u):
        for far in range(TOK):
            arrive(u, corner_clip * TOK + (t + far) % TOK)
        to_mate(u, corner_clip)

    def settle(u):
        took(u, 16, core_got)

    def drain():
        edge = jnp.logical_or(t == 0, t == TOK - 1)
        for u in range(len(units)):
            took(u, 28, out_sem)

        def wait_z(count):
            for u in range(len(units)):
                took(u, count, z_sem)

        pl.when(edge)(functools.partial(wait_z, 1))
        pl.when(jnp.logical_not(edge))(functools.partial(wait_z, 5))

    return begin, along, crossing, corner, settle, drain


def gather_sems(count):
    dma = pltpu.SemaphoreType.DMA
    return [
        dma((count,)),
        dma((count, 32)),
        dma((count,)),
        dma((count,)),
        dma((count,)),
    ]


def rows_from(flat, out):
    rows, n = out.shape[0], out.shape[1] // 128
    for c in range(n):
        out[:, c * 128 : (c + 1) * 128] = flat[pl.ds(c, rows, stride=n), :].astype(out.dtype)


def join_affine(blocks, out):
    lane = lax.broadcasted_iota(jnp.int32, (16, 128), 1)
    tiles = [jnp.zeros((16, 128), jnp.float32) for _ in range(6)]
    for i in range(32):
        block = jnp.where(lane < EACH, blocks[i].astype(jnp.float32), 0.0)
        tile, shift = (i * EACH) // 128, (i * EACH) % 128
        turned = pltpu.roll(block, shift, 1) if shift else block
        tiles[tile] = tiles[tile] + jnp.where(lane >= shift, turned, 0.0)
        if shift + EACH > 128:
            tiles[tile + 1] = tiles[tile + 1] + jnp.where(lane < shift, turned, 0.0)
    for i in range(6):
        out[:, i * 128 : (i + 1) * 128] = tiles[i]


def scatter_steps(units, parts, held, core_in, side_in, part_in, z_in, sems, finals):
    load_sem, c_send, c_recv, d_send, d_recv, s_send, s_recv, z_send, z_recv = sems
    y, x, core, t = spot()
    here, by_x, by_y = clip_of(y, x, core), clip_of(y, 1 - x, core), clip_of(1 - y, x, core)
    mate = clip_of(y, x, 1 - core)
    homes = [(1 - y, 1 - x), (y, 1 - x), (1 - y, x), (y, x)]

    def cols(u):
        k, c, width = units[u]
        return pl.ds(c, width)

    def remote(src, dst, send_sem, recv_sem, to, tok=None):
        return pltpu.make_async_remote_copy(
            src_ref=src,
            dst_ref=dst,
            send_sem=send_sem,
            recv_sem=recv_sem,
            device_id=(to, t if tok is None else tok),
            device_id_type=MESH,
        )

    def load(u, g):
        k = units[u][0]
        ya, xa = homes[g]
        return pltpu.make_async_copy(
            parts[k].at[pl.ds(clip_of(ya, xa, core) * TOK, TOK), :, cols(u)],
            held[u].at[g],
            load_sem.at[u, g],
        )

    def to_mate(u, g):
        k = units[u][0]
        ya, xa = homes[g]
        return remote(
            parts[k].at[pl.ds(clip_of(ya, xa, 1 - core) * TOK, TOK), :, cols(u)],
            core_in[u].at[g],
            c_send.at[u],
            c_recv.at[u, g],
            mate,
        )

    def begin(u):
        for g in range(4):
            load(u, g).start()
            to_mate(u, g).start()

    def ready(u, g):
        load(u, g).wait()
        to_mate(u, g).wait_recv()

    def add_into(u, g, lo, hi, pieces):
        def one(j, carry):
            total = up(held[u][g, j])
            for piece in pieces:
                total = total + up(piece[j])
            held[u][g, j] = low(total)
            return carry

        lax.fori_loop(lo, hi, one, 0)

    def first(u, half):
        return remote(
            held[u].at[0, pl.ds(2 * half, 2)],
            side_in[u].at[pl.ds(2 * half, 2)],
            d_send.at[u],
            d_recv.at[u, half],
            by_y if half else by_x,
        )

    def second(u, across):
        return remote(
            held[u].at[1 if across == 0 else 2],
            part_in[u].at[across],
            s_send.at[u],
            s_recv.at[u, across],
            by_x if across == 0 else by_y,
        )

    def last(u, far):
        tok = (t + far) % TOK
        return remote(
            held[u].at[3, tok],
            z_in[u].at[far - 1],
            z_send.at[u],
            z_recv.at[u, far - 1],
            here,
            tok,
        )

    def step1(u):
        ready(u, 0)
        add_into(u, 0, 0, TOK, [core_in[u].at[0]])
        first(u, 0).start()
        first(u, 1).start()

    def step2(u):
        ready(u, 2)
        first(u, 0).wait_recv()
        add_into(u, 2, 0, 2, [core_in[u].at[2], side_in[u]])
        add_into(u, 2, 2, TOK, [core_in[u].at[2]])
        second(u, 1).start()
        ready(u, 1)
        first(u, 1).wait_recv()
        add_into(u, 1, 0, 2, [core_in[u].at[1]])
        add_into(u, 1, 2, TOK, [core_in[u].at[1], side_in[u]])
        second(u, 0).start()

    def step3(u):
        ready(u, 3)
        second(u, 0).wait_recv()
        second(u, 1).wait_recv()
        add_into(u, 3, 0, TOK, [core_in[u].at[3], part_in[u].at[0], part_in[u].at[1]])
        for far in range(1, TOK):
            last(u, far).start()

    def step4(u):
        total = up(held[u][3, t])
        for far in range(1, TOK):
            last(u, far).wait_recv()
            total = total + up(z_in[u][far - 1])
        finals(u, total)

    def drain():
        for u in range(len(units)):
            for place, sem in ((held, c_send), (side_in, d_send), (part_in, s_send), (z_in, z_send)):
                pltpu.make_async_copy(place[u], place[u], sem.at[u]).wait()

    return begin, step1, step2, step3, step4, drain


def scatter_scratch(units):
    bf16 = jnp.bfloat16
    shapes = [(16 if k == AFFINE else ROWS[k], width) for k, c, width in units]
    held = [pltpu.VMEM((4, TOK) + s, bf16) for s in shapes]
    side = [pltpu.VMEM((TOK,) + s, bf16) for s in shapes]
    part = [pltpu.VMEM((2, TOK) + s, bf16) for s in shapes]
    last = [pltpu.VMEM((TOK - 1,) + s, bf16) for s in shapes]
    return held + held + side + part + last


def scatter_sems(count):
    dma = pltpu.SemaphoreType.DMA
    return [
        dma((count, 4)),
        dma((count,)),
        dma((count, 4)),
        dma((count,)),
        dma((count, 2)),
        dma((count,)),
        dma((count, 2)),
        dma((count,)),
        dma((count, TOK - 1)),
    ]


STEP_FIX = 1.0 - 0.5**STEP


def adamw_rows(rate, weights, moment, square, grad, out):
    averaged = 0.5 * moment + 0.5 * grad
    squared = 0.5 * square + 0.5 * grad * grad
    out[0][...] = weights - rate * (
        averaged / STEP_FIX / (jnp.sqrt(squared / STEP_FIX) + 1e-08) + 0.1 * weights
    )
    out[1][...] = averaged
    out[2][...] = squared


RATES = (768 ** (-0.5), 384 ** (-0.5), 11 ** (-0.5), 768 ** (-0.5), 3072 ** (-0.5))


def part_affine(norms, out):
    rows = [jnp.sum(n[0:8, :], axis=0, keepdims=True) for n in norms]
    rows += [jnp.sum(n[8:16, :], axis=0, keepdims=True) for n in norms]
    table = jnp.concatenate(rows + [jnp.zeros((10, 768), jnp.float32)], axis=0)
    lane = lax.broadcasted_iota(jnp.int32, (16, 128), 1)
    for i in range(32):
        tile, shift = (i * EACH) // 128, (i * EACH) % 128
        block = table[:, tile * 128 : (tile + 1) * 128]
        block = pltpu.roll(block, (128 - shift) % 128, 1) if shift else block
        if shift + EACH > 128:
            after = pltpu.roll(table[:, (tile + 1) * 128 : (tile + 2) * 128], 128 - shift, 1)
            block = jnp.where(lane < 128 - shift, block, after)
        out[i] = jnp.where(lane < EACH, block, 0.0).astype(jnp.bfloat16)

GROUPS = 7
T_ROWS = 448
S_PAD = 208
S_ROWS = 416
CHUNK = 768
MLP_CHUNK = 512
SCALE = HEAD_DIM ** (-0.5)
BIG = -1e30
NT = (((1,), (1,)), ((), ()))
TN = (((0,), (0,)), ((), ()))


def dot(left, right, dims=(((1,), (0,)), ((), ()))):
    return lax.dot_general(left, right, dims, preferred_element_type=jnp.float32)


def low(values):
    return values.astype(jnp.bfloat16)


def up(values):
    return values.astype(jnp.float32)


def center_rows(values):
    center = values - jnp.mean(values, axis=-1, keepdims=True)
    inverse = lax.rsqrt(jnp.mean(center * center, axis=-1, keepdims=True) + 1e-06)
    return center * inverse, inverse


def back_rows(upstream, unit, inverse, gain):
    scaled = upstream * gain
    inner = (
        scaled
        - jnp.mean(scaled, axis=-1, keepdims=True)
        - unit * jnp.mean(scaled * unit, axis=-1, keepdims=True)
    )
    return inner * inverse


def fold(values):
    return jnp.sum(values.reshape(-1, 8, values.shape[-1]), axis=0)


def columns(j, width):
    return pl.ds(pl.multiple_of(j * width, 128), width)


def rows_of(i, height):
    return pl.ds(pl.multiple_of(i * height, 8), height)


def times(out, left, weight, width=CHUNK):
    def step(j, carry):
        at = columns(j, width)
        out[:, at] = dot(left[...], weight[:, at]).astype(out.dtype)
        return carry

    lax.fori_loop(0, out.shape[1] // width, step, 0)


def lane_half(shape):
    return lax.broadcasted_iota(jnp.int32, shape, 1) < HEAD_DIM


def soft(query, keys, mask):
    scores = jnp.where(mask, dot(keys, query, NT), BIG)
    expo = jnp.exp(scores - jnp.max(scores, axis=0, keepdims=True))
    return expo * (1.0 / jnp.sum(expo, axis=0, keepdims=True))


def attend(query, keys, values, mask):
    half = lane_half(query.shape)
    zero = jnp.zeros_like(query)
    query = query * jnp.bfloat16(SCALE)
    first = dot(low(soft(jnp.where(half, query, zero), keys, mask)), values, TN)
    second = dot(low(soft(jnp.where(half, zero, query), keys, mask)), values, TN)
    return low(jnp.where(half, first, second))


def attend_back(query, keys, values, upstream, mask):
    half = lane_half(query.shape)
    zero = jnp.zeros_like(query)
    query = query * jnp.bfloat16(SCALE)
    scaled = keys * jnp.bfloat16(SCALE)

    def one(pick):
        probs = soft(pick(query, zero), keys, mask)
        dprobs = dot(values, pick(upstream, zero), NT)
        dscores = low(probs * (dprobs - jnp.sum(dprobs * probs, axis=0, keepdims=True)))
        return dot(dscores, scaled, TN), dot(dscores, query), dot(low(probs), upstream)

    first = one(lambda a, b: jnp.where(half, a, b))
    second = one(lambda a, b: jnp.where(half, b, a))
    return tuple(low(jnp.where(half, a, b)) for a, b in zip(first, second))


def frame_mask(size):
    patch = lambda axis: (lambda i: (i // 64) * 8 + i % 8)(
        lax.broadcasted_iota(jnp.int32, (size, size), axis)
    )
    return patch(0) == patch(1)


def patch_mask():
    return lax.broadcasted_iota(jnp.int32, (S_PAD, S_PAD), 0) < PATCHES


T_BLOCKS = ((0, 192), (192, 256))


def mlp_kernel(lowered, after_s, cotangent, widen, narrow, affine, result, d_narrow, d_widen, d_after, d_norm, cot, turned, total, back):
    j = pl.program_id(0)

    @pl.when(j == 0)
    def start():
        cot[...] = jnp.zeros_like(cot)
        for f in range(2):
            back[pl.ds(f * S_PAD, PATCHES), :] = up(cotangent[f])
            back[pl.ds(f * S_PAD + PATCHES, S_PAD - PATCHES), :] = jnp.zeros((S_PAD - PATCHES, D), jnp.float32)
        cot[...] = low(back[...])
        turned[...] = lowered[...].T
        total[...] = after_s[...]
        back[...] = jnp.zeros_like(back)

    wide = dot(lowered[...], widen[...])
    phi = 0.5 * (1.0 + lax.erf(wide * 0.7071067811865476))
    active = low(wide * phi)
    slope = phi + wide * jnp.exp(-0.5 * wide * wide) * 0.3989422804014327
    d_wide = low(dot(cot[...], narrow[...], NT) * slope)
    total[...] += dot(active, narrow[...])
    d_narrow[...] = low(dot(active, cot[...], TN))
    d_widen[...] = low(dot(turned[...], d_wide))
    back[...] += dot(d_wide, widen[...], NT)

    @pl.when(j == pl.num_programs(0) - 1)
    def finish():
        for f in range(2):
            result[f] = low(total[pl.ds(f * S_PAD, PATCHES), :])

        def norm(b, carry):
            rows = rows_of(b, 32)
            unit, inverse = center_rows(after_s[rows, :])
            upstream = back[rows, :]
            d_after[rows, :] = up(cot[rows, :]) + back_rows(upstream, unit, inverse, affine[2:3, :])
            return carry[0] + fold(upstream * unit), carry[1] + fold(upstream)

        zero = jnp.zeros((8, D), jnp.float32)
        gain, shift = lax.fori_loop(0, S_ROWS // 32, norm, (zero, zero))
        d_norm[0:8, :] = gain
        d_norm[8:16, :] = shift


def mlp(lowered, after_s, cotangent, widen, narrow, affine):
    whole = lambda shape: pl.BlockSpec(shape, lambda j: (0,) * len(shape))
    steps = HID // MLP_CHUNK
    return pl.pallas_call(
        mlp_kernel,
        grid=(steps,),
        in_specs=[
            whole((S_ROWS, D)),
            whole((S_ROWS, D)),
            whole((2, PATCHES, D)),
            pl.BlockSpec((D, MLP_CHUNK), lambda j: (0, j)),
            pl.BlockSpec((MLP_CHUNK, D), lambda j: (j, 0)),
            whole((16, D)),
        ],
        out_specs=[
            whole((2, PATCHES, D)),
            pl.BlockSpec((MLP_CHUNK, D), lambda j: (j, 0)),
            pl.BlockSpec((D, MLP_CHUNK), lambda j: (0, j)),
            whole((S_ROWS, D)),
            whole((16, D)),
        ],
        out_shape=[
            jax.ShapeDtypeStruct((2, PATCHES, D), jnp.bfloat16),
            jax.ShapeDtypeStruct((HID, D), jnp.bfloat16),
            jax.ShapeDtypeStruct((D, HID), jnp.bfloat16),
            jax.ShapeDtypeStruct((S_ROWS, D), jnp.float32),
            jax.ShapeDtypeStruct((16, D), jnp.float32),
        ],
        scratch_shapes=[
            pltpu.VMEM((S_ROWS, D), jnp.bfloat16),
            pltpu.VMEM((D, S_ROWS), jnp.bfloat16),
            pltpu.VMEM((S_ROWS, D), jnp.float32),
            pltpu.VMEM((S_ROWS, D), jnp.float32),
        ],
        compiler_params=pltpu.CompilerParams(vmem_limit_bytes=56 * 1024 * 1024),
        cost_estimate=pl.CostEstimate(flops=12000000000, bytes_accessed=30000000, transcendentals=0),
    )(lowered, after_s, cotangent, widen, narrow, affine)

def pack(box, rows):
    extra = [rows(f, 192, 4) for f in range(2)]
    line = lax.broadcasted_iota(jnp.int32, (16, D), 0)
    for s in range(TOK):
        wide = [rows(f, 48 * s, 48) for f in range(2)]
        for b in range(6):
            pair = [w[8 * b : 8 * b + 8, :] for w in wide]
            box[s, b] = low(jnp.concatenate(pair, axis=0))
        one = [jnp.broadcast_to(e[s : s + 1, :], (16, D)) for e in extra]
        box[s, 6] = low(jnp.where(line == 0, one[0], jnp.where(line == 8, one[1], 0.0)))


def unpack(box, f, put):
    for s in range(TOK):
        for b in range(6):
            slab = up(box[s, b])
            put(48 * s + 8 * b, 8, slab[8 * f : 8 * f + 8, :])
    last = [up(box[s, 6])[8 * f : 8 * f + 1, :] for s in range(TOK)]
    put(192, TOK, jnp.concatenate(last, axis=0))


class Exchange:
    def __init__(self, source, target, sems, flight):
        self.source, self.target, self.flight = source, target, flight
        self.local, self.sent, self.got = sems
        self.clip, self.t = lax.axis_index("clip"), lax.axis_index("tok")

    def copy(self, far):
        return pltpu.make_async_remote_copy(
            src_ref=self.source((self.t + far) % TOK),
            dst_ref=self.target(self.t),
            send_sem=self.sent.at[far - 1],
            recv_sem=self.got.at[far - 1],
            device_id=(self.clip, (self.t + far) % TOK),
            device_id_type=MESH,
        )

    def own(self):
        return pltpu.make_async_copy(self.source(self.t), self.target(self.t), self.local.at[0])

    def start(self):
        for far in range(1, TOK):
            self.flight.go(self.copy(far))
        self.own().start()

    def wait(self):
        for far in range(1, TOK):
            there = self.target((self.t - far + TOK) % TOK)
            pltpu.make_async_copy(there, there, self.got.at[far - 1]).wait()
        self.own().wait()


def exchange_sems():
    dma = pltpu.SemaphoreType.DMA
    return [dma((1,)), dma((TOK - 1,)), dma((TOK - 1,))]


def pieces(count, step, size):
    def run(lo, hi):
        def one(j, carry):
            step(j)
            return carry

        lax.fori_loop(lo, hi, one, 0)

    return [functools.partial(run, lo, min(lo + size, count)) for lo in range(0, count, size)]


def product(out, left, weight, width=CHUNK):
    def step(j):
        at = columns(j, width)
        out[:, at] = dot(left(), weight[:, at]).astype(out.dtype)

    return step


def product_back(out, left, weight, width=CHUNK):
    def step(j):
        at = columns(j, width)
        out[:, at] = dot(left(), weight[at, :], NT).astype(out.dtype)

    return step


def gradient(out, turned, upstream, width=CHUNK):
    def step(j):
        at = columns(j, width)
        out[:, at] = low(dot(turned[...], upstream(at)))

    return step


SUM_START = 5
SUM_RATE = 1.8
SUM_SHIFTS = (0, 1, 2, 3)


def spaced(compute, rest):
    done = 0
    for i, call in enumerate(compute):
        call()
        while done < len(rest) and SUM_START + done * SUM_RATE <= i + 1:
            rest[done]()
            done += 1
    for call in rest[done:]:
        call()


def full_kernel_steps(units, steps, shifts, lo, hi):
    calls = []
    for n in range(lo, hi):
        for shift, step in zip(shifts, steps):
            if 0 <= n - shift < len(units):
                calls.append(functools.partial(step, n - shift))
    return calls


A2A_AT = 10


def gather_head(units):
    count = len(units)
    last = [n for n in range(count) if units[n][0] == 1][-1]
    names = ("begin", "along", "crossing", "corner")
    calls = []
    for n in range(last + 3):
        calls += [(name, n - shift) for shift, name in enumerate(names) if 0 <= n - shift < count]
    return calls + [("begin", last + 3), ("along", last + 2), ("corner", last)]


def forward_kernel(units, *refs):
    masters, block, frames = refs[:5], refs[5], refs[6]
    full = list(refs[7:12])
    affine, early_out, mixed_s, after_s, lowered = refs[12], refs[13:21], refs[21], refs[22], refs[23]
    owned, gathered = list(refs[24:29]), refs[29]
    entry_w, temporal_w, spatial_w, outbox, sent, inbox, load_sem = refs[30:37]
    early = refs[37:45]
    patch, normed_t, merged_t, mixed_t, first_t, after_t, normed_s, merged_s = early
    there_sems, back_sems = refs[45:48], refs[48:51]
    sems = refs[51:]
    stores = [
        pltpu.make_async_copy(a, b, load_sem.at[4 + i]) for i, (a, b) in enumerate(zip(early, early_out))
    ]

    def store(lo, hi):
        def begin_stores():
            for copy in stores[lo:hi]:
                copy.start()

        return [begin_stores]

    greet()
    full.append(gathered)
    owned.append(block)
    flight = Flight()
    begin, along, crossing, corner, settle, drain = gather_steps(units, owned, full, sems)
    count = len(units)
    place = {k: [n for n in range(count) if units[n][0] == k] for k in range(6)}
    there = Exchange(lambda s: outbox.at[s], lambda s: patch.at[:, s], there_sems, flight)
    back = Exchange(lambda s: sent.at[:, s], lambda s: inbox.at[s], back_sems, flight)
    def settle_all(k):
        for n in place[k]:
            settle(n)

    ready = set()
    original = begin

    def begin(n):
        k = units[n][0]
        if k not in ready and k != AFFINE:
            rows_from(masters[k], owned[k])
            ready.add(k)
        original(n)

    steps = {"begin": begin, "along": along, "crossing": crossing, "corner": corner}
    head = [functools.partial(steps[name], n) for name, n in gather_head(units)]
    step = lambda name, n: [functools.partial(steps[name], n)]
    for call in head[:A2A_AT]:
        call()
    pack(outbox, lambda f, start, size: up(frames[f, start : start + size, :]))
    there.start()
    for call in head[A2A_AT:]:
        call()

    def load(part, source, target):
        return pltpu.make_async_copy(source, target, load_sem.at[part])

    loads = {
        "entry": load(0, full[0].at[pl.ds(0, 16)], entry_w),
        "temporal": load(1, full[1], temporal_w),
        "later": load(2, full[0].at[pl.ds(16, 16)], entry_w),
        "spatial": load(3, full[2], spatial_w),
    }
    settle_all(AFFINE)
    join_affine(gathered, affine)
    there.wait()

    def norm_t(b):
        unit, unused = center_rows(up(patch[b].reshape(64, D)))
        normed_t[rows_of(b, 64), :] = low(unit * affine[0:1, :] + affine[3:4, :])

    def heads_t(p):
        found = []
        for start, size in T_BLOCKS:
            rows = pl.ds(start, size)
            query, keys, values = (merged_t[rows, columns(p + 6 * i, 128)] for i in range(3))
            found.append(attend(query, keys, values, frame_mask(size)))
        for (start, size), value in zip(T_BLOCKS, found):
            mixed_t[pl.ds(start, size), columns(p, 128)] = value

    entry_m = lambda at: entry_w[:, :, at].reshape(D, CHUNK)

    def merge(out, left):
        def step(j):
            at = columns(j, CHUNK)
            out[:, at] = low(dot(left[...], entry_m(at)))

        return step

    def first_step(j):
        at = columns(j, CHUNK)
        first_t[:, at] = low(dot(mixed_t[...], temporal_w[0:16, :, at].reshape(D, CHUNK)))

    def branch_step(j):
        at = columns(j, CHUNK)
        value = low(dot(first_t[...], temporal_w[16:32, :, at].reshape(D, CHUNK)))
        sent[:, :, :, at] = value.reshape(GROUPS, TOK, 16, CHUNK)

    def start_temporal():
        settle_all(0)
        settle_all(1)
        loads["entry"].start()
        loads["temporal"].start()
        for call in pieces(GROUPS, norm_t, GROUPS):
            call()
        loads["entry"].wait()
        loads["temporal"].wait()

    def start_spatial():
        settle_all(2)
        loads["later"].start()
        loads["spatial"].start()
        back.wait()
        for f in range(2):

            def put(start, size, rows, f=f):
                after_t[f * S_PAD + start : f * S_PAD + start + size, :] = (
                    up(frames[f, start : start + size, :]) + rows
                )

            unpack(inbox, f, put)
            tail = f * S_PAD + PATCHES
            after_t[tail : (f + 1) * S_PAD, :] = jnp.zeros((S_PAD - PATCHES, D), jnp.float32)

    def norm_s(b):
        unit, unused = center_rows(after_t[rows_of(b, 32), :])
        normed_s[rows_of(b, 32), :] = low(unit * affine[1:2, :] + affine[4:5, :])

    def wait_spatial():
        loads["later"].wait()
        loads["spatial"].wait()

    def heads_s(p):
        found = []
        for f in range(2):
            rows = pl.ds(f * S_PAD, S_PAD)
            query, keys, values = (merged_s[rows, columns(p + 6 * i, 128)] for i in range(3))
            found.append(attend(query, keys, values, patch_mask()))
        for f in range(2):
            mixed_s[pl.ds(f * S_PAD, S_PAD), columns(p, 128)] = found[f]

    def out_s(j):
        at = columns(j, CHUNK)
        weight = low(up(spatial_w[:, :, at]).reshape(D, CHUNK))
        after_s[:, at] = after_t[:, at] + dot(mixed_s[...], weight)

    def norm_m(b):
        unit, unused = center_rows(after_s[rows_of(b, 32), :])
        lowered[rows_of(b, 32), :] = low(unit * affine[2:3, :] + affine[5:6, :])

    order = (
        [start_temporal]
        + pieces(3, merge(merged_t, normed_t), 1)
        + step("crossing", 3)
        + step("along", 5)
        + step("corner", 3)
        + pieces(6, heads_t, 2)
        + step("crossing", 4)
        + pieces(1, first_step, 1)
        + pieces(1, branch_step, 1)
        + [back.start]
        + store(0, 5)
        + step("corner", 4)
        + step("crossing", 5)
        + [start_spatial]
        + pieces(13, norm_s, 13)
        + [wait_spatial]
        + pieces(3, merge(merged_s, normed_s), 1)
        + pieces(6, heads_s, 3)
        + store(5, 8)
        + step("corner", 5)
        + pieces(1, out_s, 1)
        + pieces(13, norm_m, 13)
    )
    for call in order:
        call()
    for k in (3, 4):
        settle_all(k)
    drain()
    flight.drain()
    for copy in stores:
        copy.wait()


def forward(masters, block, frames):
    units = units_of(ORDER_IN, HID)
    vmem = pl.BlockSpec(memory_space=pltpu.VMEM)
    anywhere = pl.BlockSpec(memory_space=pl.ANY)
    bf16, f32 = jnp.bfloat16, jnp.float32
    slab = (TOK, GROUPS, 16, D)
    group = (GROUPS, TOK, 16, D)
    saved = [
        ((16, D), f32),
        (group, bf16),
        ((T_ROWS, D), bf16),
        ((T_ROWS, 3 * D), bf16),
        ((T_ROWS, D), bf16),
        ((T_ROWS, D), bf16),
        ((S_ROWS, D), f32),
        ((S_ROWS, D), bf16),
        ((S_ROWS, 3 * D), bf16),
        ((S_ROWS, D), bf16),
        ((S_ROWS, D), f32),
        ((S_ROWS, D), bf16),
    ]
    early = [pltpu.VMEM(s, t) for s, t in saved[1:9]]
    return pl.pallas_call(
        functools.partial(forward_kernel, units),
        out_shape=[jax.ShapeDtypeStruct((32, r, w), bf16) for r, w in zip(ROWS, WIDTHS)]
        + [jax.ShapeDtypeStruct(s, t) for s, t in saved],
        in_specs=[vmem] * 7,
        out_specs=[anywhere] * 5 + [vmem] + [anywhere] * 8 + [vmem] * 3,
        scratch_shapes=[pltpu.VMEM((r, w), bf16) for r, w in zip(ROWS, WIDTHS)]
        + [
            pltpu.VMEM((32, 16, 128), bf16),
            pltpu.VMEM((16, 48, 3 * D), bf16),
            pltpu.VMEM((32, 48, D), bf16),
            pltpu.VMEM((32, 24, D), bf16),
            pltpu.VMEM(slab, bf16),
            pltpu.VMEM(group, bf16),
            pltpu.VMEM(slab, bf16),
            pltpu.SemaphoreType.DMA((12,)),
        ]
        + early
        + exchange_sems()
        + exchange_sems()
        + gather_sems(len(units)),
        compiler_params=pltpu.CompilerParams(
            collective_id=0, has_side_effects=True, vmem_limit_bytes=VMEM_LIMIT
        ),
    )(*masters, block, frames)


def finals_of(grads, affine_out=None):
    def finals(unit, total):
        k, c, width = unit
        if k == AFFINE:
            affine_out[...] = total
            return
        n, rows = WIDTHS[k] // 128, ROWS[k]
        for i in range(width // 128):
            grads[k][pl.ds(c // 128 + i, rows, stride=n), :] = total[:, i * 128 : (i + 1) * 128]

    return finals


def back_kernel(units, *refs):
    parts = dict(zip((3, 4), refs[:2]))
    d_after_s, after_t, affine, spatial = refs[2:6]
    normed_s_in, merged_s_in, mixed_s_in, entry_in = refs[6:10]
    patch_in, normed_t_in, merged_t_in, mixed_t_in, first_t_in, temporal_in = refs[10:16]
    grads = dict(zip((2, 3, 4), refs[16:19]))
    sent, d_after_t, d_entry_out, d_temporal, norm_s_out, norm_t_out = refs[19:25]
    pos = 25
    pools = []
    for i in range(5):
        pools.append(refs[pos : pos + len(units)])
        pos += len(units)
    parts[2] = refs[pos]
    pos += 1
    normed_s, merged_s, mixed_s, entry_w = refs[pos : pos + 4]
    patch, normed_t, merged_t, mixed_t, first_t, temporal_w = refs[pos + 4 : pos + 10]
    d_entry, lowered, d_mixed, d_first, d_merged, turned_s, turned_t, back, outbox, grouped, load_sem = refs[
        pos + 10 : pos + 21
    ]
    pos += 21
    there_sems = refs[pos : pos + 3]
    sems = refs[pos + 3 :]
    sources = (normed_s_in, merged_s_in, mixed_s_in, entry_in.at[1])
    targets = (normed_s, merged_s, mixed_s, entry_w)
    sources += (patch_in, normed_t_in, merged_t_in, mixed_t_in, first_t_in, temporal_in)
    targets += (patch, normed_t, merged_t, mixed_t, first_t, temporal_w)
    loads = [pltpu.make_async_copy(a, b, load_sem.at[i]) for i, (a, b) in enumerate(zip(sources, targets))]
    for copy in loads:
        copy.start()
    entry_load = pltpu.make_async_copy(entry_in.at[0], entry_w, load_sem.at[10])
    entry_stores = [pltpu.make_async_copy(d_entry, d_entry_out.at[i], load_sem.at[12 - i]) for i in range(2)]
    greet()
    flight = Flight()
    finals = finals_of(grads)
    steps = scatter_steps(
        units, parts, *pools, sems, lambda u, total: finals(units[u], total)
    )
    there = Exchange(lambda s: outbox.at[s], lambda s: grouped.at[:, s], there_sems, flight)
    zero = jnp.zeros((8, D), jnp.float32)

    def begin_s():
        lowered[...] = low(d_after_s[...])
        for copy in loads[:3]:
            copy.wait()
        turned_s[...] = mixed_s[...].T

    def turn_s():
        turned_s[...] = normed_s[...].T

    def heads_s(p):
        found = []
        for f in range(2):
            rows = pl.ds(f * S_PAD, S_PAD)
            query, keys, values = (merged_s[rows, columns(p + 6 * i, 128)] for i in range(3))
            found.append(
                attend_back(query, keys, values, d_mixed[rows, columns(p, 128)], patch_mask())
            )
        for f in range(2):
            for i in range(3):
                d_merged[pl.ds(f * S_PAD, S_PAD), columns(p + 6 * i, 128)] = found[f][i]

    def s_back(j):
        at = columns(j, CHUNK)
        back[0:S_ROWS, at] = dot(d_merged[0:S_ROWS, :], entry_w[at, :], NT)

    def end_s():
        entry_load.start()

        def norm(b, carry):
            rows = rows_of(b, 32)
            unit, inverse = center_rows(after_t[rows, :])
            upstream = back[rows, :]
            d_after_t[rows, :] = d_after_s[rows, :] + back_rows(upstream, unit, inverse, affine[1:2, :])
            return carry[0] + fold(upstream * unit), carry[1] + fold(upstream)

        gain, shift = lax.fori_loop(0, S_ROWS // 32, norm, (zero, zero))
        norm_s_out[0:8, :] = gain
        norm_s_out[8:16, :] = shift
        pack(outbox, lambda f, start, size: d_after_t[f * S_PAD + start : f * S_PAD + start + size, :])
        there.start()

    def wait_entry():
        loads[3].wait()

    def spatial_sum():
        parts[2][...] = low(dot(turned_s[...], lowered[...]).reshape(32, 24, D))
        steps[0](len(units) - 1)

    d_mixed_s = d_mixed.at[0:S_ROWS]
    compute = (
        [begin_s]
        + [spatial_sum]
        + pieces(1, product_back(d_mixed_s, lambda: lowered[...], spatial), 1)
        + [turn_s]
        + pieces(6, heads_s, 1)
        + [wait_entry]
        + pieces(1, s_back, 1)
        + [end_s]
        + pieces(3, gradient(d_entry, turned_s, lambda at: d_merged[0:S_ROWS, at]), 1)
        + [entry_stores[1].start]
    )

    def begin_t():
        for copy in loads[4:]:
            copy.wait()
        turned_t[...] = first_t[...].T
        there.wait()

    group_cols = lambda at: grouped[:, :, :, at].reshape(T_ROWS, CHUNK)

    def turn_mixed():
        turned_t[...] = mixed_t[...].T

    def turn_normed():
        turned_t[...] = normed_t[...].T

    def heads_t(p):
        found = []
        for start, size in T_BLOCKS:
            rows = pl.ds(start, size)
            query, keys, values = (merged_t[rows, columns(p + 6 * i, 128)] for i in range(3))
            found.append(
                attend_back(query, keys, values, d_mixed[rows, columns(p, 128)], frame_mask(size))
            )
        for (start, size), values in zip(T_BLOCKS, found):
            for i in range(3):
                d_merged[pl.ds(start, size), columns(p + 6 * i, 128)] = values[i]

    def t_back(j):
        at = columns(j, CHUNK)
        back[:, at] = dot(d_merged[...], entry_w[at, :], NT)

    def end_t():
        def norm(b, carry):
            rows = rows_of(b, 64)
            unit, inverse = center_rows(up(patch[b].reshape(64, D)))
            upstream = back[rows, :]
            value = back_rows(upstream, unit, inverse, affine[0:1, :])
            sent[b] = low(value).reshape(TOK, 16, D)
            return carry[0] + fold(upstream * unit), carry[1] + fold(upstream)

        gain, shift = lax.fori_loop(0, GROUPS, norm, (zero, zero))
        norm_t_out[0:8, :] = gain
        norm_t_out[8:16, :] = shift

    def free_entry():
        entry_stores[1].wait()
        entry_load.wait()

    compute += (
        [begin_t]
        + pieces(1, gradient(d_temporal.at[1], turned_t, group_cols), 1)
        + pieces(1, product_back(d_first, lambda: grouped[...].reshape(T_ROWS, D), temporal_w.at[1]), 1)
        + [turn_mixed]
        + pieces(1, gradient(d_temporal.at[0], turned_t, lambda at: d_first[:, at]), 1)
        + pieces(1, product_back(d_mixed, lambda: d_first[...], temporal_w.at[0]), 1)
        + [turn_normed]
        + pieces(6, heads_t, 1)
        + [free_entry]
        + pieces(1, t_back, 1)
        + [end_t]
        + pieces(3, gradient(d_entry, turned_t, lambda at: d_merged[:, at]), 1)
        + [entry_stores[0].start]
    )
    for u in range(len(units) - 1):
        steps[0](u)
    rest = full_kernel_steps(units, steps[1:5], SUM_SHIFTS, 0, len(units) + SUM_SHIFTS[-1])
    spaced(compute, rest)
    entry_stores[0].wait()
    steps[5]()
    flight.drain()


def backward(parts, d_after_s, after_t, affine, spatial, entry, temporal, saved_s, saved_t):
    units = units_of(ORDER_MLP, 1536)
    vmem = pl.BlockSpec(memory_space=pltpu.VMEM)
    anywhere = pl.BlockSpec(memory_space=pl.ANY)
    bf16, f32 = jnp.bfloat16, jnp.float32
    flat = [(ROWS[k] * WIDTHS[k] // 128, 128) for k in (2, 3, 4)]
    slab = (TOK, GROUPS, 16, D)
    group = (GROUPS, TOK, 16, D)
    outs = [(s, f32) for s in flat] + [
        (group, bf16),
        ((S_ROWS, D), f32),
        ((2, D, 3 * D), bf16),
        ((2, D, D), bf16),
        ((16, D), f32),
        ((16, D), f32),
    ]
    return pl.pallas_call(
        functools.partial(back_kernel, units),
        out_shape=[jax.ShapeDtypeStruct(s, t) for s, t in outs],
        in_specs=[anywhere] * 2 + [vmem] * 4 + [anywhere] * 10,
        out_specs=[vmem] * 5 + [anywhere] + [vmem] * 3,
        scratch_shapes=scatter_scratch(units)
        + [
            pltpu.VMEM((32, 24, D), bf16),
            pltpu.VMEM((S_ROWS, D), bf16),
            pltpu.VMEM((S_ROWS, 3 * D), bf16),
            pltpu.VMEM((S_ROWS, D), bf16),
            pltpu.VMEM((D, 3 * D), bf16),
            pltpu.VMEM(group, bf16),
            pltpu.VMEM((T_ROWS, D), bf16),
            pltpu.VMEM((T_ROWS, 3 * D), bf16),
            pltpu.VMEM((T_ROWS, D), bf16),
            pltpu.VMEM((T_ROWS, D), bf16),
            pltpu.VMEM((2, D, D), bf16),
            pltpu.VMEM((D, 3 * D), bf16),
            pltpu.VMEM((S_ROWS, D), bf16),
            pltpu.VMEM((T_ROWS, D), bf16),
            pltpu.VMEM((T_ROWS, D), bf16),
            pltpu.VMEM((T_ROWS, 3 * D), bf16),
            pltpu.VMEM((D, S_ROWS), bf16),
            pltpu.VMEM((D, T_ROWS), bf16),
            pltpu.VMEM((T_ROWS, D), f32),
            pltpu.VMEM(slab, bf16),
            pltpu.VMEM(group, bf16),
            pltpu.SemaphoreType.DMA((13,)),
        ]
        + exchange_sems()
        + scatter_sems(len(units)),
        compiler_params=pltpu.CompilerParams(
            collective_id=1, has_side_effects=True, vmem_limit_bytes=VMEM_LIMIT
        ),
    )(*parts, d_after_s, after_t, affine, spatial, *saved_s, entry, *saved_t, temporal)


HOME_AT = 4
HOME_END = 24


def rest_kernel(units, *refs):
    parts = dict(zip((0, 1), refs[:2]))
    norms = refs[2:5]
    sent, d_after_t = refs[5:7]
    grads = dict(zip((0, 1), refs[7:9]))
    affine_out, input_gradient = refs[9:11]
    pos = 11
    pools = []
    for i in range(5):
        pools.append(refs[pos : pos + len(units)])
        pos += len(units)
    parts[AFFINE] = refs[pos]
    inbox, home_sems = refs[pos + 1], refs[pos + 2 : pos + 5]
    sems = refs[pos + 5 :]
    greet()
    flight = Flight()
    home = Exchange(lambda s: sent.at[:, s], lambda s: inbox.at[s], home_sems, flight)
    finals = finals_of(grads, affine_out)
    steps = scatter_steps(
        units, parts, *pools, sems, lambda u, total: finals(units[u], total)
    )
    begin = steps[0]

    def begin_after(u):
        if units[u][0] == AFFINE:
            part_affine(norms, parts[AFFINE])
        begin(u)

    def receive():
        home.wait()
        for f in range(2):

            def put(start, size, rows, f=f):
                at = f * S_PAD + start
                input_gradient[f, start : start + size, :] = d_after_t[at : at + size, :] + rows

            unpack(inbox, f, put)

    calls = full_kernel_steps(units, (begin_after,) + steps[1:5], (0, 2, 3, 4, 5), 0, len(units) + 5)
    calls.insert(HOME_AT, home.start)
    calls.insert(HOME_END, receive)
    for call in calls:
        call()
    steps[5]()
    flight.drain()


def scatter_rest(parts, norms, sent, d_after_t):
    units = units_of(ORDER_REST)
    vmem = pl.BlockSpec(memory_space=pltpu.VMEM)
    flat = [(ROWS[k] * WIDTHS[k] // 128, 128) for k in (0, 1)]
    return pl.pallas_call(
        functools.partial(rest_kernel, units),
        out_shape=[jax.ShapeDtypeStruct(s, jnp.float32) for s in flat]
        + [
            jax.ShapeDtypeStruct((16, 128), jnp.float32),
            jax.ShapeDtypeStruct((2, PATCHES, D), jnp.float32),
        ],
        in_specs=[pl.BlockSpec(memory_space=pl.ANY)] * 2 + [vmem] * 5,
        out_specs=[vmem] * 4,
        scratch_shapes=scatter_scratch(units)
        + [pltpu.VMEM((32, 16, 128), jnp.bfloat16)]
        + [pltpu.VMEM((TOK, GROUPS, 16, D), jnp.bfloat16)]
        + exchange_sems()
        + scatter_sems(len(units)),
        compiler_params=pltpu.CompilerParams(
            collective_id=2, has_side_effects=True, vmem_limit_bytes=VMEM_LIMIT
        ),
    )(*parts, *norms, sent, d_after_t)


def update_kernel(*refs):
    for k in range(5):
        weights, moment, square = (refs[5 + 3 * k + i][...] for i in range(3))
        adamw_rows(RATES[k], weights, moment, square, refs[k][...], refs[20 + 3 * k : 23 + 3 * k])


def update(grads, states):
    steps = 6
    blocks = [pl.BlockSpec((g.shape[0] // steps, 128), lambda i: (i, 0)) for g in grads]
    triples = [b for b in blocks for _ in range(3)]
    return pl.pallas_call(
        update_kernel,
        grid=(steps,),
        out_shape=[jax.ShapeDtypeStruct(s.shape, jnp.float32) for s in states],
        in_specs=blocks + triples,
        out_specs=triples,
    )(*grads, *states)


def on_device(
    frames,
    cotangent,
    entry_weights,
    entry_momentum,
    entry_variance,
    temporal_weights,
    temporal_momentum,
    temporal_variance,
    spatial_weights,
    spatial_momentum,
    spatial_variance,
    widen_weights,
    widen_momentum,
    widen_variance,
    narrow_weights,
    narrow_momentum,
    narrow_variance,
    norm_affine,
    affine_momentum,
    affine_variance,
):
    masters = (entry_weights, temporal_weights, spatial_weights, widen_weights, narrow_weights)
    block = jnp.pad(low(norm_affine).reshape(6, EACH), ((0, 10), (0, 128 - EACH)))
    found = forward(masters, block, frames[0])
    entry, temporal, spatial, widen, narrow = found[:5]
    entry = entry.reshape(2, D, 3 * D)
    temporal = temporal.reshape(2, D, D)
    spatial = spatial.reshape(D, D)
    widen = widen.reshape(D, HID)
    narrow = narrow.reshape(HID, D)
    affine, patch, normed_t, merged_t, mixed_t, first_t = found[5:11]
    after_t, normed_s, merged_s, mixed_s, after_s, lowered = found[11:17]
    result, narrow_grad, widen_grad, d_after_s, norm_m = mlp(
        lowered, after_s, cotangent[0], widen, narrow, affine
    )
    found = backward(
        (widen_grad.reshape(32, -1, HID), narrow_grad.reshape(32, -1, D)),
        d_after_s,
        after_t,
        affine,
        spatial,
        entry,
        temporal,
        (normed_s, merged_s, mixed_s),
        (patch, normed_t, merged_t, mixed_t, first_t),
    )
    spatial_sum, widen_sum, narrow_sum = found[:3]
    sent, d_after_t, d_entry, d_temporal, norm_s, norm_t = found[3:9]
    entry_sum, temporal_sum, affine_sum, input_gradient = scatter_rest(
        (d_entry.reshape(32, -1, 3 * D), d_temporal.reshape(32, -1, D)),
        (norm_t, norm_s, norm_m),
        sent,
        d_after_t,
    )
    updated = update(
        (entry_sum, temporal_sum, spatial_sum, widen_sum, narrow_sum),
        (
            entry_weights,
            entry_momentum,
            entry_variance,
            temporal_weights,
            temporal_momentum,
            temporal_variance,
            spatial_weights,
            spatial_momentum,
            spatial_variance,
            widen_weights,
            widen_momentum,
            widen_variance,
            narrow_weights,
            narrow_momentum,
            narrow_variance,
        ),
    )
    affine_sum = affine_sum[:6, :EACH].reshape(2, 3, EACH)
    affine_new = adamw(norm_affine, affine_momentum, affine_variance, affine_sum, 0.5)
    return (
        result[None],
        input_gradient[None],
        *updated,
        affine_new[0],
        affine_new[1],
        affine_new[2][:, 0:2],
        affine_new[2][:, 2],
    )

def solution(mesh):
    return jax.shard_map(
        on_device if mesh.shape["clip"] == 8 and mesh.shape["tok"] == TOK else on_any,
        mesh=mesh,
        in_specs=(
            P("clip", "tok", None, None),
            P("clip", "tok", None, None),
            P(("clip", "tok"), None),
            P(("clip", "tok"), None),
            P(("clip", "tok"), None),
            P(("clip", "tok"), None),
            P(("clip", "tok"), None),
            P(("clip", "tok"), None),
            P(("clip", "tok"), None),
            P(("clip", "tok"), None),
            P(("clip", "tok"), None),
            P(("clip", "tok"), None),
            P(("clip", "tok"), None),
            P(("clip", "tok"), None),
            P(("clip", "tok"), None),
            P(("clip", "tok"), None),
            P(("clip", "tok"), None),
            P(None, None, ("clip", "tok")),
            P(None, None, ("clip", "tok")),
            P(None, None, ("clip", "tok")),
        ),
        out_specs=(
            P("clip", "tok", None, None),
            P("clip", "tok", None, None),
            P(("clip", "tok"), None),
            P(("clip", "tok"), None),
            P(("clip", "tok"), None),
            P(("clip", "tok"), None),
            P(("clip", "tok"), None),
            P(("clip", "tok"), None),
            P(("clip", "tok"), None),
            P(("clip", "tok"), None),
            P(("clip", "tok"), None),
            P(("clip", "tok"), None),
            P(("clip", "tok"), None),
            P(("clip", "tok"), None),
            P(("clip", "tok"), None),
            P(("clip", "tok"), None),
            P(("clip", "tok"), None),
            P(None, None, ("clip", "tok")),
            P(None, None, ("clip", "tok")),
            P(None, None, ("clip", "tok")),
            P(None, ("clip", "tok")),
        ),
        check_vma=False,
    )
```
